32 devices in a mesh: gx: 2 (over y), gy: 4 (over z), lev: 4 (over x, core).
Axes of the slice: x: 2, y: 2, z: 4, core: 2. Of those that a mesh axis runs over, the one named last changes fastest.
Arguments:
- wind_x: float32 [128, 64, 512], P('lev', 'gx', 'gy'), may hold values from -6 to 6
- wind_y: float32 [128, 64, 512], P('lev', 'gx', 'gy'), may hold values from -6 to 6
- wind_z: float32 [128, 64, 512], P('lev', 'gx', 'gy'), may hold values from -6 to 6
- pressure: float32 [128, 64, 512], P('lev', 'gx', 'gy'), may hold values from -6 to 6
- jacobian: float32 [64, 512], P('gx', 'gy'), may hold values from 0.5 to 2
- slope_x: float32 [64, 512], P('gx', 'gy'), may hold values from -3 to 3
- slope_y: float32 [64, 512], P('gx', 'gy'), may hold values from -3 to 3
- stiffness: float32 [128, 64, 512], P('lev', 'gx', 'gy'), may hold values from 10 to 1000
Outputs:
- wind_x_out: float32 [128, 64, 512], P('lev', 'gx', 'gy')
- wind_y_out: float32 [128, 64, 512], P('lev', 'gx', 'gy')
- wind_z_out: float32 [128, 64, 512], P('lev', 'gx', 'gy')
- pressure_out: float32 [128, 64, 512], P('lev', 'gx', 'gy')
The draws below stay inside these ranges and needn't reach their ends.
All inputs are finite; a program needn't handle non-finite values.
Results may differ from the reference program's by a relative error of at most 0.000096.
Values sent between devices are 32-bit elements; how exact they have to be, the bound alone decides.
No kernel may reach another device: no remote copies, remote signals or barrier semaphores. Data moves between devices by JAX's collectives and lax.ppermute only.
A program may use at most 64 MiB of HBM per device.

```python
import math
import jax
import jax.numpy as jnp
from jax import lax

SUBSTEPS = 2
NX = 64
NY = 512
NZ = 128


def steps_of(key, extent, cuts, least, high):
    gain = 1.0
    for position, parts in cuts:
        draws = jax.random.uniform(jax.random.fold_in(jax.random.fold_in(key, 6), position), (parts,), jnp.float32, least / len(cuts), high / len(cuts))
        gain = gain * jnp.repeat(jnp.exp(draws), extent[position] // parts).reshape((-1,) + (1,) * (len(extent) - 1 - position))
    return gain


def centred(rng, dims, width, bound, shards=(), dtype=jnp.bfloat16):
    array = width * jax.random.normal(rng, dims, jnp.float32)
    if shards:
        array = array * steps_of(rng, dims, shards, -0.22, 0.18)
    return jnp.clip(array, -bound, bound).astype(dtype)


def setup_inputs(seed: int = 0) -> dict:
    splits = jax.random.split(jax.random.key(seed), 9)
    return {
        "wind_x": centred(splits[0], (NZ, NX, NY), 1.0, 6.0, ((0, 4), (1, 2), (2, 4)), jnp.float32),
        "wind_y": centred(splits[1], (NZ, NX, NY), 1.0, 6.0, ((0, 4), (1, 2), (2, 4)), jnp.float32),
        "wind_z": centred(splits[2], (NZ, NX, NY), 1.0, 6.0, ((0, 4), (1, 2), (2, 4)), jnp.float32),
        "pressure": centred(splits[3], (NZ, NX, NY), 1.0, 6.0, ((0, 4), (1, 2), (2, 4)), jnp.float32),
        "jacobian": jnp.clip(jnp.exp(math.log(2.0) - 1.3862944 * jax.random.uniform(splits[4], (NX, NY), jnp.float32) ** steps_of(splits[4], (NX, NY), ((0, 2), (1, 4)), -0.2, 0.2)), 0.5, 2.0),
        "slope_x": centred(splits[5], (NX, NY), 0.5, 3.0, ((0, 2), (1, 4)), jnp.float32),
        "slope_y": centred(splits[6], (NX, NY), 0.5, 3.0, ((0, 2), (1, 4)), jnp.float32),
        "stiffness": jnp.clip(jnp.exp(math.log(1000.0) - 4.6051702 * jax.random.uniform(splits[7], (NZ, NX, NY), jnp.float32) ** steps_of(splits[7], (NZ, NX, NY), ((0, 4), (1, 2), (2, 4)), -0.2, 0.2)), 10.0, 1000.0),
    }


grad_coef = 0.35
div_coef = 0.35
vert_coef = 0.25


def diff_four(field, axis):
    return (jnp.roll(field, 2, axis) - 8.0 * jnp.roll(field, 1, axis) + 8.0 * jnp.roll(field, -1, axis) - jnp.roll(field, -2, axis)) / 12.0


def vert_diff(field):
    padded = jnp.pad(field, ((1, 1), (0, 0), (0, 0)))
    return padded[2:] - padded[:-2]


def column_thomas(stiffness, source):
    def forward(carry, level):
        ratio, value = carry
        coef, rhs = level
        denom = 1.0 + 2.0 * coef + coef * ratio
        new_ratio = -coef / denom
        new_value = (rhs + coef * value) / denom
        return (new_ratio, new_value), (new_ratio, new_value)

    start = jnp.zeros(source.shape[1:], jnp.float32)
    _, (ratios, values) = lax.scan(forward, (start, start), (stiffness, source))

    def backward(upper, level):
        ratio, value = level
        result = value - ratio * upper
        return result, result

    _, solved = lax.scan(backward, start, (ratios, values), reverse=True)
    return solved


def reference(wind_x, wind_y, wind_z, pressure, jacobian, slope_x, slope_y, stiffness):
    for substep in range(SUBSTEPS):
        new_x = wind_x - grad_coef * diff_four(pressure, 1)
        new_y = wind_y - grad_coef * diff_four(pressure, 2)
        divergence = (diff_four(jacobian * new_x, 1) + diff_four(jacobian * new_y, 2)) / jacobian
        pres_star = pressure - div_coef * divergence
        source = wind_z + slope_x * new_x + slope_y * new_y - vert_coef * vert_diff(pres_star)
        wind_z = column_thomas(stiffness, source)
        pressure = pres_star - vert_coef * vert_diff(wind_z)
        wind_x, wind_y = new_x, new_y
    return (wind_x, wind_y, wind_z, pressure)
```

```python
import functools

import jax
import jax.numpy as jnp
from jax import lax
from jax.experimental import pallas as pl
from jax.experimental.pallas import tpu as pltpu
from jax.sharding import PartitionSpec as P

SUBSTEPS = 2

grad_coef = 0.35
div_coef = 0.35
vert_coef = 0.25

CG = grad_coef / 12.0
CD = div_coef / 12.0
ROWS = 8
SLOT = 4


def lane_index():
    return lax.broadcasted_iota(jnp.int32, (ROWS, 128), 1)


def row_index():
    return lax.broadcasted_iota(jnp.int32, (ROWS, 128), 0)


def only(mask, value):
    return jnp.where(mask, jnp.float32(value), jnp.float32(0.0))


def tiles_of(ref, level, count):
    return [ref[level, ROWS * t : ROWS * (t + 1), :] for t in range(count)]


def planes_of(ref, count):
    return [ref[ROWS * t : ROWS * (t + 1), :] for t in range(count)]


def put_tiles(ref, level, tiles):
    for t, tile in enumerate(tiles):
        ref[level, ROWS * t : ROWS * (t + 1), :] = tile


def put_planes(ref, tiles):
    for t, tile in enumerate(tiles):
        ref[ROWS * t : ROWS * (t + 1), :] = tile


class Stencil:
    def __init__(self, scale):
        lane, row = lane_index(), row_index()
        self.lane, self.row = lane, row
        self.scale = scale
        self.back2 = only(lane >= 2, scale)
        self.back1 = only(lane >= 1, -8.0 * scale)
        self.ahead1 = only(lane < 127, 8.0 * scale)
        self.ahead2 = only(lane < 126, -scale)

    def along_y(self, tile):
        return (
            self.back2 * pltpu.roll(tile, 2, 1)
            + self.back1 * pltpu.roll(tile, 1, 1)
            + self.ahead1 * pltpu.roll(tile, 127, 1)
            + self.ahead2 * pltpu.roll(tile, 126, 1)
        )

    def moved(self, tiles, by):
        count = len(tiles)
        rolled = [pltpu.roll(tile, by % ROWS, 0) for tile in tiles]
        zero = jnp.zeros_like(tiles[0])
        out = []
        for t in range(count):
            if by > 0:
                other = rolled[t - 1] if t > 0 else zero
                out.append(jnp.where(self.row < by, other, rolled[t]))
            else:
                other = rolled[t + 1] if t < count - 1 else zero
                out.append(jnp.where(self.row >= ROWS + by, other, rolled[t]))
        return out

    def along_x(self, tiles):
        back2, back1 = self.moved(tiles, 2), self.moved(tiles, 1)
        ahead1, ahead2 = self.moved(tiles, -1), self.moved(tiles, -2)
        return [
            self.scale * (b2 - a2) + (8.0 * self.scale) * (a1 - b1)
            for b2, b1, a1, a2 in zip(back2, back1, ahead1, ahead2)
        ]


def edge_of(tile, axis, place, near, cross, sign):
    size = 128 if axis == 1 else ROWS
    low = pltpu.roll(tile, 1, axis)
    high = pltpu.roll(tile, size - 1, axis)
    alpha = only(place < 2, sign * near) + only(place >= size - 2, near)
    beta = only(place == 1, cross)
    gamma = only(place == size - 2, sign * cross)
    return alpha * tile + beta * low + gamma * high


class Packer:
    def __init__(self):
        self.lane, self.row = lane_index(), row_index()

    def lanes(self, first, second):
        lane = self.lane
        far = jnp.where(lane < 64, pltpu.roll(second, 2, 1), pltpu.roll(second, 126, 1))
        return jnp.where((lane < 2) | (lane >= 126), first, far)

    def rows(self, first_low, first_high, second_low, second_high):
        row = self.row
        second = pltpu.roll(jnp.where(row < 4, second_low, second_high), 4, 0)
        first = jnp.where(row < 4, pltpu.roll(first_high, 2, 0), pltpu.roll(first_low, 6, 0))
        return jnp.where((row >= 2) & (row < 6), second, first)


def near_value(tile, axis, place, scale):
    size = 128 if axis == 1 else ROWS
    low = pltpu.roll(tile, 1, axis)
    high = pltpu.roll(tile, size - 1, axis)
    picked = jnp.where(place == 1, low, jnp.where(place == size - 2, high, tile))
    return scale * picked


def start_level(stencil, packer, level, pres, wind_x, wind_y, jac, low, high):
    lane, row = stencil.lane, stencil.row
    count = len(pres)
    new_y = [w - stencil.along_y(p) for w, p in zip(wind_y, pres)]
    new_x = [w - d for w, d in zip(wind_x, stencil.along_x(pres))]
    slot = lax.shift_right_logical(lane, 2)
    before = lax.rem(level + 31, 32)
    low_out, high_out = [], []
    for t in range(count):
        first = edge_of(pres[t], 1, lane, CG, 8.0 * CG, -1.0)
        second = edge_of(jac[t] * new_y[t], 1, lane, CD, 8.0 * CD, -1.0)
        packed = pltpu.roll(packer.lanes(first, second), SLOT * level, 1)
        low_out.append(jnp.where(slot == level, packed, low[t]))
        high_out.append(jnp.where(slot == before, packed, high[t]))
    last = count - 1
    rows = packer.rows(
        edge_of(pres[0], 0, row, CG, 8.0 * CG, -1.0),
        edge_of(pres[last], 0, row, CG, 8.0 * CG, -1.0),
        edge_of(jac[0] * new_x[0], 0, row, CD, 8.0 * CD, -1.0),
        edge_of(jac[last] * new_x[last], 0, row, CD, 8.0 * CD, -1.0),
    )
    return new_x, new_y, rows, low_out, high_out


def kernel_a(p_ref, wx_ref, wy_ref, jac_ref, nx_ref, ny_ref, rows_ref, low_ref, high_ref):
    levels, rows, _ = p_ref.shape
    count = rows // ROWS
    stencil, packer = Stencil(CG), Packer()
    lane, row = stencil.lane, stencil.row
    jac = planes_of(jac_ref, count)

    def step(level, carry):
        new_x, new_y, edge, low, high = start_level(
            stencil,
            packer,
            level,
            tiles_of(p_ref, level, count),
            tiles_of(wx_ref, level, count),
            tiles_of(wy_ref, level, count),
            jac,
            *carry,
        )
        put_tiles(nx_ref, level, new_x)
        put_tiles(ny_ref, level, new_y)
        rows_ref[level] = edge
        return low, high

    zeros = [jnp.zeros((ROWS, 128), jnp.float32)] * count
    low, high = lax.fori_loop(0, levels, step, (zeros, zeros))
    both = CG * CD
    static = [
        packer.lanes(
            edge_of(j, 1, lane, both, 64.0 * both, 1.0), near_value(j, 1, lane, -8.0 * both)
        )
        for j in jac
    ]
    put_tiles(low_ref, 0, low)
    put_tiles(high_ref, 0, high)
    put_tiles(low_ref, 1, static)
    put_tiles(high_ref, 1, static)
    rows_ref[levels] = packer.rows(
        edge_of(jac[0], 0, row, both, 64.0 * both, 1.0),
        edge_of(jac[-1], 0, row, both, 64.0 * both, 1.0),
        near_value(jac[0], 0, row, -8.0 * both),
        near_value(jac[-1], 0, row, -8.0 * both),
    )


def kernel_f(s_ref, r_ref, i_ref, q_ref, v_ref, stat_ref):
    levels, rows, _ = s_ref.shape

    def down(level, carry):
        excess, prod = carry
        rate = 1.0 / s_ref[level]
        excess = rate + excess
        inv = 1.0 / (1.0 + excess)
        prod = prod * inv
        r_ref[level] = rate
        i_ref[level] = inv
        q_ref[level] = prod
        return excess * inv, prod

    ones = jnp.ones((rows, 128), jnp.float32)
    lax.fori_loop(0, levels, down, (ones, ones))

    def up(step, value):
        level = levels - 1 - step
        value = q_ref[level] + i_ref[level] * value
        v_ref[level] = value
        return value

    first = lax.fori_loop(0, levels, up, jnp.zeros((rows, 128), jnp.float32))
    stat_ref[0] = first
    stat_ref[1] = q_ref[levels - 1]
    stat_ref[2] = i_ref[levels - 1]
    stat_ref[3] = r_ref[0]
    stat_ref[4] = r_ref[levels - 1]


def unpack_lanes(lane, low, high, level):
    turn = 128 - SLOT * level

    def placed(from_low, from_high):
        above = pltpu.roll(low, lax.rem(turn + from_low, 128), 1)
        below = pltpu.roll(high, lax.rem(turn + from_high, 128), 1)
        return jnp.where(lane < 2, below, jnp.where(lane >= 126, above, 0.0))

    return placed(126, 2), placed(124, 4)


def unpack_rows(row, tile):
    zero = jnp.zeros_like(tile)
    first = jnp.where(row < 2, tile, zero), jnp.where(row >= 6, tile, zero)
    near, far = pltpu.roll(tile, 6, 0), pltpu.roll(tile, 2, 0)
    second = jnp.where(row < 2, near, zero), jnp.where(row >= 6, far, zero)
    return first, second


def kernel_b(
    p_ref,
    nxz_ref,
    nyz_ref,
    wz_ref,
    jac_ref,
    sx_ref,
    sy_ref,
    r_ref,
    i_ref,
    v_ref,
    rows_ref,
    low_ref,
    high_ref,
    srows_ref,
    slow_ref,
    shigh_ref,
    nx_ref,
    ny_ref,
    ps_ref,
    y_ref,
    face_ref,
):
    levels, rows, _ = p_ref.shape
    count = rows // ROWS
    last = count - 1
    stencil = Stencil(CD)
    lane, row = stencil.lane, stencil.row
    jac = planes_of(jac_ref, count)
    inv_jac = [1.0 / j for j in jac]
    low = [low_ref[0, ROWS * t : ROWS * (t + 1), :] for t in range(count)]
    high = [high_ref[0, ROWS * t : ROWS * (t + 1), :] for t in range(count)]
    lane_stat = [
        unpack_lanes(
            lane,
            slow_ref[1, ROWS * t : ROWS * (t + 1), :],
            shigh_ref[1, ROWS * t : ROWS * (t + 1), :],
            0,
        )
        for t in range(count)
    ]
    row_self, row_cross = unpack_rows(row, srows_ref[levels])
    even_lane = (lane & 1) == 0
    even_row = (row & 1) == 0

    def cross(tile, axis, even, size):
        return jnp.where(even, pltpu.roll(tile, size - 1, axis), pltpu.roll(tile, 1, axis))

    def star(level):
        pres = tiles_of(p_ref, level, count)
        new_x = tiles_of(nxz_ref, level, count)
        new_y = tiles_of(nyz_ref, level, count)
        edge, flux = unpack_rows(row, rows_ref[level])
        new_x[0] = new_x[0] - edge[0]
        new_x[last] = new_x[last] - edge[1]
        lanes = [unpack_lanes(lane, low[t], high[t], level) for t in range(count)]
        new_y = [n - e[0] for n, e in zip(new_y, lanes)]
        put_tiles(nx_ref, level, new_x)
        put_tiles(ny_ref, level, new_y)
        total = stencil.along_x([j * n for j, n in zip(jac, new_x)])
        for side, t in ((0, 0), (1, last)):
            total[t] = (
                total[t]
                + flux[side]
                + row_self[side] * pres[t]
                + row_cross[side] * cross(pres[t], 0, even_row, ROWS)
            )
        stars, forces = [], []
        for t in range(count):
            spread = (
                total[t]
                + stencil.along_y(jac[t] * new_y[t])
                + lanes[t][1]
                + lane_stat[t][0] * pres[t]
                + lane_stat[t][1] * cross(pres[t], 1, even_lane, 128)
            )
            stars.append(pres[t] - inv_jac[t] * spread)
            part = slice(ROWS * t, ROWS * (t + 1))
            forces.append(
                wz_ref[level, part, :]
                + sx_ref[part, :] * new_x[t]
                + sy_ref[part, :] * new_y[t]
            )
        put_tiles(ps_ref, level, stars)
        return stars, forces

    def sweep(level, below, above, force, value, first):
        rate = tiles_of(r_ref, level, count)
        inv = tiles_of(i_ref, level, count)
        gain = tiles_of(v_ref, level, count)
        values, firsts = [], []
        for t in range(count):
            rhs = rate[t] * (force[t] - vert_coef * (above[t] - below[t]))
            firsts.append(first[t] + gain[t] * rhs)
            values.append((rhs + value[t]) * inv[t])
        put_tiles(y_ref, level, values)
        return values, firsts

    zeros = [jnp.zeros((ROWS, 128), jnp.float32)] * count
    here, force = star(0)
    put_tiles(face_ref, 2, here)

    def step(level, carry):
        below, here, force, value, first = carry
        above, force_next = star(level)
        value, first = sweep(level - 1, below, above, force, value, first)
        return here, above, force_next, value, first

    below, here, force, value, first = lax.fori_loop(
        1, levels, step, (zeros, here, force, zeros, zeros)
    )
    value, first = sweep(levels - 1, below, zeros, force, value, first)
    put_tiles(face_ref, 0, first)
    put_tiles(face_ref, 1, value)
    put_tiles(face_ref, 3, here)


def reduced(blocks, mine, face, stat):
    faces = [face(j) for j in range(blocks)]
    stats = [stat(j) for j in range(blocks)]
    up = [
        faces[j][1] + vert_coef * stats[j + 1][3] * faces[j][3] if j < blocks - 1 else None
        for j in range(blocks)
    ]
    down = [
        faces[j][0] - vert_coef * stats[j - 1][4] * faces[j][2] if j > 0 else None
        for j in range(blocks)
    ]
    base, slope = [up[0]], [stats[0][2]]
    scale, known = [None], [None]
    for j in range(1, blocks):
        near, link, far = stats[j][0], stats[j][1], stats[j][2]
        scale.append(1.0 / (1.0 - near * slope[j - 1]))
        known.append(scale[j] * (down[j] + near * base[j - 1]))
        if j < blocks - 1:
            base.append(up[j] + link * (base[j - 1] + slope[j - 1] * known[j]))
            slope.append(far + link * link * slope[j - 1] * scale[j])
    zero = jnp.zeros_like(faces[0][0])
    above = [None] * blocks + [zero]
    below = [zero] + [None] * blocks
    for j in range(blocks - 1, 0, -1):
        above[j] = known[j] + scale[j] * stats[j][1] * above[j + 1]
        below[j] = base[j - 1] + slope[j - 1] * above[j]
    lower, upper, under, over = zero, zero, zero, zero
    for j in range(blocks):
        here = mine == j
        if j > 0:
            lower = jnp.where(here, below[j], lower)
            under = jnp.where(
                here, below[j] - vert_coef * stats[j][3] * faces[j - 1][3], under
            )
        if j < blocks - 1:
            upper = jnp.where(here, above[j + 1], upper)
            over = jnp.where(
                here, above[j + 1] + vert_coef * stats[j][4] * faces[j + 1][2], over
            )
    return lower, upper, under, over


def boundary(blocks, mine, count, face_refs, stat_refs):
    def solve(t):
        part = slice(ROWS * t, ROWS * (t + 1))

        def read(refs, planes):
            own = [
                [ref[k, part, :] for k in range(planes)] for ref in refs
            ]

            def block(j):
                out = []
                for k in range(planes):
                    value = own[0][k]
                    for shift in range(1, blocks):
                        value = jnp.where(mine == (j ^ shift), own[shift][k], value)
                    out.append(value)
                return out

            return block

        return reduced(blocks, mine, read(face_refs, 4), read(stat_refs, 5))

    parts = [solve(t) for t in range(count)]
    return [[part[k] for part in parts] for k in range(4)]


def finish(blocks, count, levels, y_ref, q_ref, i_ref, ps_ref, x_ref, p_ref, face_refs, stat_refs, use):
    mine = lax.axis_index("lev")
    lower, upper, under, over = boundary(blocks, mine, count, face_refs, stat_refs)

    def solved(level, above):
        value = tiles_of(y_ref, level, count)
        prod = tiles_of(q_ref, level, count)
        inv = tiles_of(i_ref, level, count)
        out = [y + q * u + i * a for y, q, u, i, a in zip(value, prod, lower, inv, above)]
        put_tiles(x_ref, level, out)
        return out

    def pressed(level, above, below, state):
        star = tiles_of(ps_ref, level, count)
        pres = [s - vert_coef * (a - b) for s, a, b in zip(star, above, below)]
        put_tiles(p_ref, level, pres)
        return use(level, pres, state)

    def step(index, carry):
        above, here, state = carry
        level = levels - 2 - index
        below = solved(level, here)
        state = pressed(level + 1, above, below, state)
        return here, below, state

    top = solved(levels - 1, upper)
    zeros = [jnp.zeros((ROWS, 128), jnp.float32)] * count
    above, here, state = lax.fori_loop(0, levels - 1, step, (over, top, (zeros, zeros)))
    return pressed(0, above, under, state)


def kernel_c(blocks, y_ref, q_ref, i_ref, ps_ref, wx_ref, wy_ref, jac_ref, *refs):
    face_refs, stat_refs = refs[:blocks], refs[blocks : 2 * blocks]
    x_ref, p_ref, nx_ref, ny_ref, rows_ref, low_ref, high_ref = refs[2 * blocks :]
    levels, rows, _ = y_ref.shape
    count = rows // ROWS
    stencil, packer = Stencil(CG), Packer()

    def use(level, pres, state):
        new_x, new_y, edge, low, high = start_level(
            stencil,
            packer,
            level,
            pres,
            tiles_of(wx_ref, level, count),
            tiles_of(wy_ref, level, count),
            planes_of(jac_ref, count),
            *state,
        )
        put_tiles(nx_ref, level, new_x)
        put_tiles(ny_ref, level, new_y)
        rows_ref[level] = edge
        return low, high

    low, high = finish(
        blocks, count, levels, y_ref, q_ref, i_ref, ps_ref, x_ref, p_ref, face_refs, stat_refs, use
    )
    put_tiles(low_ref, 0, low)
    put_tiles(high_ref, 0, high)


def kernel_d(blocks, y_ref, q_ref, i_ref, ps_ref, *refs):
    face_refs, stat_refs = refs[:blocks], refs[blocks : 2 * blocks]
    x_ref, p_ref = refs[2 * blocks :]
    levels, rows, _ = y_ref.shape
    finish(
        blocks,
        rows // ROWS,
        levels,
        y_ref,
        q_ref,
        i_ref,
        ps_ref,
        x_ref,
        p_ref,
        face_refs,
        stat_refs,
        lambda level, pres, state: state,
    )


def call(kernel, name, shapes, *args):
    space = pl.BlockSpec(memory_space=pltpu.VMEM)
    size = sum(a.size for a in args) + sum(functools.reduce(lambda a, b: a * b, s) for s in shapes)
    return pl.pallas_call(
        kernel,
        out_shape=[jax.ShapeDtypeStruct(s, jnp.float32) for s in shapes],
        in_specs=[space] * len(args),
        out_specs=[space] * len(shapes),
        compiler_params=pltpu.CompilerParams(vmem_limit_bytes=32 * 1024 * 1024),
        cost_estimate=pl.CostEstimate(
            flops=8 * size, bytes_accessed=4 * size, transcendentals=0
        ),
        name=name,
    )(*args)


def swap(value, axis, partner):
    count = lax.axis_size(axis)
    return lax.ppermute(value, axis, [(i, partner(i)) for i in range(count)])


def exchange_rows(rows):
    count = lax.axis_size("gx")
    if count == 2:
        return swap(rows, "gx", lambda i: 1 - i)
    up = swap(rows[:, : ROWS // 2], "gx", lambda i: (i + 1) % count)
    down = swap(rows[:, ROWS // 2 :], "gx", lambda i: (i - 1) % count)
    return jnp.concatenate([up, down], axis=1)


def exchange_lanes(low, high):
    count = lax.axis_size("gy")
    from_above = swap(low, "gy", lambda i: (i - 1) % count)
    from_below = swap(high, "gy", lambda i: (i + 1) % count)
    return from_above, from_below


def gather_levels(planes):
    count = lax.axis_size("lev")
    return [planes] + [
        swap(planes, "lev", lambda i, shift=shift: i ^ shift) for shift in range(1, count)
    ]


def local(wind_x, wind_y, wind_z, pressure, jacobian, slope_x, slope_y, stiffness):
    field = wind_x.shape
    levels, rows, lanes = field
    blocks = lax.axis_size("lev")
    plane = (rows, lanes)
    assert lanes == 128 and levels * SLOT == 128 and rows % ROWS == 0
    assert blocks & (blocks - 1) == 0

    nxz, nyz, edge, low, high = call(
        kernel_a,
        "start",
        [field, field, (levels + 1, ROWS, lanes), (2,) + plane, (2,) + plane],
        pressure,
        wind_x,
        wind_y,
        jacobian,
    )
    edge = exchange_rows(edge)
    low, high = exchange_lanes(low, high)
    static_edges = (edge, low, high)
    rate, inv, prod, gain, stat = call(
        kernel_f, "factor", [field, field, field, field, (5,) + plane], stiffness
    )
    stats = gather_levels(stat)
    for substep in range(SUBSTEPS):
        new_x, new_y, star, value, face = call(
            kernel_b,
            "sweep",
            [field, field, field, field, (4,) + plane],
            pressure,
            nxz,
            nyz,
            wind_z,
            jacobian,
            slope_x,
            slope_y,
            rate,
            inv,
            gain,
            edge,
            low,
            high,
            *static_edges,
        )
        faces = gather_levels(face)
        if substep < SUBSTEPS - 1:
            wind_z, pressure, nxz, nyz, edge, low, high = call(
                functools.partial(kernel_c, blocks),
                "finish",
                [field, field, field, field, (levels, ROWS, lanes), (1,) + plane, (1,) + plane],
                value,
                prod,
                inv,
                star,
                new_x,
                new_y,
                jacobian,
                *faces,
                *stats,
            )
            edge = exchange_rows(edge)
            low, high = exchange_lanes(low, high)
        else:
            wind_z, pressure = call(
                functools.partial(kernel_d, blocks),
                "last",
                [field, field],
                value,
                prod,
                inv,
                star,
                *faces,
                *stats,
            )
    return new_x, new_y, wind_z, pressure


def solution(mesh):
    field = P("lev", "gx", "gy")
    column = P("gx", "gy")
    return jax.shard_map(
        local,
        mesh=mesh,
        in_specs=(field,) * 4 + (column,) * 3 + (field,),
        out_specs=(field,) * 4,
        check_vma=False,
    )
```

```python
import functools

import jax
import jax.numpy as jnp
from jax import lax
from jax.experimental import pallas as pl
from jax.experimental.pallas import tpu as pltpu
from jax.sharding import PartitionSpec as P

SUBSTEPS = 2

grad_coef = 0.35
div_coef = 0.35
vert_coef = 0.25

CG = grad_coef / 12.0
CD = div_coef / 12.0
ROWS = 8
SLOT = 4
UNROLL = 4


def lane_index():
    return lax.broadcasted_iota(jnp.int32, (ROWS, 128), 1)


def row_index():
    return lax.broadcasted_iota(jnp.int32, (ROWS, 128), 0)


def only(mask, value):
    return jnp.where(mask, jnp.float32(value), jnp.float32(0.0))


def tiles_of(ref, level, count):
    return [ref[level, ROWS * t : ROWS * (t + 1), :] for t in range(count)]


def planes_of(ref, count):
    return [ref[ROWS * t : ROWS * (t + 1), :] for t in range(count)]


def put_tiles(ref, level, tiles):
    for t, tile in enumerate(tiles):
        ref[level, ROWS * t : ROWS * (t + 1), :] = tile


def put_planes(ref, tiles):
    for t, tile in enumerate(tiles):
        ref[ROWS * t : ROWS * (t + 1), :] = tile


class Edge:
    def __init__(self, place, axis, held):
        self.place, self.axis, self.held = place, axis, held
        self.size = place.shape[axis]

    def at(self, places):
        total = None
        for position, value in places.items():
            if position in self.held:
                term = only(self.place == position, value)
                total = term if total is None else total + term
        return total

    def shifted(self, field, by):
        return field if by == 0 else pltpu.roll(field, (-by) % self.size, self.axis)

    def mix(self, field, table):
        total = None
        for by, places in table.items():
            weight = self.at(places)
            if weight is not None:
                term = weight * self.shifted(field, by)
                total = term if total is None else total + term
        return total

    def payload(self, pres, wind, jac):
        partial = self.mix(
            pres,
            {
                1: {0: 8.0, 1: 8.0, 6: 8.0},
                2: {0: -1.0, 1: -1.0},
                -1: {1: -8.0, 6: -8.0, 7: -8.0},
                -2: {6: 1.0, 7: 1.0},
            },
        )
        flux = jac * (wind - CG * partial)
        outer = self.mix(pres, {0: {0: 1.0, 1: 1.0, 6: 1.0, 7: 1.0}})
        return outer + self.mix(flux, {-2: {2: 1.0, 3: 1.0}, 2: {4: 1.0, 5: 1.0}})

    def correct(self, delta, pres, jac, delta_jac):
        grad = self.mix(
            delta, {2: {0: 1.0, 1: 1.0}, 3: {0: -8.0}, -2: {6: -1.0, 7: -1.0}, -3: {7: 8.0}}
        )
        wind = CG * grad
        own = -(jac * wind)
        far = self.mix(delta, {0: {0: 1.0, 1: 1.0, 6: 1.0, 7: 1.0}}) + CG * delta_jac * self.mix(
            pres, {0: {0: 1.0, 1: 1.0, 6: -1.0, 7: -1.0}, -1: {1: -8.0}, 1: {6: 8.0}}
        )
        spread = (
            self.mix(far, {0: {0: 1.0, 1: 1.0, 6: -1.0, 7: -1.0}})
            + self.mix(far - own, {1: {0: -8.0}, -1: {7: 8.0}})
            + self.mix(
                own,
                {
                    -1: {1: -8.0, 2: -8.0},
                    -2: {2: 1.0, 3: 1.0},
                    1: {5: 8.0, 6: 8.0},
                    2: {4: -1.0, 5: -1.0},
                },
            )
        )
        return wind, CD * spread / jac


LOW, HIGH = (0, 1, 2, 3), (4, 5, 6, 7)


def row_edge():
    return Edge(row_index(), 0, LOW + HIGH)


def lane_edge(held):
    return Edge((lane_index() & 3) + held[0], 1, held)


def both_ends(tiles):
    return jnp.where(row_index() < 4, tiles[0], tiles[-1])


def spread_slots(tile, low):
    lane = lane_index()
    if low:
        out = jnp.where(lane < SLOT, tile, 0.0)
    else:
        out = pltpu.roll(jnp.where(lane >= 128 - SLOT, tile, 0.0), SLOT, 1)
    by = SLOT
    while by < 128:
        out = out + pltpu.roll(out, by, 1)
        by *= 2
    return out


class Packer:
    def __init__(self, count):
        self.slot = lax.shift_right_logical(lane_index(), 2)
        self.start = [jnp.zeros((ROWS, 128), jnp.float32)] * (2 * count)
        self.count = count

    def add(self, level, tiles, state):
        before = lax.rem(level + 31, 32)
        rolled = [pltpu.roll(tile, SLOT * level, 1) for tile in tiles]
        low = [jnp.where(self.slot == level, r, s) for r, s in zip(rolled, state)]
        high = [jnp.where(self.slot == before, r, s) for r, s in zip(rolled, state[self.count :])]
        return low + high

    def done(self, state):
        return state[: self.count], [pltpu.roll(s, SLOT, 1) for s in state[self.count :]]


class Closed:
    def __init__(self):
        self.row = row_index()

    def along_y(self, tile):
        pair = tile - pltpu.roll(tile, 126, 1)
        return (pltpu.roll(pair, 2, 1) + pair) - 8.0 * pltpu.roll(pair, 1, 1)

    def moved(self, tiles, by):
        count = len(tiles)
        rolled = [pltpu.roll(tile, by % ROWS, 0) for tile in tiles]
        if by > 0:
            return [jnp.where(self.row < by, rolled[t - 1], rolled[t]) for t in range(count)]
        return [
            jnp.where(self.row >= ROWS + by, rolled[(t + 1) % count], rolled[t])
            for t in range(count)
        ]

    def along_x(self, tiles):
        pair = [f - m for f, m in zip(tiles, self.moved(tiles, -2))]
        return [
            (two + here) - 8.0 * one
            for two, here, one in zip(self.moved(pair, 2), pair, self.moved(pair, 1))
        ]


def lane_payload(pres, wind, jac):
    low, high = lane_edge(LOW), lane_edge(HIGH)
    down = [
        low.payload(p, w, spread_slots(j, True)) for p, w, j in zip(pres[0], wind[0], jac)
    ]
    up = [
        high.payload(p, w, spread_slots(j, False)) for p, w, j in zip(pres[1], wind[1], jac)
    ]
    return down, up


def pack_levels(ref, count, levels):
    packer = Packer(count)

    def step(level, state):
        return packer.add(level, tiles_of(ref, level, count), state)

    return packer.done(lax.fori_loop(0, levels, step, packer.start, unroll=UNROLL))


def kernel_a(p_ref, wx_ref, wy_ref, jac_ref, rows_ref, down_ref, up_ref, pp_ref):
    levels, rows, _ = p_ref.shape
    count = rows // ROWS
    jac = planes_of(jac_ref, count)
    ends = both_ends(jac)
    edge = row_edge()

    def step(level, state):
        rows_ref[level] = edge.payload(
            both_ends(tiles_of(p_ref, level, count)),
            both_ends(tiles_of(wx_ref, level, count)),
            ends,
        )
        return state

    lax.fori_loop(0, levels, step, 0, unroll=UNROLL)
    rows_ref[levels] = ends
    pres = pack_levels(p_ref, count, levels)
    wind = pack_levels(wy_ref, count, levels)
    down, up = lane_payload(pres, wind, jac)
    put_tiles(down_ref, 0, down)
    put_tiles(up_ref, 0, up)
    put_tiles(down_ref, 1, [spread_slots(j, True) for j in jac])
    put_tiles(up_ref, 1, [spread_slots(j, False) for j in jac])
    put_tiles(pp_ref, 0, pres[0])
    put_tiles(pp_ref, 1, pres[1])


def kernel_n(wy_ref, pw_ref):
    levels, rows, _ = wy_ref.shape
    count = rows // ROWS
    wind = pack_levels(wy_ref, count, levels)
    put_tiles(pw_ref, 0, wind[0])
    put_tiles(pw_ref, 1, wind[1])


def kernel_m(p_ref, wx_ref, wy_ref, jac_ref, nx_ref, ny_ref, ps_ref):
    levels, rows, _ = p_ref.shape
    count = rows // ROWS
    jac = planes_of(jac_ref, count)
    inv_jac = [CD / j for j in jac]
    closed = Closed()

    def step(level, state):
        pres = tiles_of(p_ref, level, count)
        wind_x = tiles_of(wx_ref, level, count)
        wind_y = tiles_of(wy_ref, level, count)
        new_x = [w - CG * d for w, d in zip(wind_x, closed.along_x(pres))]
        new_y = [w - CG * closed.along_y(p) for w, p in zip(wind_y, pres)]
        put_tiles(nx_ref, level, new_x)
        put_tiles(ny_ref, level, new_y)
        spread_x = closed.along_x([j * n for j, n in zip(jac, new_x)])
        spread_y = [closed.along_y(j * n) for j, n in zip(jac, new_y)]
        put_tiles(
            ps_ref,
            level,
            [p - i * (x + y) for p, i, x, y in zip(pres, inv_jac, spread_x, spread_y)],
        )
        return state

    lax.fori_loop(0, levels, step, 0, unroll=UNROLL)


def kernel_b(
    p_ref,
    nxc_ref,
    nyc_ref,
    psc_ref,
    wz_ref,
    jac_ref,
    sx_ref,
    sy_ref,
    r_ref,
    i_ref,
    v_ref,
    pp_ref,
    rows_ref,
    down_ref,
    up_ref,
    got_rows_ref,
    got_down_ref,
    got_up_ref,
    srows_ref,
    sdown_ref,
    sup_ref,
    got_srows_ref,
    got_sdown_ref,
    got_sup_ref,
    nx_ref,
    ny_ref,
    ps_ref,
    y_ref,
    face_ref,
):
    levels, rows, _ = p_ref.shape
    count = rows // ROWS
    last = count - 1
    lane, row = lane_index(), row_index()
    low_edge, high_edge, edge = lane_edge(LOW), lane_edge(HIGH), row_edge()
    wind_fix, low_fix, high_fix = [], [], []
    for t in range(count):
        part = slice(ROWS * t, ROWS * (t + 1))
        jac_low, jac_high = sdown_ref[1, part, :], sup_ref[1, part, :]
        low_wind, low_star = low_edge.correct(
            got_up_ref[0, part, :] - up_ref[0, part, :],
            pp_ref[0, part, :],
            jac_low,
            low_edge.shifted(got_sup_ref[1, part, :] - jac_high, 2),
        )
        high_wind, high_star = high_edge.correct(
            got_down_ref[0, part, :] - down_ref[0, part, :],
            pp_ref[1, part, :],
            jac_high,
            high_edge.shifted(got_sdown_ref[1, part, :] - jac_low, -2),
        )
        wind_fix.append(low_wind + pltpu.roll(high_wind, 128 - SLOT, 1))
        low_fix.append(low_star)
        high_fix.append(pltpu.roll(high_star, 128 - SLOT, 1))
    ends = srows_ref[levels]
    change = got_srows_ref[levels] - ends
    ends_change = jnp.where(row < 4, edge.shifted(change, -2), edge.shifted(change, 2))
    outer = (lane < 2) | (lane >= 126)
    low_lanes, high_lanes = lane < SLOT, lane >= 128 - SLOT
    first_rows = row < 4

    def star(level):
        new_x = tiles_of(nxc_ref, level, count)
        new_y = tiles_of(nyc_ref, level, count)
        stars = tiles_of(psc_ref, level, count)
        wind, press = edge.correct(
            pltpu.roll(got_rows_ref[level] - rows_ref[level], 4, 0),
            jnp.where(first_rows, p_ref[level, :ROWS, :], p_ref[level, ROWS * last :, :]),
            ends,
            ends_change,
        )
        new_x[0] = new_x[0] - jnp.where(first_rows, wind, 0.0)
        new_x[last] = new_x[last] - jnp.where(first_rows, 0.0, wind)
        stars[0] = stars[0] - jnp.where(first_rows, press, 0.0)
        stars[last] = stars[last] - jnp.where(first_rows, 0.0, press)
        back = lax.rem(128 - SLOT * level, 128)
        forces = []
        for t in range(count):
            part = slice(ROWS * t, ROWS * (t + 1))
            new_y[t] = new_y[t] - jnp.where(outer, pltpu.roll(wind_fix[t], back, 1), 0.0)
            fix = jnp.where(
                low_lanes,
                pltpu.roll(low_fix[t], back, 1),
                jnp.where(high_lanes, pltpu.roll(high_fix[t], back, 1), 0.0),
            )
            stars[t] = stars[t] - fix
            forces.append(
                wz_ref[level, part, :]
                + sx_ref[part, :] * new_x[t]
                + sy_ref[part, :] * new_y[t]
            )
        put_tiles(nx_ref, level, new_x)
        put_tiles(ny_ref, level, new_y)
        put_tiles(ps_ref, level, stars)
        return stars, forces

    def sweep(level, below, above, force, value, first):
        rate = tiles_of(r_ref, level, count)
        inv = tiles_of(i_ref, level, count)
        gain = tiles_of(v_ref, level, count)
        values, firsts = [], []
        for t in range(count):
            rhs = rate[t] * (force[t] - vert_coef * (above[t] - below[t]))
            firsts.append(first[t] + gain[t] * rhs)
            values.append((rhs + value[t]) * inv[t])
        put_tiles(y_ref, level, values)
        return values, firsts

    zeros = [jnp.zeros((ROWS, 128), jnp.float32)] * count
    here, force = star(0)
    put_tiles(face_ref, 2, here)

    def step(level, carry):
        below, here, force, value, first = carry
        above, force_next = star(level)
        value, first = sweep(level - 1, below, above, force, value, first)
        return here, above, force_next, value, first

    below, here, force, value, first = lax.fori_loop(
        1, levels, step, (zeros, here, force, zeros, zeros), unroll=UNROLL
    )
    value, first = sweep(levels - 1, below, zeros, force, value, first)
    put_tiles(face_ref, 0, first)
    put_tiles(face_ref, 1, value)
    put_tiles(face_ref, 3, here)


def kernel_f(s_ref, r_ref, i_ref, q_ref, v_ref, stat_ref):
    levels, rows, _ = s_ref.shape

    def down(level, carry):
        excess, prod = carry
        rate = 1.0 / s_ref[level]
        excess = rate + excess
        inv = 1.0 / (1.0 + excess)
        prod = prod * inv
        r_ref[level] = rate
        i_ref[level] = inv
        q_ref[level] = prod
        return excess * inv, prod

    ones = jnp.ones((rows, 128), jnp.float32)
    lax.fori_loop(0, levels, down, (ones, ones))

    def up(step, value):
        level = levels - 1 - step
        value = q_ref[level] + i_ref[level] * value
        v_ref[level] = value
        return value

    first = lax.fori_loop(0, levels, up, jnp.zeros((rows, 128), jnp.float32))
    stat_ref[0] = first
    stat_ref[1] = q_ref[levels - 1]
    stat_ref[2] = i_ref[levels - 1]
    stat_ref[3] = r_ref[0]
    stat_ref[4] = r_ref[levels - 1]


def reduced(blocks, mine, face, stat):
    faces = [face(j) for j in range(blocks)]
    stats = [stat(j) for j in range(blocks)]
    up = [
        faces[j][1] + vert_coef * stats[j + 1][3] * faces[j][3] if j < blocks - 1 else None
        for j in range(blocks)
    ]
    down = [
        faces[j][0] - vert_coef * stats[j - 1][4] * faces[j][2] if j > 0 else None
        for j in range(blocks)
    ]
    base, slope = [up[0]], [stats[0][2]]
    scale, known = [None], [None]
    for j in range(1, blocks):
        near, link, far = stats[j][0], stats[j][1], stats[j][2]
        scale.append(1.0 / (1.0 - near * slope[j - 1]))
        known.append(scale[j] * (down[j] + near * base[j - 1]))
        if j < blocks - 1:
            base.append(up[j] + link * (base[j - 1] + slope[j - 1] * known[j]))
            slope.append(far + link * link * slope[j - 1] * scale[j])
    zero = jnp.zeros_like(faces[0][0])
    above = [None] * blocks + [zero]
    below = [zero] + [None] * blocks
    for j in range(blocks - 1, 0, -1):
        above[j] = known[j] + scale[j] * stats[j][1] * above[j + 1]
        below[j] = base[j - 1] + slope[j - 1] * above[j]
    lower, upper, under, over = zero, zero, zero, zero
    for j in range(blocks):
        here = mine == j
        if j > 0:
            lower = jnp.where(here, below[j], lower)
            under = jnp.where(
                here, below[j] - vert_coef * stats[j][3] * faces[j - 1][3], under
            )
        if j < blocks - 1:
            upper = jnp.where(here, above[j + 1], upper)
            over = jnp.where(
                here, above[j + 1] + vert_coef * stats[j][4] * faces[j + 1][2], over
            )
    return lower, upper, under, over


def boundary(blocks, mine, count, face_refs, stat_refs):
    def solve(t):
        part = slice(ROWS * t, ROWS * (t + 1))

        def read(refs, planes):
            own = [
                [ref[k, part, :] for k in range(planes)] for ref in refs
            ]

            def block(j):
                out = []
                for k in range(planes):
                    value = own[0][k]
                    for shift in range(1, blocks):
                        value = jnp.where(mine == (j ^ shift), own[shift][k], value)
                    out.append(value)
                return out

            return block

        return reduced(blocks, mine, read(face_refs, 4), read(stat_refs, 5))

    parts = [solve(t) for t in range(count)]
    return [[part[k] for part in parts] for k in range(4)]


def finish(blocks, count, levels, y_ref, q_ref, i_ref, ps_ref, x_ref, p_ref, face_refs, stat_refs, use):
    mine = lax.axis_index("lev")
    lower, upper, under, over = boundary(blocks, mine, count, face_refs, stat_refs)

    def solved(level, above):
        value = tiles_of(y_ref, level, count)
        prod = tiles_of(q_ref, level, count)
        inv = tiles_of(i_ref, level, count)
        out = [y + q * u + i * a for y, q, u, i, a in zip(value, prod, lower, inv, above)]
        put_tiles(x_ref, level, out)
        return out

    def pressed(level, above, below, state):
        star = tiles_of(ps_ref, level, count)
        pres = [s - vert_coef * (a - b) for s, a, b in zip(star, above, below)]
        put_tiles(p_ref, level, pres)
        return use(level, pres, state)

    def step(index, carry):
        above, here, state = carry
        level = levels - 2 - index
        below = solved(level, here)
        state = pressed(level + 1, above, below, state)
        return here, below, state

    top = solved(levels - 1, upper)
    zeros = [jnp.zeros((ROWS, 128), jnp.float32)] * count
    above, here, state = lax.fori_loop(0, levels - 1, step, (over, top, (zeros, zeros)))
    return pressed(0, above, under, state)


def finish(blocks, count, levels, y_ref, q_ref, i_ref, ps_ref, x_ref, p_ref, face_refs, stat_refs, use, state):
    mine = lax.axis_index("lev")
    lower, upper, under, over = boundary(blocks, mine, count, face_refs, stat_refs)

    def solved(level, above):
        value = tiles_of(y_ref, level, count)
        prod = tiles_of(q_ref, level, count)
        inv = tiles_of(i_ref, level, count)
        out = [(y + q * u) + i * a for y, q, u, i, a in zip(value, prod, lower, inv, above)]
        put_tiles(x_ref, level, out)
        return out

    def pressed(level, above, below, state):
        star = tiles_of(ps_ref, level, count)
        pres = [s - vert_coef * (a - b) for s, a, b in zip(star, above, below)]
        put_tiles(p_ref, level, pres)
        return use(level, pres, state)

    def step(index, carry):
        above, here, state = carry
        level = levels - 2 - index
        below = solved(level, here)
        state = pressed(level + 1, above, below, state)
        return here, below, state

    top = solved(levels - 1, upper)
    above, here, state = lax.fori_loop(0, levels - 1, step, (over, top, state), unroll=UNROLL)
    return pressed(0, above, under, state)


def kernel_c(blocks, y_ref, q_ref, i_ref, ps_ref, wx_ref, pw_ref, jac_ref, *refs):
    face_refs, stat_refs = refs[:blocks], refs[blocks : 2 * blocks]
    x_ref, p_ref, rows_ref, down_ref, up_ref, pp_ref = refs[2 * blocks :]
    levels, rows, _ = y_ref.shape
    count = rows // ROWS
    packer = Packer(count)
    edge = row_edge()
    ends = both_ends(planes_of(jac_ref, count))

    def use(level, pres, state):
        rows_ref[level] = edge.payload(
            both_ends(pres), both_ends(tiles_of(wx_ref, level, count)), ends
        )
        return packer.add(level, pres, state)

    state = finish(
        blocks,
        count,
        levels,
        y_ref,
        q_ref,
        i_ref,
        ps_ref,
        x_ref,
        p_ref,
        face_refs,
        stat_refs,
        use,
        packer.start,
    )
    pres = packer.done(state)
    wind = tiles_of(pw_ref, 0, count), tiles_of(pw_ref, 1, count)
    down, up = lane_payload(pres, wind, planes_of(jac_ref, count))
    put_tiles(down_ref, 0, down)
    put_tiles(up_ref, 0, up)
    put_tiles(pp_ref, 0, pres[0])
    put_tiles(pp_ref, 1, pres[1])


def kernel_d(blocks, y_ref, q_ref, i_ref, ps_ref, *refs):
    face_refs, stat_refs = refs[:blocks], refs[blocks : 2 * blocks]
    x_ref, p_ref = refs[2 * blocks :]
    levels, rows, _ = y_ref.shape
    finish(
        blocks,
        rows // ROWS,
        levels,
        y_ref,
        q_ref,
        i_ref,
        ps_ref,
        x_ref,
        p_ref,
        face_refs,
        stat_refs,
        lambda level, pres, state: state,
        0,
    )


def call(kernel, name, shapes, *args):
    space = pl.BlockSpec(memory_space=pltpu.VMEM)
    size = sum(a.size for a in args) + sum(functools.reduce(lambda a, b: a * b, s) for s in shapes)
    return pl.pallas_call(
        kernel,
        out_shape=[jax.ShapeDtypeStruct(s, jnp.float32) for s in shapes],
        in_specs=[space] * len(args),
        out_specs=[space] * len(shapes),
        compiler_params=pltpu.CompilerParams(vmem_limit_bytes=32 * 1024 * 1024),
        cost_estimate=pl.CostEstimate(
            flops=8 * size, bytes_accessed=4 * size, transcendentals=0
        ),
        name=name,
    )(*args)


def swap(value, axis, partner):
    count = lax.axis_size(axis)
    return lax.ppermute(value, axis, [(i, partner(i)) for i in range(count)])


def exchange_rows(rows):
    count = lax.axis_size("gx")
    if count == 2:
        return swap(rows, "gx", lambda i: 1 - i)
    down = swap(rows[:, : ROWS // 2], "gx", lambda i: (i - 1) % count)
    up = swap(rows[:, ROWS // 2 :], "gx", lambda i: (i + 1) % count)
    return jnp.concatenate([down, up], axis=1)


def exchange_lanes(down, up):
    count = lax.axis_size("gy")
    from_above = swap(down, "gy", lambda i: (i - 1) % count)
    from_below = swap(up, "gy", lambda i: (i + 1) % count)
    return from_above, from_below


def gather_levels(planes):
    count = lax.axis_size("lev")
    return [planes] + [
        swap(planes, "lev", lambda i, shift=shift: i ^ shift) for shift in range(1, count)
    ]


def local(wind_x, wind_y, wind_z, pressure, jacobian, slope_x, slope_y, stiffness):
    field = wind_x.shape
    levels, rows, lanes = field
    blocks = lax.axis_size("lev")
    plane = (rows, lanes)
    pair = (2,) + plane
    assert lanes == 128 and levels * SLOT == 128 and rows % ROWS == 0
    assert blocks & (blocks - 1) == 0

    edge, down, up, ends = call(
        kernel_a,
        "start",
        [(levels + 1, ROWS, lanes), pair, pair, pair],
        pressure,
        wind_x,
        wind_y,
        jacobian,
    )
    sent = (edge, down, up)
    got = (exchange_rows(edge),) + exchange_lanes(down, up)
    static_edges = sent + got
    rate, inv, prod, gain, stat = call(
        kernel_f, "factor", [field, field, field, field, (5,) + plane], stiffness
    )
    stats = gather_levels(stat)
    for substep in range(SUBSTEPS):
        closed = call(
            kernel_m, "interior", [field, field, field], pressure, wind_x, wind_y, jacobian
        )
        wind_x, wind_y, star, value, face = call(
            kernel_b,
            "sweep",
            [field, field, field, field, (4,) + plane],
            pressure,
            *closed,
            wind_z,
            jacobian,
            slope_x,
            slope_y,
            rate,
            inv,
            gain,
            ends,
            *sent,
            *got,
            *static_edges,
        )
        faces = gather_levels(face)
        if substep < SUBSTEPS - 1:
            (packed,) = call(kernel_n, "pack", [pair], wind_y)
            wind_z, pressure, edge, down, up, ends = call(
                functools.partial(kernel_c, blocks),
                "finish",
                [field, field, (levels, ROWS, lanes), (1,) + plane, (1,) + plane, pair],
                value,
                prod,
                inv,
                star,
                wind_x,
                packed,
                jacobian,
                *faces,
                *stats,
            )
            sent = (edge, down, up)
            got = (exchange_rows(edge),) + exchange_lanes(down, up)
        else:
            wind_z, pressure = call(
                functools.partial(kernel_d, blocks),
                "last",
                [field, field],
                value,
                prod,
                inv,
                star,
                *faces,
                *stats,
            )
    return wind_x, wind_y, wind_z, pressure


def solution(mesh):
    field = P("lev", "gx", "gy")
    column = P("gx", "gy")
    return jax.shard_map(
        local,
        mesh=mesh,
        in_specs=(field,) * 4 + (column,) * 3 + (field,),
        out_specs=(field,) * 4,
        check_vma=False,
    )
```

```python
import functools

import jax
import jax.numpy as jnp
from jax import lax
from jax.experimental import pallas as pl
from jax.experimental.pallas import tpu as pltpu
from jax.sharding import PartitionSpec as P

SUBSTEPS = 2

grad_coef = 0.35
div_coef = 0.35
vert_coef = 0.25

CG = grad_coef / 12.0
CD = div_coef / 12.0
ROWS = 8
SLOT = 4
UNROLL = 4
CHUNKS = 4


def lane_index():
    return lax.broadcasted_iota(jnp.int32, (ROWS, 128), 1)


def row_index():
    return lax.broadcasted_iota(jnp.int32, (ROWS, 128), 0)


def only(mask, value):
    return jnp.where(mask, jnp.float32(value), jnp.float32(0.0))


def tiles_of(ref, level, count):
    return [ref[level, ROWS * t : ROWS * (t + 1), :] for t in range(count)]


def planes_of(ref, count):
    return [ref[ROWS * t : ROWS * (t + 1), :] for t in range(count)]


def put_tiles(ref, level, tiles):
    for t, tile in enumerate(tiles):
        ref[level, ROWS * t : ROWS * (t + 1), :] = tile


def put_planes(ref, tiles):
    for t, tile in enumerate(tiles):
        ref[ROWS * t : ROWS * (t + 1), :] = tile


class Edge:
    def __init__(self, place, axis, held):
        self.place, self.axis, self.held = place, axis, held
        self.size = place.shape[axis]

    def at(self, places):
        total = None
        for position, value in places.items():
            if position in self.held:
                term = only(self.place == position, value)
                total = term if total is None else total + term
        return total

    def shifted(self, field, by):
        return field if by == 0 else pltpu.roll(field, (-by) % self.size, self.axis)

    def mix(self, field, table):
        total = None
        for by, places in table.items():
            weight = self.at(places)
            if weight is not None:
                term = weight * self.shifted(field, by)
                total = term if total is None else total + term
        return total

    def payload(self, pres, wind, jac):
        partial = self.mix(
            pres,
            {
                1: {0: 8.0, 1: 8.0, 6: 8.0},
                2: {0: -1.0, 1: -1.0},
                -1: {1: -8.0, 6: -8.0, 7: -8.0},
                -2: {6: 1.0, 7: 1.0},
            },
        )
        flux = jac * (wind - CG * partial)
        outer = self.mix(pres, {0: {0: 1.0, 1: 1.0, 6: 1.0, 7: 1.0}})
        return outer + self.mix(flux, {-2: {2: 1.0, 3: 1.0}, 2: {4: 1.0, 5: 1.0}})

    def correct(self, delta, pres, jac, delta_jac):
        grad = self.mix(
            delta, {2: {0: 1.0, 1: 1.0}, 3: {0: -8.0}, -2: {6: -1.0, 7: -1.0}, -3: {7: 8.0}}
        )
        wind = CG * grad
        own = -(jac * wind)
        far = self.mix(delta, {0: {0: 1.0, 1: 1.0, 6: 1.0, 7: 1.0}}) + CG * delta_jac * self.mix(
            pres, {0: {0: 1.0, 1: 1.0, 6: -1.0, 7: -1.0}, -1: {1: -8.0}, 1: {6: 8.0}}
        )
        spread = (
            self.mix(far, {0: {0: 1.0, 1: 1.0, 6: -1.0, 7: -1.0}})
            + self.mix(far - own, {1: {0: -8.0}, -1: {7: 8.0}})
            + self.mix(
                own,
                {
                    -1: {1: -8.0, 2: -8.0},
                    -2: {2: 1.0, 3: 1.0},
                    1: {5: 8.0, 6: 8.0},
                    2: {4: -1.0, 5: -1.0},
                },
            )
        )
        return wind, CD * spread / jac


LOW, HIGH = (0, 1, 2, 3), (4, 5, 6, 7)


def row_edge():
    return Edge(row_index(), 0, LOW + HIGH)


def lane_edge(held):
    return Edge((lane_index() & 3) + held[0], 1, held)


def both_ends(tiles):
    return jnp.where(row_index() < 4, tiles[0], tiles[-1])


def spread_slots(tile, low):
    lane = lane_index()
    if low:
        out = jnp.where(lane < SLOT, tile, 0.0)
    else:
        out = pltpu.roll(jnp.where(lane >= 128 - SLOT, tile, 0.0), SLOT, 1)
    by = SLOT
    while by < 128:
        out = out + pltpu.roll(out, by, 1)
        by *= 2
    return out


class Packer:
    def __init__(self, count):
        self.slot = lax.shift_right_logical(lane_index(), 2)
        self.start = [jnp.zeros((ROWS, 128), jnp.float32)] * (2 * count)
        self.count = count

    def add(self, level, tiles, state):
        before = lax.rem(level + 31, 32)
        rolled = [pltpu.roll(tile, SLOT * level, 1) for tile in tiles]
        low = [jnp.where(self.slot == level, r, s) for r, s in zip(rolled, state)]
        high = [jnp.where(self.slot == before, r, s) for r, s in zip(rolled, state[self.count :])]
        return low + high

    def done(self, state):
        return state[: self.count], [pltpu.roll(s, SLOT, 1) for s in state[self.count :]]


class Closed:
    def __init__(self):
        self.row = row_index()

    def along_y(self, tile):
        pair = tile - pltpu.roll(tile, 126, 1)
        return (pltpu.roll(pair, 2, 1) + pair) - 8.0 * pltpu.roll(pair, 1, 1)

    def moved(self, tiles, by):
        count = len(tiles)
        rolled = [pltpu.roll(tile, by % ROWS, 0) for tile in tiles]
        if by > 0:
            return [jnp.where(self.row < by, rolled[t - 1], rolled[t]) for t in range(count)]
        return [
            jnp.where(self.row >= ROWS + by, rolled[(t + 1) % count], rolled[t])
            for t in range(count)
        ]

    def along_x(self, tiles):
        pair = [f - m for f, m in zip(tiles, self.moved(tiles, -2))]
        return [
            (two + here) - 8.0 * one
            for two, here, one in zip(self.moved(pair, 2), pair, self.moved(pair, 1))
        ]


def even_place():
    return lax.rem(lax.axis_index("gy"), 2) == 0


def put_pair(inner_ref, outer_ref, index, down, up):
    even = even_place()
    put_tiles(inner_ref, index, [jnp.where(even, u, d) for u, d in zip(up, down)])
    put_tiles(outer_ref, index, [jnp.where(even, d, u) for u, d in zip(up, down)])


def get_pair(inner_ref, outer_ref, index, part):
    even = even_place()
    inner, outer = inner_ref[index, part, :], outer_ref[index, part, :]
    return jnp.where(even, outer, inner), jnp.where(even, inner, outer)


def lane_payload(pres, wind, jac):
    low, high = lane_edge(LOW), lane_edge(HIGH)
    down = [
        low.payload(p, w, spread_slots(j, True)) for p, w, j in zip(pres[0], wind[0], jac)
    ]
    up = [
        high.payload(p, w, spread_slots(j, False)) for p, w, j in zip(pres[1], wind[1], jac)
    ]
    return down, up


def pack_levels(ref, count, levels):
    packer = Packer(count)

    def step(level, state):
        return packer.add(level, tiles_of(ref, level, count), state)

    return packer.done(lax.fori_loop(0, levels, step, packer.start, unroll=UNROLL))


def kernel_a(
    p_hbm, wx_hbm, wy_hbm, jac_hbm, rows_ref, inner_ref, outer_ref, pp_ref, p_ref, wx_ref, wy_ref, jac_ref, sems
):
    levels, rows, _ = p_hbm.shape
    count = rows // ROWS
    share = levels // CHUNKS

    def fetch(source, target, sem):
        copy = pltpu.make_async_copy(source, target, sem)
        copy.start()
        return copy

    tail = pl.ds(rows - ROWS, ROWS)
    parts = [pl.ds(c * share, share) for c in range(CHUNKS)]
    pres_in = [fetch(p_hbm.at[s], p_ref.at[s], sems.at[0, c]) for c, s in enumerate(parts)]
    wind_in = [fetch(wy_hbm.at[s], wy_ref.at[s], sems.at[1, c]) for c, s in enumerate(parts)]
    ends_in = [
        fetch(jac_hbm, jac_ref, sems.at[2, 0]),
        fetch(wx_hbm.at[:, pl.ds(0, ROWS)], wx_ref.at[:, pl.ds(0, ROWS)], sems.at[2, 1]),
        fetch(wx_hbm.at[:, tail], wx_ref.at[:, pl.ds(ROWS, ROWS)], sems.at[2, 2]),
    ]

    def pack(ref, copies):
        packer = Packer(count)
        state = packer.start
        for c, copy in enumerate(copies):
            copy.wait()
            state = lax.fori_loop(
                c * share,
                (c + 1) * share,
                lambda level, state: packer.add(level, tiles_of(ref, level, count), state),
                state,
                unroll=UNROLL,
            )
        return packer.done(state)

    pres = pack(p_ref, pres_in)
    wind = pack(wy_ref, wind_in)
    for copy in ends_in:
        copy.wait()
    jac = planes_of(jac_ref, count)
    ends = both_ends(jac)
    edge = row_edge()

    def step(level, state):
        rows_ref[level] = edge.payload(
            both_ends(tiles_of(p_ref, level, count)), both_ends(tiles_of(wx_ref, level, 2)), ends
        )
        return state

    lax.fori_loop(0, levels, step, 0, unroll=UNROLL)
    rows_ref[levels] = ends
    down, up = lane_payload(pres, wind, jac)
    put_pair(inner_ref, outer_ref, 0, down, up)
    put_pair(
        inner_ref,
        outer_ref,
        1,
        [spread_slots(j, True) for j in jac],
        [spread_slots(j, False) for j in jac],
    )
    put_tiles(pp_ref, 0, pres[0])
    put_tiles(pp_ref, 1, pres[1])


def kernel_n(wy_ref, pw_ref):
    levels, rows, _ = wy_ref.shape
    count = rows // ROWS
    wind = pack_levels(wy_ref, count, levels)
    put_tiles(pw_ref, 0, wind[0])
    put_tiles(pw_ref, 1, wind[1])


def kernel_m(p_ref, wx_ref, wy_ref, jac_ref, nx_ref, ny_ref, ps_ref):
    levels, rows, _ = p_ref.shape
    count = rows // ROWS
    jac = planes_of(jac_ref, count)
    inv_jac = [CD / j for j in jac]
    closed = Closed()

    def step(level, state):
        pres = tiles_of(p_ref, level, count)
        wind_x = tiles_of(wx_ref, level, count)
        wind_y = tiles_of(wy_ref, level, count)
        new_x = [w - CG * d for w, d in zip(wind_x, closed.along_x(pres))]
        new_y = [w - CG * closed.along_y(p) for w, p in zip(wind_y, pres)]
        put_tiles(nx_ref, level, new_x)
        put_tiles(ny_ref, level, new_y)
        spread_x = closed.along_x([j * n for j, n in zip(jac, new_x)])
        spread_y = [closed.along_y(j * n) for j, n in zip(jac, new_y)]
        put_tiles(
            ps_ref,
            level,
            [p - i * (x + y) for p, i, x, y in zip(pres, inv_jac, spread_x, spread_y)],
        )
        return state

    lax.fori_loop(0, levels, step, 0, unroll=UNROLL)


def kernel_b(
    p_ref,
    nxc_ref,
    nyc_ref,
    psc_ref,
    wz_ref,
    jac_ref,
    sx_ref,
    sy_ref,
    r_ref,
    i_ref,
    v_ref,
    pp_ref,
    rows_ref,
    inner_ref,
    outer_ref,
    got_rows_ref,
    got_inner_ref,
    got_outer_ref,
    srows_ref,
    sinner_ref,
    souter_ref,
    got_srows_ref,
    got_sinner_ref,
    got_souter_ref,
    nx_ref,
    ny_ref,
    ps_ref,
    y_ref,
    face_ref,
):
    levels, rows, _ = p_ref.shape
    count = rows // ROWS
    last = count - 1
    lane, row = lane_index(), row_index()
    low_edge, high_edge, edge = lane_edge(LOW), lane_edge(HIGH), row_edge()
    wind_fix, low_fix, high_fix = [], [], []
    for t in range(count):
        part = slice(ROWS * t, ROWS * (t + 1))
        jac_low, jac_high = get_pair(sinner_ref, souter_ref, 1, part)
        jac_below, jac_above = get_pair(got_sinner_ref, got_souter_ref, 1, part)
        down, up = get_pair(inner_ref, outer_ref, 0, part)
        below, above = get_pair(got_inner_ref, got_outer_ref, 0, part)
        low_wind, low_star = low_edge.correct(
            below - up, pp_ref[0, part, :], jac_low, low_edge.shifted(jac_below - jac_high, 2)
        )
        high_wind, high_star = high_edge.correct(
            above - down, pp_ref[1, part, :], jac_high, high_edge.shifted(jac_above - jac_low, -2)
        )
        wind_fix.append(low_wind + pltpu.roll(high_wind, 128 - SLOT, 1))
        low_fix.append(low_star)
        high_fix.append(pltpu.roll(high_star, 128 - SLOT, 1))
    ends = srows_ref[levels]
    change = got_srows_ref[levels] - ends
    ends_change = jnp.where(row < 4, edge.shifted(change, -2), edge.shifted(change, 2))
    outer = (lane < 2) | (lane >= 126)
    low_lanes, high_lanes = lane < SLOT, lane >= 128 - SLOT
    first_rows = row < 4

    def star(level):
        new_x = tiles_of(nxc_ref, level, count)
        new_y = tiles_of(nyc_ref, level, count)
        stars = tiles_of(psc_ref, level, count)
        wind, press = edge.correct(
            pltpu.roll(got_rows_ref[level] - rows_ref[level], 4, 0),
            jnp.where(first_rows, p_ref[level, :ROWS, :], p_ref[level, ROWS * last :, :]),
            ends,
            ends_change,
        )
        new_x[0] = new_x[0] - jnp.where(first_rows, wind, 0.0)
        new_x[last] = new_x[last] - jnp.where(first_rows, 0.0, wind)
        stars[0] = stars[0] - jnp.where(first_rows, press, 0.0)
        stars[last] = stars[last] - jnp.where(first_rows, 0.0, press)
        back = lax.rem(128 - SLOT * level, 128)
        forces = []
        for t in range(count):
            part = slice(ROWS * t, ROWS * (t + 1))
            new_y[t] = new_y[t] - jnp.where(outer, pltpu.roll(wind_fix[t], back, 1), 0.0)
            fix = jnp.where(
                low_lanes,
                pltpu.roll(low_fix[t], back, 1),
                jnp.where(high_lanes, pltpu.roll(high_fix[t], back, 1), 0.0),
            )
            stars[t] = stars[t] - fix
            forces.append(
                wz_ref[level, part, :]
                + sx_ref[part, :] * new_x[t]
                + sy_ref[part, :] * new_y[t]
            )
        put_tiles(nx_ref, level, new_x)
        put_tiles(ny_ref, level, new_y)
        put_tiles(ps_ref, level, stars)
        return stars, forces

    def sweep(level, below, above, force, value, first):
        rate = tiles_of(r_ref, level, count)
        inv = tiles_of(i_ref, level, count)
        gain = tiles_of(v_ref, level, count)
        values, firsts = [], []
        for t in range(count):
            rhs = rate[t] * (force[t] - vert_coef * (above[t] - below[t]))
            firsts.append(first[t] + gain[t] * rhs)
            values.append((rhs + value[t]) * inv[t])
        put_tiles(y_ref, level, values)
        return values, firsts

    zeros = [jnp.zeros((ROWS, 128), jnp.float32)] * count
    here, force = star(0)
    put_tiles(face_ref, 2, here)

    def step(level, carry):
        below, here, force, value, first = carry
        above, force_next = star(level)
        value, first = sweep(level - 1, below, above, force, value, first)
        return here, above, force_next, value, first

    below, here, force, value, first = lax.fori_loop(
        1, levels, step, (zeros, here, force, zeros, zeros), unroll=UNROLL
    )
    value, first = sweep(levels - 1, below, zeros, force, value, first)
    put_tiles(face_ref, 0, first)
    put_tiles(face_ref, 1, value)
    put_tiles(face_ref, 3, here)


def kernel_f(s_ref, r_ref, i_ref, q_ref, v_ref, stat_ref):
    levels, rows, _ = s_ref.shape

    def down(level, carry):
        excess, prod = carry
        rate = 1.0 / s_ref[level]
        excess = rate + excess
        inv = 1.0 / (1.0 + excess)
        prod = prod * inv
        r_ref[level] = rate
        i_ref[level] = inv
        q_ref[level] = prod
        return excess * inv, prod

    ones = jnp.ones((rows, 128), jnp.float32)
    lax.fori_loop(0, levels, down, (ones, ones))

    def up(step, value):
        level = levels - 1 - step
        value = q_ref[level] + i_ref[level] * value
        v_ref[level] = value
        return value

    first = lax.fori_loop(0, levels, up, jnp.zeros((rows, 128), jnp.float32))
    stat_ref[0] = first
    stat_ref[1] = q_ref[levels - 1]
    stat_ref[2] = i_ref[levels - 1]
    stat_ref[3] = r_ref[0]
    stat_ref[4] = r_ref[levels - 1]


def reduced(blocks, mine, face, stat):
    faces = [face(j) for j in range(blocks)]
    stats = [stat(j) for j in range(blocks)]
    up = [
        faces[j][1] + vert_coef * stats[j + 1][3] * faces[j][3] if j < blocks - 1 else None
        for j in range(blocks)
    ]
    down = [
        faces[j][0] - vert_coef * stats[j - 1][4] * faces[j][2] if j > 0 else None
        for j in range(blocks)
    ]
    base, slope = [up[0]], [stats[0][2]]
    scale, known = [None], [None]
    for j in range(1, blocks):
        near, link, far = stats[j][0], stats[j][1], stats[j][2]
        scale.append(1.0 / (1.0 - near * slope[j - 1]))
        known.append(scale[j] * (down[j] + near * base[j - 1]))
        if j < blocks - 1:
            base.append(up[j] + link * (base[j - 1] + slope[j - 1] * known[j]))
            slope.append(far + link * link * slope[j - 1] * scale[j])
    zero = jnp.zeros_like(faces[0][0])
    above = [None] * blocks + [zero]
    below = [zero] + [None] * blocks
    for j in range(blocks - 1, 0, -1):
        above[j] = known[j] + scale[j] * stats[j][1] * above[j + 1]
        below[j] = base[j - 1] + slope[j - 1] * above[j]
    lower, upper, under, over = zero, zero, zero, zero
    for j in range(blocks):
        here = mine == j
        if j > 0:
            lower = jnp.where(here, below[j], lower)
            under = jnp.where(
                here, below[j] - vert_coef * stats[j][3] * faces[j - 1][3], under
            )
        if j < blocks - 1:
            upper = jnp.where(here, above[j + 1], upper)
            over = jnp.where(
                here, above[j + 1] + vert_coef * stats[j][4] * faces[j + 1][2], over
            )
    return lower, upper, under, over


def boundary(blocks, mine, count, face_refs, stat_refs):
    def solve(t):
        part = slice(ROWS * t, ROWS * (t + 1))

        def read(refs, planes):
            own = [
                [ref[k, part, :] for k in range(planes)] for ref in refs
            ]

            def block(j):
                out = []
                for k in range(planes):
                    value = own[0][k]
                    for shift in range(1, blocks):
                        value = jnp.where(mine == (j ^ shift), own[shift][k], value)
                    out.append(value)
                return out

            return block

        return reduced(blocks, mine, read(face_refs, 4), read(stat_refs, 5))

    parts = [solve(t) for t in range(count)]
    return [[part[k] for part in parts] for k in range(4)]


def finish(blocks, count, levels, y_ref, q_ref, i_ref, ps_ref, x_ref, p_ref, face_refs, stat_refs, use):
    mine = lax.axis_index("lev")
    lower, upper, under, over = boundary(blocks, mine, count, face_refs, stat_refs)

    def solved(level, above):
        value = tiles_of(y_ref, level, count)
        prod = tiles_of(q_ref, level, count)
        inv = tiles_of(i_ref, level, count)
        out = [y + q * u + i * a for y, q, u, i, a in zip(value, prod, lower, inv, above)]
        put_tiles(x_ref, level, out)
        return out

    def pressed(level, above, below, state):
        star = tiles_of(ps_ref, level, count)
        pres = [s - vert_coef * (a - b) for s, a, b in zip(star, above, below)]
        put_tiles(p_ref, level, pres)
        return use(level, pres, state)

    def step(index, carry):
        above, here, state = carry
        level = levels - 2 - index
        below = solved(level, here)
        state = pressed(level + 1, above, below, state)
        return here, below, state

    top = solved(levels - 1, upper)
    zeros = [jnp.zeros((ROWS, 128), jnp.float32)] * count
    above, here, state = lax.fori_loop(0, levels - 1, step, (over, top, (zeros, zeros)))
    return pressed(0, above, under, state)


def finish(blocks, count, levels, y_ref, q_ref, i_ref, ps_ref, x_ref, p_ref, face_refs, stat_refs, use, state, ready=None):
    mine = lax.axis_index("lev")
    lower, upper, under, over = boundary(blocks, mine, count, face_refs, stat_refs)

    def solved(level, above):
        value = tiles_of(y_ref, level, count)
        prod = tiles_of(q_ref, level, count)
        inv = tiles_of(i_ref, level, count)
        out = [(y + q * u) + i * a for y, q, u, i, a in zip(value, prod, lower, inv, above)]
        put_tiles(x_ref, level, out)
        return out

    def pressed(level, above, below, state):
        star = tiles_of(ps_ref, level, count)
        pres = [s - vert_coef * (a - b) for s, a, b in zip(star, above, below)]
        put_tiles(p_ref, level, pres)
        return use(level, pres, state)

    def step(index, carry):
        above, here, state = carry
        level = levels - 2 - index
        below = solved(level, here)
        state = pressed(level + 1, above, below, state)
        return here, below, state

    top = solved(levels - 1, upper)
    carry = (over, top, state)
    if ready is None:
        carry = lax.fori_loop(0, levels - 1, step, carry, unroll=UNROLL)
    else:
        done, share = 0, levels // CHUNKS
        for c in range(CHUNKS - 1, -1, -1):
            goal = levels - 1 - c * share
            carry = lax.fori_loop(done, goal, step, carry, unroll=UNROLL)
            done = goal
            ready(c)
    above, here, state = carry
    return pressed(0, above, under, state)


def kernel_c(blocks, y_ref, q_ref, i_ref, ps_ref, wx_ref, pw_ref, jac_ref, *refs):
    face_refs, stat_refs = refs[:blocks], refs[blocks : 2 * blocks]
    x_ref, p_ref, rows_ref, inner_ref, outer_ref, pp_ref = refs[2 * blocks :]
    levels, rows, _ = y_ref.shape
    count = rows // ROWS
    packer = Packer(count)
    edge = row_edge()
    ends = both_ends(planes_of(jac_ref, count))

    def use(level, pres, state):
        rows_ref[level] = edge.payload(
            both_ends(pres), both_ends(tiles_of(wx_ref, level, count)), ends
        )
        return packer.add(level, pres, state)

    state = finish(
        blocks,
        count,
        levels,
        y_ref,
        q_ref,
        i_ref,
        ps_ref,
        x_ref,
        p_ref,
        face_refs,
        stat_refs,
        use,
        packer.start,
    )
    pres = packer.done(state)
    wind = tiles_of(pw_ref, 0, count), tiles_of(pw_ref, 1, count)
    down, up = lane_payload(pres, wind, planes_of(jac_ref, count))
    put_pair(inner_ref, outer_ref, 0, down, up)
    put_tiles(pp_ref, 0, pres[0])
    put_tiles(pp_ref, 1, pres[1])


def kernel_d(blocks, y_ref, q_ref, i_ref, ps_ref, *refs):
    face_refs, stat_refs = refs[:blocks], refs[blocks : 2 * blocks]
    x_hbm, p_hbm, x_ref, p_ref, sems = refs[2 * blocks :]
    levels, rows, _ = y_ref.shape
    share = levels // CHUNKS
    copies = []

    def send(index, source, target, c):
        part = pl.ds(c * share, share)
        copy = pltpu.make_async_copy(source.at[part], target.at[part], sems.at[index, c])
        copy.start()
        copies.append(copy)

    def ready(c):
        send(0, x_ref, x_hbm, c)
        if c < CHUNKS - 1:
            send(1, p_ref, p_hbm, c + 1)

    finish(
        blocks,
        rows // ROWS,
        levels,
        y_ref,
        q_ref,
        i_ref,
        ps_ref,
        x_ref,
        p_ref,
        face_refs,
        stat_refs,
        lambda level, pres, state: state,
        0,
        ready,
    )
    send(1, p_ref, p_hbm, 0)
    for copy in copies:
        copy.wait()


def call(kernel, name, shapes, *args, far_in=False, far_out=False, scratch=(), keep=()):
    near, far = pl.BlockSpec(memory_space=pltpu.VMEM), pl.BlockSpec(memory_space=pl.ANY)
    size = sum(a.size for a in args) + sum(functools.reduce(lambda a, b: a * b, s) for s in shapes)
    if far_in:
        args = [pltpu.with_memory_space_constraint(a, pltpu.HBM) for a in args]
    return pl.pallas_call(
        kernel,
        out_shape=[
            pltpu.VMEM(s, jnp.float32) if k in keep else jax.ShapeDtypeStruct(s, jnp.float32)
            for k, s in enumerate(shapes)
        ],
        in_specs=[far if far_in else near] * len(args),
        out_specs=[far if far_out else near] * len(shapes),
        scratch_shapes=list(scratch),
        compiler_params=pltpu.CompilerParams(vmem_limit_bytes=32 * 1024 * 1024),
        cost_estimate=pl.CostEstimate(
            flops=8 * size, bytes_accessed=4 * size, transcendentals=0
        ),
        name=name,
    )(*args)


def swap(value, axis, partner):
    count = lax.axis_size(axis)
    return lax.ppermute(value, axis, [(i, partner(i)) for i in range(count)])


def exchange_rows(rows):
    count = lax.axis_size("gx")
    if count == 2:
        return swap(rows, "gx", lambda i: 1 - i)
    down = swap(rows[:, : ROWS // 2], "gx", lambda i: (i - 1) % count)
    up = swap(rows[:, ROWS // 2 :], "gx", lambda i: (i + 1) % count)
    return jnp.concatenate([down, up], axis=1)


def exchange_lanes(inner, outer):
    count = lax.axis_size("gy")
    got_outer = swap(outer, "gy", lambda i: (i + 1 if i % 2 else i - 1) % count)
    got_inner = swap(inner, "gy", lambda i: i ^ 1)
    return got_inner, got_outer


def gather_levels(planes):
    count = lax.axis_size("lev")
    return [planes] + [
        swap(planes, "lev", lambda i, shift=shift: i ^ shift) for shift in range(1, count)
    ]


def local(wind_x, wind_y, wind_z, pressure, jacobian, slope_x, slope_y, stiffness):
    field = wind_x.shape
    levels, rows, lanes = field
    blocks = lax.axis_size("lev")
    plane = (rows, lanes)
    pair = (2,) + plane
    assert lanes == 128 and levels * SLOT == 128 and rows % ROWS == 0
    assert blocks & (blocks - 1) == 0 and lax.axis_size("gy") % 2 == 0

    edge, inner, outer, ends = call(
        kernel_a,
        "start",
        [(levels + 1, ROWS, lanes), pair, pair, pair],
        pressure,
        wind_x,
        wind_y,
        jacobian,
        far_in=True,
        scratch=[
            pltpu.VMEM(field, jnp.float32),
            pltpu.VMEM((levels, 2 * ROWS, lanes), jnp.float32),
            pltpu.VMEM(field, jnp.float32),
            pltpu.VMEM(plane, jnp.float32),
            pltpu.SemaphoreType.DMA((3, CHUNKS)),
        ],
    )
    sent = (edge, inner, outer)
    got = (exchange_rows(edge),) + exchange_lanes(inner, outer)
    static_edges = sent + got
    rate, inv, prod, gain, stat = call(
        kernel_f, "factor", [field, field, field, field, (5,) + plane], stiffness
    )
    stats = gather_levels(stat)
    for substep in range(SUBSTEPS):
        closed = call(
            kernel_m, "interior", [field, field, field], pressure, wind_x, wind_y, jacobian
        )
        wind_x, wind_y, star, value, face = call(
            kernel_b,
            "sweep",
            [field, field, field, field, (4,) + plane],
            pressure,
            *closed,
            wind_z,
            jacobian,
            slope_x,
            slope_y,
            rate,
            inv,
            gain,
            ends,
            *sent,
            *got,
            *static_edges,
            keep=(0, 1, 2, 3, 4),
        )
        faces = gather_levels(face)
        if substep < SUBSTEPS - 1:
            (packed,) = call(kernel_n, "pack", [pair], wind_y)
            wind_z, pressure, edge, inner, outer, ends = call(
                functools.partial(kernel_c, blocks),
                "finish",
                [field, field, (levels, ROWS, lanes), (1,) + plane, (1,) + plane, pair],
                value,
                prod,
                inv,
                star,
                wind_x,
                packed,
                jacobian,
                *faces,
                *stats,
            )
            sent = (edge, inner, outer)
            got = (exchange_rows(edge),) + exchange_lanes(inner, outer)
        else:
            wind_z, pressure = call(
                functools.partial(kernel_d, blocks),
                "last",
                [field, field],
                value,
                prod,
                inv,
                star,
                *faces,
                *stats,
                far_out=True,
                scratch=[
                    pltpu.VMEM(field, jnp.float32),
                    pltpu.VMEM(field, jnp.float32),
                    pltpu.SemaphoreType.DMA((2, CHUNKS)),
                ],
            )
    return wind_x, wind_y, wind_z, pressure


def solution(mesh):
    field = P("lev", "gx", "gy")
    column = P("gx", "gy")
    return jax.shard_map(
        local,
        mesh=mesh,
        in_specs=(field,) * 4 + (column,) * 3 + (field,),
        out_specs=(field,) * 4,
        check_vma=False,
    )
```

```python
import functools

import jax
import jax.numpy as jnp
from jax import lax
from jax.experimental import pallas as pl
from jax.experimental.pallas import tpu as pltpu
from jax.sharding import PartitionSpec as P

SUBSTEPS = 2

grad_coef = 0.35
div_coef = 0.35
vert_coef = 0.25

CG = grad_coef / 12.0
CD = div_coef / 12.0
ROWS = 8
SLOT = 4
UNROLL = 8
CHUNKS = 4


def lane_index():
    return lax.broadcasted_iota(jnp.int32, (ROWS, 128), 1)


def row_index():
    return lax.broadcasted_iota(jnp.int32, (ROWS, 128), 0)


def only(mask, value):
    return jnp.where(mask, jnp.float32(value), jnp.float32(0.0))


def tiles_of(ref, level, count):
    return [ref[level, ROWS * t : ROWS * (t + 1), :] for t in range(count)]


def planes_of(ref, count):
    return [ref[ROWS * t : ROWS * (t + 1), :] for t in range(count)]


def put_tiles(ref, level, tiles):
    for t, tile in enumerate(tiles):
        ref[level, ROWS * t : ROWS * (t + 1), :] = tile


def put_planes(ref, tiles):
    for t, tile in enumerate(tiles):
        ref[ROWS * t : ROWS * (t + 1), :] = tile


class Edge:
    def __init__(self, place, axis, held):
        self.place, self.axis, self.held = place, axis, held
        self.size = place.shape[axis]

    def at(self, places):
        total = None
        for position, value in places.items():
            if position in self.held:
                term = only(self.place == position, value)
                total = term if total is None else total + term
        return total

    def shifted(self, field, by):
        return field if by == 0 else pltpu.roll(field, (-by) % self.size, self.axis)

    def mix(self, field, table):
        total = None
        for by, places in table.items():
            weight = self.at(places)
            if weight is not None:
                term = weight * self.shifted(field, by)
                total = term if total is None else total + term
        return total

    def payload(self, pres, wind, jac):
        partial = self.mix(
            pres,
            {
                1: {0: 8.0, 1: 8.0, 6: 8.0},
                2: {0: -1.0, 1: -1.0},
                -1: {1: -8.0, 6: -8.0, 7: -8.0},
                -2: {6: 1.0, 7: 1.0},
            },
        )
        flux = jac * (wind - CG * partial)
        outer = self.mix(pres, {0: {0: 1.0, 1: 1.0, 6: 1.0, 7: 1.0}})
        return outer + self.mix(flux, {-2: {2: 1.0, 3: 1.0}, 2: {4: 1.0, 5: 1.0}})

    def correct(self, delta, pres, jac, delta_jac):
        grad = self.mix(
            delta, {2: {0: 1.0, 1: 1.0}, 3: {0: -8.0}, -2: {6: -1.0, 7: -1.0}, -3: {7: 8.0}}
        )
        wind = CG * grad
        own = -(jac * wind)
        far = self.mix(delta, {0: {0: 1.0, 1: 1.0, 6: 1.0, 7: 1.0}}) + CG * delta_jac * self.mix(
            pres, {0: {0: 1.0, 1: 1.0, 6: -1.0, 7: -1.0}, -1: {1: -8.0}, 1: {6: 8.0}}
        )
        spread = (
            self.mix(far, {0: {0: 1.0, 1: 1.0, 6: -1.0, 7: -1.0}})
            + self.mix(far - own, {1: {0: -8.0}, -1: {7: 8.0}})
            + self.mix(
                own,
                {
                    -1: {1: -8.0, 2: -8.0},
                    -2: {2: 1.0, 3: 1.0},
                    1: {5: 8.0, 6: 8.0},
                    2: {4: -1.0, 5: -1.0},
                },
            )
        )
        return wind, CD * spread / jac


LOW, HIGH = (0, 1, 2, 3), (4, 5, 6, 7)


def row_edge():
    return Edge(row_index(), 0, LOW + HIGH)


def lane_edge(held):
    return Edge((lane_index() & 3) + held[0], 1, held)


def both_ends(tiles):
    return jnp.where(row_index() < 4, tiles[0], tiles[-1])


def spread_slots(tile, low):
    lane = lane_index()
    if low:
        out = jnp.where(lane < SLOT, tile, 0.0)
    else:
        out = pltpu.roll(jnp.where(lane >= 128 - SLOT, tile, 0.0), SLOT, 1)
    by = SLOT
    while by < 128:
        out = out + pltpu.roll(out, by, 1)
        by *= 2
    return out


class Packer:
    def __init__(self, count):
        self.slot = lax.shift_right_logical(lane_index(), 2)
        self.start = [jnp.zeros((ROWS, 128), jnp.float32)] * (2 * count)
        self.count = count

    def add(self, level, tiles, state):
        before = lax.rem(level + 31, 32)
        rolled = [pltpu.roll(tile, SLOT * level, 1) for tile in tiles]
        low = [jnp.where(self.slot == level, r, s) for r, s in zip(rolled, state)]
        high = [jnp.where(self.slot == before, r, s) for r, s in zip(rolled, state[self.count :])]
        return low + high

    def done(self, state):
        return state[: self.count], [pltpu.roll(s, SLOT, 1) for s in state[self.count :]]


class Closed:
    def __init__(self):
        self.row = row_index()

    def along_y(self, tile):
        pair = tile - pltpu.roll(tile, 126, 1)
        return (pltpu.roll(pair, 2, 1) + pair) - 8.0 * pltpu.roll(pair, 1, 1)

    def moved(self, tiles, by):
        count = len(tiles)
        rolled = [pltpu.roll(tile, by % ROWS, 0) for tile in tiles]
        if by > 0:
            return [jnp.where(self.row < by, rolled[t - 1], rolled[t]) for t in range(count)]
        return [
            jnp.where(self.row >= ROWS + by, rolled[(t + 1) % count], rolled[t])
            for t in range(count)
        ]

    def along_x(self, tiles):
        pair = [f - m for f, m in zip(tiles, self.moved(tiles, -2))]
        return [
            (two + here) - 8.0 * one
            for two, here, one in zip(self.moved(pair, 2), pair, self.moved(pair, 1))
        ]


def even_place():
    return lax.rem(lax.axis_index("gy"), 2) == 0


def put_pair(inner_ref, outer_ref, index, down, up):
    even = even_place()
    put_tiles(inner_ref, index, [jnp.where(even, u, d) for u, d in zip(up, down)])
    put_tiles(outer_ref, index, [jnp.where(even, d, u) for u, d in zip(up, down)])


def get_pair(inner_ref, outer_ref, index, part):
    even = even_place()
    inner, outer = inner_ref[index, part, :], outer_ref[index, part, :]
    return jnp.where(even, outer, inner), jnp.where(even, inner, outer)


def lane_payload(pres, wind, jac):
    low, high = lane_edge(LOW), lane_edge(HIGH)
    down = [
        low.payload(p, w, spread_slots(j, True)) for p, w, j in zip(pres[0], wind[0], jac)
    ]
    up = [
        high.payload(p, w, spread_slots(j, False)) for p, w, j in zip(pres[1], wind[1], jac)
    ]
    return down, up


def pack_levels(ref, count, levels):
    packer = Packer(count)

    def step(level, state):
        return packer.add(level, tiles_of(ref, level, count), state)

    return packer.done(lax.fori_loop(0, levels, step, packer.start, unroll=UNROLL))


def kernel_a(
    p_hbm, wx_hbm, wy_hbm, jac_hbm, rows_ref, inner_ref, outer_ref, pp_ref, p_ref, wx_ref, wy_ref, jac_ref, sems
):
    levels, rows, _ = p_hbm.shape
    count = rows // ROWS
    share = levels // CHUNKS

    def fetch(source, target, sem):
        copy = pltpu.make_async_copy(source, target, sem)
        copy.start()
        return copy

    tail = pl.ds(rows - ROWS, ROWS)
    parts = [pl.ds(c * share, share) for c in range(CHUNKS)]
    pres_in = [fetch(p_hbm.at[s], p_ref.at[s], sems.at[0, c]) for c, s in enumerate(parts)]
    wind_in = [fetch(wy_hbm.at[s], wy_ref.at[s], sems.at[1, c]) for c, s in enumerate(parts)]
    ends_in = [
        fetch(jac_hbm, jac_ref, sems.at[2, 0]),
        fetch(wx_hbm.at[:, pl.ds(0, ROWS)], wx_ref.at[:, pl.ds(0, ROWS)], sems.at[2, 1]),
        fetch(wx_hbm.at[:, tail], wx_ref.at[:, pl.ds(ROWS, ROWS)], sems.at[2, 2]),
    ]

    def pack(ref, copies):
        packer = Packer(count)
        state = packer.start
        for c, copy in enumerate(copies):
            copy.wait()
            state = lax.fori_loop(
                c * share,
                (c + 1) * share,
                lambda level, state: packer.add(level, tiles_of(ref, level, count), state),
                state,
                unroll=UNROLL,
            )
        return packer.done(state)

    pres = pack(p_ref, pres_in)
    wind = pack(wy_ref, wind_in)
    for copy in ends_in:
        copy.wait()
    jac = planes_of(jac_ref, count)
    ends = both_ends(jac)
    edge = row_edge()

    def step(level, state):
        rows_ref[level] = edge.payload(
            both_ends(tiles_of(p_ref, level, count)), both_ends(tiles_of(wx_ref, level, 2)), ends
        )
        return state

    lax.fori_loop(0, levels, step, 0, unroll=2 * UNROLL)
    rows_ref[levels] = ends
    down, up = lane_payload(pres, wind, jac)
    put_pair(inner_ref, outer_ref, 0, down, up)
    put_pair(
        inner_ref,
        outer_ref,
        1,
        [spread_slots(j, True) for j in jac],
        [spread_slots(j, False) for j in jac],
    )
    put_tiles(pp_ref, 0, pres[0])
    put_tiles(pp_ref, 1, pres[1])


def kernel_n(wy_ref, pw_ref):
    levels, rows, _ = wy_ref.shape
    count = rows // ROWS
    wind = pack_levels(wy_ref, count, levels)
    put_tiles(pw_ref, 0, wind[0])
    put_tiles(pw_ref, 1, wind[1])


def kernel_m(p_ref, wx_ref, wy_ref, jac_ref, nx_ref, ny_ref, ps_ref):
    levels, rows, _ = p_ref.shape
    count = rows // ROWS
    jac = planes_of(jac_ref, count)
    inv_jac = [CD / j for j in jac]
    closed = Closed()

    def step(level, state):
        pres = tiles_of(p_ref, level, count)
        wind_x = tiles_of(wx_ref, level, count)
        wind_y = tiles_of(wy_ref, level, count)
        new_x = [w - CG * d for w, d in zip(wind_x, closed.along_x(pres))]
        new_y = [w - CG * closed.along_y(p) for w, p in zip(wind_y, pres)]
        put_tiles(nx_ref, level, new_x)
        put_tiles(ny_ref, level, new_y)
        spread_x = closed.along_x([j * n for j, n in zip(jac, new_x)])
        spread_y = [closed.along_y(j * n) for j, n in zip(jac, new_y)]
        put_tiles(
            ps_ref,
            level,
            [p - i * (x + y) for p, i, x, y in zip(pres, inv_jac, spread_x, spread_y)],
        )
        return state

    lax.fori_loop(0, levels, step, 0, unroll=UNROLL)


def kernel_b(
    p_ref,
    nxc_ref,
    nyc_ref,
    psc_ref,
    wz_ref,
    jac_ref,
    sx_ref,
    sy_ref,
    r_ref,
    i_ref,
    v_ref,
    pp_ref,
    rows_ref,
    inner_ref,
    outer_ref,
    got_rows_ref,
    got_inner_ref,
    got_outer_ref,
    srows_ref,
    sinner_ref,
    souter_ref,
    got_srows_ref,
    got_sinner_ref,
    got_souter_ref,
    nx_ref,
    ny_ref,
    ps_ref,
    y_ref,
    face_ref,
):
    levels, rows, _ = p_ref.shape
    count = rows // ROWS
    last = count - 1
    lane, row = lane_index(), row_index()
    low_edge, high_edge, edge = lane_edge(LOW), lane_edge(HIGH), row_edge()
    wind_fix, low_fix, high_fix = [], [], []
    for t in range(count):
        part = slice(ROWS * t, ROWS * (t + 1))
        jac_low, jac_high = get_pair(sinner_ref, souter_ref, 1, part)
        jac_below, jac_above = get_pair(got_sinner_ref, got_souter_ref, 1, part)
        down, up = get_pair(inner_ref, outer_ref, 0, part)
        below, above = get_pair(got_inner_ref, got_outer_ref, 0, part)
        low_wind, low_star = low_edge.correct(
            below - up, pp_ref[0, part, :], jac_low, low_edge.shifted(jac_below - jac_high, 2)
        )
        high_wind, high_star = high_edge.correct(
            above - down, pp_ref[1, part, :], jac_high, high_edge.shifted(jac_above - jac_low, -2)
        )
        wind_fix.append(low_wind + pltpu.roll(high_wind, 128 - SLOT, 1))
        low_fix.append(low_star)
        high_fix.append(pltpu.roll(high_star, 128 - SLOT, 1))
    ends = srows_ref[levels]
    change = got_srows_ref[levels] - ends
    ends_change = jnp.where(row < 4, edge.shifted(change, -2), edge.shifted(change, 2))
    outer = (lane < 2) | (lane >= 126)
    low_lanes, high_lanes = lane < SLOT, lane >= 128 - SLOT
    first_rows = row < 4

    def star(level):
        new_x = tiles_of(nxc_ref, level, count)
        new_y = tiles_of(nyc_ref, level, count)
        stars = tiles_of(psc_ref, level, count)
        wind, press = edge.correct(
            pltpu.roll(got_rows_ref[level] - rows_ref[level], 4, 0),
            jnp.where(first_rows, p_ref[level, :ROWS, :], p_ref[level, ROWS * last :, :]),
            ends,
            ends_change,
        )
        new_x[0] = new_x[0] - jnp.where(first_rows, wind, 0.0)
        new_x[last] = new_x[last] - jnp.where(first_rows, 0.0, wind)
        stars[0] = stars[0] - jnp.where(first_rows, press, 0.0)
        stars[last] = stars[last] - jnp.where(first_rows, 0.0, press)
        back = lax.rem(128 - SLOT * level, 128)
        forces = []
        for t in range(count):
            part = slice(ROWS * t, ROWS * (t + 1))
            new_y[t] = new_y[t] - jnp.where(outer, pltpu.roll(wind_fix[t], back, 1), 0.0)
            fix = jnp.where(
                low_lanes,
                pltpu.roll(low_fix[t], back, 1),
                jnp.where(high_lanes, pltpu.roll(high_fix[t], back, 1), 0.0),
            )
            stars[t] = stars[t] - fix
            forces.append(
                wz_ref[level, part, :]
                + sx_ref[part, :] * new_x[t]
                + sy_ref[part, :] * new_y[t]
            )
        put_tiles(nx_ref, level, new_x)
        put_tiles(ny_ref, level, new_y)
        put_tiles(ps_ref, level, stars)
        return stars, forces

    def sweep(level, below, above, force, value, first):
        rate = tiles_of(r_ref, level, count)
        inv = tiles_of(i_ref, level, count)
        gain = tiles_of(v_ref, level, count)
        values, firsts = [], []
        for t in range(count):
            rhs = rate[t] * (force[t] - vert_coef * (above[t] - below[t]))
            firsts.append(first[t] + gain[t] * rhs)
            values.append((rhs + value[t]) * inv[t])
        put_tiles(y_ref, level, values)
        return values, firsts

    zeros = [jnp.zeros((ROWS, 128), jnp.float32)] * count
    here, force = star(0)
    put_tiles(face_ref, 2, here)

    def step(level, carry):
        below, here, force, value, first = carry
        above, force_next = star(level)
        value, first = sweep(level - 1, below, above, force, value, first)
        return here, above, force_next, value, first

    below, here, force, value, first = lax.fori_loop(
        1, levels, step, (zeros, here, force, zeros, zeros), unroll=UNROLL
    )
    value, first = sweep(levels - 1, below, zeros, force, value, first)
    put_tiles(face_ref, 0, first)
    put_tiles(face_ref, 1, value)
    put_tiles(face_ref, 3, here)


def kernel_f(s_ref, r_ref, i_ref, q_ref, v_ref, stat_ref):
    levels, rows, _ = s_ref.shape

    def down(level, carry):
        excess, prod = carry
        rate = 1.0 / s_ref[level]
        excess = rate + excess
        inv = 1.0 / (1.0 + excess)
        prod = prod * inv
        r_ref[level] = rate
        i_ref[level] = inv
        q_ref[level] = prod
        return excess * inv, prod

    ones = jnp.ones((rows, 128), jnp.float32)
    lax.fori_loop(0, levels, down, (ones, ones))

    def up(step, value):
        level = levels - 1 - step
        value = q_ref[level] + i_ref[level] * value
        v_ref[level] = value
        return value

    first = lax.fori_loop(0, levels, up, jnp.zeros((rows, 128), jnp.float32))
    stat_ref[0] = first
    stat_ref[1] = q_ref[levels - 1]
    stat_ref[2] = i_ref[levels - 1]
    stat_ref[3] = r_ref[0]
    stat_ref[4] = r_ref[levels - 1]


def reduced(blocks, mine, face, stat):
    faces = [face(j) for j in range(blocks)]
    stats = [stat(j) for j in range(blocks)]
    up = [
        faces[j][1] + vert_coef * stats[j + 1][3] * faces[j][3] if j < blocks - 1 else None
        for j in range(blocks)
    ]
    down = [
        faces[j][0] - vert_coef * stats[j - 1][4] * faces[j][2] if j > 0 else None
        for j in range(blocks)
    ]
    base, slope = [up[0]], [stats[0][2]]
    scale, known = [None], [None]
    for j in range(1, blocks):
        near, link, far = stats[j][0], stats[j][1], stats[j][2]
        scale.append(1.0 / (1.0 - near * slope[j - 1]))
        known.append(scale[j] * (down[j] + near * base[j - 1]))
        if j < blocks - 1:
            base.append(up[j] + link * (base[j - 1] + slope[j - 1] * known[j]))
            slope.append(far + link * link * slope[j - 1] * scale[j])
    zero = jnp.zeros_like(faces[0][0])
    above = [None] * blocks + [zero]
    below = [zero] + [None] * blocks
    for j in range(blocks - 1, 0, -1):
        above[j] = known[j] + scale[j] * stats[j][1] * above[j + 1]
        below[j] = base[j - 1] + slope[j - 1] * above[j]
    lower, upper, under, over = zero, zero, zero, zero
    for j in range(blocks):
        here = mine == j
        if j > 0:
            lower = jnp.where(here, below[j], lower)
            under = jnp.where(
                here, below[j] - vert_coef * stats[j][3] * faces[j - 1][3], under
            )
        if j < blocks - 1:
            upper = jnp.where(here, above[j + 1], upper)
            over = jnp.where(
                here, above[j + 1] + vert_coef * stats[j][4] * faces[j + 1][2], over
            )
    return lower, upper, under, over


def boundary(blocks, mine, count, face_refs, stat_refs):
    def solve(t):
        part = slice(ROWS * t, ROWS * (t + 1))

        def read(refs, planes):
            own = [
                [ref[k, part, :] for k in range(planes)] for ref in refs
            ]

            def block(j):
                out = []
                for k in range(planes):
                    value = own[0][k]
                    for shift in range(1, blocks):
                        value = jnp.where(mine == (j ^ shift), own[shift][k], value)
                    out.append(value)
                return out

            return block

        return reduced(blocks, mine, read(face_refs, 4), read(stat_refs, 5))

    parts = [solve(t) for t in range(count)]
    return [[part[k] for part in parts] for k in range(4)]


def finish(blocks, count, levels, y_ref, q_ref, i_ref, ps_ref, x_ref, p_ref, face_refs, stat_refs, use):
    mine = lax.axis_index("lev")
    lower, upper, under, over = boundary(blocks, mine, count, face_refs, stat_refs)

    def solved(level, above):
        value = tiles_of(y_ref, level, count)
        prod = tiles_of(q_ref, level, count)
        inv = tiles_of(i_ref, level, count)
        out = [y + q * u + i * a for y, q, u, i, a in zip(value, prod, lower, inv, above)]
        put_tiles(x_ref, level, out)
        return out

    def pressed(level, above, below, state):
        star = tiles_of(ps_ref, level, count)
        pres = [s - vert_coef * (a - b) for s, a, b in zip(star, above, below)]
        put_tiles(p_ref, level, pres)
        return use(level, pres, state)

    def step(index, carry):
        above, here, state = carry
        level = levels - 2 - index
        below = solved(level, here)
        state = pressed(level + 1, above, below, state)
        return here, below, state

    top = solved(levels - 1, upper)
    zeros = [jnp.zeros((ROWS, 128), jnp.float32)] * count
    above, here, state = lax.fori_loop(0, levels - 1, step, (over, top, (zeros, zeros)))
    return pressed(0, above, under, state)


def finish(blocks, count, levels, y_ref, q_ref, i_ref, ps_ref, x_ref, p_ref, face_refs, stat_refs, use, state, ready=None):
    mine = lax.axis_index("lev")
    lower, upper, under, over = boundary(blocks, mine, count, face_refs, stat_refs)

    def solved(level, above):
        value = tiles_of(y_ref, level, count)
        prod = tiles_of(q_ref, level, count)
        inv = tiles_of(i_ref, level, count)
        out = [(y + q * u) + i * a for y, q, u, i, a in zip(value, prod, lower, inv, above)]
        put_tiles(x_ref, level, out)
        return out

    def pressed(level, above, below, state):
        star = tiles_of(ps_ref, level, count)
        pres = [s - vert_coef * (a - b) for s, a, b in zip(star, above, below)]
        put_tiles(p_ref, level, pres)
        return use(level, pres, state)

    def step(index, carry):
        above, here, state = carry
        level = levels - 2 - index
        below = solved(level, here)
        state = pressed(level + 1, above, below, state)
        return here, below, state

    top = solved(levels - 1, upper)
    carry = (over, top, state)
    if ready is None:
        carry = lax.fori_loop(0, levels - 1, step, carry, unroll=UNROLL)
    else:
        done, share = 0, levels // CHUNKS
        for c in range(CHUNKS - 1, -1, -1):
            goal = levels - 1 - c * share
            carry = lax.fori_loop(done, goal, step, carry, unroll=UNROLL)
            done = goal
            ready(c)
    above, here, state = carry
    return pressed(0, above, under, state)


def kernel_c(blocks, y_ref, q_ref, i_ref, ps_ref, wx_ref, pw_ref, jac_ref, *refs):
    face_refs, stat_refs = refs[:blocks], refs[blocks : 2 * blocks]
    x_ref, p_ref, rows_ref, inner_ref, outer_ref, pp_ref = refs[2 * blocks :]
    levels, rows, _ = y_ref.shape
    count = rows // ROWS
    packer = Packer(count)
    edge = row_edge()
    ends = both_ends(planes_of(jac_ref, count))

    def use(level, pres, state):
        rows_ref[level] = edge.payload(
            both_ends(pres), both_ends(tiles_of(wx_ref, level, count)), ends
        )
        return packer.add(level, pres, state)

    state = finish(
        blocks,
        count,
        levels,
        y_ref,
        q_ref,
        i_ref,
        ps_ref,
        x_ref,
        p_ref,
        face_refs,
        stat_refs,
        use,
        packer.start,
    )
    pres = packer.done(state)
    wind = tiles_of(pw_ref, 0, count), tiles_of(pw_ref, 1, count)
    down, up = lane_payload(pres, wind, planes_of(jac_ref, count))
    put_pair(inner_ref, outer_ref, 0, down, up)
    put_tiles(pp_ref, 0, pres[0])
    put_tiles(pp_ref, 1, pres[1])


def kernel_d(blocks, y_ref, q_ref, i_ref, ps_ref, *refs):
    face_refs, stat_refs = refs[:blocks], refs[blocks : 2 * blocks]
    x_hbm, p_hbm, x_ref, p_ref, sems = refs[2 * blocks :]
    levels, rows, _ = y_ref.shape
    share = levels // CHUNKS
    copies = []

    def send(index, source, target, c):
        part = pl.ds(c * share, share)
        copy = pltpu.make_async_copy(source.at[part], target.at[part], sems.at[index, c])
        copy.start()
        copies.append(copy)

    def ready(c):
        send(0, x_ref, x_hbm, c)
        if c < CHUNKS - 1:
            send(1, p_ref, p_hbm, c + 1)

    finish(
        blocks,
        rows // ROWS,
        levels,
        y_ref,
        q_ref,
        i_ref,
        ps_ref,
        x_ref,
        p_ref,
        face_refs,
        stat_refs,
        lambda level, pres, state: state,
        0,
        ready,
    )
    send(1, p_ref, p_hbm, 0)
    for copy in copies:
        copy.wait()


def call(kernel, name, shapes, *args, far_in=False, far_out=False, scratch=(), keep=()):
    near, far = pl.BlockSpec(memory_space=pltpu.VMEM), pl.BlockSpec(memory_space=pl.ANY)
    size = sum(a.size for a in args) + sum(functools.reduce(lambda a, b: a * b, s) for s in shapes)
    if far_in:
        args = [pltpu.with_memory_space_constraint(a, pltpu.HBM) for a in args]
    return pl.pallas_call(
        kernel,
        out_shape=[
            pltpu.VMEM(s, jnp.float32) if k in keep else jax.ShapeDtypeStruct(s, jnp.float32)
            for k, s in enumerate(shapes)
        ],
        in_specs=[far if far_in else near] * len(args),
        out_specs=[far if far_out else near] * len(shapes),
        scratch_shapes=list(scratch),
        compiler_params=pltpu.CompilerParams(vmem_limit_bytes=32 * 1024 * 1024),
        cost_estimate=pl.CostEstimate(
            flops=8 * size, bytes_accessed=4 * size, transcendentals=0
        ),
        name=name,
    )(*args)


def swap(value, axis, partner):
    count = lax.axis_size(axis)
    return lax.ppermute(value, axis, [(i, partner(i)) for i in range(count)])


def exchange_rows(rows):
    count = lax.axis_size("gx")
    if count == 2:
        return swap(rows, "gx", lambda i: 1 - i)
    down = swap(rows[:, : ROWS // 2], "gx", lambda i: (i - 1) % count)
    up = swap(rows[:, ROWS // 2 :], "gx", lambda i: (i + 1) % count)
    return jnp.concatenate([down, up], axis=1)


def exchange_lanes(inner, outer):
    count = lax.axis_size("gy")
    got_outer = swap(outer, "gy", lambda i: (i + 1 if i % 2 else i - 1) % count)
    got_inner = swap(inner, "gy", lambda i: i ^ 1)
    return got_inner, got_outer


def gather_levels(planes):
    count = lax.axis_size("lev")
    return [planes] + [
        swap(planes, "lev", lambda i, shift=shift: i ^ shift) for shift in range(1, count)
    ]


def local(wind_x, wind_y, wind_z, pressure, jacobian, slope_x, slope_y, stiffness):
    field = wind_x.shape
    levels, rows, lanes = field
    blocks = lax.axis_size("lev")
    plane = (rows, lanes)
    pair = (2,) + plane
    assert lanes == 128 and levels * SLOT == 128 and rows % ROWS == 0
    assert blocks & (blocks - 1) == 0 and lax.axis_size("gy") % 2 == 0

    edge, inner, outer, ends = call(
        kernel_a,
        "start",
        [(levels + 1, ROWS, lanes), pair, pair, pair],
        pressure,
        wind_x,
        wind_y,
        jacobian,
        far_in=True,
        scratch=[
            pltpu.VMEM(field, jnp.float32),
            pltpu.VMEM((levels, 2 * ROWS, lanes), jnp.float32),
            pltpu.VMEM(field, jnp.float32),
            pltpu.VMEM(plane, jnp.float32),
            pltpu.SemaphoreType.DMA((3, CHUNKS)),
        ],
    )
    sent = (edge, inner, outer)
    got = (exchange_rows(edge),) + exchange_lanes(inner, outer)
    static_edges = sent + got
    rate, inv, prod, gain, stat = call(
        kernel_f, "factor", [field, field, field, field, (5,) + plane], stiffness
    )
    stats = gather_levels(stat)
    for substep in range(SUBSTEPS):
        closed = call(
            kernel_m, "interior", [field, field, field], pressure, wind_x, wind_y, jacobian
        )
        wind_x, wind_y, star, value, face = call(
            kernel_b,
            "sweep",
            [field, field, field, field, (4,) + plane],
            pressure,
            *closed,
            wind_z,
            jacobian,
            slope_x,
            slope_y,
            rate,
            inv,
            gain,
            ends,
            *sent,
            *got,
            *static_edges,
            keep=(0, 1, 2, 3, 4),
        )
        faces = gather_levels(face)
        if substep < SUBSTEPS - 1:
            (packed,) = call(kernel_n, "pack", [pair], wind_y)
            wind_z, pressure, edge, inner, outer, ends = call(
                functools.partial(kernel_c, blocks),
                "finish",
                [field, field, (levels, ROWS, lanes), (1,) + plane, (1,) + plane, pair],
                value,
                prod,
                inv,
                star,
                wind_x,
                packed,
                jacobian,
                *faces,
                *stats,
            )
            sent = (edge, inner, outer)
            got = (exchange_rows(edge),) + exchange_lanes(inner, outer)
        else:
            wind_z, pressure = call(
                functools.partial(kernel_d, blocks),
                "last",
                [field, field],
                value,
                prod,
                inv,
                star,
                *faces,
                *stats,
                far_out=True,
                scratch=[
                    pltpu.VMEM(field, jnp.float32),
                    pltpu.VMEM(field, jnp.float32),
                    pltpu.SemaphoreType.DMA((2, CHUNKS)),
                ],
            )
    return wind_x, wind_y, wind_z, pressure


def solution(mesh):
    field = P("lev", "gx", "gy")
    column = P("gx", "gy")
    return jax.shard_map(
        local,
        mesh=mesh,
        in_specs=(field,) * 4 + (column,) * 3 + (field,),
        out_specs=(field,) * 4,
        check_vma=False,
    )
```

```python
import functools

import jax
import jax.numpy as jnp
from jax import lax
from jax.experimental import pallas as pl
from jax.experimental.pallas import tpu as pltpu
from jax.sharding import PartitionSpec as P

SUBSTEPS = 2

grad_coef = 0.35
div_coef = 0.35
vert_coef = 0.25

CG = grad_coef / 12.0
CD = div_coef / 12.0
ROWS = 8
SLOT = 4
UNROLL = 8
CHUNKS = 4
COLUMN = 7


def lane_index():
    return lax.broadcasted_iota(jnp.int32, (ROWS, 128), 1)


def row_index():
    return lax.broadcasted_iota(jnp.int32, (ROWS, 128), 0)


def only(mask, value):
    return jnp.where(mask, jnp.float32(value), jnp.float32(0.0))


def tiles_of(ref, level, count):
    return [ref[level, ROWS * t : ROWS * (t + 1), :] for t in range(count)]


def planes_of(ref, count):
    return [ref[ROWS * t : ROWS * (t + 1), :] for t in range(count)]


def put_tiles(ref, level, tiles):
    for t, tile in enumerate(tiles):
        ref[level, ROWS * t : ROWS * (t + 1), :] = tile


def put_planes(ref, tiles):
    for t, tile in enumerate(tiles):
        ref[ROWS * t : ROWS * (t + 1), :] = tile


class Edge:
    def __init__(self, place, axis, held):
        self.place, self.axis, self.held = place, axis, held
        self.size = place.shape[axis]

    def at(self, places):
        total = None
        for position, value in places.items():
            if position in self.held:
                term = only(self.place == position, value)
                total = term if total is None else total + term
        return total

    def shifted(self, field, by):
        return field if by == 0 else pltpu.roll(field, (-by) % self.size, self.axis)

    def mix(self, field, table):
        total = None
        for by, places in table.items():
            weight = self.at(places)
            if weight is not None:
                term = weight * self.shifted(field, by)
                total = term if total is None else total + term
        return total

    def payload(self, pres, wind, jac):
        partial = self.mix(
            pres,
            {
                1: {0: 8.0, 1: 8.0, 6: 8.0},
                2: {0: -1.0, 1: -1.0},
                -1: {1: -8.0, 6: -8.0, 7: -8.0},
                -2: {6: 1.0, 7: 1.0},
            },
        )
        flux = jac * (wind - CG * partial)
        outer = self.mix(pres, {0: {0: 1.0, 1: 1.0, 6: 1.0, 7: 1.0}})
        return outer + self.mix(flux, {-2: {2: 1.0, 3: 1.0}, 2: {4: 1.0, 5: 1.0}})

    def correct(self, delta, pres, jac, delta_jac):
        grad = self.mix(
            delta, {2: {0: 1.0, 1: 1.0}, 3: {0: -8.0}, -2: {6: -1.0, 7: -1.0}, -3: {7: 8.0}}
        )
        wind = CG * grad
        own = -(jac * wind)
        far = self.mix(delta, {0: {0: 1.0, 1: 1.0, 6: 1.0, 7: 1.0}}) + CG * delta_jac * self.mix(
            pres, {0: {0: 1.0, 1: 1.0, 6: -1.0, 7: -1.0}, -1: {1: -8.0}, 1: {6: 8.0}}
        )
        spread = (
            self.mix(far, {0: {0: 1.0, 1: 1.0, 6: -1.0, 7: -1.0}})
            + self.mix(far - own, {1: {0: -8.0}, -1: {7: 8.0}})
            + self.mix(
                own,
                {
                    -1: {1: -8.0, 2: -8.0},
                    -2: {2: 1.0, 3: 1.0},
                    1: {5: 8.0, 6: 8.0},
                    2: {4: -1.0, 5: -1.0},
                },
            )
        )
        return wind, CD * spread / jac


LOW, HIGH = (0, 1, 2, 3), (4, 5, 6, 7)


def row_edge():
    return Edge(row_index(), 0, LOW + HIGH)


def lane_edge(held):
    return Edge((lane_index() & 3) + held[0], 1, held)


def both_ends(tiles):
    return jnp.where(row_index() < 4, tiles[0], tiles[-1])


def spread_slots(tile, low):
    lane = lane_index()
    if low:
        out = jnp.where(lane < SLOT, tile, 0.0)
    else:
        out = pltpu.roll(jnp.where(lane >= 128 - SLOT, tile, 0.0), SLOT, 1)
    by = SLOT
    while by < 128:
        out = out + pltpu.roll(out, by, 1)
        by *= 2
    return out


class Packer:
    def __init__(self, count):
        self.slot = lax.shift_right_logical(lane_index(), 2)
        self.start = [jnp.zeros((ROWS, 128), jnp.float32)] * (2 * count)
        self.count = count

    def add(self, level, tiles, state):
        before = lax.rem(level + 31, 32)
        rolled = [pltpu.roll(tile, SLOT * level, 1) for tile in tiles]
        low = [jnp.where(self.slot == level, r, s) for r, s in zip(rolled, state)]
        high = [jnp.where(self.slot == before, r, s) for r, s in zip(rolled, state[self.count :])]
        return low + high

    def done(self, state):
        return state[: self.count], [pltpu.roll(s, SLOT, 1) for s in state[self.count :]]


class Closed:
    def __init__(self):
        self.row = row_index()

    def along_y(self, tile):
        pair = tile - pltpu.roll(tile, 126, 1)
        return (pltpu.roll(pair, 2, 1) + pair) - 8.0 * pltpu.roll(pair, 1, 1)

    def moved(self, tiles, by):
        count = len(tiles)
        rolled = [pltpu.roll(tile, by % ROWS, 0) for tile in tiles]
        if by > 0:
            return [jnp.where(self.row < by, rolled[t - 1], rolled[t]) for t in range(count)]
        return [
            jnp.where(self.row >= ROWS + by, rolled[(t + 1) % count], rolled[t])
            for t in range(count)
        ]

    def along_x(self, tiles):
        pair = [f - m for f, m in zip(tiles, self.moved(tiles, -2))]
        return [
            (two + here) - 8.0 * one
            for two, here, one in zip(self.moved(pair, 2), pair, self.moved(pair, 1))
        ]


def even_place():
    return lax.rem(lax.axis_index("gy"), 2) == 0


def put_pair(inner_ref, outer_ref, index, down, up):
    even = even_place()
    put_tiles(inner_ref, index, [jnp.where(even, u, d) for u, d in zip(up, down)])
    put_tiles(outer_ref, index, [jnp.where(even, d, u) for u, d in zip(up, down)])


def get_pair(inner_ref, outer_ref, index, part):
    even = even_place()
    inner, outer = inner_ref[index, part, :], outer_ref[index, part, :]
    return jnp.where(even, outer, inner), jnp.where(even, inner, outer)


def lane_payload(pres, wind, jac):
    low, high = lane_edge(LOW), lane_edge(HIGH)
    down = [
        low.payload(p, w, spread_slots(j, True)) for p, w, j in zip(pres[0], wind[0], jac)
    ]
    up = [
        high.payload(p, w, spread_slots(j, False)) for p, w, j in zip(pres[1], wind[1], jac)
    ]
    return down, up


def pack_levels(ref, count, levels):
    packer = Packer(count)

    def step(level, state):
        return packer.add(level, tiles_of(ref, level, count), state)

    return packer.done(lax.fori_loop(0, levels, step, packer.start, unroll=UNROLL))


def kernel_a(
    p_hbm, wx_hbm, wy_hbm, jac_hbm, rows_ref, inner_ref, outer_ref, pp_ref, p_ref, wx_ref, wy_ref, jac_ref, sems
):
    levels, rows, _ = p_hbm.shape
    count = rows // ROWS
    share = levels // CHUNKS

    def fetch(source, target, sem):
        copy = pltpu.make_async_copy(source, target, sem)
        copy.start()
        return copy

    tail = pl.ds(rows - ROWS, ROWS)
    parts = [pl.ds(c * share, share) for c in range(CHUNKS)]
    pres_in = [fetch(p_hbm.at[s], p_ref.at[s], sems.at[0, c]) for c, s in enumerate(parts)]
    wind_in = [fetch(wy_hbm.at[s], wy_ref.at[s], sems.at[1, c]) for c, s in enumerate(parts)]
    ends_in = [
        fetch(jac_hbm, jac_ref, sems.at[2, 0]),
        fetch(wx_hbm.at[:, pl.ds(0, ROWS)], wx_ref.at[:, pl.ds(0, ROWS)], sems.at[2, 1]),
        fetch(wx_hbm.at[:, tail], wx_ref.at[:, pl.ds(ROWS, ROWS)], sems.at[2, 2]),
    ]

    def pack(ref, copies):
        packer = Packer(count)
        state = packer.start
        for c, copy in enumerate(copies):
            copy.wait()
            state = lax.fori_loop(
                c * share,
                (c + 1) * share,
                lambda level, state: packer.add(level, tiles_of(ref, level, count), state),
                state,
                unroll=UNROLL,
            )
        return packer.done(state)

    pres = pack(p_ref, pres_in)
    wind = pack(wy_ref, wind_in)
    for copy in ends_in:
        copy.wait()
    jac = planes_of(jac_ref, count)
    ends = both_ends(jac)
    edge = row_edge()

    def step(level, state):
        rows_ref[level] = edge.payload(
            both_ends(tiles_of(p_ref, level, count)), both_ends(tiles_of(wx_ref, level, 2)), ends
        )
        return state

    lax.fori_loop(0, levels, step, 0, unroll=2 * UNROLL)
    rows_ref[levels] = ends
    down, up = lane_payload(pres, wind, jac)
    put_pair(inner_ref, outer_ref, 0, down, up)
    put_pair(
        inner_ref,
        outer_ref,
        1,
        [spread_slots(j, True) for j in jac],
        [spread_slots(j, False) for j in jac],
    )
    put_tiles(pp_ref, 0, pres[0])
    put_tiles(pp_ref, 1, pres[1])


def kernel_n(wy_ref, pw_ref):
    levels, rows, _ = wy_ref.shape
    count = rows // ROWS
    wind = pack_levels(wy_ref, count, levels)
    put_tiles(pw_ref, 0, wind[0])
    put_tiles(pw_ref, 1, wind[1])


def kernel_m(p_ref, wx_ref, wy_ref, jac_ref, nx_ref, ny_ref, ps_ref):
    levels, rows, _ = p_ref.shape
    count = rows // ROWS
    jac = planes_of(jac_ref, count)
    inv_jac = [CD / j for j in jac]
    closed = Closed()

    def step(level, state):
        pres = tiles_of(p_ref, level, count)
        wind_x = tiles_of(wx_ref, level, count)
        wind_y = tiles_of(wy_ref, level, count)
        new_x = [w - CG * d for w, d in zip(wind_x, closed.along_x(pres))]
        new_y = [w - CG * closed.along_y(p) for w, p in zip(wind_y, pres)]
        put_tiles(nx_ref, level, new_x)
        put_tiles(ny_ref, level, new_y)
        spread_x = closed.along_x([j * n for j, n in zip(jac, new_x)])
        spread_y = [closed.along_y(j * n) for j, n in zip(jac, new_y)]
        put_tiles(
            ps_ref,
            level,
            [p - i * (x + y) for p, i, x, y in zip(pres, inv_jac, spread_x, spread_y)],
        )
        return state

    lax.fori_loop(0, levels, step, 0, unroll=UNROLL)


def kernel_b(
    p_ref,
    nxc_ref,
    nyc_ref,
    psc_ref,
    wz_ref,
    jac_ref,
    sx_ref,
    sy_ref,
    r_ref,
    i_ref,
    v_ref,
    pp_ref,
    rows_ref,
    inner_ref,
    outer_ref,
    got_rows_ref,
    got_inner_ref,
    got_outer_ref,
    srows_ref,
    sinner_ref,
    souter_ref,
    got_srows_ref,
    got_sinner_ref,
    got_souter_ref,
    coef_ref,
    far_ref,
    nx_ref,
    ny_ref,
    ps_ref,
    y_ref,
    near_ref,
    cross_ref,
    next_ref,
):
    levels, rows, _ = p_ref.shape
    count = rows // ROWS
    last = count - 1
    lane, row = lane_index(), row_index()
    low_edge, high_edge, edge = lane_edge(LOW), lane_edge(HIGH), row_edge()
    wind_fix, low_fix, high_fix = [], [], []
    for t in range(count):
        part = slice(ROWS * t, ROWS * (t + 1))
        jac_low, jac_high = get_pair(sinner_ref, souter_ref, 1, part)
        jac_below, jac_above = get_pair(got_sinner_ref, got_souter_ref, 1, part)
        down, up = get_pair(inner_ref, outer_ref, 0, part)
        below, above = get_pair(got_inner_ref, got_outer_ref, 0, part)
        low_wind, low_star = low_edge.correct(
            below - up, pp_ref[0, part, :], jac_low, low_edge.shifted(jac_below - jac_high, 2)
        )
        high_wind, high_star = high_edge.correct(
            above - down, pp_ref[1, part, :], jac_high, high_edge.shifted(jac_above - jac_low, -2)
        )
        wind_fix.append(low_wind + pltpu.roll(high_wind, 128 - SLOT, 1))
        low_fix.append(low_star)
        high_fix.append(pltpu.roll(high_star, 128 - SLOT, 1))
    ends = srows_ref[levels]
    change = got_srows_ref[levels] - ends
    ends_change = jnp.where(row < 4, edge.shifted(change, -2), edge.shifted(change, 2))
    outer = (lane < 2) | (lane >= 126)
    low_lanes, high_lanes = lane < SLOT, lane >= 128 - SLOT
    first_rows = row < 4

    def star(level):
        new_x = tiles_of(nxc_ref, level, count)
        new_y = tiles_of(nyc_ref, level, count)
        stars = tiles_of(psc_ref, level, count)
        wind, press = edge.correct(
            pltpu.roll(got_rows_ref[level] - rows_ref[level], 4, 0),
            jnp.where(first_rows, p_ref[level, :ROWS, :], p_ref[level, ROWS * last :, :]),
            ends,
            ends_change,
        )
        new_x[0] = new_x[0] - jnp.where(first_rows, wind, 0.0)
        new_x[last] = new_x[last] - jnp.where(first_rows, 0.0, wind)
        stars[0] = stars[0] - jnp.where(first_rows, press, 0.0)
        stars[last] = stars[last] - jnp.where(first_rows, 0.0, press)
        back = lax.rem(128 - SLOT * level, 128)
        forces = []
        for t in range(count):
            part = slice(ROWS * t, ROWS * (t + 1))
            new_y[t] = new_y[t] - jnp.where(outer, pltpu.roll(wind_fix[t], back, 1), 0.0)
            fix = jnp.where(
                low_lanes,
                pltpu.roll(low_fix[t], back, 1),
                jnp.where(high_lanes, pltpu.roll(high_fix[t], back, 1), 0.0),
            )
            stars[t] = stars[t] - fix
            forces.append(
                wz_ref[level, part, :]
                + sx_ref[part, :] * new_x[t]
                + sy_ref[part, :] * new_y[t]
            )
        put_tiles(nx_ref, level, new_x)
        put_tiles(ny_ref, level, new_y)
        put_tiles(ps_ref, level, stars)
        return stars, forces

    def sweep(level, below, above, force, value, first):
        rate = tiles_of(r_ref, level, count)
        inv = tiles_of(i_ref, level, count)
        gain = tiles_of(v_ref, level, count)
        values, firsts = [], []
        for t in range(count):
            rhs = rate[t] * (force[t] - vert_coef * (above[t] - below[t]))
            firsts.append(first[t] + gain[t] * rhs)
            values.append((rhs + value[t]) * inv[t])
        put_tiles(y_ref, level, values)
        return values, firsts

    zeros = [jnp.zeros((ROWS, 128), jnp.float32)] * count
    here, force = star(0)
    bottom = here

    def step(level, carry):
        below, here, force, value, first = carry
        above, force_next = star(level)
        value, first = sweep(level - 1, below, above, force, value, first)
        return here, above, force_next, value, first

    below, here, force, value, first = lax.fori_loop(
        1, levels, step, (zeros, here, force, zeros, zeros), unroll=UNROLL
    )
    value, first = sweep(levels - 1, below, zeros, force, value, first)
    interface(first, value, bottom, here, coef_ref, far_ref, near_ref, cross_ref, next_ref)


def kernel_f(s_ref, r_ref, i_ref, q_ref, v_ref, stat_ref):
    levels, rows, _ = s_ref.shape

    def down(level, carry):
        excess, prod = carry
        rate = 1.0 / s_ref[level]
        excess = rate + excess
        inv = 1.0 / (1.0 + excess)
        prod = prod * inv
        r_ref[level] = rate
        i_ref[level] = inv
        q_ref[level] = prod
        return excess * inv, prod

    ones = jnp.ones((rows, 128), jnp.float32)
    lax.fori_loop(0, levels, down, (ones, ones))

    def up(step, value):
        level = levels - 1 - step
        value = q_ref[level] + i_ref[level] * value
        v_ref[level] = value
        return value

    first = lax.fori_loop(0, levels, up, jnp.zeros((rows, 128), jnp.float32))
    stat_ref[0] = first
    stat_ref[1] = q_ref[levels - 1]
    stat_ref[2] = i_ref[levels - 1]
    stat_ref[3] = r_ref[0]
    stat_ref[4] = r_ref[levels - 1]


PAIR_COEFS = ("own", "other", "den", "den_end", "den_link", "outer", "total", "facing")


def place_in_column():
    mine = lax.axis_index("lev")
    return (mine == 0) | (mine == 3), mine < 2, lax.rem(mine, 2) == 0


def kernel_s(stat_ref, mate_ref, coef_ref, send_ref):
    outermost, lower, even = place_in_column()
    count = stat_ref.shape[1] // ROWS
    for t in range(count):
        part = slice(ROWS * t, ROWS * (t + 1))
        mine = [stat_ref[k, part, :] for k in range(5)]
        mate = [mate_ref[k, part, :] for k in range(5)]
        outer = [jnp.where(outermost, a, b) for a, b in zip(mine, mate)]
        inner = [jnp.where(outermost, b, a) for a, b in zip(mine, mate)]
        outer_end = jnp.where(lower, outer[2], outer[0])
        end = jnp.where(lower, inner[0], inner[2])
        centre = jnp.where(lower, inner[2], inner[0])
        link = inner[1]
        den = 1.0 / (1.0 - end * outer_end)
        den_link = den * link
        weight = outer_end * den_link
        one, zero = jnp.ones_like(den), jnp.zeros_like(den)
        coefs = dict(
            own=jnp.where(outermost, den_link, one),
            other=jnp.where(outermost, zero, weight),
            den=den,
            den_end=den * end,
            den_link=den_link,
            outer=outer_end,
            total=centre + weight * link,
            facing=vert_coef * jnp.where(even, mate[3], mate[4]),
        )
        for k, name in enumerate(PAIR_COEFS):
            coef_ref[k, part, :] = coefs[name]
        send_ref[0, part, :] = coefs["total"]
        send_ref[1, part, :] = vert_coef * jnp.where(lower, inner[4], inner[3])


def interface(first, value, star_first, star_last, coef_ref, far_ref, near_ref, cross_ref, next_ref):
    outermost, lower, even = place_in_column()
    for t in range(len(first)):
        part = slice(ROWS * t, ROWS * (t + 1))
        coef = {name: coef_ref[k, part, :] for k, name in enumerate(PAIR_COEFS)}
        sign = jnp.where(lower, 1.0, -1.0)
        star_centre = jnp.where(lower, star_last[t], star_first[t])
        star_outer = jnp.where(lower, star_first[t], star_last[t])
        facing = jnp.where(outermost, coef["facing"], far_ref[1, part, :])
        centre = jnp.where(lower, value[t], first[t]) + sign * facing * star_centre
        outer = jnp.where(lower, first[t], value[t]) - sign * coef["facing"] * star_outer
        total = coef["own"] * centre + coef["other"] * outer
        near_ref[0, part, :] = jnp.where(outermost, centre, outer)
        near_ref[1, part, :] = jnp.where(even, star_last[t], star_first[t])
        near_ref[2, part, :] = total
        cross_ref[0, part, :] = total
        next_ref[0, part, :] = total
        next_ref[1, part, :] = star_centre


def boundary(count, coef_ref, far_ref, stat_ref, near_ref, got_near_ref, got_cross_ref, got_next_ref):
    outermost, lower, _ = place_in_column()
    parts = []
    for t in range(count):
        part = slice(ROWS * t, ROWS * (t + 1))
        coef = {name: coef_ref[k, part, :] for k, name in enumerate(PAIR_COEFS)}
        far_total = far_ref[0, part, :]
        own, got = near_ref[0, part, :], got_near_ref[0, part, :]
        this = near_ref[2, part, :] + got_near_ref[2, part, :]
        that = got_cross_ref[0, part, :] + got_next_ref[0, part, :]
        middle = (that + far_total * this) / (1.0 - coef["total"] * far_total)
        from_outer = jnp.where(outermost, own, got)
        from_inner = jnp.where(outermost, got, own)
        between = (
            coef["den"] * from_inner + coef["den_end"] * from_outer + coef["den_link"] * middle
        )
        zero = jnp.zeros_like(own)
        centre = jnp.where(outermost, between, middle)
        outer = jnp.where(outermost, zero, from_outer + coef["outer"] * between)
        mate_star, next_star = got_near_ref[1, part, :], got_next_ref[1, part, :]
        star_centre = jnp.where(outermost, mate_star, next_star)
        star_outer = jnp.where(outermost, zero, mate_star)
        below, above = jnp.where(lower, outer, centre), jnp.where(lower, centre, outer)
        star_below = jnp.where(lower, star_outer, star_centre)
        star_above = jnp.where(lower, star_centre, star_outer)
        under = below - vert_coef * stat_ref[3, part, :] * star_below
        over = above + vert_coef * stat_ref[4, part, :] * star_above
        parts.append((below, above, under, over))
    return [[part[k] for part in parts] for k in range(4)]


def finish(count, levels, y_ref, q_ref, i_ref, ps_ref, x_ref, p_ref, column_refs, use, state, ready=None):
    lower, upper, under, over = boundary(count, *column_refs)

    def solved(level, above):
        value = tiles_of(y_ref, level, count)
        prod = tiles_of(q_ref, level, count)
        inv = tiles_of(i_ref, level, count)
        out = [(y + q * u) + i * a for y, q, u, i, a in zip(value, prod, lower, inv, above)]
        put_tiles(x_ref, level, out)
        return out

    def pressed(level, above, below, state):
        star = tiles_of(ps_ref, level, count)
        pres = [s - vert_coef * (a - b) for s, a, b in zip(star, above, below)]
        put_tiles(p_ref, level, pres)
        return use(level, pres, state)

    def step(index, carry):
        above, here, state = carry
        level = levels - 2 - index
        below = solved(level, here)
        state = pressed(level + 1, above, below, state)
        return here, below, state

    top = solved(levels - 1, upper)
    carry = (over, top, state)
    if ready is None:
        carry = lax.fori_loop(0, levels - 1, step, carry, unroll=UNROLL)
    else:
        done, share = 0, levels // CHUNKS
        for c in range(CHUNKS - 1, -1, -1):
            goal = levels - 1 - c * share
            carry = lax.fori_loop(done, goal, step, carry, unroll=UNROLL)
            done = goal
            ready(c)
    above, here, state = carry
    return pressed(0, above, under, state)


def kernel_c(y_ref, q_ref, i_ref, ps_ref, wx_ref, pw_ref, jac_ref, *refs):
    column_refs = refs[:COLUMN]
    x_ref, p_ref, rows_ref, inner_ref, outer_ref, pp_ref = refs[COLUMN:]
    levels, rows, _ = y_ref.shape
    count = rows // ROWS
    packer = Packer(count)
    edge = row_edge()
    ends = both_ends(planes_of(jac_ref, count))

    def use(level, pres, state):
        rows_ref[level] = edge.payload(
            both_ends(pres), both_ends(tiles_of(wx_ref, level, count)), ends
        )
        return packer.add(level, pres, state)

    state = finish(
        count,
        levels,
        y_ref,
        q_ref,
        i_ref,
        ps_ref,
        x_ref,
        p_ref,
        column_refs,
        use,
        packer.start,
    )
    pres = packer.done(state)
    wind = tiles_of(pw_ref, 0, count), tiles_of(pw_ref, 1, count)
    down, up = lane_payload(pres, wind, planes_of(jac_ref, count))
    put_pair(inner_ref, outer_ref, 0, down, up)
    put_tiles(pp_ref, 0, pres[0])
    put_tiles(pp_ref, 1, pres[1])


def kernel_d(y_ref, q_ref, i_ref, ps_ref, *refs):
    column_refs = refs[:COLUMN]
    x_hbm, p_hbm, x_ref, p_ref, sems = refs[COLUMN:]
    levels, rows, _ = y_ref.shape
    share = levels // CHUNKS
    copies = []

    def send(index, source, target, c):
        part = pl.ds(c * share, share)
        copy = pltpu.make_async_copy(source.at[part], target.at[part], sems.at[index, c])
        copy.start()
        copies.append(copy)

    def ready(c):
        send(0, x_ref, x_hbm, c)
        if c < CHUNKS - 1:
            send(1, p_ref, p_hbm, c + 1)

    finish(
        rows // ROWS,
        levels,
        y_ref,
        q_ref,
        i_ref,
        ps_ref,
        x_ref,
        p_ref,
        column_refs,
        lambda level, pres, state: state,
        0,
        ready,
    )
    send(1, p_ref, p_hbm, 0)
    for copy in copies:
        copy.wait()


def call(kernel, name, shapes, *args, far_in=False, far_out=False, scratch=(), keep=()):
    near, far = pl.BlockSpec(memory_space=pltpu.VMEM), pl.BlockSpec(memory_space=pl.ANY)
    size = sum(a.size for a in args) + sum(functools.reduce(lambda a, b: a * b, s) for s in shapes)
    if far_in:
        args = [pltpu.with_memory_space_constraint(a, pltpu.HBM) for a in args]
    return pl.pallas_call(
        kernel,
        out_shape=[
            pltpu.VMEM(s, jnp.float32) if k in keep else jax.ShapeDtypeStruct(s, jnp.float32)
            for k, s in enumerate(shapes)
        ],
        in_specs=[far if far_in else near] * len(args),
        out_specs=[far if far_out else near] * len(shapes),
        scratch_shapes=list(scratch),
        compiler_params=pltpu.CompilerParams(vmem_limit_bytes=32 * 1024 * 1024),
        cost_estimate=pl.CostEstimate(
            flops=8 * size, bytes_accessed=4 * size, transcendentals=0
        ),
        name=name,
    )(*args)


def swap(value, axis, partner):
    count = lax.axis_size(axis)
    return lax.ppermute(value, axis, [(i, partner(i)) for i in range(count)])


def exchange_rows(rows):
    count = lax.axis_size("gx")
    if count == 2:
        return swap(rows, "gx", lambda i: 1 - i)
    down = swap(rows[:, : ROWS // 2], "gx", lambda i: (i - 1) % count)
    up = swap(rows[:, ROWS // 2 :], "gx", lambda i: (i + 1) % count)
    return jnp.concatenate([down, up], axis=1)


def exchange_lanes(inner, outer):
    count = lax.axis_size("gy")
    got_outer = swap(outer, "gy", lambda i: (i + 1 if i % 2 else i - 1) % count)
    got_inner = swap(inner, "gy", lambda i: i ^ 1)
    return got_inner, got_outer


def exchange_column(near, cross, following):
    got_next = swap(following, "lev", lambda i: i ^ 3)
    got_cross = swap(cross, "lev", lambda i: i ^ 2)
    got_near = swap(near, "lev", lambda i: i ^ 1)
    return near, got_near, got_cross, got_next


def local(wind_x, wind_y, wind_z, pressure, jacobian, slope_x, slope_y, stiffness):
    field = wind_x.shape
    levels, rows, lanes = field
    plane = (rows, lanes)
    pair = (2,) + plane
    assert lanes == 128 and levels * SLOT == 128 and rows % ROWS == 0
    assert lax.axis_size("lev") == 4 and lax.axis_size("gy") % 2 == 0

    edge, inner, outer, ends = call(
        kernel_a,
        "start",
        [(levels + 1, ROWS, lanes), pair, pair, pair],
        pressure,
        wind_x,
        wind_y,
        jacobian,
        far_in=True,
        scratch=[
            pltpu.VMEM(field, jnp.float32),
            pltpu.VMEM((levels, 2 * ROWS, lanes), jnp.float32),
            pltpu.VMEM(field, jnp.float32),
            pltpu.VMEM(plane, jnp.float32),
            pltpu.SemaphoreType.DMA((3, CHUNKS)),
        ],
    )
    sent = (edge, inner, outer)
    got = (exchange_rows(edge),) + exchange_lanes(inner, outer)
    static_edges = sent + got
    rate, inv, prod, gain, stat = call(
        kernel_f, "factor", [field, field, field, field, (5,) + plane], stiffness
    )
    mate = swap(stat, "lev", lambda i: i ^ 1)
    coef, send = call(kernel_s, "pairs", [(len(PAIR_COEFS),) + plane, pair], stat, mate)
    far = swap(send, "lev", lambda i: i ^ 2)
    for substep in range(SUBSTEPS):
        closed = call(
            kernel_m, "interior", [field, field, field], pressure, wind_x, wind_y, jacobian
        )
        wind_x, wind_y, star, value, *faces = call(
            kernel_b,
            "sweep",
            [field, field, field, field, (3,) + plane, (1,) + plane, pair],
            pressure,
            *closed,
            wind_z,
            jacobian,
            slope_x,
            slope_y,
            rate,
            inv,
            gain,
            ends,
            *sent,
            *got,
            *static_edges,
            coef,
            far,
            keep=tuple(range(7)),
        )
        column = (coef, far, stat) + exchange_column(*faces)
        if substep < SUBSTEPS - 1:
            (packed,) = call(kernel_n, "pack", [pair], wind_y)
            wind_z, pressure, edge, inner, outer, ends = call(
                kernel_c,
                "finish",
                [field, field, (levels, ROWS, lanes), (1,) + plane, (1,) + plane, pair],
                value,
                prod,
                inv,
                star,
                wind_x,
                packed,
                jacobian,
                *column,
            )
            sent = (edge, inner, outer)
            got = (exchange_rows(edge),) + exchange_lanes(inner, outer)
        else:
            wind_z, pressure = call(
                kernel_d,
                "last",
                [field, field],
                value,
                prod,
                inv,
                star,
                *column,
                far_out=True,
                scratch=[
                    pltpu.VMEM(field, jnp.float32),
                    pltpu.VMEM(field, jnp.float32),
                    pltpu.SemaphoreType.DMA((2, CHUNKS)),
                ],
            )
    return wind_x, wind_y, wind_z, pressure


def solution(mesh):
    field = P("lev", "gx", "gy")
    column = P("gx", "gy")
    return jax.shard_map(
        local,
        mesh=mesh,
        in_specs=(field,) * 4 + (column,) * 3 + (field,),
        out_specs=(field,) * 4,
        check_vma=False,
    )
```

```python
import functools

import jax
import jax.numpy as jnp
from jax import lax
from jax.experimental import pallas as pl
from jax.experimental.pallas import tpu as pltpu
from jax.sharding import PartitionSpec as P

SUBSTEPS = 2

grad_coef = 0.35
div_coef = 0.35
vert_coef = 0.25

CG = grad_coef / 12.0
CD = div_coef / 12.0
ROWS = 8
SLOT = 4
UNROLL = 8
CHUNKS = 4
COLUMN = 6


def lane_index():
    return lax.broadcasted_iota(jnp.int32, (ROWS, 128), 1)


def row_index():
    return lax.broadcasted_iota(jnp.int32, (ROWS, 128), 0)


def only(mask, value):
    return jnp.where(mask, jnp.float32(value), jnp.float32(0.0))


def tiles_of(ref, level, count):
    return [ref[level, ROWS * t : ROWS * (t + 1), :] for t in range(count)]


def planes_of(ref, count):
    return [ref[ROWS * t : ROWS * (t + 1), :] for t in range(count)]


def put_tiles(ref, level, tiles):
    for t, tile in enumerate(tiles):
        ref[level, ROWS * t : ROWS * (t + 1), :] = tile


def put_planes(ref, tiles):
    for t, tile in enumerate(tiles):
        ref[ROWS * t : ROWS * (t + 1), :] = tile


class Edge:
    def __init__(self, place, axis, held):
        self.place, self.axis, self.held = place, axis, held
        self.size = place.shape[axis]

    def at(self, places):
        total = None
        for position, value in places.items():
            if position in self.held:
                term = only(self.place == position, value)
                total = term if total is None else total + term
        return total

    def shifted(self, field, by):
        return field if by == 0 else pltpu.roll(field, (-by) % self.size, self.axis)

    def mix(self, field, table):
        total = None
        for by, places in table.items():
            weight = self.at(places)
            if weight is not None:
                term = weight * self.shifted(field, by)
                total = term if total is None else total + term
        return total

    def payload(self, pres, wind, jac):
        partial = self.mix(
            pres,
            {
                1: {0: 8.0, 1: 8.0, 6: 8.0},
                2: {0: -1.0, 1: -1.0},
                -1: {1: -8.0, 6: -8.0, 7: -8.0},
                -2: {6: 1.0, 7: 1.0},
            },
        )
        flux = jac * (wind - CG * partial)
        outer = self.mix(pres, {0: {0: 1.0, 1: 1.0, 6: 1.0, 7: 1.0}})
        return outer + self.mix(flux, {-2: {2: 1.0, 3: 1.0}, 2: {4: 1.0, 5: 1.0}})

    def correct(self, delta, pres, jac, delta_jac):
        grad = self.mix(
            delta, {2: {0: 1.0, 1: 1.0}, 3: {0: -8.0}, -2: {6: -1.0, 7: -1.0}, -3: {7: 8.0}}
        )
        wind = CG * grad
        own = -(jac * wind)
        far = self.mix(delta, {0: {0: 1.0, 1: 1.0, 6: 1.0, 7: 1.0}}) + CG * delta_jac * self.mix(
            pres, {0: {0: 1.0, 1: 1.0, 6: -1.0, 7: -1.0}, -1: {1: -8.0}, 1: {6: 8.0}}
        )
        spread = (
            self.mix(far, {0: {0: 1.0, 1: 1.0, 6: -1.0, 7: -1.0}})
            + self.mix(far - own, {1: {0: -8.0}, -1: {7: 8.0}})
            + self.mix(
                own,
                {
                    -1: {1: -8.0, 2: -8.0},
                    -2: {2: 1.0, 3: 1.0},
                    1: {5: 8.0, 6: 8.0},
                    2: {4: -1.0, 5: -1.0},
                },
            )
        )
        return wind, CD * spread / jac


LOW, HIGH = (0, 1, 2, 3), (4, 5, 6, 7)


def row_edge():
    return Edge(row_index(), 0, LOW + HIGH)


def lane_edge(held):
    return Edge((lane_index() & 3) + held[0], 1, held)


def both_ends(tiles):
    return jnp.where(row_index() < 4, tiles[0], tiles[-1])


def spread_slots(tile, low):
    lane = lane_index()
    if low:
        out = jnp.where(lane < SLOT, tile, 0.0)
    else:
        out = pltpu.roll(jnp.where(lane >= 128 - SLOT, tile, 0.0), SLOT, 1)
    by = SLOT
    while by < 128:
        out = out + pltpu.roll(out, by, 1)
        by *= 2
    return out


class Packer:
    def __init__(self, count):
        self.slot = lax.shift_right_logical(lane_index(), 2)
        self.start = [jnp.zeros((ROWS, 128), jnp.float32)] * (2 * count)
        self.count = count

    def add(self, level, tiles, state):
        before = lax.rem(level + 31, 32)
        rolled = [pltpu.roll(tile, SLOT * level, 1) for tile in tiles]
        low = [jnp.where(self.slot == level, r, s) for r, s in zip(rolled, state)]
        high = [jnp.where(self.slot == before, r, s) for r, s in zip(rolled, state[self.count :])]
        return low + high

    def done(self, state):
        return state[: self.count], [pltpu.roll(s, SLOT, 1) for s in state[self.count :]]


class Closed:
    def __init__(self):
        self.row = row_index()

    def along_y(self, tile):
        pair = tile - pltpu.roll(tile, 126, 1)
        return (pltpu.roll(pair, 2, 1) + pair) - 8.0 * pltpu.roll(pair, 1, 1)

    def moved(self, tiles, by):
        count = len(tiles)
        rolled = [pltpu.roll(tile, by % ROWS, 0) for tile in tiles]
        if by > 0:
            return [jnp.where(self.row < by, rolled[t - 1], rolled[t]) for t in range(count)]
        return [
            jnp.where(self.row >= ROWS + by, rolled[(t + 1) % count], rolled[t])
            for t in range(count)
        ]

    def along_x(self, tiles):
        pair = [f - m for f, m in zip(tiles, self.moved(tiles, -2))]
        return [
            (two + here) - 8.0 * one
            for two, here, one in zip(self.moved(pair, 2), pair, self.moved(pair, 1))
        ]


def even_place():
    return lax.rem(lax.axis_index("gy"), 2) == 0


def put_pair(inner_ref, outer_ref, index, down, up):
    even = even_place()
    put_tiles(inner_ref, index, [jnp.where(even, u, d) for u, d in zip(up, down)])
    put_tiles(outer_ref, index, [jnp.where(even, d, u) for u, d in zip(up, down)])


def get_pair(inner_ref, outer_ref, index, part):
    even = even_place()
    inner, outer = inner_ref[index, part, :], outer_ref[index, part, :]
    return jnp.where(even, outer, inner), jnp.where(even, inner, outer)


def lane_payload(pres, wind, jac):
    low, high = lane_edge(LOW), lane_edge(HIGH)
    down = [
        low.payload(p, w, spread_slots(j, True)) for p, w, j in zip(pres[0], wind[0], jac)
    ]
    up = [
        high.payload(p, w, spread_slots(j, False)) for p, w, j in zip(pres[1], wind[1], jac)
    ]
    return down, up


def pack_levels(ref, count, levels):
    packer = Packer(count)

    def step(level, state):
        return packer.add(level, tiles_of(ref, level, count), state)

    return packer.done(lax.fori_loop(0, levels, step, packer.start, unroll=UNROLL))


def kernel_a(
    p_hbm, wx_hbm, wy_hbm, jac_hbm, rows_ref, inner_ref, outer_ref, pp_ref, p_ref, wx_ref, wy_ref, jac_ref, sems
):
    levels, rows, _ = p_hbm.shape
    count = rows // ROWS
    share = levels // CHUNKS

    def fetch(source, target, sem):
        copy = pltpu.make_async_copy(source, target, sem)
        copy.start()
        return copy

    tail = pl.ds(rows - ROWS, ROWS)
    parts = [pl.ds(c * share, share) for c in range(CHUNKS)]
    pres_in = [fetch(p_hbm.at[s], p_ref.at[s], sems.at[0, c]) for c, s in enumerate(parts)]
    wind_in = [fetch(wy_hbm.at[s], wy_ref.at[s], sems.at[1, c]) for c, s in enumerate(parts)]
    ends_in = [
        fetch(jac_hbm, jac_ref, sems.at[2, 0]),
        fetch(wx_hbm.at[:, pl.ds(0, ROWS)], wx_ref.at[:, pl.ds(0, ROWS)], sems.at[2, 1]),
        fetch(wx_hbm.at[:, tail], wx_ref.at[:, pl.ds(ROWS, ROWS)], sems.at[2, 2]),
    ]

    def pack(ref, copies):
        packer = Packer(count)
        state = packer.start
        for c, copy in enumerate(copies):
            copy.wait()
            state = lax.fori_loop(
                c * share,
                (c + 1) * share,
                lambda level, state: packer.add(level, tiles_of(ref, level, count), state),
                state,
                unroll=UNROLL,
            )
        return packer.done(state)

    pres = pack(p_ref, pres_in)
    wind = pack(wy_ref, wind_in)
    for copy in ends_in:
        copy.wait()
    jac = planes_of(jac_ref, count)
    ends = both_ends(jac)
    edge = row_edge()

    def step(level, state):
        rows_ref[level] = edge.payload(
            both_ends(tiles_of(p_ref, level, count)), both_ends(tiles_of(wx_ref, level, 2)), ends
        )
        return state

    lax.fori_loop(0, levels, step, 0, unroll=2 * UNROLL)
    rows_ref[levels] = ends
    down, up = lane_payload(pres, wind, jac)
    put_pair(inner_ref, outer_ref, 0, down, up)
    put_pair(
        inner_ref,
        outer_ref,
        1,
        [spread_slots(j, True) for j in jac],
        [spread_slots(j, False) for j in jac],
    )
    put_tiles(pp_ref, 0, pres[0])
    put_tiles(pp_ref, 1, pres[1])


def kernel_n(wy_ref, pw_ref):
    levels, rows, _ = wy_ref.shape
    count = rows // ROWS
    wind = pack_levels(wy_ref, count, levels)
    put_tiles(pw_ref, 0, wind[0])
    put_tiles(pw_ref, 1, wind[1])


def kernel_m(p_ref, wx_ref, wy_ref, jac_ref, nx_ref, ny_ref, ps_ref):
    levels, rows, _ = p_ref.shape
    count = rows // ROWS
    jac = planes_of(jac_ref, count)
    inv_jac = [CD / j for j in jac]
    closed = Closed()

    def step(level, state):
        pres = tiles_of(p_ref, level, count)
        wind_x = tiles_of(wx_ref, level, count)
        wind_y = tiles_of(wy_ref, level, count)
        new_x = [w - CG * d for w, d in zip(wind_x, closed.along_x(pres))]
        new_y = [w - CG * closed.along_y(p) for w, p in zip(wind_y, pres)]
        put_tiles(nx_ref, level, new_x)
        put_tiles(ny_ref, level, new_y)
        spread_x = closed.along_x([j * n for j, n in zip(jac, new_x)])
        spread_y = [closed.along_y(j * n) for j, n in zip(jac, new_y)]
        put_tiles(
            ps_ref,
            level,
            [p - i * (x + y) for p, i, x, y in zip(pres, inv_jac, spread_x, spread_y)],
        )
        return state

    lax.fori_loop(0, levels, step, 0, unroll=UNROLL)


def kernel_b(
    p_ref,
    nxc_ref,
    nyc_ref,
    psc_ref,
    wz_ref,
    jac_ref,
    sx_ref,
    sy_ref,
    r_ref,
    i_ref,
    v_ref,
    pp_ref,
    rows_ref,
    inner_ref,
    outer_ref,
    got_rows_ref,
    got_inner_ref,
    got_outer_ref,
    srows_ref,
    sinner_ref,
    souter_ref,
    got_srows_ref,
    got_sinner_ref,
    got_souter_ref,
    coef_ref,
    far_ref,
    nx_ref,
    ny_ref,
    ps_ref,
    y_ref,
    near_ref,
    wind_ref,
    press_ref,
):
    levels, rows, _ = p_ref.shape
    count = rows // ROWS
    last = count - 1
    lane, row = lane_index(), row_index()
    low_edge, high_edge, edge = lane_edge(LOW), lane_edge(HIGH), row_edge()
    wind_fix, low_fix, high_fix = [], [], []
    for t in range(count):
        part = slice(ROWS * t, ROWS * (t + 1))
        jac_low, jac_high = get_pair(sinner_ref, souter_ref, 1, part)
        jac_below, jac_above = get_pair(got_sinner_ref, got_souter_ref, 1, part)
        down, up = get_pair(inner_ref, outer_ref, 0, part)
        below, above = get_pair(got_inner_ref, got_outer_ref, 0, part)
        low_wind, low_star = low_edge.correct(
            below - up, pp_ref[0, part, :], jac_low, low_edge.shifted(jac_below - jac_high, 2)
        )
        high_wind, high_star = high_edge.correct(
            above - down, pp_ref[1, part, :], jac_high, high_edge.shifted(jac_above - jac_low, -2)
        )
        wind_fix.append(low_wind + pltpu.roll(high_wind, 128 - SLOT, 1))
        low_fix.append(low_star)
        high_fix.append(pltpu.roll(high_star, 128 - SLOT, 1))
    ends = srows_ref[levels]
    change = got_srows_ref[levels] - ends
    ends_change = jnp.where(row < 4, edge.shifted(change, -2), edge.shifted(change, 2))
    outer = (lane < 2) | (lane >= 126)
    low_lanes, high_lanes = lane < SLOT, lane >= 128 - SLOT
    first_rows = row < 4

    def correct_rows(level, state):
        wind_ref[level], press_ref[level] = edge.correct(
            pltpu.roll(got_rows_ref[level] - rows_ref[level], 4, 0),
            jnp.where(first_rows, p_ref[level, :ROWS, :], p_ref[level, ROWS * last :, :]),
            ends,
            ends_change,
        )
        return state

    lax.fori_loop(0, levels, correct_rows, 0, unroll=2 * UNROLL)

    def star(level):
        new_x = tiles_of(nxc_ref, level, count)
        new_y = tiles_of(nyc_ref, level, count)
        stars = tiles_of(psc_ref, level, count)
        wind, press = wind_ref[level], press_ref[level]
        new_x[0] = new_x[0] - jnp.where(first_rows, wind, 0.0)
        new_x[last] = new_x[last] - jnp.where(first_rows, 0.0, wind)
        stars[0] = stars[0] - jnp.where(first_rows, press, 0.0)
        stars[last] = stars[last] - jnp.where(first_rows, 0.0, press)
        back = lax.rem(128 - SLOT * level, 128)
        forces = []
        for t in range(count):
            part = slice(ROWS * t, ROWS * (t + 1))
            new_y[t] = new_y[t] - jnp.where(outer, pltpu.roll(wind_fix[t], back, 1), 0.0)
            fix = jnp.where(
                low_lanes,
                pltpu.roll(low_fix[t], back, 1),
                jnp.where(high_lanes, pltpu.roll(high_fix[t], back, 1), 0.0),
            )
            stars[t] = stars[t] - fix
            forces.append(
                wz_ref[level, part, :]
                + sx_ref[part, :] * new_x[t]
                + sy_ref[part, :] * new_y[t]
            )
        put_tiles(nx_ref, level, new_x)
        put_tiles(ny_ref, level, new_y)
        put_tiles(ps_ref, level, stars)
        return stars, forces

    def sweep(level, below, above, force, value, first):
        rate = tiles_of(r_ref, level, count)
        inv = tiles_of(i_ref, level, count)
        gain = tiles_of(v_ref, level, count)
        values, firsts = [], []
        for t in range(count):
            rhs = rate[t] * (force[t] - vert_coef * (above[t] - below[t]))
            firsts.append(first[t] + gain[t] * rhs)
            values.append((rhs + value[t]) * inv[t])
        put_tiles(y_ref, level, values)
        return values, firsts

    zeros = [jnp.zeros((ROWS, 128), jnp.float32)] * count
    here, force = star(0)
    bottom = here

    def step(level, carry):
        below, here, force, value, first = carry
        above, force_next = star(level)
        value, first = sweep(level - 1, below, above, force, value, first)
        return here, above, force_next, value, first

    below, here, force, value, first = lax.fori_loop(
        1, levels, step, (zeros, here, force, zeros, zeros), unroll=UNROLL
    )
    value, first = sweep(levels - 1, below, zeros, force, value, first)
    interface(first, value, bottom, here, coef_ref, far_ref, near_ref)


def kernel_f(s_ref, r_ref, i_ref, q_ref, v_ref, stat_ref):
    levels, rows, _ = s_ref.shape

    def down(level, carry):
        excess, prod = carry
        rate = 1.0 / s_ref[level]
        excess = rate + excess
        inv = 1.0 / (1.0 + excess)
        prod = prod * inv
        r_ref[level] = rate
        i_ref[level] = inv
        q_ref[level] = prod
        return excess * inv, prod

    ones = jnp.ones((rows, 128), jnp.float32)
    lax.fori_loop(0, levels, down, (ones, ones))

    def up(step, value):
        level = levels - 1 - step
        value = q_ref[level] + i_ref[level] * value
        v_ref[level] = value
        return value

    first = lax.fori_loop(0, levels, up, jnp.zeros((rows, 128), jnp.float32))
    stat_ref[0] = first
    stat_ref[1] = q_ref[levels - 1]
    stat_ref[2] = i_ref[levels - 1]
    stat_ref[3] = r_ref[0]
    stat_ref[4] = r_ref[levels - 1]


PAIR_COEFS = ("own", "other", "den", "den_end", "den_link", "outer", "total", "facing")


def place_in_column():
    mine = lax.axis_index("lev")
    return (mine == 0) | (mine == 3), mine < 2, lax.rem(mine, 2) == 0


def kernel_s(stat_ref, mate_ref, coef_ref, send_ref):
    outermost, lower, even = place_in_column()
    count = stat_ref.shape[1] // ROWS
    for t in range(count):
        part = slice(ROWS * t, ROWS * (t + 1))
        mine = [stat_ref[k, part, :] for k in range(5)]
        mate = [mate_ref[k, part, :] for k in range(5)]
        outer = [jnp.where(outermost, a, b) for a, b in zip(mine, mate)]
        inner = [jnp.where(outermost, b, a) for a, b in zip(mine, mate)]
        outer_end = jnp.where(lower, outer[2], outer[0])
        end = jnp.where(lower, inner[0], inner[2])
        centre = jnp.where(lower, inner[2], inner[0])
        link = inner[1]
        den = 1.0 / (1.0 - end * outer_end)
        den_link = den * link
        weight = outer_end * den_link
        one, zero = jnp.ones_like(den), jnp.zeros_like(den)
        coefs = dict(
            own=jnp.where(outermost, den_link, one),
            other=jnp.where(outermost, zero, weight),
            den=den,
            den_end=den * end,
            den_link=den_link,
            outer=outer_end,
            total=centre + weight * link,
            facing=vert_coef * jnp.where(even, mate[3], mate[4]),
        )
        for k, name in enumerate(PAIR_COEFS):
            coef_ref[k, part, :] = coefs[name]
        send_ref[0, part, :] = coefs["total"]
        send_ref[1, part, :] = vert_coef * jnp.where(lower, inner[4], inner[3])


def interface(first, value, star_first, star_last, coef_ref, far_ref, near_ref):
    outermost, lower, even = place_in_column()
    for t in range(len(first)):
        part = slice(ROWS * t, ROWS * (t + 1))
        coef = {name: coef_ref[k, part, :] for k, name in enumerate(PAIR_COEFS)}
        sign = jnp.where(lower, 1.0, -1.0)
        star_centre = jnp.where(lower, star_last[t], star_first[t])
        star_outer = jnp.where(lower, star_first[t], star_last[t])
        facing = jnp.where(outermost, coef["facing"], far_ref[1, part, :])
        centre = jnp.where(lower, value[t], first[t]) + sign * facing * star_centre
        outer = jnp.where(lower, first[t], value[t]) - sign * coef["facing"] * star_outer
        total = coef["own"] * centre + coef["other"] * outer
        near_ref[0, part, :] = jnp.where(outermost, centre, outer)
        near_ref[1, part, :] = jnp.where(even, star_last[t], star_first[t])
        near_ref[2, part, :] = total
        near_ref[3, part, :] = star_centre


def kernel_u(near_ref, got_ref, send_ref):
    outermost, _, _ = place_in_column()
    send_ref[0] = near_ref[2] + got_ref[2]
    send_ref[1] = jnp.where(outermost, got_ref[3], near_ref[3])


def boundary(count, coef_ref, far_ref, stat_ref, near_ref, got_near_ref, got_far_ref):
    outermost, lower, _ = place_in_column()
    parts = []
    for t in range(count):
        part = slice(ROWS * t, ROWS * (t + 1))
        coef = {name: coef_ref[k, part, :] for k, name in enumerate(PAIR_COEFS)}
        far_total = far_ref[0, part, :]
        own, got = near_ref[0, part, :], got_near_ref[0, part, :]
        this = near_ref[2, part, :] + got_near_ref[2, part, :]
        that = got_far_ref[0, part, :]
        middle = (that + far_total * this) / (1.0 - coef["total"] * far_total)
        from_outer = jnp.where(outermost, own, got)
        from_inner = jnp.where(outermost, got, own)
        between = (
            coef["den"] * from_inner + coef["den_end"] * from_outer + coef["den_link"] * middle
        )
        zero = jnp.zeros_like(own)
        centre = jnp.where(outermost, between, middle)
        outer = jnp.where(outermost, zero, from_outer + coef["outer"] * between)
        mate_star, next_star = got_near_ref[1, part, :], got_far_ref[1, part, :]
        star_centre = jnp.where(outermost, mate_star, next_star)
        star_outer = jnp.where(outermost, zero, mate_star)
        below, above = jnp.where(lower, outer, centre), jnp.where(lower, centre, outer)
        star_below = jnp.where(lower, star_outer, star_centre)
        star_above = jnp.where(lower, star_centre, star_outer)
        under = below - vert_coef * stat_ref[3, part, :] * star_below
        over = above + vert_coef * stat_ref[4, part, :] * star_above
        parts.append((below, above, under, over))
    return [[part[k] for part in parts] for k in range(4)]


def finish(count, levels, y_ref, q_ref, i_ref, ps_ref, x_ref, p_ref, column_refs, ready=None):
    lower, upper, under, over = boundary(count, *column_refs)

    def solved(level, above):
        value = tiles_of(y_ref, level, count)
        prod = tiles_of(q_ref, level, count)
        inv = tiles_of(i_ref, level, count)
        out = [(y + q * u) + i * a for y, q, u, i, a in zip(value, prod, lower, inv, above)]
        put_tiles(x_ref, level, out)
        return out

    def pressed(level, above, below):
        star = tiles_of(ps_ref, level, count)
        put_tiles(p_ref, level, [s - vert_coef * (a - b) for s, a, b in zip(star, above, below)])

    def step(index, carry):
        above, here = carry
        level = levels - 2 - index
        below = solved(level, here)
        pressed(level + 1, above, below)
        return here, below

    carry = over, solved(levels - 1, upper)
    if ready is None:
        carry = lax.fori_loop(0, levels - 1, step, carry, unroll=UNROLL)
    else:
        done, share = 0, levels // CHUNKS
        for c in range(CHUNKS - 1, -1, -1):
            goal = levels - 1 - c * share
            carry = lax.fori_loop(done, goal, step, carry, unroll=UNROLL)
            done = goal
            ready(c)
    above, here = carry
    pressed(0, above, under)


def kernel_c(y_ref, q_ref, i_ref, ps_ref, wx_ref, pw_ref, jac_ref, *refs):
    column_refs = refs[:COLUMN]
    x_ref, p_ref, rows_ref, inner_ref, outer_ref, pp_ref = refs[COLUMN:]
    levels, rows, _ = y_ref.shape
    count = rows // ROWS
    edge = row_edge()
    ends = both_ends(planes_of(jac_ref, count))
    finish(count, levels, y_ref, q_ref, i_ref, ps_ref, x_ref, p_ref, column_refs)

    def step(level, state):
        rows_ref[level] = edge.payload(
            both_ends(tiles_of(p_ref, level, count)),
            both_ends(tiles_of(wx_ref, level, count)),
            ends,
        )
        return state

    lax.fori_loop(0, levels, step, 0, unroll=2 * UNROLL)
    pres = pack_levels(p_ref, count, levels)
    wind = tiles_of(pw_ref, 0, count), tiles_of(pw_ref, 1, count)
    down, up = lane_payload(pres, wind, planes_of(jac_ref, count))
    put_pair(inner_ref, outer_ref, 0, down, up)
    put_tiles(pp_ref, 0, pres[0])
    put_tiles(pp_ref, 1, pres[1])


def kernel_d(y_ref, q_ref, i_ref, ps_ref, *refs):
    column_refs = refs[:COLUMN]
    x_hbm, p_hbm, x_ref, p_ref, sems = refs[COLUMN:]
    levels, rows, _ = y_ref.shape
    share = levels // CHUNKS
    copies = []

    def send(index, source, target, c):
        part = pl.ds(c * share, share)
        copy = pltpu.make_async_copy(source.at[part], target.at[part], sems.at[index, c])
        copy.start()
        copies.append(copy)

    def ready(c):
        send(0, x_ref, x_hbm, c)
        if c < CHUNKS - 1:
            send(1, p_ref, p_hbm, c + 1)

    finish(
        rows // ROWS,
        levels,
        y_ref,
        q_ref,
        i_ref,
        ps_ref,
        x_ref,
        p_ref,
        column_refs,
        ready,
    )
    send(1, p_ref, p_hbm, 0)
    for copy in copies:
        copy.wait()


def call(kernel, name, shapes, *args, weight=1, far_in=False, far_out=False, scratch=(), keep=()):
    near, far = pl.BlockSpec(memory_space=pltpu.VMEM), pl.BlockSpec(memory_space=pl.ANY)
    size = sum(a.size for a in args) + sum(functools.reduce(lambda a, b: a * b, s) for s in shapes)
    if far_in:
        args = [pltpu.with_memory_space_constraint(a, pltpu.HBM) for a in args]
    return pl.pallas_call(
        kernel,
        out_shape=[
            pltpu.VMEM(s, jnp.float32) if k in keep else jax.ShapeDtypeStruct(s, jnp.float32)
            for k, s in enumerate(shapes)
        ],
        in_specs=[far if far_in else near] * len(args),
        out_specs=[far if far_out else near] * len(shapes),
        scratch_shapes=list(scratch),
        compiler_params=pltpu.CompilerParams(vmem_limit_bytes=32 * 1024 * 1024),
        cost_estimate=pl.CostEstimate(
            flops=weight * size, bytes_accessed=4 * weight * size, transcendentals=0
        ),
        name=name,
    )(*args)


def swap(value, axis, partner):
    count = lax.axis_size(axis)
    return lax.ppermute(value, axis, [(i, partner(i)) for i in range(count)])


def exchange_rows(rows):
    count = lax.axis_size("gx")
    if count == 2:
        return swap(rows, "gx", lambda i: 1 - i)
    down = swap(rows[:, : ROWS // 2], "gx", lambda i: (i - 1) % count)
    up = swap(rows[:, ROWS // 2 :], "gx", lambda i: (i + 1) % count)
    return jnp.concatenate([down, up], axis=1)


def exchange_lanes(inner, outer):
    count = lax.axis_size("gy")
    got_outer = swap(outer, "gy", lambda i: (i + 1 if i % 2 else i - 1) % count)
    got_inner = swap(inner, "gy", lambda i: i ^ 1)
    return got_inner, got_outer


def exchange_column(near):
    plane = near.shape[1:]
    got_near = swap(near, "lev", lambda i: i ^ 1)
    (send,) = call(kernel_u, "meet", [(2,) + plane], near, got_near)
    return near, got_near, swap(send, "lev", lambda i: i ^ 2)


def local(wind_x, wind_y, wind_z, pressure, jacobian, slope_x, slope_y, stiffness):
    field = wind_x.shape
    levels, rows, lanes = field
    plane = (rows, lanes)
    pair = (2,) + plane
    assert lanes == 128 and levels * SLOT == 128 and rows % ROWS == 0
    assert lax.axis_size("lev") == 4 and lax.axis_size("gy") % 2 == 0

    edge, inner, outer, ends = call(
        kernel_a,
        "start",
        [(levels + 1, ROWS, lanes), pair, pair, pair],
        pressure,
        wind_x,
        wind_y,
        jacobian,
        far_in=True,
        scratch=[
            pltpu.VMEM(field, jnp.float32),
            pltpu.VMEM((levels, 2 * ROWS, lanes), jnp.float32),
            pltpu.VMEM(field, jnp.float32),
            pltpu.VMEM(plane, jnp.float32),
            pltpu.SemaphoreType.DMA((3, CHUNKS)),
        ],
    )
    sent = (edge, inner, outer)
    got = (exchange_rows(edge),) + exchange_lanes(inner, outer)
    static_edges = sent + got
    rate, inv, prod, gain, stat = call(
        kernel_f, "factor", [field, field, field, field, (5,) + plane], stiffness
    )
    mate = swap(stat, "lev", lambda i: i ^ 1)
    coef, send = call(kernel_s, "pairs", [(len(PAIR_COEFS),) + plane, pair], stat, mate)
    far = swap(send, "lev", lambda i: i ^ 2)
    for substep in range(SUBSTEPS):
        closed = call(
            kernel_m, "interior", [field, field, field], pressure, wind_x, wind_y, jacobian
        )
        wind_x, wind_y, star, value, near = call(
            kernel_b,
            "sweep",
            [field, field, field, field, (4,) + plane],
            pressure,
            *closed,
            wind_z,
            jacobian,
            slope_x,
            slope_y,
            rate,
            inv,
            gain,
            ends,
            *sent,
            *got,
            *static_edges,
            coef,
            far,
            keep=tuple(range(5)),
            scratch=[pltpu.VMEM((levels, ROWS, lanes), jnp.float32)] * 2,
        )
        column = (coef, far, stat) + exchange_column(near)
        if substep < SUBSTEPS - 1:
            (packed,) = call(kernel_n, "pack", [pair], wind_y)
            wind_z, pressure, edge, inner, outer, ends = call(
                kernel_c,
                "finish",
                [field, field, (levels, ROWS, lanes), (1,) + plane, (1,) + plane, pair],
                value,
                prod,
                inv,
                star,
                wind_x,
                packed,
                jacobian,
                *column,
            )
            sent = (edge, inner, outer)
            got = (exchange_rows(edge),) + exchange_lanes(inner, outer)
        else:
            wind_z, pressure = call(
                kernel_d,
                "last",
                [field, field],
                value,
                prod,
                inv,
                star,
                *column,
                far_out=True,
                scratch=[
                    pltpu.VMEM(field, jnp.float32),
                    pltpu.VMEM(field, jnp.float32),
                    pltpu.SemaphoreType.DMA((2, CHUNKS)),
                ],
            )
    return wind_x, wind_y, wind_z, pressure


def solution(mesh):
    field = P("lev", "gx", "gy")
    column = P("gx", "gy")
    return jax.shard_map(
        local,
        mesh=mesh,
        in_specs=(field,) * 4 + (column,) * 3 + (field,),
        out_specs=(field,) * 4,
        check_vma=False,
    )
```

```python
import functools

import jax
import jax.numpy as jnp
from jax import lax
from jax.experimental import pallas as pl
from jax.experimental.pallas import tpu as pltpu
from jax.sharding import PartitionSpec as P

SUBSTEPS = 2

grad_coef = 0.35
div_coef = 0.35
vert_coef = 0.25

CG = grad_coef / 12.0
CD = div_coef / 12.0
ROWS = 8
SLOT = 4
UNROLL = 8
CHUNKS = 4
COLUMN = 10


def lane_index():
    return lax.broadcasted_iota(jnp.int32, (ROWS, 128), 1)


def row_index():
    return lax.broadcasted_iota(jnp.int32, (ROWS, 128), 0)


def only(mask, value):
    return jnp.where(mask, jnp.float32(value), jnp.float32(0.0))


def tiles_of(ref, level, count):
    return [ref[level, ROWS * t : ROWS * (t + 1), :] for t in range(count)]


def planes_of(ref, count):
    return [ref[ROWS * t : ROWS * (t + 1), :] for t in range(count)]


def put_tiles(ref, level, tiles):
    for t, tile in enumerate(tiles):
        ref[level, ROWS * t : ROWS * (t + 1), :] = tile


def put_planes(ref, tiles):
    for t, tile in enumerate(tiles):
        ref[ROWS * t : ROWS * (t + 1), :] = tile


class Edge:
    def __init__(self, place, axis, held):
        self.place, self.axis, self.held = place, axis, held
        self.size = place.shape[axis]

    def at(self, places):
        total = None
        for position, value in places.items():
            if position in self.held:
                term = only(self.place == position, value)
                total = term if total is None else total + term
        return total

    def shifted(self, field, by):
        return field if by == 0 else pltpu.roll(field, (-by) % self.size, self.axis)

    def mix(self, field, table):
        total = None
        for by, places in table.items():
            weight = self.at(places)
            if weight is not None:
                term = weight * self.shifted(field, by)
                total = term if total is None else total + term
        return total

    def payload(self, pres, wind, jac):
        partial = self.mix(
            pres,
            {
                1: {0: 8.0, 1: 8.0, 6: 8.0},
                2: {0: -1.0, 1: -1.0},
                -1: {1: -8.0, 6: -8.0, 7: -8.0},
                -2: {6: 1.0, 7: 1.0},
            },
        )
        flux = jac * (wind - CG * partial)
        outer = self.mix(pres, {0: {0: 1.0, 1: 1.0, 6: 1.0, 7: 1.0}})
        return outer + self.mix(flux, {-2: {2: 1.0, 3: 1.0}, 2: {4: 1.0, 5: 1.0}})

    def correct(self, delta, pres, jac, delta_jac):
        grad = self.mix(
            delta, {2: {0: 1.0, 1: 1.0}, 3: {0: -8.0}, -2: {6: -1.0, 7: -1.0}, -3: {7: 8.0}}
        )
        wind = CG * grad
        own = -(jac * wind)
        far = self.mix(delta, {0: {0: 1.0, 1: 1.0, 6: 1.0, 7: 1.0}}) + CG * delta_jac * self.mix(
            pres, {0: {0: 1.0, 1: 1.0, 6: -1.0, 7: -1.0}, -1: {1: -8.0}, 1: {6: 8.0}}
        )
        spread = (
            self.mix(far, {0: {0: 1.0, 1: 1.0, 6: -1.0, 7: -1.0}})
            + self.mix(far - own, {1: {0: -8.0}, -1: {7: 8.0}})
            + self.mix(
                own,
                {
                    -1: {1: -8.0, 2: -8.0},
                    -2: {2: 1.0, 3: 1.0},
                    1: {5: 8.0, 6: 8.0},
                    2: {4: -1.0, 5: -1.0},
                },
            )
        )
        return wind, CD * spread / jac


LOW, HIGH = (0, 1, 2, 3), (4, 5, 6, 7)


def row_edge():
    return Edge(row_index(), 0, LOW + HIGH)


def lane_edge(held):
    return Edge((lane_index() & 3) + held[0], 1, held)


def both_ends(tiles):
    return jnp.where(row_index() < 4, tiles[0], tiles[-1])


def spread_slots(tile, low):
    lane = lane_index()
    if low:
        out = jnp.where(lane < SLOT, tile, 0.0)
    else:
        out = pltpu.roll(jnp.where(lane >= 128 - SLOT, tile, 0.0), SLOT, 1)
    by = SLOT
    while by < 128:
        out = out + pltpu.roll(out, by, 1)
        by *= 2
    return out


class Packer:
    def __init__(self, count):
        self.slot = lax.shift_right_logical(lane_index(), 2)
        self.start = [jnp.zeros((ROWS, 128), jnp.float32)] * (2 * count)
        self.count = count

    def add(self, level, tiles, state):
        before = lax.rem(level + 31, 32)
        rolled = [pltpu.roll(tile, SLOT * level, 1) for tile in tiles]
        low = [jnp.where(self.slot == level, r, s) for r, s in zip(rolled, state)]
        high = [jnp.where(self.slot == before, r, s) for r, s in zip(rolled, state[self.count :])]
        return low + high

    def done(self, state):
        return state[: self.count], [pltpu.roll(s, SLOT, 1) for s in state[self.count :]]


class Closed:
    def __init__(self):
        self.row = row_index()

    def along_y(self, tile):
        pair = tile - pltpu.roll(tile, 126, 1)
        return (pltpu.roll(pair, 2, 1) + pair) - 8.0 * pltpu.roll(pair, 1, 1)

    def moved(self, tiles, by):
        count = len(tiles)
        rolled = [pltpu.roll(tile, by % ROWS, 0) for tile in tiles]
        if by > 0:
            return [jnp.where(self.row < by, rolled[t - 1], rolled[t]) for t in range(count)]
        return [
            jnp.where(self.row >= ROWS + by, rolled[(t + 1) % count], rolled[t])
            for t in range(count)
        ]

    def along_x(self, tiles):
        pair = [f - m for f, m in zip(tiles, self.moved(tiles, -2))]
        return [
            (two + here) - 8.0 * one
            for two, here, one in zip(self.moved(pair, 2), pair, self.moved(pair, 1))
        ]


def even_place():
    return lax.rem(lax.axis_index("gy"), 2) == 0


def put_pair(inner_ref, outer_ref, index, down, up):
    even = even_place()
    put_tiles(inner_ref, index, [jnp.where(even, u, d) for u, d in zip(up, down)])
    put_tiles(outer_ref, index, [jnp.where(even, d, u) for u, d in zip(up, down)])


def get_pair(inner_ref, outer_ref, index, part):
    even = even_place()
    inner, outer = inner_ref[index, part, :], outer_ref[index, part, :]
    return jnp.where(even, outer, inner), jnp.where(even, inner, outer)


def lane_payload(pres, wind, jac):
    low, high = lane_edge(LOW), lane_edge(HIGH)
    down = [
        low.payload(p, w, spread_slots(j, True)) for p, w, j in zip(pres[0], wind[0], jac)
    ]
    up = [
        high.payload(p, w, spread_slots(j, False)) for p, w, j in zip(pres[1], wind[1], jac)
    ]
    return down, up


def pack_levels(ref, count, levels):
    packer = Packer(count)

    def step(level, state):
        return packer.add(level, tiles_of(ref, level, count), state)

    return packer.done(lax.fori_loop(0, levels, step, packer.start, unroll=UNROLL))


def kernel_a(
    p_hbm, wx_hbm, wy_hbm, jac_hbm, rows_ref, inner_ref, outer_ref, pp_ref, p_ref, wx_ref, wy_ref, jac_ref, sems
):
    levels, rows, _ = p_hbm.shape
    count = rows // ROWS
    share = levels // CHUNKS

    def fetch(source, target, sem):
        copy = pltpu.make_async_copy(source, target, sem)
        copy.start()
        return copy

    tail = pl.ds(rows - ROWS, ROWS)
    parts = [pl.ds(c * share, share) for c in range(CHUNKS)]
    pres_in = [fetch(p_hbm.at[s], p_ref.at[s], sems.at[0, c]) for c, s in enumerate(parts)]
    wind_in = [fetch(wy_hbm.at[s], wy_ref.at[s], sems.at[1, c]) for c, s in enumerate(parts)]
    ends_in = [
        fetch(jac_hbm, jac_ref, sems.at[2, 0]),
        fetch(wx_hbm.at[:, pl.ds(0, ROWS)], wx_ref.at[:, pl.ds(0, ROWS)], sems.at[2, 1]),
        fetch(wx_hbm.at[:, tail], wx_ref.at[:, pl.ds(ROWS, ROWS)], sems.at[2, 2]),
    ]

    def pack(ref, copies):
        packer = Packer(count)
        state = packer.start
        for c, copy in enumerate(copies):
            copy.wait()
            state = lax.fori_loop(
                c * share,
                (c + 1) * share,
                lambda level, state: packer.add(level, tiles_of(ref, level, count), state),
                state,
                unroll=UNROLL,
            )
        return packer.done(state)

    pres = pack(p_ref, pres_in)
    wind = pack(wy_ref, wind_in)
    for copy in ends_in:
        copy.wait()
    jac = planes_of(jac_ref, count)
    ends = both_ends(jac)
    edge = row_edge()

    def step(level, state):
        rows_ref[level] = edge.payload(
            both_ends(tiles_of(p_ref, level, count)), both_ends(tiles_of(wx_ref, level, 2)), ends
        )
        return state

    lax.fori_loop(0, levels, step, 0, unroll=2 * UNROLL)
    rows_ref[levels] = ends
    down, up = lane_payload(pres, wind, jac)
    put_pair(inner_ref, outer_ref, 0, down, up)
    put_pair(
        inner_ref,
        outer_ref,
        1,
        [spread_slots(j, True) for j in jac],
        [spread_slots(j, False) for j in jac],
    )
    put_tiles(pp_ref, 0, pres[0])
    put_tiles(pp_ref, 1, pres[1])


def kernel_n(wy_ref, pw_ref):
    levels, rows, _ = wy_ref.shape
    count = rows // ROWS
    wind = pack_levels(wy_ref, count, levels)
    put_tiles(pw_ref, 0, wind[0])
    put_tiles(pw_ref, 1, wind[1])


def kernel_m(p_ref, wx_ref, wy_ref, jac_ref, nx_ref, ny_ref, ps_ref):
    levels, rows, _ = p_ref.shape
    count = rows // ROWS
    jac = planes_of(jac_ref, count)
    inv_jac = [CD / j for j in jac]
    closed = Closed()

    def step(level, state):
        pres = tiles_of(p_ref, level, count)
        wind_x = tiles_of(wx_ref, level, count)
        wind_y = tiles_of(wy_ref, level, count)
        new_x = [w - CG * d for w, d in zip(wind_x, closed.along_x(pres))]
        new_y = [w - CG * closed.along_y(p) for w, p in zip(wind_y, pres)]
        put_tiles(nx_ref, level, new_x)
        put_tiles(ny_ref, level, new_y)
        spread_x = closed.along_x([j * n for j, n in zip(jac, new_x)])
        spread_y = [closed.along_y(j * n) for j, n in zip(jac, new_y)]
        put_tiles(
            ps_ref,
            level,
            [p - i * (x + y) for p, i, x, y in zip(pres, inv_jac, spread_x, spread_y)],
        )
        return state

    lax.fori_loop(0, levels, step, 0, unroll=UNROLL)


def kernel_b(
    p_ref,
    nxc_ref,
    nyc_ref,
    psc_ref,
    wz_ref,
    jac_ref,
    sx_ref,
    sy_ref,
    r_ref,
    i_ref,
    v_ref,
    pp_ref,
    rows_ref,
    inner_ref,
    outer_ref,
    got_rows_ref,
    got_inner_ref,
    got_outer_ref,
    srows_ref,
    sinner_ref,
    souter_ref,
    got_srows_ref,
    got_sinner_ref,
    got_souter_ref,
    coef_ref,
    nx_ref,
    ny_ref,
    ps_ref,
    y_ref,
    next_ref,
    cross_ref,
    mate_ref,
    share_ref,
):
    levels, rows, _ = p_ref.shape
    count = rows // ROWS
    last = count - 1
    lane, row = lane_index(), row_index()
    low_edge, high_edge, edge = lane_edge(LOW), lane_edge(HIGH), row_edge()
    wind_fix, low_fix, high_fix = [], [], []
    for t in range(count):
        part = slice(ROWS * t, ROWS * (t + 1))
        jac_low, jac_high = get_pair(sinner_ref, souter_ref, 1, part)
        jac_below, jac_above = get_pair(got_sinner_ref, got_souter_ref, 1, part)
        down, up = get_pair(inner_ref, outer_ref, 0, part)
        below, above = get_pair(got_inner_ref, got_outer_ref, 0, part)
        low_wind, low_star = low_edge.correct(
            below - up, pp_ref[0, part, :], jac_low, low_edge.shifted(jac_below - jac_high, 2)
        )
        high_wind, high_star = high_edge.correct(
            above - down, pp_ref[1, part, :], jac_high, high_edge.shifted(jac_above - jac_low, -2)
        )
        wind_fix.append(low_wind + pltpu.roll(high_wind, 128 - SLOT, 1))
        low_fix.append(low_star)
        high_fix.append(pltpu.roll(high_star, 128 - SLOT, 1))
    ends = srows_ref[levels]
    change = got_srows_ref[levels] - ends
    ends_change = jnp.where(row < 4, edge.shifted(change, -2), edge.shifted(change, 2))
    outer = (lane < 2) | (lane >= 126)
    low_lanes, high_lanes = lane < SLOT, lane >= 128 - SLOT
    first_rows = row < 4

    def star(level):
        new_x = tiles_of(nxc_ref, level, count)
        new_y = tiles_of(nyc_ref, level, count)
        stars = tiles_of(psc_ref, level, count)
        wind, press = edge.correct(
            pltpu.roll(got_rows_ref[level] - rows_ref[level], 4, 0),
            jnp.where(first_rows, p_ref[level, :ROWS, :], p_ref[level, ROWS * last :, :]),
            ends,
            ends_change,
        )
        new_x[0] = new_x[0] - jnp.where(first_rows, wind, 0.0)
        new_x[last] = new_x[last] - jnp.where(first_rows, 0.0, wind)
        stars[0] = stars[0] - jnp.where(first_rows, press, 0.0)
        stars[last] = stars[last] - jnp.where(first_rows, 0.0, press)
        back = lax.rem(128 - SLOT * level, 128)
        forces = []
        for t in range(count):
            part = slice(ROWS * t, ROWS * (t + 1))
            new_y[t] = new_y[t] - jnp.where(outer, pltpu.roll(wind_fix[t], back, 1), 0.0)
            fix = jnp.where(
                low_lanes,
                pltpu.roll(low_fix[t], back, 1),
                jnp.where(high_lanes, pltpu.roll(high_fix[t], back, 1), 0.0),
            )
            stars[t] = stars[t] - fix
            forces.append(
                wz_ref[level, part, :]
                + sx_ref[part, :] * new_x[t]
                + sy_ref[part, :] * new_y[t]
            )
        put_tiles(nx_ref, level, new_x)
        put_tiles(ny_ref, level, new_y)
        put_tiles(ps_ref, level, stars)
        return stars, forces

    def sweep(level, below, above, force, value, first):
        rate = tiles_of(r_ref, level, count)
        inv = tiles_of(i_ref, level, count)
        gain = tiles_of(v_ref, level, count)
        values, firsts = [], []
        for t in range(count):
            rhs = rate[t] * (force[t] - vert_coef * (above[t] - below[t]))
            firsts.append(first[t] + gain[t] * rhs)
            values.append((rhs + value[t]) * inv[t])
        put_tiles(y_ref, level, values)
        return values, firsts

    zeros = [jnp.zeros((ROWS, 128), jnp.float32)] * count
    here, force = star(0)
    bottom = here

    def step(level, carry):
        below, here, force, value, first = carry
        above, force_next = star(level)
        value, first = sweep(level - 1, below, above, force, value, first)
        return here, above, force_next, value, first

    below, here, force, value, first = lax.fori_loop(
        1, levels, step, (zeros, here, force, zeros, zeros), unroll=UNROLL
    )
    value, first = sweep(levels - 1, below, zeros, force, value, first)
    interface(first, value, bottom, here, coef_ref, next_ref, cross_ref, mate_ref, share_ref)


def kernel_f(s_ref, r_ref, i_ref, q_ref, v_ref, stat_ref):
    levels, rows, _ = s_ref.shape

    def down(level, carry):
        excess, prod = carry
        rate = 1.0 / s_ref[level]
        excess = rate + excess
        inv = 1.0 / (1.0 + excess)
        prod = prod * inv
        r_ref[level] = rate
        i_ref[level] = inv
        q_ref[level] = prod
        return excess * inv, prod

    ones = jnp.ones((rows, 128), jnp.float32)
    lax.fori_loop(0, levels, down, (ones, ones))

    def up(step, value):
        level = levels - 1 - step
        value = q_ref[level] + i_ref[level] * value
        v_ref[level] = value
        return value

    first = lax.fori_loop(0, levels, up, jnp.zeros((rows, 128), jnp.float32))
    stat_ref[0] = first
    stat_ref[1] = q_ref[levels - 1]
    stat_ref[2] = i_ref[levels - 1]
    stat_ref[3] = r_ref[0]
    stat_ref[4] = r_ref[levels - 1]


PAIR_COEFS = ("own", "other", "den", "den_end", "den_link", "outer", "total", "facing", "centre")


def place_in_column():
    mine = lax.axis_index("lev")
    return (mine == 0) | (mine == 3), mine < 2, lax.rem(mine, 2) == 0


def kernel_s(stat_ref, mate_ref, coef_ref):
    outermost, lower, even = place_in_column()
    count = stat_ref.shape[1] // ROWS
    for t in range(count):
        part = slice(ROWS * t, ROWS * (t + 1))
        mine = [stat_ref[k, part, :] for k in range(5)]
        mate = [mate_ref[k, part, :] for k in range(5)]
        outer = [jnp.where(outermost, a, b) for a, b in zip(mine, mate)]
        inner = [jnp.where(outermost, b, a) for a, b in zip(mine, mate)]
        outer_end = jnp.where(lower, outer[2], outer[0])
        end = jnp.where(lower, inner[0], inner[2])
        centre = jnp.where(lower, inner[2], inner[0])
        link = inner[1]
        den = 1.0 / (1.0 - end * outer_end)
        den_link = den * link
        weight = outer_end * den_link
        one, zero = jnp.ones_like(den), jnp.zeros_like(den)
        coefs = dict(
            own=jnp.where(outermost, den_link, one),
            other=jnp.where(outermost, zero, weight),
            den=den,
            den_end=den * end,
            den_link=den_link,
            outer=outer_end,
            total=centre + weight * link,
            facing=vert_coef * jnp.where(even, mate[3], mate[4]),
            centre=vert_coef * jnp.where(lower, inner[4], inner[3]),
        )
        for k, name in enumerate(PAIR_COEFS):
            coef_ref[k, part, :] = coefs[name]


def interface(
    first, value, star_first, star_last, coef_ref, next_ref, cross_ref, mate_ref, share_ref
):
    outermost, lower, even = place_in_column()
    for t in range(len(first)):
        part = slice(ROWS * t, ROWS * (t + 1))
        coef = {name: coef_ref[k, part, :] for k, name in enumerate(PAIR_COEFS)}
        sign = jnp.where(lower, 1.0, -1.0)
        star_centre = jnp.where(lower, star_last[t], star_first[t])
        star_outer = jnp.where(lower, star_first[t], star_last[t])
        facing = jnp.where(outermost, coef["facing"], 0.0)
        centre = jnp.where(lower, value[t], first[t]) + sign * facing * star_centre
        outer = jnp.where(lower, first[t], value[t]) - sign * coef["facing"] * star_outer
        total = coef["own"] * centre + coef["other"] * outer
        for ref in (next_ref, cross_ref, share_ref):
            ref[0, part, :] = total
            ref[1, part, :] = star_centre
        if next_ref.shape[0] > 3:
            next_ref[2, part, :] = coef["total"]
            next_ref[3, part, :] = coef["centre"]
        mate_ref[0, part, :] = jnp.where(outermost, centre, outer)
        mate_ref[1, part, :] = jnp.where(even, star_last[t], star_first[t])


def boundary(
    count,
    got_next_ref,
    got_cross_ref,
    got_mate_ref,
    got_share_ref,
    mate_ref,
    share_ref,
    coef_ref,
    far_ref,
    stat_ref,
    mate_stat_ref,
):
    outermost, lower, _ = place_in_column()
    sign = jnp.where(lower, 1.0, -1.0)
    parts = []
    for t in range(count):
        part = slice(ROWS * t, ROWS * (t + 1))
        coef = {name: coef_ref[k, part, :] for k, name in enumerate(PAIR_COEFS)}
        far_total, far_facing = far_ref[2, part, :], far_ref[3, part, :]
        own, got = mate_ref[0, part, :], got_mate_ref[0, part, :]
        this_star = jnp.where(outermost, got_share_ref[1, part, :], share_ref[1, part, :])
        next_star = jnp.where(outermost, got_cross_ref[1, part, :], got_next_ref[1, part, :])
        first_rate = jnp.where(outermost, mate_stat_ref[3, part, :], stat_ref[3, part, :])
        last_rate = jnp.where(outermost, mate_stat_ref[4, part, :], stat_ref[4, part, :])
        facing = vert_coef * jnp.where(lower, last_rate, first_rate)
        this = share_ref[0, part, :] + got_share_ref[0, part, :] + sign * far_facing * this_star
        that = got_cross_ref[0, part, :] + got_next_ref[0, part, :] - sign * facing * next_star
        middle = (that + far_total * this) / (1.0 - coef["total"] * far_total)
        from_outer = jnp.where(outermost, own, got)
        from_inner = jnp.where(outermost, got, own)
        between = (
            coef["den"] * from_inner + coef["den_end"] * from_outer + coef["den_link"] * middle
        )
        zero = jnp.zeros_like(own)
        centre = jnp.where(outermost, between, middle)
        outer = jnp.where(outermost, zero, from_outer + coef["outer"] * between)
        mate_star = got_mate_ref[1, part, :]
        star_centre = jnp.where(outermost, mate_star, next_star)
        star_outer = jnp.where(outermost, zero, mate_star)
        below, above = jnp.where(lower, outer, centre), jnp.where(lower, centre, outer)
        star_below = jnp.where(lower, star_outer, star_centre)
        star_above = jnp.where(lower, star_centre, star_outer)
        under = below - vert_coef * stat_ref[3, part, :] * star_below
        over = above + vert_coef * stat_ref[4, part, :] * star_above
        parts.append((below, above, under, over))
    return [[part[k] for part in parts] for k in range(4)]


def finish(count, levels, y_ref, q_ref, i_ref, ps_ref, x_ref, p_ref, column_refs, ready=None):
    lower, upper, under, over = boundary(count, *column_refs)

    def solved(level, above):
        value = tiles_of(y_ref, level, count)
        prod = tiles_of(q_ref, level, count)
        inv = tiles_of(i_ref, level, count)
        out = [(y + q * u) + i * a for y, q, u, i, a in zip(value, prod, lower, inv, above)]
        put_tiles(x_ref, level, out)
        return out

    def pressed(level, above, below):
        star = tiles_of(ps_ref, level, count)
        put_tiles(p_ref, level, [s - vert_coef * (a - b) for s, a, b in zip(star, above, below)])

    def step(index, carry):
        above, here = carry
        level = levels - 2 - index
        below = solved(level, here)
        pressed(level + 1, above, below)
        return here, below

    carry = over, solved(levels - 1, upper)
    if ready is None:
        carry = lax.fori_loop(0, levels - 1, step, carry, unroll=UNROLL)
    else:
        done, share = 0, levels // CHUNKS
        for c in range(CHUNKS - 1, -1, -1):
            goal = levels - 1 - c * share
            carry = lax.fori_loop(done, goal, step, carry, unroll=UNROLL)
            done = goal
            ready(c)
    above, here = carry
    pressed(0, above, under)


def kernel_c(*refs):
    column_refs = refs[:COLUMN]
    y_ref, q_ref, i_ref, ps_ref, wx_ref, pw_ref, jac_ref = refs[COLUMN : COLUMN + 7]
    x_ref, p_ref, rows_ref, inner_ref, outer_ref, pp_ref = refs[COLUMN + 7 :]
    levels, rows, _ = y_ref.shape
    count = rows // ROWS
    edge = row_edge()
    ends = both_ends(planes_of(jac_ref, count))
    finish(count, levels, y_ref, q_ref, i_ref, ps_ref, x_ref, p_ref, column_refs)

    def step(level, state):
        rows_ref[level] = edge.payload(
            both_ends(tiles_of(p_ref, level, count)),
            both_ends(tiles_of(wx_ref, level, count)),
            ends,
        )
        return state

    lax.fori_loop(0, levels, step, 0, unroll=2 * UNROLL)
    pres = pack_levels(p_ref, count, levels)
    wind = tiles_of(pw_ref, 0, count), tiles_of(pw_ref, 1, count)
    down, up = lane_payload(pres, wind, planes_of(jac_ref, count))
    put_pair(inner_ref, outer_ref, 0, down, up)
    put_tiles(pp_ref, 0, pres[0])
    put_tiles(pp_ref, 1, pres[1])


def kernel_d(*refs):
    column_refs = refs[:COLUMN]
    y_ref, q_ref, i_ref, ps_ref = refs[COLUMN : COLUMN + 4]
    x_hbm, p_hbm, x_ref, p_ref, sems = refs[COLUMN + 4 :]
    levels, rows, _ = y_ref.shape
    share = levels // CHUNKS
    copies = []

    def send(index, source, target, c):
        part = pl.ds(c * share, share)
        copy = pltpu.make_async_copy(source.at[part], target.at[part], sems.at[index, c])
        copy.start()
        copies.append(copy)

    def ready(c):
        send(0, x_ref, x_hbm, c)
        if c < CHUNKS - 1:
            send(1, p_ref, p_hbm, c + 1)

    finish(
        rows // ROWS,
        levels,
        y_ref,
        q_ref,
        i_ref,
        ps_ref,
        x_ref,
        p_ref,
        column_refs,
        ready,
    )
    send(1, p_ref, p_hbm, 0)
    for copy in copies:
        copy.wait()


def call(kernel, name, shapes, *args, weight=1, far_in=False, far_out=False, scratch=(), keep=()):
    near, far = pl.BlockSpec(memory_space=pltpu.VMEM), pl.BlockSpec(memory_space=pl.ANY)
    size = sum(a.size for a in args) + sum(functools.reduce(lambda a, b: a * b, s) for s in shapes)
    if far_in:
        args = [pltpu.with_memory_space_constraint(a, pltpu.HBM) for a in args]
    return pl.pallas_call(
        kernel,
        out_shape=[
            pltpu.VMEM(s, jnp.float32) if k in keep else jax.ShapeDtypeStruct(s, jnp.float32)
            for k, s in enumerate(shapes)
        ],
        in_specs=[far if far_in else near] * len(args),
        out_specs=[far if far_out else near] * len(shapes),
        scratch_shapes=list(scratch),
        compiler_params=pltpu.CompilerParams(vmem_limit_bytes=32 * 1024 * 1024),
        cost_estimate=pl.CostEstimate(
            flops=weight * size, bytes_accessed=4 * weight * size, transcendentals=0
        ),
        name=name,
    )(*args)


def swap(value, axis, partner):
    count = lax.axis_size(axis)
    return lax.ppermute(value, axis, [(i, partner(i)) for i in range(count)])


def exchange_rows(rows):
    count = lax.axis_size("gx")
    if count == 2:
        return swap(rows, "gx", lambda i: 1 - i)
    down = swap(rows[:, : ROWS // 2], "gx", lambda i: (i - 1) % count)
    up = swap(rows[:, ROWS // 2 :], "gx", lambda i: (i + 1) % count)
    return jnp.concatenate([down, up], axis=1)


def exchange_lanes(inner, outer):
    count = lax.axis_size("gy")
    got_inner = swap(inner, "gy", lambda i: i ^ 1)
    got_outer = swap(outer, "gy", lambda i: (i + 1 if i % 2 else i - 1) % count)
    return got_inner, got_outer


def exchange_column(following, cross, mate, share):
    got_cross = swap(cross, "lev", lambda i: i ^ 2)
    got_next = swap(following, "lev", lambda i: i ^ 3)
    got_mate = swap(mate, "lev", lambda i: i ^ 1)
    got_share = swap(share, "lev", lambda i: i ^ 1)
    return got_next, got_cross, got_mate, got_share, mate, share


def local(wind_x, wind_y, wind_z, pressure, jacobian, slope_x, slope_y, stiffness):
    field = wind_x.shape
    levels, rows, lanes = field
    plane = (rows, lanes)
    pair = (2,) + plane
    assert lanes == 128 and levels * SLOT == 128 and rows % ROWS == 0
    assert lax.axis_size("lev") == 4 and lax.axis_size("gy") % 2 == 0

    edge, inner, outer, ends = call(
        kernel_a,
        "start",
        [(levels + 1, ROWS, lanes), pair, (3,) + plane, pair],
        pressure,
        wind_x,
        wind_y,
        jacobian,
        far_in=True,
        scratch=[
            pltpu.VMEM(field, jnp.float32),
            pltpu.VMEM((levels, 2 * ROWS, lanes), jnp.float32),
            pltpu.VMEM(field, jnp.float32),
            pltpu.VMEM(plane, jnp.float32),
            pltpu.SemaphoreType.DMA((3, CHUNKS)),
        ],
    )
    sent = (edge, inner, outer)
    got = (exchange_rows(edge),) + exchange_lanes(inner, outer)
    static_edges = sent + got
    rate, inv, prod, gain, stat = call(
        kernel_f, "factor", [field, field, field, field, (5,) + plane], stiffness
    )
    mate = swap(stat, "lev", lambda i: i ^ 1)
    (coef,) = call(kernel_s, "pairs", [(len(PAIR_COEFS),) + plane], stat, mate)
    for substep in range(SUBSTEPS):
        closed = call(
            kernel_m, "interior", [field, field, field], pressure, wind_x, wind_y, jacobian
        )
        wind_x, wind_y, star, value, *faces = call(
            kernel_b,
            "sweep",
            [field, field, field, field, (3 if substep else 4,) + plane, pair, pair, pair],
            pressure,
            *closed,
            wind_z,
            jacobian,
            slope_x,
            slope_y,
            rate,
            inv,
            gain,
            ends,
            *sent,
            *got,
            *static_edges,
            coef,
            keep=tuple(range(8)),
        )
        column = exchange_column(*faces)
        if not substep:
            far = column[0]
        column += (coef, far, stat, mate)
        if substep < SUBSTEPS - 1:
            (packed,) = call(kernel_n, "pack", [pair], wind_y)
            wind_z, pressure, edge, inner, outer, ends = call(
                kernel_c,
                "finish",
                [field, field, (levels, ROWS, lanes), (1,) + plane, pair, pair],
                *column,
                value,
                prod,
                inv,
                star,
                wind_x,
                packed,
                jacobian,
            )
            sent = (edge, inner, outer)
            got = (exchange_rows(edge),) + exchange_lanes(inner, outer)
        else:
            wind_z, pressure = call(
                kernel_d,
                "last",
                [field, field],
                *column,
                value,
                prod,
                inv,
                star,
                far_out=True,
                scratch=[
                    pltpu.VMEM(field, jnp.float32),
                    pltpu.VMEM(field, jnp.float32),
                    pltpu.SemaphoreType.DMA((2, CHUNKS)),
                ],
            )
    return wind_x, wind_y, wind_z, pressure


def solution(mesh):
    field = P("lev", "gx", "gy")
    column = P("gx", "gy")
    return jax.shard_map(
        local,
        mesh=mesh,
        in_specs=(field,) * 4 + (column,) * 3 + (field,),
        out_specs=(field,) * 4,
        check_vma=False,
    )
```

```python
import functools

import jax
import jax.numpy as jnp
from jax import lax
from jax.experimental import pallas as pl
from jax.experimental.pallas import tpu as pltpu
from jax.sharding import PartitionSpec as P

SUBSTEPS = 2

grad_coef = 0.35
div_coef = 0.35
vert_coef = 0.25

CG = grad_coef / 12.0
CD = div_coef / 12.0
ROWS = 8
SLOT = 4
UNROLL = 8
CHUNKS = 4
COLUMN = 8
STATS = 5


def lane_index():
    return lax.broadcasted_iota(jnp.int32, (ROWS, 128), 1)


def row_index():
    return lax.broadcasted_iota(jnp.int32, (ROWS, 128), 0)


def only(mask, value):
    return jnp.where(mask, jnp.float32(value), jnp.float32(0.0))


def tiles_of(ref, level, count):
    return [ref[level, ROWS * t : ROWS * (t + 1), :] for t in range(count)]


def planes_of(ref, count):
    return [ref[ROWS * t : ROWS * (t + 1), :] for t in range(count)]


def put_tiles(ref, level, tiles):
    for t, tile in enumerate(tiles):
        ref[level, ROWS * t : ROWS * (t + 1), :] = tile


def put_planes(ref, tiles):
    for t, tile in enumerate(tiles):
        ref[ROWS * t : ROWS * (t + 1), :] = tile


class Edge:
    def __init__(self, place, axis, held):
        self.place, self.axis, self.held = place, axis, held
        self.size = place.shape[axis]

    def at(self, places):
        total = None
        for position, value in places.items():
            if position in self.held:
                term = only(self.place == position, value)
                total = term if total is None else total + term
        return total

    def shifted(self, field, by):
        return field if by == 0 else pltpu.roll(field, (-by) % self.size, self.axis)

    def mix(self, field, table):
        total = None
        for by, places in table.items():
            weight = self.at(places)
            if weight is not None:
                term = weight * self.shifted(field, by)
                total = term if total is None else total + term
        return total

    def payload(self, pres, wind, jac):
        partial = self.mix(
            pres,
            {
                1: {0: 8.0, 1: 8.0, 6: 8.0},
                2: {0: -1.0, 1: -1.0},
                -1: {1: -8.0, 6: -8.0, 7: -8.0},
                -2: {6: 1.0, 7: 1.0},
            },
        )
        flux = jac * (wind - CG * partial)
        outer = self.mix(pres, {0: {0: 1.0, 1: 1.0, 6: 1.0, 7: 1.0}})
        return outer + self.mix(flux, {-2: {2: 1.0, 3: 1.0}, 2: {4: 1.0, 5: 1.0}})

    def correct(self, delta, pres, jac, delta_jac):
        grad = self.mix(
            delta, {2: {0: 1.0, 1: 1.0}, 3: {0: -8.0}, -2: {6: -1.0, 7: -1.0}, -3: {7: 8.0}}
        )
        wind = CG * grad
        own = -(jac * wind)
        far = self.mix(delta, {0: {0: 1.0, 1: 1.0, 6: 1.0, 7: 1.0}}) + CG * delta_jac * self.mix(
            pres, {0: {0: 1.0, 1: 1.0, 6: -1.0, 7: -1.0}, -1: {1: -8.0}, 1: {6: 8.0}}
        )
        spread = (
            self.mix(far, {0: {0: 1.0, 1: 1.0, 6: -1.0, 7: -1.0}})
            + self.mix(far - own, {1: {0: -8.0}, -1: {7: 8.0}})
            + self.mix(
                own,
                {
                    -1: {1: -8.0, 2: -8.0},
                    -2: {2: 1.0, 3: 1.0},
                    1: {5: 8.0, 6: 8.0},
                    2: {4: -1.0, 5: -1.0},
                },
            )
        )
        return wind, CD * spread / jac


LOW, HIGH = (0, 1, 2, 3), (4, 5, 6, 7)


def row_edge():
    return Edge(row_index(), 0, LOW + HIGH)


def lane_edge(held):
    return Edge((lane_index() & 3) + held[0], 1, held)


def both_ends(tiles):
    return jnp.where(row_index() < 4, tiles[0], tiles[-1])


def spread_slots(tile, low):
    lane = lane_index()
    if low:
        out = jnp.where(lane < SLOT, tile, 0.0)
    else:
        out = pltpu.roll(jnp.where(lane >= 128 - SLOT, tile, 0.0), SLOT, 1)
    by = SLOT
    while by < 128:
        out = out + pltpu.roll(out, by, 1)
        by *= 2
    return out


class Packer:
    def __init__(self, count):
        self.slot = lax.shift_right_logical(lane_index(), 2)
        self.start = [jnp.zeros((ROWS, 128), jnp.float32)] * (2 * count)
        self.count = count

    def add(self, level, tiles, state):
        before = lax.rem(level + 31, 32)
        rolled = [pltpu.roll(tile, SLOT * level, 1) for tile in tiles]
        low = [jnp.where(self.slot == level, r, s) for r, s in zip(rolled, state)]
        high = [jnp.where(self.slot == before, r, s) for r, s in zip(rolled, state[self.count :])]
        return low + high

    def done(self, state):
        return state[: self.count], [pltpu.roll(s, SLOT, 1) for s in state[self.count :]]


class Closed:
    def __init__(self):
        self.row = row_index()

    def along_y(self, tile):
        pair = tile - pltpu.roll(tile, 126, 1)
        return (pltpu.roll(pair, 2, 1) + pair) - 8.0 * pltpu.roll(pair, 1, 1)

    def moved(self, tiles, by):
        count = len(tiles)
        rolled = [pltpu.roll(tile, by % ROWS, 0) for tile in tiles]
        if by > 0:
            return [jnp.where(self.row < by, rolled[t - 1], rolled[t]) for t in range(count)]
        return [
            jnp.where(self.row >= ROWS + by, rolled[(t + 1) % count], rolled[t])
            for t in range(count)
        ]

    def along_x(self, tiles):
        pair = [f - m for f, m in zip(tiles, self.moved(tiles, -2))]
        return [
            (two + here) - 8.0 * one
            for two, here, one in zip(self.moved(pair, 2), pair, self.moved(pair, 1))
        ]


def even_place():
    return lax.rem(lax.axis_index("gy"), 2) == 0


def put_pair(inner_ref, outer_ref, index, down, up):
    even = even_place()
    put_tiles(inner_ref, index, [jnp.where(even, u, d) for u, d in zip(up, down)])
    put_tiles(outer_ref, index, [jnp.where(even, d, u) for u, d in zip(up, down)])


def get_pair(inner_ref, outer_ref, index, part):
    even = even_place()
    inner, outer = inner_ref[index, part, :], outer_ref[index, part, :]
    return jnp.where(even, outer, inner), jnp.where(even, inner, outer)


def lane_payload(pres, wind, jac):
    low, high = lane_edge(LOW), lane_edge(HIGH)
    down = [
        low.payload(p, w, spread_slots(j, True)) for p, w, j in zip(pres[0], wind[0], jac)
    ]
    up = [
        high.payload(p, w, spread_slots(j, False)) for p, w, j in zip(pres[1], wind[1], jac)
    ]
    return down, up


def pack_levels(ref, count, levels):
    packer = Packer(count)

    def step(level, state):
        return packer.add(level, tiles_of(ref, level, count), state)

    return packer.done(lax.fori_loop(0, levels, step, packer.start, unroll=UNROLL))


def kernel_a(
    p_hbm,
    wx_hbm,
    wy_hbm,
    jac_hbm,
    s_hbm,
    rows_ref,
    inner_ref,
    outer_ref,
    pp_ref,
    r_ref,
    i_ref,
    q_ref,
    v_ref,
    stat_ref,
    p_ref,
    wx_ref,
    wy_ref,
    jac_ref,
    s_ref,
    sems,
):
    levels, rows, _ = p_hbm.shape
    count = rows // ROWS
    share = levels // CHUNKS

    def fetch(source, target, sem):
        copy = pltpu.make_async_copy(source, target, sem)
        copy.start()
        return copy

    tail = pl.ds(rows - ROWS, ROWS)
    parts = [pl.ds(c * share, share) for c in range(CHUNKS)]
    pres_in = [fetch(p_hbm.at[s], p_ref.at[s], sems.at[0, c]) for c, s in enumerate(parts)]
    stiff_in = [fetch(s_hbm.at[s], s_ref.at[s], sems.at[1, c]) for c, s in enumerate(parts)]
    wind_in = [fetch(wy_hbm.at[s], wy_ref.at[s], sems.at[2, c]) for c, s in enumerate(parts)]
    ends_in = [
        fetch(jac_hbm, jac_ref, sems.at[3, 0]),
        fetch(wx_hbm.at[:, pl.ds(0, ROWS)], wx_ref.at[:, pl.ds(0, ROWS)], sems.at[3, 1]),
        fetch(wx_hbm.at[:, tail], wx_ref.at[:, pl.ds(ROWS, ROWS)], sems.at[3, 2]),
    ]
    packer = Packer(count)

    def down(level, carry):
        state, excess, prod = carry
        for t in range(count):
            part = slice(ROWS * t, ROWS * (t + 1))
            rate = 1.0 / s_ref[level, part, :]
            grown = rate + excess[t]
            inv = 1.0 / (1.0 + grown)
            excess[t] = grown * inv
            prod[t] = prod[t] * inv
            r_ref[level, part, :] = rate
            i_ref[level, part, :] = inv
            q_ref[level, part, :] = prod[t]
        return packer.add(level, tiles_of(p_ref, level, count), state), excess, prod

    def up(step, carry):
        state, value = carry
        level = levels - 1 - step
        for t in range(count):
            part = slice(ROWS * t, ROWS * (t + 1))
            value[t] = q_ref[level, part, :] + i_ref[level, part, :] * value[t]
            v_ref[level, part, :] = value[t]
        return packer.add(step, tiles_of(wy_ref, step, count), state), value

    ones = [jnp.ones((ROWS, 128), jnp.float32)] * count
    carry = packer.start, list(ones), list(ones)
    for c in range(CHUNKS):
        pres_in[c].wait()
        stiff_in[c].wait()
        carry = lax.fori_loop(c * share, (c + 1) * share, down, carry, unroll=UNROLL)
    pres = packer.done(carry[0])
    carry = packer.start, [jnp.zeros_like(one) for one in ones]
    for c in range(CHUNKS):
        wind_in[c].wait()
        carry = lax.fori_loop(c * share, (c + 1) * share, up, carry, unroll=UNROLL)
    wind = packer.done(carry[0])
    put_tiles(stat_ref, 0, carry[1])
    stat_ref[1] = q_ref[levels - 1]
    stat_ref[2] = i_ref[levels - 1]
    stat_ref[3] = r_ref[0]
    stat_ref[4] = r_ref[levels - 1]

    for copy in ends_in:
        copy.wait()
    jac = planes_of(jac_ref, count)
    ends = both_ends(jac)
    edge = row_edge()

    def step(level, state):
        rows_ref[level] = edge.payload(
            both_ends(tiles_of(p_ref, level, count)), both_ends(tiles_of(wx_ref, level, 2)), ends
        )
        return state

    lax.fori_loop(0, levels, step, 0, unroll=2 * UNROLL)
    rows_ref[levels] = ends
    down_out, up_out = lane_payload(pres, wind, jac)
    put_pair(inner_ref, outer_ref, 0, down_out, up_out)
    put_pair(
        inner_ref,
        outer_ref,
        1,
        [spread_slots(j, True) for j in jac],
        [spread_slots(j, False) for j in jac],
    )
    put_tiles(pp_ref, 0, pres[0])
    put_tiles(pp_ref, 1, pres[1])


def kernel_n(wy_ref, pw_ref):
    levels, rows, _ = wy_ref.shape
    count = rows // ROWS
    wind = pack_levels(wy_ref, count, levels)
    put_tiles(pw_ref, 0, wind[0])
    put_tiles(pw_ref, 1, wind[1])


def kernel_m(p_ref, wx_ref, wy_ref, jac_ref, nx_ref, ny_ref, ps_ref):
    levels, rows, _ = p_ref.shape
    count = rows // ROWS
    jac = planes_of(jac_ref, count)
    inv_jac = [CD / j for j in jac]
    closed = Closed()

    def step(level, state):
        pres = tiles_of(p_ref, level, count)
        wind_x = tiles_of(wx_ref, level, count)
        wind_y = tiles_of(wy_ref, level, count)
        new_x = [w - CG * d for w, d in zip(wind_x, closed.along_x(pres))]
        new_y = [w - CG * closed.along_y(p) for w, p in zip(wind_y, pres)]
        put_tiles(nx_ref, level, new_x)
        put_tiles(ny_ref, level, new_y)
        spread_x = closed.along_x([j * n for j, n in zip(jac, new_x)])
        spread_y = [closed.along_y(j * n) for j, n in zip(jac, new_y)]
        put_tiles(
            ps_ref,
            level,
            [p - i * (x + y) for p, i, x, y in zip(pres, inv_jac, spread_x, spread_y)],
        )
        return state

    lax.fori_loop(0, levels, step, 0, unroll=UNROLL)


def kernel_b(
    p_ref,
    nxc_ref,
    nyc_ref,
    psc_ref,
    wz_ref,
    jac_ref,
    sx_ref,
    sy_ref,
    r_ref,
    i_ref,
    v_ref,
    pp_ref,
    rows_ref,
    inner_ref,
    outer_ref,
    got_rows_ref,
    got_inner_ref,
    got_outer_ref,
    srows_ref,
    sinner_ref,
    souter_ref,
    got_srows_ref,
    got_sinner_ref,
    got_souter_ref,
    coef_ref,
    nx_ref,
    ny_ref,
    ps_ref,
    y_ref,
    next_ref,
    cross_ref,
    mate_ref,
    share_ref,
):
    levels, rows, _ = p_ref.shape
    count = rows // ROWS
    last = count - 1
    lane, row = lane_index(), row_index()
    low_edge, high_edge, edge = lane_edge(LOW), lane_edge(HIGH), row_edge()
    wind_fix, low_fix, high_fix = [], [], []
    for t in range(count):
        part = slice(ROWS * t, ROWS * (t + 1))
        jac_low, jac_high = get_pair(sinner_ref, souter_ref, 1, part)
        jac_below, jac_above = get_pair(got_sinner_ref, got_souter_ref, 1, part)
        down, up = get_pair(inner_ref, outer_ref, 0, part)
        below, above = get_pair(got_inner_ref, got_outer_ref, 0, part)
        low_wind, low_star = low_edge.correct(
            below - up, pp_ref[0, part, :], jac_low, low_edge.shifted(jac_below - jac_high, 2)
        )
        high_wind, high_star = high_edge.correct(
            above - down, pp_ref[1, part, :], jac_high, high_edge.shifted(jac_above - jac_low, -2)
        )
        wind_fix.append(low_wind + pltpu.roll(high_wind, 128 - SLOT, 1))
        low_fix.append(low_star)
        high_fix.append(pltpu.roll(high_star, 128 - SLOT, 1))
    ends = srows_ref[levels]
    change = got_srows_ref[levels] - ends
    ends_change = jnp.where(row < 4, edge.shifted(change, -2), edge.shifted(change, 2))
    outer = (lane < 2) | (lane >= 126)
    low_lanes, high_lanes = lane < SLOT, lane >= 128 - SLOT
    first_rows = row < 4

    def star(level, which):
        new_x = {t: nxc_ref[level, ROWS * t : ROWS * (t + 1), :] for t in which}
        stars = {t: psc_ref[level, ROWS * t : ROWS * (t + 1), :] for t in which}
        if 0 in which:
            wind, press = edge.correct(
                pltpu.roll(got_rows_ref[level] - rows_ref[level], 4, 0),
                jnp.where(first_rows, p_ref[level, :ROWS, :], p_ref[level, ROWS * last :, :]),
                ends,
                ends_change,
            )
            new_x[0] = new_x[0] - jnp.where(first_rows, wind, 0.0)
            new_x[last] = new_x[last] - jnp.where(first_rows, 0.0, wind)
            stars[0] = stars[0] - jnp.where(first_rows, press, 0.0)
            stars[last] = stars[last] - jnp.where(first_rows, 0.0, press)
        back = lax.rem(128 - SLOT * level, 128)
        forces = []
        for t in which:
            part = slice(ROWS * t, ROWS * (t + 1))
            new_y = nyc_ref[level, part, :] - jnp.where(
                outer, pltpu.roll(wind_fix[t], back, 1), 0.0
            )
            fix = jnp.where(
                low_lanes,
                pltpu.roll(low_fix[t], back, 1),
                jnp.where(high_lanes, pltpu.roll(high_fix[t], back, 1), 0.0),
            )
            stars[t] = stars[t] - fix
            forces.append(
                wz_ref[level, part, :] + sx_ref[part, :] * new_x[t] + sy_ref[part, :] * new_y
            )
            nx_ref[level, part, :] = new_x[t]
            ny_ref[level, part, :] = new_y
            ps_ref[level, part, :] = stars[t]
        return [stars[t] for t in which], forces

    def sweep(level, which, below, above, force, value, first):
        values, firsts = [], []
        for k, t in enumerate(which):
            part = slice(ROWS * t, ROWS * (t + 1))
            rhs = r_ref[level, part, :] * (force[k] - vert_coef * (above[k] - below[k]))
            firsts.append(first[k] + v_ref[level, part, :] * rhs)
            values.append((rhs + value[k]) * i_ref[level, part, :])
            y_ref[level, part, :] = values[k]
        return values, firsts

    for which in ((0, last), tuple(range(1, last))):
        zeros = [jnp.zeros((ROWS, 128), jnp.float32)] * len(which)
        bottom, force = star(0, which)

        def step(level, carry, which=which):
            below, here, force, value, first = carry
            above, force_next = star(level, which)
            value, first = sweep(level - 1, which, below, above, force, value, first)
            return here, above, force_next, value, first

        below, here, force, value, first = lax.fori_loop(
            1, levels, step, (zeros, bottom, force, zeros, zeros), unroll=UNROLL
        )
        value, first = sweep(levels - 1, which, below, zeros, force, value, first)
        interface(
            which, first, value, bottom, here, coef_ref, next_ref, cross_ref, mate_ref, share_ref
        )


PAIR_COEFS = ("own", "other", "den", "den_end", "den_link", "outer", "total", "facing", "centre", "first", "last")


def place_in_column():
    mine = lax.axis_index("lev")
    return (mine == 0) | (mine == 3), mine < 2, lax.rem(mine, 2) == 0


def kernel_s(stat_ref, mate_ref, coef_ref):
    outermost, lower, even = place_in_column()
    for t in range(coef_ref.shape[1] // ROWS):
        part = slice(ROWS * t, ROWS * (t + 1))
        mine = [stat_ref[k, part, :] for k in range(STATS)]
        mate = [mate_ref[k, part, :] for k in range(STATS)]
        outer = [jnp.where(outermost, a, b) for a, b in zip(mine, mate)]
        inner = [jnp.where(outermost, b, a) for a, b in zip(mine, mate)]
        outer_end = jnp.where(lower, outer[2], outer[0])
        end = jnp.where(lower, inner[0], inner[2])
        centre = jnp.where(lower, inner[2], inner[0])
        link = inner[1]
        den = 1.0 / (1.0 - end * outer_end)
        den_link = den * link
        weight = outer_end * den_link
        one, zero = jnp.ones_like(den), jnp.zeros_like(den)
        coefs = dict(
            own=jnp.where(outermost, den_link, one),
            other=jnp.where(outermost, zero, weight),
            den=den,
            den_end=den * end,
            den_link=den_link,
            outer=outer_end,
            total=centre + weight * link,
            facing=vert_coef * jnp.where(even, mate[3], mate[4]),
            centre=vert_coef * jnp.where(lower, inner[4], inner[3]),
            first=vert_coef * mine[3],
            last=vert_coef * mine[4],
        )
        for k, name in enumerate(PAIR_COEFS):
            coef_ref[k, part, :] = coefs[name]


def interface(
    which, first, value, star_first, star_last, coef_ref, next_ref, cross_ref, mate_ref, share_ref
):
    outermost, lower, even = place_in_column()
    for t, tile in enumerate(which):
        part = slice(ROWS * tile, ROWS * (tile + 1))
        coef = {name: coef_ref[k, part, :] for k, name in enumerate(PAIR_COEFS)}
        sign = jnp.where(lower, 1.0, -1.0)
        star_centre = jnp.where(lower, star_last[t], star_first[t])
        star_outer = jnp.where(lower, star_first[t], star_last[t])
        facing = jnp.where(outermost, coef["facing"], 0.0)
        centre = jnp.where(lower, value[t], first[t]) + sign * facing * star_centre
        outer = jnp.where(lower, first[t], value[t]) - sign * coef["facing"] * star_outer
        total = coef["own"] * centre + coef["other"] * outer
        for ref in (next_ref, cross_ref, share_ref):
            ref[0, part, :] = total
            ref[1, part, :] = star_centre
        if next_ref.shape[0] > 3:
            next_ref[2, part, :] = coef["total"]
            next_ref[3, part, :] = coef["centre"]
        mate_ref[0, part, :] = jnp.where(outermost, centre, outer)
        mate_ref[1, part, :] = jnp.where(even, star_last[t], star_first[t])


def boundary(
    count,
    got_next_ref,
    got_cross_ref,
    got_mate_ref,
    got_share_ref,
    mate_ref,
    share_ref,
    coef_ref,
    far_ref,
):
    outermost, lower, _ = place_in_column()
    sign = jnp.where(lower, 1.0, -1.0)
    parts = []
    for t in range(count):
        part = slice(ROWS * t, ROWS * (t + 1))
        coef = {name: coef_ref[k, part, :] for k, name in enumerate(PAIR_COEFS)}
        far_total, far_facing = far_ref[2, part, :], far_ref[3, part, :]
        own, got = mate_ref[0, part, :], got_mate_ref[0, part, :]
        this_star = jnp.where(outermost, got_share_ref[1, part, :], share_ref[1, part, :])
        next_star = jnp.where(outermost, got_cross_ref[1, part, :], got_next_ref[1, part, :])
        this = share_ref[0, part, :] + got_share_ref[0, part, :] + sign * far_facing * this_star
        that = (
            got_cross_ref[0, part, :]
            + got_next_ref[0, part, :]
            - sign * coef["centre"] * next_star
        )
        middle = (that + far_total * this) / (1.0 - coef["total"] * far_total)
        from_outer = jnp.where(outermost, own, got)
        from_inner = jnp.where(outermost, got, own)
        between = (
            coef["den"] * from_inner + coef["den_end"] * from_outer + coef["den_link"] * middle
        )
        zero = jnp.zeros_like(own)
        centre = jnp.where(outermost, between, middle)
        outer = jnp.where(outermost, zero, from_outer + coef["outer"] * between)
        mate_star = got_mate_ref[1, part, :]
        star_centre = jnp.where(outermost, mate_star, next_star)
        star_outer = jnp.where(outermost, zero, mate_star)
        below, above = jnp.where(lower, outer, centre), jnp.where(lower, centre, outer)
        star_below = jnp.where(lower, star_outer, star_centre)
        star_above = jnp.where(lower, star_centre, star_outer)
        under = below - coef["first"] * star_below
        over = above + coef["last"] * star_above
        parts.append((below, above, under, over))
    return [[part[k] for part in parts] for k in range(4)]


def finish(count, levels, y_ref, q_ref, i_ref, ps_ref, x_ref, p_ref, column_refs, ready=None):
    lower, upper, under, over = boundary(count, *column_refs)

    def solved(level, above):
        value = tiles_of(y_ref, level, count)
        prod = tiles_of(q_ref, level, count)
        inv = tiles_of(i_ref, level, count)
        out = [(y + q * u) + i * a for y, q, u, i, a in zip(value, prod, lower, inv, above)]
        put_tiles(x_ref, level, out)
        return out

    def pressed(level, above, below):
        star = tiles_of(ps_ref, level, count)
        put_tiles(p_ref, level, [s - vert_coef * (a - b) for s, a, b in zip(star, above, below)])

    def step(index, carry):
        above, here = carry
        level = levels - 2 - index
        below = solved(level, here)
        pressed(level + 1, above, below)
        return here, below

    carry = over, solved(levels - 1, upper)
    if ready is None:
        carry = lax.fori_loop(0, levels - 1, step, carry, unroll=UNROLL)
    else:
        done, share = 0, levels // CHUNKS
        for c in range(CHUNKS - 1, -1, -1):
            goal = levels - 1 - c * share
            carry = lax.fori_loop(done, goal, step, carry, unroll=UNROLL)
            done = goal
            ready(c)
    above, here = carry
    pressed(0, above, under)


def kernel_c(*refs):
    column_refs = refs[:COLUMN]
    y_ref, q_ref, i_ref, ps_ref, wx_ref, pw_ref, jac_ref = refs[COLUMN : COLUMN + 7]
    x_ref, p_ref, rows_ref, inner_ref, outer_ref, pp_ref = refs[COLUMN + 7 :]
    levels, rows, _ = y_ref.shape
    count = rows // ROWS
    edge = row_edge()
    ends = both_ends(planes_of(jac_ref, count))
    finish(count, levels, y_ref, q_ref, i_ref, ps_ref, x_ref, p_ref, column_refs)

    def step(level, state):
        rows_ref[level] = edge.payload(
            both_ends(tiles_of(p_ref, level, count)),
            both_ends(tiles_of(wx_ref, level, count)),
            ends,
        )
        return state

    lax.fori_loop(0, levels, step, 0, unroll=2 * UNROLL)
    pres = pack_levels(p_ref, count, levels)
    wind = tiles_of(pw_ref, 0, count), tiles_of(pw_ref, 1, count)
    down, up = lane_payload(pres, wind, planes_of(jac_ref, count))
    put_pair(inner_ref, outer_ref, 0, down, up)
    put_tiles(pp_ref, 0, pres[0])
    put_tiles(pp_ref, 1, pres[1])


def kernel_d(*refs):
    column_refs = refs[:COLUMN]
    y_ref, q_ref, i_ref, ps_ref = refs[COLUMN : COLUMN + 4]
    x_hbm, p_hbm, x_ref, p_ref, sems = refs[COLUMN + 4 :]
    levels, rows, _ = y_ref.shape
    share = levels // CHUNKS
    copies = []

    def send(index, source, target, c):
        part = pl.ds(c * share, share)
        copy = pltpu.make_async_copy(source.at[part], target.at[part], sems.at[index, c])
        copy.start()
        copies.append(copy)

    def ready(c):
        send(0, x_ref, x_hbm, c)
        if c < CHUNKS - 1:
            send(1, p_ref, p_hbm, c + 1)

    finish(
        rows // ROWS,
        levels,
        y_ref,
        q_ref,
        i_ref,
        ps_ref,
        x_ref,
        p_ref,
        column_refs,
        ready,
    )
    send(1, p_ref, p_hbm, 0)
    for copy in copies:
        copy.wait()


def call(kernel, name, shapes, *args, far_in=(), far_out=False, scratch=(), keep=()):
    near, far = pl.BlockSpec(memory_space=pltpu.VMEM), pl.BlockSpec(memory_space=pl.ANY)
    size = sum(a.size for a in args) + sum(functools.reduce(lambda a, b: a * b, s) for s in shapes)
    if len(far_in) == len(args):
        args = [pltpu.with_memory_space_constraint(a, pltpu.HBM) for a in args]
    return pl.pallas_call(
        kernel,
        out_shape=[
            pltpu.VMEM(s, jnp.float32) if k in keep else jax.ShapeDtypeStruct(s, jnp.float32)
            for k, s in enumerate(shapes)
        ],
        in_specs=[far if k in far_in else near for k in range(len(args))],
        out_specs=[far if far_out else near] * len(shapes),
        scratch_shapes=list(scratch),
        compiler_params=pltpu.CompilerParams(vmem_limit_bytes=32 * 1024 * 1024),
        cost_estimate=pl.CostEstimate(
            flops=8 * size, bytes_accessed=4 * size, transcendentals=0
        ),
        name=name,
    )(*args)


def swap(value, axis, partner):
    count = lax.axis_size(axis)
    return lax.ppermute(value, axis, [(i, partner(i)) for i in range(count)])


def exchange_rows(rows):
    count = lax.axis_size("gx")
    if count == 2:
        return swap(rows, "gx", lambda i: 1 - i)
    down = swap(rows[:, : ROWS // 2], "gx", lambda i: (i - 1) % count)
    up = swap(rows[:, ROWS // 2 :], "gx", lambda i: (i + 1) % count)
    return jnp.concatenate([down, up], axis=1)


def exchange_lanes(inner, outer):
    count = lax.axis_size("gy")
    got_inner = swap(inner, "gy", lambda i: i ^ 1)
    got_outer = swap(outer, "gy", lambda i: (i + 1 if i % 2 else i - 1) % count)
    return got_inner, got_outer


def exchange_column(following, cross, mate, share):
    got_cross = swap(cross, "lev", lambda i: i ^ 2)
    got_next = swap(following, "lev", lambda i: i ^ 3)
    got_mate = swap(mate, "lev", lambda i: i ^ 1)
    got_share = swap(share, "lev", lambda i: i ^ 1)
    return got_next, got_cross, got_mate, got_share, mate, share


def local(wind_x, wind_y, wind_z, pressure, jacobian, slope_x, slope_y, stiffness):
    field = wind_x.shape
    levels, rows, lanes = field
    plane = (rows, lanes)
    pair = (2,) + plane
    assert lanes == 128 and levels * SLOT == 128 and rows % ROWS == 0
    assert lax.axis_size("lev") == 4 and lax.axis_size("gy") % 2 == 0

    edge, inner, outer, ends, rate, inv, prod, gain, stat = call(
        kernel_a,
        "start",
        [(levels + 1, ROWS, lanes), pair, (3,) + plane, pair] + [field] * 4 + [(STATS,) + plane],
        pressure,
        wind_x,
        wind_y,
        jacobian,
        stiffness,
        far_in=(0, 1, 2, 3, 4),
        scratch=[
            pltpu.VMEM(field, jnp.float32),
            pltpu.VMEM((levels, 2 * ROWS, lanes), jnp.float32),
            pltpu.VMEM(field, jnp.float32),
            pltpu.VMEM(plane, jnp.float32),
            pltpu.VMEM(field, jnp.float32),
            pltpu.SemaphoreType.DMA((4, CHUNKS)),
        ],
    )
    mate = swap(stat, "lev", lambda i: i ^ 1)
    (coef,) = call(kernel_s, "pairs", [(len(PAIR_COEFS),) + plane], stat, mate)
    sent = (edge, inner, outer)
    got = (exchange_rows(edge),) + exchange_lanes(inner, outer)
    static_edges = sent + got
    for substep in range(SUBSTEPS):
        closed = call(
            kernel_m, "interior", [field, field, field], pressure, wind_x, wind_y, jacobian
        )
        wind_x, wind_y, star, value, *faces = call(
            kernel_b,
            "sweep",
            [field, field, field, field, (3 if substep else 4,) + plane, pair, pair, pair],
            pressure,
            *closed,
            wind_z,
            jacobian,
            slope_x,
            slope_y,
            rate,
            inv,
            gain,
            ends,
            *sent,
            *got,
            *static_edges,
            coef,
            keep=tuple(range(8)),
        )
        column = exchange_column(*faces)
        if not substep:
            far = column[0]
        column += (coef, far)
        if substep < SUBSTEPS - 1:
            (packed,) = call(kernel_n, "pack", [pair], wind_y)
            wind_z, pressure, edge, inner, outer, ends = call(
                kernel_c,
                "finish",
                [field, field, (levels, ROWS, lanes), (1,) + plane, pair, pair],
                *column,
                value,
                prod,
                inv,
                star,
                wind_x,
                packed,
                jacobian,
            )
            sent = (edge, inner, outer)
            got = (exchange_rows(edge),) + exchange_lanes(inner, outer)
        else:
            wind_z, pressure = call(
                kernel_d,
                "last",
                [field, field],
                *column,
                value,
                prod,
                inv,
                star,
                far_out=True,
                scratch=[
                    pltpu.VMEM(field, jnp.float32),
                    pltpu.VMEM(field, jnp.float32),
                    pltpu.SemaphoreType.DMA((2, CHUNKS)),
                ],
            )
    return wind_x, wind_y, wind_z, pressure


def solution(mesh):
    field = P("lev", "gx", "gy")
    column = P("gx", "gy")
    return jax.shard_map(
        local,
        mesh=mesh,
        in_specs=(field,) * 4 + (column,) * 3 + (field,),
        out_specs=(field,) * 4,
        check_vma=False,
    )
```

```python
import functools

import jax
import jax.numpy as jnp
from jax import lax
from jax.experimental import pallas as pl
from jax.experimental.pallas import tpu as pltpu
from jax.sharding import PartitionSpec as P

SUBSTEPS = 2

grad_coef = 0.35
div_coef = 0.35
vert_coef = 0.25

CG = grad_coef / 12.0
CD = div_coef / 12.0
ROWS = 8
SLOT = 4
UNROLL = 8
CHUNKS = 4
COLUMN = 8
STATS = 5


def lane_index():
    return lax.broadcasted_iota(jnp.int32, (ROWS, 128), 1)


def row_index():
    return lax.broadcasted_iota(jnp.int32, (ROWS, 128), 0)


def only(mask, value):
    return jnp.where(mask, jnp.float32(value), jnp.float32(0.0))


def tiles_of(ref, level, count):
    return [ref[level, ROWS * t : ROWS * (t + 1), :] for t in range(count)]


def planes_of(ref, count):
    return [ref[ROWS * t : ROWS * (t + 1), :] for t in range(count)]


def put_tiles(ref, level, tiles):
    for t, tile in enumerate(tiles):
        ref[level, ROWS * t : ROWS * (t + 1), :] = tile


def put_planes(ref, tiles):
    for t, tile in enumerate(tiles):
        ref[ROWS * t : ROWS * (t + 1), :] = tile


class Edge:
    def __init__(self, place, axis, held):
        self.place, self.axis, self.held = place, axis, held
        self.size = place.shape[axis]

    def at(self, places):
        total = None
        for position, value in places.items():
            if position in self.held:
                term = only(self.place == position, value)
                total = term if total is None else total + term
        return total

    def shifted(self, field, by):
        return field if by % self.size == 0 else pltpu.roll(field, (-by) % self.size, self.axis)

    def mix(self, field, table):
        total = None
        for by, places in table.items():
            weight = self.at(places)
            if weight is not None:
                term = weight * self.shifted(field, by)
                total = term if total is None else total + term
        return total

    def payload(self, pres, wind, jac):
        partial = self.mix(
            pres,
            {
                1: {0: 8.0, 1: 8.0, 6: 8.0},
                2: {0: -1.0, 1: -1.0},
                -1: {1: -8.0, 6: -8.0, 7: -8.0},
                -2: {6: 1.0, 7: 1.0},
            },
        )
        flux = jac * (wind - CG * partial)
        outer = self.mix(pres, {0: {0: 1.0, 1: 1.0, 6: 1.0, 7: 1.0}})
        return outer + self.mix(flux, {-2: {2: 1.0, 3: 1.0}, 2: {4: 1.0, 5: 1.0}})

    def correct(self, delta, pres, jac, delta_jac, base=0):
        grad = self.mix(
            delta,
            {
                base + 2: {0: 1.0, 1: 1.0},
                base + 3: {0: -8.0},
                base - 2: {6: -1.0, 7: -1.0},
                base - 3: {7: 8.0},
            },
        )
        wind = CG * grad
        own = -(jac * wind)
        far = self.mix(delta, {base: {0: 1.0, 1: 1.0, 6: 1.0, 7: 1.0}}) + CG * delta_jac * self.mix(
            pres, {0: {0: 1.0, 1: 1.0, 6: -1.0, 7: -1.0}, -1: {1: -8.0}, 1: {6: 8.0}}
        )
        spread = (
            self.mix(far, {0: {0: 1.0, 1: 1.0, 6: -1.0, 7: -1.0}})
            + self.mix(far - own, {1: {0: -8.0}, -1: {7: 8.0}})
            + self.mix(
                own,
                {
                    -1: {1: -8.0, 2: -8.0},
                    -2: {2: 1.0, 3: 1.0},
                    1: {5: 8.0, 6: 8.0},
                    2: {4: -1.0, 5: -1.0},
                },
            )
        )
        return wind, CD * spread / jac


LOW, HIGH = (0, 1, 2, 3), (4, 5, 6, 7)


def row_edge():
    return Edge(row_index(), 0, LOW + HIGH)


def lane_edge(held):
    return Edge((lane_index() & 3) + held[0], 1, held)


def both_ends(tiles):
    return jnp.where(row_index() < 4, tiles[0], tiles[-1])


def spread_slots(tile, low):
    lane = lane_index()
    if low:
        out = jnp.where(lane < SLOT, tile, 0.0)
    else:
        out = pltpu.roll(jnp.where(lane >= 128 - SLOT, tile, 0.0), SLOT, 1)
    by = SLOT
    while by < 128:
        out = out + pltpu.roll(out, by, 1)
        by *= 2
    return out


class Packer:
    def __init__(self, count):
        self.slot = lax.shift_right_logical(lane_index(), 2)
        self.start = [jnp.zeros((ROWS, 128), jnp.float32)] * (2 * count)
        self.count = count

    def add(self, level, tiles, state):
        before = lax.rem(level + 31, 32)
        rolled = [pltpu.roll(tile, SLOT * level, 1) for tile in tiles]
        low = [jnp.where(self.slot == level, r, s) for r, s in zip(rolled, state)]
        high = [jnp.where(self.slot == before, r, s) for r, s in zip(rolled, state[self.count :])]
        return low + high

    def done(self, state):
        return state[: self.count], [pltpu.roll(s, SLOT, 1) for s in state[self.count :]]


class Closed:
    def __init__(self):
        self.row = row_index()

    def along_y(self, tile):
        pair = tile - pltpu.roll(tile, 126, 1)
        return (pltpu.roll(pair, 2, 1) + pair) - 8.0 * pltpu.roll(pair, 1, 1)

    def moved(self, tiles, by):
        count = len(tiles)
        rolled = [pltpu.roll(tile, by % ROWS, 0) for tile in tiles]
        if by > 0:
            return [jnp.where(self.row < by, rolled[t - 1], rolled[t]) for t in range(count)]
        return [
            jnp.where(self.row >= ROWS + by, rolled[(t + 1) % count], rolled[t])
            for t in range(count)
        ]

    def along_x(self, tiles):
        pair = [f - m for f, m in zip(tiles, self.moved(tiles, -2))]
        return [
            (two + here) - 8.0 * one
            for two, here, one in zip(self.moved(pair, 2), pair, self.moved(pair, 1))
        ]


def even_place():
    return lax.rem(lax.axis_index("gy"), 2) == 0


def put_pair(inner_ref, outer_ref, index, down, up):
    even = even_place()
    put_tiles(inner_ref, index, [jnp.where(even, u, d) for u, d in zip(up, down)])
    put_tiles(outer_ref, index, [jnp.where(even, d, u) for u, d in zip(up, down)])


def get_pair(inner_ref, outer_ref, index, part):
    even = even_place()
    inner, outer = inner_ref[index, part, :], outer_ref[index, part, :]
    return jnp.where(even, outer, inner), jnp.where(even, inner, outer)


def lane_payload(pres, wind, jac):
    low, high = lane_edge(LOW), lane_edge(HIGH)
    down = [
        low.payload(p, w, spread_slots(j, True)) for p, w, j in zip(pres[0], wind[0], jac)
    ]
    up = [
        high.payload(p, w, spread_slots(j, False)) for p, w, j in zip(pres[1], wind[1], jac)
    ]
    return down, up


def pack_levels(ref, count, levels):
    packer = Packer(count)

    def step(level, state):
        return packer.add(level, tiles_of(ref, level, count), state)

    return packer.done(lax.fori_loop(0, levels, step, packer.start, unroll=UNROLL))


def kernel_a(
    p_hbm,
    wx_hbm,
    wy_hbm,
    jac_hbm,
    s_hbm,
    rows_ref,
    inner_ref,
    outer_ref,
    pp_ref,
    r_ref,
    i_ref,
    q_ref,
    v_ref,
    stat_ref,
    p_ref,
    wx_ref,
    wy_ref,
    jac_ref,
    s_ref,
    sems,
):
    levels, rows, _ = p_hbm.shape
    count = rows // ROWS
    share = levels // CHUNKS

    def fetch(source, target, sem):
        copy = pltpu.make_async_copy(source, target, sem)
        copy.start()
        return copy

    tail = pl.ds(rows - ROWS, ROWS)
    parts = [pl.ds(c * share, share) for c in range(CHUNKS)]
    pres_in = [fetch(p_hbm.at[s], p_ref.at[s], sems.at[0, c]) for c, s in enumerate(parts)]
    stiff_in = [fetch(s_hbm.at[s], s_ref.at[s], sems.at[1, c]) for c, s in enumerate(parts)]
    wind_in = [fetch(wy_hbm.at[s], wy_ref.at[s], sems.at[2, c]) for c, s in enumerate(parts)]
    ends_in = [
        fetch(jac_hbm, jac_ref, sems.at[3, 0]),
        fetch(wx_hbm.at[:, pl.ds(0, ROWS)], wx_ref.at[:, pl.ds(0, ROWS)], sems.at[3, 1]),
        fetch(wx_hbm.at[:, tail], wx_ref.at[:, pl.ds(ROWS, ROWS)], sems.at[3, 2]),
    ]
    packer = Packer(count)

    def down(level, carry):
        state, excess, prod = carry
        for t in range(count):
            part = slice(ROWS * t, ROWS * (t + 1))
            rate = 1.0 / s_ref[level, part, :]
            grown = rate + excess[t]
            inv = 1.0 / (1.0 + grown)
            excess[t] = grown * inv
            prod[t] = prod[t] * inv
            r_ref[level, part, :] = rate
            i_ref[level, part, :] = inv
            q_ref[level, part, :] = prod[t]
        return packer.add(level, tiles_of(p_ref, level, count), state), excess, prod

    def up(step, carry):
        state, value = carry
        level = levels - 1 - step
        for t in range(count):
            part = slice(ROWS * t, ROWS * (t + 1))
            value[t] = q_ref[level, part, :] + i_ref[level, part, :] * value[t]
            v_ref[level, part, :] = value[t]
        return packer.add(step, tiles_of(wy_ref, step, count), state), value

    ones = [jnp.ones((ROWS, 128), jnp.float32)] * count
    carry = packer.start, list(ones), list(ones)
    for c in range(CHUNKS):
        pres_in[c].wait()
        stiff_in[c].wait()
        carry = lax.fori_loop(c * share, (c + 1) * share, down, carry, unroll=UNROLL)
    pres = packer.done(carry[0])
    carry = packer.start, [jnp.zeros_like(one) for one in ones]
    for c in range(CHUNKS):
        wind_in[c].wait()
        carry = lax.fori_loop(c * share, (c + 1) * share, up, carry, unroll=UNROLL)
    wind = packer.done(carry[0])
    put_tiles(stat_ref, 0, carry[1])
    stat_ref[1] = q_ref[levels - 1]
    stat_ref[2] = i_ref[levels - 1]
    stat_ref[3] = r_ref[0]
    stat_ref[4] = r_ref[levels - 1]

    for copy in ends_in:
        copy.wait()
    jac = planes_of(jac_ref, count)
    ends = both_ends(jac)
    edge = row_edge()

    def step(level, state):
        rows_ref[level] = edge.payload(
            both_ends(tiles_of(p_ref, level, count)), both_ends(tiles_of(wx_ref, level, 2)), ends
        )
        return state

    lax.fori_loop(0, levels, step, 0, unroll=2 * UNROLL)
    rows_ref[levels] = ends
    down_out, up_out = lane_payload(pres, wind, jac)
    put_pair(inner_ref, outer_ref, 0, down_out, up_out)
    put_pair(
        inner_ref,
        outer_ref,
        1,
        [spread_slots(j, True) for j in jac],
        [spread_slots(j, False) for j in jac],
    )
    put_tiles(pp_ref, 0, pres[0])
    put_tiles(pp_ref, 1, pres[1])


def kernel_n(wy_ref, pw_ref):
    levels, rows, _ = wy_ref.shape
    count = rows // ROWS
    wind = pack_levels(wy_ref, count, levels)
    put_tiles(pw_ref, 0, wind[0])
    put_tiles(pw_ref, 1, wind[1])


def kernel_m(p_ref, wx_ref, wy_ref, jac_ref, nx_ref, ny_ref, ps_ref):
    levels, rows, _ = p_ref.shape
    count = rows // ROWS
    jac = planes_of(jac_ref, count)
    inv_jac = [CD / j for j in jac]
    closed = Closed()

    def step(level, state):
        pres = tiles_of(p_ref, level, count)
        wind_x = tiles_of(wx_ref, level, count)
        wind_y = tiles_of(wy_ref, level, count)
        new_x = [w - CG * d for w, d in zip(wind_x, closed.along_x(pres))]
        new_y = [w - CG * closed.along_y(p) for w, p in zip(wind_y, pres)]
        put_tiles(nx_ref, level, new_x)
        put_tiles(ny_ref, level, new_y)
        spread_x = closed.along_x([j * n for j, n in zip(jac, new_x)])
        spread_y = [closed.along_y(j * n) for j, n in zip(jac, new_y)]
        put_tiles(
            ps_ref,
            level,
            [p - i * (x + y) for p, i, x, y in zip(pres, inv_jac, spread_x, spread_y)],
        )
        return state

    lax.fori_loop(0, levels, step, 0, unroll=UNROLL)


def kernel_b(
    p_ref,
    nxc_ref,
    nyc_ref,
    psc_ref,
    wz_ref,
    jac_ref,
    sx_ref,
    sy_ref,
    r_ref,
    i_ref,
    v_ref,
    pp_ref,
    rows_ref,
    inner_ref,
    outer_ref,
    got_rows_ref,
    got_inner_ref,
    got_outer_ref,
    srows_ref,
    sinner_ref,
    souter_ref,
    got_srows_ref,
    got_sinner_ref,
    got_souter_ref,
    coef_ref,
    nx_ref,
    ny_ref,
    ps_ref,
    y_ref,
    next_ref,
    cross_ref,
    mate_ref,
    share_ref,
):
    levels, rows, _ = p_ref.shape
    count = rows // ROWS
    last = count - 1
    lane, row = lane_index(), row_index()
    low_edge, high_edge, edge = lane_edge(LOW), lane_edge(HIGH), row_edge()
    wind_fix, low_fix, high_fix = [], [], []
    for t in range(count):
        part = slice(ROWS * t, ROWS * (t + 1))
        jac_low, jac_high = get_pair(sinner_ref, souter_ref, 1, part)
        jac_below, jac_above = get_pair(got_sinner_ref, got_souter_ref, 1, part)
        down, up = get_pair(inner_ref, outer_ref, 0, part)
        below, above = get_pair(got_inner_ref, got_outer_ref, 0, part)
        low_wind, low_star = low_edge.correct(
            below - up, pp_ref[0, part, :], jac_low, low_edge.shifted(jac_below - jac_high, 2)
        )
        high_wind, high_star = high_edge.correct(
            above - down, pp_ref[1, part, :], jac_high, high_edge.shifted(jac_above - jac_low, -2)
        )
        wind_fix.append(low_wind + pltpu.roll(high_wind, 128 - SLOT, 1))
        low_fix.append(low_star)
        high_fix.append(pltpu.roll(high_star, 128 - SLOT, 1))
    ends = srows_ref[levels]
    change = got_srows_ref[levels] - ends
    ends_change = jnp.where(row < 4, edge.shifted(change, -2), edge.shifted(change, 2))
    outer = (lane < 2) | (lane >= 126)
    low_lanes, high_lanes = lane < SLOT, lane >= 128 - SLOT
    first_rows = row < 4

    def star(level, which):
        new_x = {t: nxc_ref[level, ROWS * t : ROWS * (t + 1), :] for t in which}
        stars = {t: psc_ref[level, ROWS * t : ROWS * (t + 1), :] for t in which}
        if 0 in which:
            wind, press = edge.correct(
                got_rows_ref[level] - rows_ref[level],
                jnp.where(first_rows, p_ref[level, :ROWS, :], p_ref[level, ROWS * last :, :]),
                ends,
                ends_change,
                base=4,
            )
            new_x[0] = new_x[0] - jnp.where(first_rows, wind, 0.0)
            new_x[last] = new_x[last] - jnp.where(first_rows, 0.0, wind)
            stars[0] = stars[0] - jnp.where(first_rows, press, 0.0)
            stars[last] = stars[last] - jnp.where(first_rows, 0.0, press)
        back = lax.rem(128 - SLOT * level, 128)
        forces = []
        for t in which:
            part = slice(ROWS * t, ROWS * (t + 1))
            new_y = nyc_ref[level, part, :] - jnp.where(
                outer, pltpu.roll(wind_fix[t], back, 1), 0.0
            )
            fix = jnp.where(
                low_lanes,
                pltpu.roll(low_fix[t], back, 1),
                jnp.where(high_lanes, pltpu.roll(high_fix[t], back, 1), 0.0),
            )
            stars[t] = stars[t] - fix
            forces.append(
                wz_ref[level, part, :] + sx_ref[part, :] * new_x[t] + sy_ref[part, :] * new_y
            )
            nx_ref[level, part, :] = new_x[t]
            ny_ref[level, part, :] = new_y
            ps_ref[level, part, :] = stars[t]
        return [stars[t] for t in which], forces

    def sweep(level, which, below, above, force, value, first):
        values, firsts = [], []
        for k, t in enumerate(which):
            part = slice(ROWS * t, ROWS * (t + 1))
            rhs = r_ref[level, part, :] * (force[k] - vert_coef * (above[k] - below[k]))
            firsts.append(first[k] + v_ref[level, part, :] * rhs)
            values.append((rhs + value[k]) * i_ref[level, part, :])
            y_ref[level, part, :] = values[k]
        return values, firsts

    for which in (tuple(range(count)),):
        zeros = [jnp.zeros((ROWS, 128), jnp.float32)] * len(which)
        bottom, force = star(0, which)

        def step(level, carry, which=which):
            below, here, force, value, first = carry
            above, force_next = star(level, which)
            value, first = sweep(level - 1, which, below, above, force, value, first)
            return here, above, force_next, value, first

        below, here, force, value, first = lax.fori_loop(
            1, levels, step, (zeros, bottom, force, zeros, zeros), unroll=2 * UNROLL
        )
        value, first = sweep(levels - 1, which, below, zeros, force, value, first)
        interface(
            which, first, value, bottom, here, coef_ref, next_ref, cross_ref, mate_ref, share_ref
        )


PAIR_COEFS = ("own", "other", "den", "den_end", "den_link", "outer", "total", "facing", "centre", "first", "last")


def place_in_column():
    mine = lax.axis_index("lev")
    return (mine == 0) | (mine == 3), mine < 2, lax.rem(mine, 2) == 0


def kernel_s(stat_ref, mate_ref, coef_ref):
    outermost, lower, even = place_in_column()
    for t in range(coef_ref.shape[1] // ROWS):
        part = slice(ROWS * t, ROWS * (t + 1))
        mine = [stat_ref[k, part, :] for k in range(STATS)]
        mate = [mate_ref[k, part, :] for k in range(STATS)]
        outer = [jnp.where(outermost, a, b) for a, b in zip(mine, mate)]
        inner = [jnp.where(outermost, b, a) for a, b in zip(mine, mate)]
        outer_end = jnp.where(lower, outer[2], outer[0])
        end = jnp.where(lower, inner[0], inner[2])
        centre = jnp.where(lower, inner[2], inner[0])
        link = inner[1]
        den = 1.0 / (1.0 - end * outer_end)
        den_link = den * link
        weight = outer_end * den_link
        one, zero = jnp.ones_like(den), jnp.zeros_like(den)
        coefs = dict(
            own=jnp.where(outermost, den_link, one),
            other=jnp.where(outermost, zero, weight),
            den=den,
            den_end=den * end,
            den_link=den_link,
            outer=outer_end,
            total=centre + weight * link,
            facing=vert_coef * jnp.where(even, mate[3], mate[4]),
            centre=vert_coef * jnp.where(lower, inner[4], inner[3]),
            first=vert_coef * mine[3],
            last=vert_coef * mine[4],
        )
        for k, name in enumerate(PAIR_COEFS):
            coef_ref[k, part, :] = coefs[name]


def interface(
    which, first, value, star_first, star_last, coef_ref, next_ref, cross_ref, mate_ref, share_ref
):
    outermost, lower, even = place_in_column()
    for t, tile in enumerate(which):
        part = slice(ROWS * tile, ROWS * (tile + 1))
        coef = {name: coef_ref[k, part, :] for k, name in enumerate(PAIR_COEFS)}
        sign = jnp.where(lower, 1.0, -1.0)
        star_centre = jnp.where(lower, star_last[t], star_first[t])
        star_outer = jnp.where(lower, star_first[t], star_last[t])
        facing = jnp.where(outermost, coef["facing"], 0.0)
        centre = jnp.where(lower, value[t], first[t]) + sign * facing * star_centre
        outer = jnp.where(lower, first[t], value[t]) - sign * coef["facing"] * star_outer
        total = coef["own"] * centre + coef["other"] * outer
        for ref in (next_ref, cross_ref, share_ref):
            ref[0, part, :] = total
            ref[1, part, :] = star_centre
        if next_ref.shape[0] > 3:
            next_ref[2, part, :] = coef["total"]
            next_ref[3, part, :] = coef["centre"]
        mate_ref[0, part, :] = jnp.where(outermost, centre, outer)
        mate_ref[1, part, :] = jnp.where(even, star_last[t], star_first[t])


def boundary(
    count,
    got_next_ref,
    got_cross_ref,
    got_mate_ref,
    got_share_ref,
    mate_ref,
    share_ref,
    coef_ref,
    far_ref,
):
    outermost, lower, _ = place_in_column()
    sign = jnp.where(lower, 1.0, -1.0)
    parts = []
    for t in range(count):
        part = slice(ROWS * t, ROWS * (t + 1))
        coef = {name: coef_ref[k, part, :] for k, name in enumerate(PAIR_COEFS)}
        far_total, far_facing = far_ref[2, part, :], far_ref[3, part, :]
        own, got = mate_ref[0, part, :], got_mate_ref[0, part, :]
        this_star = jnp.where(outermost, got_share_ref[1, part, :], share_ref[1, part, :])
        next_star = jnp.where(outermost, got_cross_ref[1, part, :], got_next_ref[1, part, :])
        this = share_ref[0, part, :] + got_share_ref[0, part, :] + sign * far_facing * this_star
        that = (
            got_cross_ref[0, part, :]
            + got_next_ref[0, part, :]
            - sign * coef["centre"] * next_star
        )
        middle = (that + far_total * this) / (1.0 - coef["total"] * far_total)
        from_outer = jnp.where(outermost, own, got)
        from_inner = jnp.where(outermost, got, own)
        between = (
            coef["den"] * from_inner + coef["den_end"] * from_outer + coef["den_link"] * middle
        )
        zero = jnp.zeros_like(own)
        centre = jnp.where(outermost, between, middle)
        outer = jnp.where(outermost, zero, from_outer + coef["outer"] * between)
        mate_star = got_mate_ref[1, part, :]
        star_centre = jnp.where(outermost, mate_star, next_star)
        star_outer = jnp.where(outermost, zero, mate_star)
        below, above = jnp.where(lower, outer, centre), jnp.where(lower, centre, outer)
        star_below = jnp.where(lower, star_outer, star_centre)
        star_above = jnp.where(lower, star_centre, star_outer)
        under = below - coef["first"] * star_below
        over = above + coef["last"] * star_above
        parts.append((below, above, under, over))
    return [[part[k] for part in parts] for k in range(4)]


def finish(count, levels, y_ref, q_ref, i_ref, ps_ref, x_ref, p_ref, column_refs, ready=None):
    lower, upper, under, over = boundary(count, *column_refs)

    def solved(level, above):
        value = tiles_of(y_ref, level, count)
        prod = tiles_of(q_ref, level, count)
        inv = tiles_of(i_ref, level, count)
        out = [(y + q * u) + i * a for y, q, u, i, a in zip(value, prod, lower, inv, above)]
        put_tiles(x_ref, level, out)
        return out

    def pressed(level, above, below):
        star = tiles_of(ps_ref, level, count)
        put_tiles(p_ref, level, [s - vert_coef * (a - b) for s, a, b in zip(star, above, below)])

    def step(index, carry):
        above, here = carry
        level = levels - 2 - index
        below = solved(level, here)
        pressed(level + 1, above, below)
        return here, below

    carry = over, solved(levels - 1, upper)
    if ready is None:
        carry = lax.fori_loop(0, levels - 1, step, carry, unroll=UNROLL)
    else:
        done, share = 0, levels // CHUNKS
        for c in range(CHUNKS - 1, -1, -1):
            goal = levels - 1 - c * share
            carry = lax.fori_loop(done, goal, step, carry, unroll=UNROLL)
            done = goal
            ready(c)
    above, here = carry
    pressed(0, above, under)


def kernel_c(*refs):
    column_refs = refs[:COLUMN]
    y_ref, q_ref, i_ref, ps_ref, wx_ref, pw_ref, jac_ref = refs[COLUMN : COLUMN + 7]
    x_ref, p_ref, rows_ref, inner_ref, outer_ref, pp_ref = refs[COLUMN + 7 :]
    levels, rows, _ = y_ref.shape
    count = rows // ROWS
    edge = row_edge()
    ends = both_ends(planes_of(jac_ref, count))
    finish(count, levels, y_ref, q_ref, i_ref, ps_ref, x_ref, p_ref, column_refs)

    def step(level, state):
        rows_ref[level] = edge.payload(
            both_ends(tiles_of(p_ref, level, count)),
            both_ends(tiles_of(wx_ref, level, count)),
            ends,
        )
        return state

    lax.fori_loop(0, levels, step, 0, unroll=2 * UNROLL)
    pres = pack_levels(p_ref, count, levels)
    wind = tiles_of(pw_ref, 0, count), tiles_of(pw_ref, 1, count)
    down, up = lane_payload(pres, wind, planes_of(jac_ref, count))
    put_pair(inner_ref, outer_ref, 0, down, up)
    put_tiles(pp_ref, 0, pres[0])
    put_tiles(pp_ref, 1, pres[1])


def kernel_d(*refs):
    column_refs = refs[:COLUMN]
    y_ref, q_ref, i_ref, ps_ref = refs[COLUMN : COLUMN + 4]
    x_hbm, p_hbm, x_ref, p_ref, sems = refs[COLUMN + 4 :]
    levels, rows, _ = y_ref.shape
    share = levels // CHUNKS
    copies = []

    def send(index, source, target, c):
        part = pl.ds(c * share, share)
        copy = pltpu.make_async_copy(source.at[part], target.at[part], sems.at[index, c])
        copy.start()
        copies.append(copy)

    def ready(c):
        send(0, x_ref, x_hbm, c)
        if c < CHUNKS - 1:
            send(1, p_ref, p_hbm, c + 1)

    finish(
        rows // ROWS,
        levels,
        y_ref,
        q_ref,
        i_ref,
        ps_ref,
        x_ref,
        p_ref,
        column_refs,
        ready,
    )
    send(1, p_ref, p_hbm, 0)
    for copy in copies:
        copy.wait()


def call(kernel, name, shapes, *args, far_in=(), far_out=False, scratch=(), keep=()):
    near, far = pl.BlockSpec(memory_space=pltpu.VMEM), pl.BlockSpec(memory_space=pl.ANY)
    size = sum(a.size for a in args) + sum(functools.reduce(lambda a, b: a * b, s) for s in shapes)
    if len(far_in) == len(args):
        args = [pltpu.with_memory_space_constraint(a, pltpu.HBM) for a in args]
    return pl.pallas_call(
        kernel,
        out_shape=[
            pltpu.VMEM(s, jnp.float32) if k in keep else jax.ShapeDtypeStruct(s, jnp.float32)
            for k, s in enumerate(shapes)
        ],
        in_specs=[far if k in far_in else near for k in range(len(args))],
        out_specs=[far if far_out else near] * len(shapes),
        scratch_shapes=list(scratch),
        compiler_params=pltpu.CompilerParams(vmem_limit_bytes=32 * 1024 * 1024),
        cost_estimate=pl.CostEstimate(
            flops=8 * size, bytes_accessed=4 * size, transcendentals=0
        ),
        name=name,
    )(*args)


def swap(value, axis, partner):
    count = lax.axis_size(axis)
    return lax.ppermute(value, axis, [(i, partner(i)) for i in range(count)])


def exchange_rows(rows):
    count = lax.axis_size("gx")
    if count == 2:
        return swap(rows, "gx", lambda i: 1 - i)
    down = swap(rows[:, : ROWS // 2], "gx", lambda i: (i - 1) % count)
    up = swap(rows[:, ROWS // 2 :], "gx", lambda i: (i + 1) % count)
    return jnp.concatenate([down, up], axis=1)


def exchange_lanes(inner, outer):
    count = lax.axis_size("gy")
    got_inner = swap(inner, "gy", lambda i: i ^ 1)
    got_outer = swap(outer, "gy", lambda i: (i + 1 if i % 2 else i - 1) % count)
    return got_inner, got_outer


def exchange_column(following, cross, mate, share):
    got_cross = swap(cross, "lev", lambda i: i ^ 2)
    got_next = swap(following, "lev", lambda i: i ^ 3)
    got_mate = swap(mate, "lev", lambda i: i ^ 1)
    got_share = swap(share, "lev", lambda i: i ^ 1)
    return got_next, got_cross, got_mate, got_share, mate, share


def local(wind_x, wind_y, wind_z, pressure, jacobian, slope_x, slope_y, stiffness):
    field = wind_x.shape
    levels, rows, lanes = field
    plane = (rows, lanes)
    pair = (2,) + plane
    assert lanes == 128 and levels * SLOT == 128 and rows % ROWS == 0
    assert lax.axis_size("lev") == 4 and lax.axis_size("gy") % 2 == 0

    edge, inner, outer, ends, rate, inv, prod, gain, stat = call(
        kernel_a,
        "start",
        [(levels + 1, ROWS, lanes), pair, (3,) + plane, pair] + [field] * 4 + [(STATS,) + plane],
        pressure,
        wind_x,
        wind_y,
        jacobian,
        stiffness,
        far_in=(0, 1, 2, 3, 4),
        scratch=[
            pltpu.VMEM(field, jnp.float32),
            pltpu.VMEM((levels, 2 * ROWS, lanes), jnp.float32),
            pltpu.VMEM(field, jnp.float32),
            pltpu.VMEM(plane, jnp.float32),
            pltpu.VMEM(field, jnp.float32),
            pltpu.SemaphoreType.DMA((4, CHUNKS)),
        ],
    )
    mate = swap(stat, "lev", lambda i: i ^ 1)
    (coef,) = call(kernel_s, "pairs", [(len(PAIR_COEFS),) + plane], stat, mate)
    sent = (edge, inner, outer)
    got = (exchange_rows(edge),) + exchange_lanes(inner, outer)
    static_edges = sent + got
    for substep in range(SUBSTEPS):
        closed = call(
            kernel_m, "interior", [field, field, field], pressure, wind_x, wind_y, jacobian
        )
        wind_x, wind_y, star, value, *faces = call(
            kernel_b,
            "sweep",
            [field, field, field, field, (3 if substep else 4,) + plane, pair, pair, pair],
            pressure,
            *closed,
            wind_z,
            jacobian,
            slope_x,
            slope_y,
            rate,
            inv,
            gain,
            ends,
            *sent,
            *got,
            *static_edges,
            coef,
            keep=tuple(range(8)),
        )
        column = exchange_column(*faces)
        if not substep:
            far = column[0]
        column += (coef, far)
        if substep < SUBSTEPS - 1:
            (packed,) = call(kernel_n, "pack", [pair], wind_y)
            wind_z, pressure, edge, inner, outer, ends = call(
                kernel_c,
                "finish",
                [field, field, (levels, ROWS, lanes), (1,) + plane, pair, pair],
                *column,
                value,
                prod,
                inv,
                star,
                wind_x,
                packed,
                jacobian,
            )
            sent = (edge, inner, outer)
            got = (exchange_rows(edge),) + exchange_lanes(inner, outer)
        else:
            wind_z, pressure = call(
                kernel_d,
                "last",
                [field, field],
                *column,
                value,
                prod,
                inv,
                star,
                far_out=True,
                scratch=[
                    pltpu.VMEM(field, jnp.float32),
                    pltpu.VMEM(field, jnp.float32),
                    pltpu.SemaphoreType.DMA((2, CHUNKS)),
                ],
            )
    return wind_x, wind_y, wind_z, pressure


def solution(mesh):
    field = P("lev", "gx", "gy")
    column = P("gx", "gy")
    return jax.shard_map(
        local,
        mesh=mesh,
        in_specs=(field,) * 4 + (column,) * 3 + (field,),
        out_specs=(field,) * 4,
        check_vma=False,
    )
```

```python
import functools

import jax
import jax.numpy as jnp
from jax import lax
from jax.experimental import pallas as pl
from jax.experimental.pallas import tpu as pltpu
from jax.sharding import PartitionSpec as P

SUBSTEPS = 2

grad_coef = 0.35
div_coef = 0.35
vert_coef = 0.25

CG = grad_coef / 12.0
CD = div_coef / 12.0
ROWS = 8
SLOT = 4
UNROLL = 8
CHUNKS = 4
COLUMN = 8
STATS = 5


def lane_index():
    return lax.broadcasted_iota(jnp.int32, (ROWS, 128), 1)


def row_index():
    return lax.broadcasted_iota(jnp.int32, (ROWS, 128), 0)


def only(mask, value):
    return jnp.where(mask, jnp.float32(value), jnp.float32(0.0))


def tiles_of(ref, level, count):
    return [ref[level, ROWS * t : ROWS * (t + 1), :] for t in range(count)]


def planes_of(ref, count):
    return [ref[ROWS * t : ROWS * (t + 1), :] for t in range(count)]


def put_tiles(ref, level, tiles):
    for t, tile in enumerate(tiles):
        ref[level, ROWS * t : ROWS * (t + 1), :] = tile


def put_planes(ref, tiles):
    for t, tile in enumerate(tiles):
        ref[ROWS * t : ROWS * (t + 1), :] = tile


class Edge:
    def __init__(self, place, axis, held):
        self.place, self.axis, self.held = place, axis, held
        self.size = place.shape[axis]

    def at(self, places):
        total = None
        for position, value in places.items():
            if position in self.held:
                term = only(self.place == position, value)
                total = term if total is None else total + term
        return total

    def shifted(self, field, by):
        return field if by % self.size == 0 else pltpu.roll(field, (-by) % self.size, self.axis)

    def mix(self, field, table):
        total = None
        for by, places in table.items():
            weight = self.at(places)
            if weight is not None:
                term = weight * self.shifted(field, by)
                total = term if total is None else total + term
        return total

    def payload(self, pres, wind, jac):
        partial = self.mix(
            pres,
            {
                1: {0: 8.0, 1: 8.0, 6: 8.0},
                2: {0: -1.0, 1: -1.0},
                -1: {1: -8.0, 6: -8.0, 7: -8.0},
                -2: {6: 1.0, 7: 1.0},
            },
        )
        flux = jac * (wind - CG * partial)
        outer = self.mix(pres, {0: {0: 1.0, 1: 1.0, 6: 1.0, 7: 1.0}})
        return outer + self.mix(flux, {-2: {2: 1.0, 3: 1.0}, 2: {4: 1.0, 5: 1.0}})

    def correct(self, delta, pres, jac, delta_jac, base=0):
        grad = self.mix(
            delta,
            {
                base + 2: {0: 1.0, 1: 1.0},
                base + 3: {0: -8.0},
                base - 2: {6: -1.0, 7: -1.0},
                base - 3: {7: 8.0},
            },
        )
        wind = CG * grad
        own = -(jac * wind)
        far = self.mix(delta, {base: {0: 1.0, 1: 1.0, 6: 1.0, 7: 1.0}}) + CG * delta_jac * self.mix(
            pres, {0: {0: 1.0, 1: 1.0, 6: -1.0, 7: -1.0}, -1: {1: -8.0}, 1: {6: 8.0}}
        )
        spread = (
            self.mix(far, {0: {0: 1.0, 1: 1.0, 6: -1.0, 7: -1.0}})
            + self.mix(far - own, {1: {0: -8.0}, -1: {7: 8.0}})
            + self.mix(
                own,
                {
                    -1: {1: -8.0, 2: -8.0},
                    -2: {2: 1.0, 3: 1.0},
                    1: {5: 8.0, 6: 8.0},
                    2: {4: -1.0, 5: -1.0},
                },
            )
        )
        return wind, CD * spread / jac


LOW, HIGH = (0, 1, 2, 3), (4, 5, 6, 7)


def row_edge():
    return Edge(row_index(), 0, LOW + HIGH)


def lane_edge(held):
    return Edge((lane_index() & 3) + held[0], 1, held)


def both_ends(tiles):
    return jnp.where(row_index() < 4, tiles[0], tiles[-1])


def spread_slots(tile, low):
    lane = lane_index()
    if low:
        out = jnp.where(lane < SLOT, tile, 0.0)
    else:
        out = pltpu.roll(jnp.where(lane >= 128 - SLOT, tile, 0.0), SLOT, 1)
    by = SLOT
    while by < 128:
        out = out + pltpu.roll(out, by, 1)
        by *= 2
    return out


class Packer:
    def __init__(self, count):
        self.slot = lax.shift_right_logical(lane_index(), 2)
        self.start = [jnp.zeros((ROWS, 128), jnp.float32)] * (2 * count)
        self.count = count

    def add(self, level, tiles, state):
        before = lax.rem(level + 31, 32)
        rolled = [pltpu.roll(tile, SLOT * level, 1) for tile in tiles]
        low = [jnp.where(self.slot == level, r, s) for r, s in zip(rolled, state)]
        high = [jnp.where(self.slot == before, r, s) for r, s in zip(rolled, state[self.count :])]
        return low + high

    def done(self, state):
        return state[: self.count], [pltpu.roll(s, SLOT, 1) for s in state[self.count :]]


class Closed:
    def __init__(self):
        self.row = row_index()

    def along_y(self, tile):
        pair = tile - pltpu.roll(tile, 126, 1)
        return (pltpu.roll(pair, 2, 1) + pair) - 8.0 * pltpu.roll(pair, 1, 1)

    def moved(self, tiles, by):
        count = len(tiles)
        rolled = [pltpu.roll(tile, by % ROWS, 0) for tile in tiles]
        if by > 0:
            return [jnp.where(self.row < by, rolled[t - 1], rolled[t]) for t in range(count)]
        return [
            jnp.where(self.row >= ROWS + by, rolled[(t + 1) % count], rolled[t])
            for t in range(count)
        ]

    def along_x(self, tiles):
        pair = [f - m for f, m in zip(tiles, self.moved(tiles, -2))]
        return [
            (two + here) - 8.0 * one
            for two, here, one in zip(self.moved(pair, 2), pair, self.moved(pair, 1))
        ]


def even_place():
    return lax.rem(lax.axis_index("gy"), 2) == 0


def put_pair(inner_ref, outer_ref, index, down, up):
    even = even_place()
    put_tiles(inner_ref, index, [jnp.where(even, u, d) for u, d in zip(up, down)])
    put_tiles(outer_ref, index, [jnp.where(even, d, u) for u, d in zip(up, down)])


def get_pair(inner_ref, outer_ref, index, part):
    even = even_place()
    inner, outer = inner_ref[index, part, :], outer_ref[index, part, :]
    return jnp.where(even, outer, inner), jnp.where(even, inner, outer)


def lane_payload(pres, wind, jac):
    low, high = lane_edge(LOW), lane_edge(HIGH)
    down = [
        low.payload(p, w, spread_slots(j, True)) for p, w, j in zip(pres[0], wind[0], jac)
    ]
    up = [
        high.payload(p, w, spread_slots(j, False)) for p, w, j in zip(pres[1], wind[1], jac)
    ]
    return down, up


def levels_of(chunk, share, body, carry):
    for k in range(share):
        carry = body(chunk * share + k, carry)
    return carry


def pack_levels(ref, count, levels):
    packer = Packer(count)

    def step(level, state):
        return packer.add(level, tiles_of(ref, level, count), state)

    return packer.done(lax.fori_loop(0, levels, step, packer.start, unroll=UNROLL))


def kernel_a(
    p_hbm,
    wx_hbm,
    wy_hbm,
    jac_hbm,
    s_hbm,
    rows_ref,
    inner_ref,
    outer_ref,
    pp_ref,
    r_ref,
    i_ref,
    q_ref,
    v_ref,
    stat_ref,
    p_ref,
    wx_ref,
    wy_ref,
    jac_ref,
    s_ref,
    sems,
):
    levels, rows, _ = p_hbm.shape
    count = rows // ROWS
    share = levels // CHUNKS

    def fetch(source, target, sem):
        copy = pltpu.make_async_copy(source, target, sem)
        copy.start()
        return copy

    def chunk(index, source, target, c):
        part = pl.ds(c * share, share)
        return pltpu.make_async_copy(source.at[part], target.at[part], sems.at[index, c])

    for c in range(CHUNKS):
        chunk(0, p_hbm, p_ref, c).start()
        chunk(1, s_hbm, s_ref, c).start()
    for c in range(CHUNKS):
        chunk(2, wy_hbm, wy_ref, c).start()
    tail = pl.ds(rows - ROWS, ROWS)
    ends_in = [
        fetch(jac_hbm, jac_ref, sems.at[3, 0]),
        fetch(wx_hbm.at[:, pl.ds(0, ROWS)], wx_ref.at[:, pl.ds(0, ROWS)], sems.at[3, 1]),
        fetch(wx_hbm.at[:, tail], wx_ref.at[:, pl.ds(ROWS, ROWS)], sems.at[3, 2]),
    ]
    packer = Packer(count)

    def down(level, carry):
        state, excess, prod = carry[0], list(carry[1]), list(carry[2])
        for t in range(count):
            part = slice(ROWS * t, ROWS * (t + 1))
            rate = 1.0 / s_ref[level, part, :]
            grown = rate + excess[t]
            inv = 1.0 / (1.0 + grown)
            excess[t] = grown * inv
            prod[t] = prod[t] * inv
            r_ref[level, part, :] = rate
            i_ref[level, part, :] = inv
            q_ref[level, part, :] = prod[t]
        return packer.add(level, tiles_of(p_ref, level, count), state), excess, prod

    def up(step, carry):
        state, value = carry[0], list(carry[1])
        level = levels - 1 - step
        for t in range(count):
            part = slice(ROWS * t, ROWS * (t + 1))
            value[t] = q_ref[level, part, :] + i_ref[level, part, :] * value[t]
            v_ref[level, part, :] = value[t]
        return packer.add(step, tiles_of(wy_ref, step, count), state), value

    ones = [jnp.ones((ROWS, 128), jnp.float32)] * count

    def down_chunk(c, carry):
        chunk(0, p_hbm, p_ref, c).wait()
        chunk(1, s_hbm, s_ref, c).wait()
        return levels_of(c, share, down, carry)

    def up_chunk(c, carry):
        chunk(2, wy_hbm, wy_ref, c).wait()
        return levels_of(c, share, up, carry)

    carry = lax.fori_loop(0, CHUNKS, down_chunk, (packer.start, ones, ones))
    pres = packer.done(carry[0])
    zeros = [jnp.zeros_like(one) for one in ones]
    carry = lax.fori_loop(0, CHUNKS, up_chunk, (packer.start, zeros))
    wind = packer.done(carry[0])
    put_tiles(stat_ref, 0, carry[1])
    stat_ref[1] = q_ref[levels - 1]
    stat_ref[2] = i_ref[levels - 1]
    stat_ref[3] = r_ref[0]
    stat_ref[4] = r_ref[levels - 1]

    for copy in ends_in:
        copy.wait()
    jac = planes_of(jac_ref, count)
    ends = both_ends(jac)
    edge = row_edge()

    def step(level, state):
        rows_ref[level] = edge.payload(
            both_ends(tiles_of(p_ref, level, count)), both_ends(tiles_of(wx_ref, level, 2)), ends
        )
        return state

    lax.fori_loop(0, levels, step, 0, unroll=UNROLL)
    rows_ref[levels] = ends
    down_out, up_out = lane_payload(pres, wind, jac)
    put_pair(inner_ref, outer_ref, 0, down_out, up_out)
    put_pair(
        inner_ref,
        outer_ref,
        1,
        [spread_slots(j, True) for j in jac],
        [spread_slots(j, False) for j in jac],
    )
    put_tiles(pp_ref, 0, pres[0])
    put_tiles(pp_ref, 1, pres[1])


def kernel_n(wy_ref, pw_ref):
    levels, rows, _ = wy_ref.shape
    count = rows // ROWS
    wind = pack_levels(wy_ref, count, levels)
    put_tiles(pw_ref, 0, wind[0])
    put_tiles(pw_ref, 1, wind[1])


def kernel_m(p_ref, wx_ref, wy_ref, jac_ref, nx_ref, ny_ref, ps_ref):
    levels, rows, _ = p_ref.shape
    count = rows // ROWS
    jac = planes_of(jac_ref, count)
    inv_jac = [CD / j for j in jac]
    closed = Closed()

    def step(level, state):
        pres = tiles_of(p_ref, level, count)
        wind_x = tiles_of(wx_ref, level, count)
        wind_y = tiles_of(wy_ref, level, count)
        new_x = [w - CG * d for w, d in zip(wind_x, closed.along_x(pres))]
        new_y = [w - CG * closed.along_y(p) for w, p in zip(wind_y, pres)]
        put_tiles(nx_ref, level, new_x)
        put_tiles(ny_ref, level, new_y)
        spread_x = closed.along_x([j * n for j, n in zip(jac, new_x)])
        spread_y = [closed.along_y(j * n) for j, n in zip(jac, new_y)]
        put_tiles(
            ps_ref,
            level,
            [p - i * (x + y) for p, i, x, y in zip(pres, inv_jac, spread_x, spread_y)],
        )
        return state

    lax.fori_loop(0, levels, step, 0, unroll=UNROLL)


def kernel_b(
    p_ref,
    nxc_ref,
    nyc_ref,
    psc_ref,
    wz_ref,
    jac_ref,
    sx_ref,
    sy_ref,
    r_ref,
    i_ref,
    v_ref,
    pp_ref,
    rows_ref,
    inner_ref,
    outer_ref,
    got_rows_ref,
    got_inner_ref,
    got_outer_ref,
    srows_ref,
    sinner_ref,
    souter_ref,
    got_srows_ref,
    got_sinner_ref,
    got_souter_ref,
    coef_ref,
    nx_ref,
    ny_ref,
    ps_ref,
    y_ref,
    next_ref,
    cross_ref,
    mate_ref,
    share_ref,
):
    levels, rows, _ = p_ref.shape
    count = rows // ROWS
    last = count - 1
    lane, row = lane_index(), row_index()
    low_edge, high_edge, edge = lane_edge(LOW), lane_edge(HIGH), row_edge()
    wind_fix, low_fix, high_fix = [], [], []
    for t in range(count):
        part = slice(ROWS * t, ROWS * (t + 1))
        jac_low, jac_high = get_pair(sinner_ref, souter_ref, 1, part)
        jac_below, jac_above = get_pair(got_sinner_ref, got_souter_ref, 1, part)
        down, up = get_pair(inner_ref, outer_ref, 0, part)
        below, above = get_pair(got_inner_ref, got_outer_ref, 0, part)
        low_wind, low_star = low_edge.correct(
            below - up, pp_ref[0, part, :], jac_low, low_edge.shifted(jac_below - jac_high, 2)
        )
        high_wind, high_star = high_edge.correct(
            above - down, pp_ref[1, part, :], jac_high, high_edge.shifted(jac_above - jac_low, -2)
        )
        wind_fix.append(low_wind + pltpu.roll(high_wind, 128 - SLOT, 1))
        low_fix.append(low_star)
        high_fix.append(pltpu.roll(high_star, 128 - SLOT, 1))
    ends = srows_ref[levels]
    change = got_srows_ref[levels] - ends
    ends_change = jnp.where(row < 4, edge.shifted(change, -2), edge.shifted(change, 2))
    outer = (lane < 2) | (lane >= 126)
    low_lanes, high_lanes = lane < SLOT, lane >= 128 - SLOT
    first_rows = row < 4

    def star(level, which):
        new_x = {t: nxc_ref[level, ROWS * t : ROWS * (t + 1), :] for t in which}
        stars = {t: psc_ref[level, ROWS * t : ROWS * (t + 1), :] for t in which}
        if 0 in which:
            wind, press = edge.correct(
                got_rows_ref[level] - rows_ref[level],
                jnp.where(first_rows, p_ref[level, :ROWS, :], p_ref[level, ROWS * last :, :]),
                ends,
                ends_change,
                base=4,
            )
            new_x[0] = new_x[0] - jnp.where(first_rows, wind, 0.0)
            new_x[last] = new_x[last] - jnp.where(first_rows, 0.0, wind)
            stars[0] = stars[0] - jnp.where(first_rows, press, 0.0)
            stars[last] = stars[last] - jnp.where(first_rows, 0.0, press)
        back = lax.rem(128 - SLOT * level, 128)
        forces = []
        for t in which:
            part = slice(ROWS * t, ROWS * (t + 1))
            new_y = nyc_ref[level, part, :] - jnp.where(
                outer, pltpu.roll(wind_fix[t], back, 1), 0.0
            )
            fix = jnp.where(
                low_lanes,
                pltpu.roll(low_fix[t], back, 1),
                jnp.where(high_lanes, pltpu.roll(high_fix[t], back, 1), 0.0),
            )
            stars[t] = stars[t] - fix
            forces.append(
                wz_ref[level, part, :] + sx_ref[part, :] * new_x[t] + sy_ref[part, :] * new_y
            )
            nx_ref[level, part, :] = new_x[t]
            ny_ref[level, part, :] = new_y
            ps_ref[level, part, :] = stars[t]
        return [stars[t] for t in which], forces

    def sweep(level, which, below, above, force, value, first):
        values, firsts = [], []
        for k, t in enumerate(which):
            part = slice(ROWS * t, ROWS * (t + 1))
            rhs = r_ref[level, part, :] * (force[k] - vert_coef * (above[k] - below[k]))
            firsts.append(first[k] + v_ref[level, part, :] * rhs)
            values.append((rhs + value[k]) * i_ref[level, part, :])
            y_ref[level, part, :] = values[k]
        return values, firsts

    which = tuple(range(count))
    put_tiles(y_ref, 0, [jnp.zeros((ROWS, 128), jnp.float32)] * count)
    zeros = tiles_of(y_ref, 0, count)

    def step(level, carry):
        below, here, force, value, first = carry
        above, force_next = star(level, which)
        before = jnp.maximum(level - 1, 0)
        new_value, new_first = sweep(before, which, below, above, force, value, first)
        started = jnp.where(level > 0, 1.0, 0.0)
        value = [started * n for n in new_value]
        first = [started * n for n in new_first]
        return here, above, force_next, value, first

    below, here, force, value, first = lax.fori_loop(
        0, levels, step, (zeros, zeros, zeros, zeros, zeros), unroll=UNROLL // 2
    )
    value, first = sweep(levels - 1, which, below, zeros, force, value, first)
    bottom = tiles_of(ps_ref, 0, count)
    interface(
        which, first, value, bottom, here, coef_ref, next_ref, cross_ref, mate_ref, share_ref
    )


PAIR_COEFS = ("own", "other", "den", "den_end", "den_link", "outer", "total", "facing", "centre", "first", "last")


def place_in_column():
    mine = lax.axis_index("lev")
    return (mine == 0) | (mine == 3), mine < 2, lax.rem(mine, 2) == 0


def kernel_s(stat_ref, mate_ref, coef_ref):
    outermost, lower, even = place_in_column()
    for t in range(coef_ref.shape[1] // ROWS):
        part = slice(ROWS * t, ROWS * (t + 1))
        mine = [stat_ref[k, part, :] for k in range(STATS)]
        mate = [mate_ref[k, part, :] for k in range(STATS)]
        outer = [jnp.where(outermost, a, b) for a, b in zip(mine, mate)]
        inner = [jnp.where(outermost, b, a) for a, b in zip(mine, mate)]
        outer_end = jnp.where(lower, outer[2], outer[0])
        end = jnp.where(lower, inner[0], inner[2])
        centre = jnp.where(lower, inner[2], inner[0])
        link = inner[1]
        den = 1.0 / (1.0 - end * outer_end)
        den_link = den * link
        weight = outer_end * den_link
        one, zero = jnp.ones_like(den), jnp.zeros_like(den)
        coefs = dict(
            own=jnp.where(outermost, den_link, one),
            other=jnp.where(outermost, zero, weight),
            den=den,
            den_end=den * end,
            den_link=den_link,
            outer=outer_end,
            total=centre + weight * link,
            facing=vert_coef * jnp.where(even, mate[3], mate[4]),
            centre=vert_coef * jnp.where(lower, inner[4], inner[3]),
            first=vert_coef * mine[3],
            last=vert_coef * mine[4],
        )
        for k, name in enumerate(PAIR_COEFS):
            coef_ref[k, part, :] = coefs[name]


def interface(
    which, first, value, star_first, star_last, coef_ref, next_ref, cross_ref, mate_ref, share_ref
):
    outermost, lower, even = place_in_column()
    for t, tile in enumerate(which):
        part = slice(ROWS * tile, ROWS * (tile + 1))
        coef = {name: coef_ref[k, part, :] for k, name in enumerate(PAIR_COEFS)}
        sign = jnp.where(lower, 1.0, -1.0)
        star_centre = jnp.where(lower, star_last[t], star_first[t])
        star_outer = jnp.where(lower, star_first[t], star_last[t])
        facing = jnp.where(outermost, coef["facing"], 0.0)
        centre = jnp.where(lower, value[t], first[t]) + sign * facing * star_centre
        outer = jnp.where(lower, first[t], value[t]) - sign * coef["facing"] * star_outer
        total = coef["own"] * centre + coef["other"] * outer
        for ref in (next_ref, cross_ref, share_ref):
            ref[0, part, :] = total
            ref[1, part, :] = star_centre
        if next_ref.shape[0] > 3:
            next_ref[2, part, :] = coef["total"]
            next_ref[3, part, :] = coef["centre"]
        mate_ref[0, part, :] = jnp.where(outermost, centre, outer)
        mate_ref[1, part, :] = jnp.where(even, star_last[t], star_first[t])


def boundary(
    count,
    got_next_ref,
    got_cross_ref,
    got_mate_ref,
    got_share_ref,
    mate_ref,
    share_ref,
    coef_ref,
    far_ref,
):
    outermost, lower, _ = place_in_column()
    sign = jnp.where(lower, 1.0, -1.0)
    parts = []
    for t in range(count):
        part = slice(ROWS * t, ROWS * (t + 1))
        coef = {name: coef_ref[k, part, :] for k, name in enumerate(PAIR_COEFS)}
        far_total, far_facing = far_ref[2, part, :], far_ref[3, part, :]
        own, got = mate_ref[0, part, :], got_mate_ref[0, part, :]
        this_star = jnp.where(outermost, got_share_ref[1, part, :], share_ref[1, part, :])
        next_star = jnp.where(outermost, got_cross_ref[1, part, :], got_next_ref[1, part, :])
        this = share_ref[0, part, :] + got_share_ref[0, part, :] + sign * far_facing * this_star
        that = (
            got_cross_ref[0, part, :]
            + got_next_ref[0, part, :]
            - sign * coef["centre"] * next_star
        )
        middle = (that + far_total * this) / (1.0 - coef["total"] * far_total)
        from_outer = jnp.where(outermost, own, got)
        from_inner = jnp.where(outermost, got, own)
        between = (
            coef["den"] * from_inner + coef["den_end"] * from_outer + coef["den_link"] * middle
        )
        zero = jnp.zeros_like(own)
        centre = jnp.where(outermost, between, middle)
        outer = jnp.where(outermost, zero, from_outer + coef["outer"] * between)
        mate_star = got_mate_ref[1, part, :]
        star_centre = jnp.where(outermost, mate_star, next_star)
        star_outer = jnp.where(outermost, zero, mate_star)
        below, above = jnp.where(lower, outer, centre), jnp.where(lower, centre, outer)
        star_below = jnp.where(lower, star_outer, star_centre)
        star_above = jnp.where(lower, star_centre, star_outer)
        under = below - coef["first"] * star_below
        over = above + coef["last"] * star_above
        parts.append((below, above, under, over))
    return [[part[k] for part in parts] for k in range(4)]


def finish(count, levels, y_ref, q_ref, i_ref, ps_ref, x_ref, p_ref, column_refs, ready=None):
    lower, upper, under, over = boundary(count, *column_refs)

    def solved(level, above):
        value = tiles_of(y_ref, level, count)
        prod = tiles_of(q_ref, level, count)
        inv = tiles_of(i_ref, level, count)
        out = [(y + q * u) + i * a for y, q, u, i, a in zip(value, prod, lower, inv, above)]
        put_tiles(x_ref, level, out)
        return out

    def pressed(level, above, below):
        star = tiles_of(ps_ref, level, count)
        put_tiles(p_ref, level, [s - vert_coef * (a - b) for s, a, b in zip(star, above, below)])

    def step(index, carry):
        above, here = carry
        level = levels - 1 - index
        below = solved(level, here)
        pressed(jnp.minimum(level + 1, levels - 1), above, below)
        return [jnp.where(index == 0, o, h) for o, h in zip(over, here)], below

    share = levels // CHUNKS

    def chunk(c, carry):
        carry = levels_of(c, share, step, carry)
        if ready is not None:
            ready(c)
        return carry

    above, here = lax.fori_loop(0, CHUNKS, chunk, (over, upper))
    pressed(0, above, under)


def kernel_c(*refs):
    column_refs = refs[:COLUMN]
    y_ref, q_ref, i_ref, ps_ref, wx_ref, pw_ref, jac_ref = refs[COLUMN : COLUMN + 7]
    x_ref, p_ref, rows_ref, inner_ref, outer_ref, pp_ref = refs[COLUMN + 7 :]
    levels, rows, _ = y_ref.shape
    count = rows // ROWS
    edge = row_edge()
    ends = both_ends(planes_of(jac_ref, count))
    finish(count, levels, y_ref, q_ref, i_ref, ps_ref, x_ref, p_ref, column_refs)

    def step(level, state):
        rows_ref[level] = edge.payload(
            both_ends(tiles_of(p_ref, level, count)),
            both_ends(tiles_of(wx_ref, level, count)),
            ends,
        )
        return state

    lax.fori_loop(0, levels, step, 0, unroll=UNROLL)
    pres = pack_levels(p_ref, count, levels)
    wind = tiles_of(pw_ref, 0, count), tiles_of(pw_ref, 1, count)
    down, up = lane_payload(pres, wind, planes_of(jac_ref, count))
    put_pair(inner_ref, outer_ref, 0, down, up)
    put_tiles(pp_ref, 0, pres[0])
    put_tiles(pp_ref, 1, pres[1])


def kernel_d(*refs):
    column_refs = refs[:COLUMN]
    y_ref, q_ref, i_ref, ps_ref = refs[COLUMN : COLUMN + 4]
    x_hbm, p_hbm, x_ref, p_ref, sems = refs[COLUMN + 4 :]
    levels, rows, _ = y_ref.shape
    share = levels // CHUNKS

    def copy(index, source, target, c):
        part = pl.ds(c * share, share)
        return pltpu.make_async_copy(source.at[part], target.at[part], sems.at[index, c])

    def ready(step):
        c = CHUNKS - 1 - step
        copy(0, x_ref, x_hbm, c).start()

        @pl.when(step > 0)
        def _():
            copy(1, p_ref, p_hbm, c + 1).start()

    finish(
        rows // ROWS,
        levels,
        y_ref,
        q_ref,
        i_ref,
        ps_ref,
        x_ref,
        p_ref,
        column_refs,
        ready,
    )
    copy(1, p_ref, p_hbm, 0).start()
    for c in range(CHUNKS):
        copy(0, x_ref, x_hbm, c).wait()
        copy(1, p_ref, p_hbm, c).wait()


def call(kernel, name, shapes, *args, far_in=(), far_out=False, scratch=(), keep=()):
    near, far = pl.BlockSpec(memory_space=pltpu.VMEM), pl.BlockSpec(memory_space=pl.ANY)
    size = sum(a.size for a in args) + sum(functools.reduce(lambda a, b: a * b, s) for s in shapes)
    if len(far_in) == len(args):
        args = [pltpu.with_memory_space_constraint(a, pltpu.HBM) for a in args]
    return pl.pallas_call(
        kernel,
        out_shape=[
            pltpu.VMEM(s, jnp.float32) if k in keep else jax.ShapeDtypeStruct(s, jnp.float32)
            for k, s in enumerate(shapes)
        ],
        in_specs=[far if k in far_in else near for k in range(len(args))],
        out_specs=[far if far_out else near] * len(shapes),
        scratch_shapes=list(scratch),
        compiler_params=pltpu.CompilerParams(vmem_limit_bytes=32 * 1024 * 1024),
        cost_estimate=pl.CostEstimate(
            flops=8 * size, bytes_accessed=4 * size, transcendentals=0
        ),
        name=name,
    )(*args)


def swap(value, axis, partner):
    count = lax.axis_size(axis)
    return lax.ppermute(value, axis, [(i, partner(i)) for i in range(count)])


def exchange_rows(rows):
    count = lax.axis_size("gx")
    if count == 2:
        return swap(rows, "gx", lambda i: 1 - i)
    down = swap(rows[:, : ROWS // 2], "gx", lambda i: (i - 1) % count)
    up = swap(rows[:, ROWS // 2 :], "gx", lambda i: (i + 1) % count)
    return jnp.concatenate([down, up], axis=1)


def exchange_lanes(inner, outer):
    count = lax.axis_size("gy")
    got_inner = swap(inner, "gy", lambda i: i ^ 1)
    got_outer = swap(outer, "gy", lambda i: (i + 1 if i % 2 else i - 1) % count)
    return got_inner, got_outer


def exchange_column(following, cross, mate, share):
    got_cross = swap(cross, "lev", lambda i: i ^ 2)
    got_next = swap(following, "lev", lambda i: i ^ 3)
    got_mate = swap(mate, "lev", lambda i: i ^ 1)
    got_share = swap(share, "lev", lambda i: i ^ 1)
    return got_next, got_cross, got_mate, got_share, mate, share


def local(wind_x, wind_y, wind_z, pressure, jacobian, slope_x, slope_y, stiffness):
    field = wind_x.shape
    levels, rows, lanes = field
    plane = (rows, lanes)
    pair = (2,) + plane
    assert lanes == 128 and levels * SLOT == 128 and rows % ROWS == 0
    assert lax.axis_size("lev") == 4 and lax.axis_size("gy") % 2 == 0

    edge, inner, outer, ends, rate, inv, prod, gain, stat = call(
        kernel_a,
        "start",
        [(levels + 1, ROWS, lanes), pair, (3,) + plane, pair] + [field] * 4 + [(STATS,) + plane],
        pressure,
        wind_x,
        wind_y,
        jacobian,
        stiffness,
        far_in=(0, 1, 2, 3, 4),
        scratch=[
            pltpu.VMEM(field, jnp.float32),
            pltpu.VMEM((levels, 2 * ROWS, lanes), jnp.float32),
            pltpu.VMEM(field, jnp.float32),
            pltpu.VMEM(plane, jnp.float32),
            pltpu.VMEM(field, jnp.float32),
            pltpu.SemaphoreType.DMA((4, CHUNKS)),
        ],
    )
    mate = swap(stat, "lev", lambda i: i ^ 1)
    (coef,) = call(kernel_s, "pairs", [(len(PAIR_COEFS),) + plane], stat, mate)
    sent = (edge, inner, outer)
    got = (exchange_rows(edge),) + exchange_lanes(inner, outer)
    static_edges = sent + got
    for substep in range(SUBSTEPS):
        closed = call(
            kernel_m, "interior", [field, field, field], pressure, wind_x, wind_y, jacobian
        )
        wind_x, wind_y, star, value, *faces = call(
            kernel_b,
            "sweep",
            [field, field, field, field, (3 if substep else 4,) + plane, pair, pair, pair],
            pressure,
            *closed,
            wind_z,
            jacobian,
            slope_x,
            slope_y,
            rate,
            inv,
            gain,
            ends,
            *sent,
            *got,
            *static_edges,
            coef,
            keep=tuple(range(8)),
        )
        column = exchange_column(*faces)
        if not substep:
            far = column[0]
        column += (coef, far)
        if substep < SUBSTEPS - 1:
            (packed,) = call(kernel_n, "pack", [pair], wind_y)
            wind_z, pressure, edge, inner, outer, ends = call(
                kernel_c,
                "finish",
                [field, field, (levels, ROWS, lanes), (1,) + plane, pair, pair],
                *column,
                value,
                prod,
                inv,
                star,
                wind_x,
                packed,
                jacobian,
            )
            sent = (edge, inner, outer)
            got = (exchange_rows(edge),) + exchange_lanes(inner, outer)
        else:
            wind_z, pressure = call(
                kernel_d,
                "last",
                [field, field],
                *column,
                value,
                prod,
                inv,
                star,
                far_out=True,
                scratch=[
                    pltpu.VMEM(field, jnp.float32),
                    pltpu.VMEM(field, jnp.float32),
                    pltpu.SemaphoreType.DMA((2, CHUNKS)),
                ],
            )
    return wind_x, wind_y, wind_z, pressure


def solution(mesh):
    field = P("lev", "gx", "gy")
    column = P("gx", "gy")
    return jax.shard_map(
        local,
        mesh=mesh,
        in_specs=(field,) * 4 + (column,) * 3 + (field,),
        out_specs=(field,) * 4,
        check_vma=False,
    )
```

```python
import functools

import jax
import jax.numpy as jnp
from jax import lax
from jax.experimental import pallas as pl
from jax.experimental.pallas import tpu as pltpu
from jax.sharding import PartitionSpec as P

SUBSTEPS = 2

grad_coef = 0.35
div_coef = 0.35
vert_coef = 0.25

CG = grad_coef / 12.0
CD = div_coef / 12.0
ROWS = 8
SLOT = 4
UNROLL = 8
CHUNKS = 4
COLUMN = 9
STATS = 5


def lane_index():
    return lax.broadcasted_iota(jnp.int32, (ROWS, 128), 1)


def row_index():
    return lax.broadcasted_iota(jnp.int32, (ROWS, 128), 0)


def only(mask, value):
    return jnp.where(mask, jnp.float32(value), jnp.float32(0.0))


def tiles_of(ref, level, count):
    return [ref[level, ROWS * t : ROWS * (t + 1), :] for t in range(count)]


def planes_of(ref, count):
    return [ref[ROWS * t : ROWS * (t + 1), :] for t in range(count)]


def put_tiles(ref, level, tiles):
    for t, tile in enumerate(tiles):
        ref[level, ROWS * t : ROWS * (t + 1), :] = tile


def put_planes(ref, tiles):
    for t, tile in enumerate(tiles):
        ref[ROWS * t : ROWS * (t + 1), :] = tile


class Edge:
    def __init__(self, place, axis, held):
        self.place, self.axis, self.held = place, axis, held
        self.size = place.shape[axis]

    def at(self, places):
        total = None
        for position, value in places.items():
            if position in self.held:
                term = only(self.place == position, value)
                total = term if total is None else total + term
        return total

    def shifted(self, field, by):
        return field if by % self.size == 0 else pltpu.roll(field, (-by) % self.size, self.axis)

    def mix(self, field, table):
        total = None
        for by, places in table.items():
            weight = self.at(places)
            if weight is not None:
                term = weight * self.shifted(field, by)
                total = term if total is None else total + term
        return total

    def payload(self, pres, wind, jac):
        partial = self.mix(
            pres,
            {
                1: {0: 8.0, 1: 8.0, 6: 8.0},
                2: {0: -1.0, 1: -1.0},
                -1: {1: -8.0, 6: -8.0, 7: -8.0},
                -2: {6: 1.0, 7: 1.0},
            },
        )
        flux = jac * (wind - CG * partial)
        outer = self.mix(pres, {0: {0: 1.0, 1: 1.0, 6: 1.0, 7: 1.0}})
        return outer + self.mix(flux, {-2: {2: 1.0, 3: 1.0}, 2: {4: 1.0, 5: 1.0}})

    def correct(self, delta, pres, jac, delta_jac, base=0):
        grad = self.mix(
            delta,
            {
                base + 2: {0: 1.0, 1: 1.0},
                base + 3: {0: -8.0},
                base - 2: {6: -1.0, 7: -1.0},
                base - 3: {7: 8.0},
            },
        )
        wind = CG * grad
        own = -(jac * wind)
        far = self.mix(delta, {base: {0: 1.0, 1: 1.0, 6: 1.0, 7: 1.0}}) + CG * delta_jac * self.mix(
            pres, {0: {0: 1.0, 1: 1.0, 6: -1.0, 7: -1.0}, -1: {1: -8.0}, 1: {6: 8.0}}
        )
        spread = (
            self.mix(far, {0: {0: 1.0, 1: 1.0, 6: -1.0, 7: -1.0}})
            + self.mix(far - own, {1: {0: -8.0}, -1: {7: 8.0}})
            + self.mix(
                own,
                {
                    -1: {1: -8.0, 2: -8.0},
                    -2: {2: 1.0, 3: 1.0},
                    1: {5: 8.0, 6: 8.0},
                    2: {4: -1.0, 5: -1.0},
                },
            )
        )
        return wind, CD * spread / jac


LOW, HIGH = (0, 1, 2, 3), (4, 5, 6, 7)


def row_edge():
    return Edge(row_index(), 0, LOW + HIGH)


def lane_edge(held):
    return Edge((lane_index() & 3) + held[0], 1, held)


def both_ends(tiles):
    return jnp.where(row_index() < 4, tiles[0], tiles[-1])


def spread_slots(tile, low):
    lane = lane_index()
    if low:
        out = jnp.where(lane < SLOT, tile, 0.0)
    else:
        out = pltpu.roll(jnp.where(lane >= 128 - SLOT, tile, 0.0), SLOT, 1)
    by = SLOT
    while by < 128:
        out = out + pltpu.roll(out, by, 1)
        by *= 2
    return out


class Packer:
    def __init__(self, count):
        self.slot = lax.shift_right_logical(lane_index(), 2)
        self.start = [jnp.zeros((ROWS, 128), jnp.float32)] * (2 * count)
        self.count = count

    def add(self, level, tiles, state):
        before = lax.rem(level + 31, 32)
        rolled = [pltpu.roll(tile, SLOT * level, 1) for tile in tiles]
        low = [jnp.where(self.slot == level, r, s) for r, s in zip(rolled, state)]
        high = [jnp.where(self.slot == before, r, s) for r, s in zip(rolled, state[self.count :])]
        return low + high

    def done(self, state):
        return state[: self.count], [pltpu.roll(s, SLOT, 1) for s in state[self.count :]]


class Closed:
    def __init__(self):
        self.row = row_index()

    def along_y(self, tile):
        pair = tile - pltpu.roll(tile, 126, 1)
        return (pltpu.roll(pair, 2, 1) + pair) - 8.0 * pltpu.roll(pair, 1, 1)

    def moved(self, tiles, by):
        count = len(tiles)
        rolled = [pltpu.roll(tile, by % ROWS, 0) for tile in tiles]
        if by > 0:
            return [jnp.where(self.row < by, rolled[t - 1], rolled[t]) for t in range(count)]
        return [
            jnp.where(self.row >= ROWS + by, rolled[(t + 1) % count], rolled[t])
            for t in range(count)
        ]

    def along_x(self, tiles):
        pair = [f - m for f, m in zip(tiles, self.moved(tiles, -2))]
        return [
            (two + here) - 8.0 * one
            for two, here, one in zip(self.moved(pair, 2), pair, self.moved(pair, 1))
        ]


def even_place():
    return lax.rem(lax.axis_index("gy"), 2) == 0


def put_pair(inner_ref, outer_ref, index, down, up):
    even = even_place()
    put_tiles(inner_ref, index, [jnp.where(even, u, d) for u, d in zip(up, down)])
    put_tiles(outer_ref, index, [jnp.where(even, d, u) for u, d in zip(up, down)])


def get_pair(inner_ref, outer_ref, index, part):
    even = even_place()
    inner, outer = inner_ref[index, part, :], outer_ref[index, part, :]
    return jnp.where(even, outer, inner), jnp.where(even, inner, outer)


def lane_payload(pres, wind, jac):
    low, high = lane_edge(LOW), lane_edge(HIGH)
    down = [
        low.payload(p, w, spread_slots(j, True)) for p, w, j in zip(pres[0], wind[0], jac)
    ]
    up = [
        high.payload(p, w, spread_slots(j, False)) for p, w, j in zip(pres[1], wind[1], jac)
    ]
    return down, up


def levels_of(chunk, share, body, carry):
    for k in range(share):
        carry = body(chunk * share + k, carry)
    return carry


def pack_levels(ref, count, levels):
    packer = Packer(count)

    def step(level, state):
        return packer.add(level, tiles_of(ref, level, count), state)

    return packer.done(lax.fori_loop(0, levels, step, packer.start, unroll=UNROLL))


def kernel_a(
    p_hbm,
    wx_hbm,
    wy_hbm,
    jac_hbm,
    s_hbm,
    rows_ref,
    inner_ref,
    outer_ref,
    pp_ref,
    r_ref,
    i_ref,
    q_ref,
    v_ref,
    stat_ref,
    p_ref,
    wx_ref,
    wy_ref,
    jac_ref,
    s_ref,
    sems,
):
    levels, rows, _ = p_hbm.shape
    count = rows // ROWS
    share = levels // CHUNKS

    def fetch(source, target, sem):
        copy = pltpu.make_async_copy(source, target, sem)
        copy.start()
        return copy

    def chunk(index, source, target, c):
        part = pl.ds(c * share, share)
        return pltpu.make_async_copy(source.at[part], target.at[part], sems.at[index, c])

    for c in range(CHUNKS):
        chunk(0, p_hbm, p_ref, c).start()
        chunk(1, s_hbm, s_ref, c).start()
    for c in range(CHUNKS):
        chunk(2, wy_hbm, wy_ref, c).start()
    ends_in = [
        fetch(jac_hbm, jac_ref, sems.at[3, 0]),
        fetch(wx_hbm, wx_ref, sems.at[3, 1]),
    ]
    packer = Packer(count)

    def down(level, carry):
        state, excess, prod = carry[0], list(carry[1]), list(carry[2])
        for t in range(count):
            part = slice(ROWS * t, ROWS * (t + 1))
            rate = 1.0 / s_ref[level, part, :]
            grown = rate + excess[t]
            inv = 1.0 / (1.0 + grown)
            excess[t] = grown * inv
            prod[t] = prod[t] * inv
            r_ref[level, part, :] = rate
            i_ref[level, part, :] = inv
            q_ref[level, part, :] = prod[t]
        return packer.add(level, tiles_of(p_ref, level, count), state), excess, prod

    def up(step, carry):
        state, value = carry[0], list(carry[1])
        level = levels - 1 - step
        for t in range(count):
            part = slice(ROWS * t, ROWS * (t + 1))
            value[t] = q_ref[level, part, :] + i_ref[level, part, :] * value[t]
            v_ref[level, part, :] = value[t]
        return packer.add(step, tiles_of(wy_ref, step, count), state), value

    ones = [jnp.ones((ROWS, 128), jnp.float32)] * count

    def down_chunk(c, carry):
        chunk(0, p_hbm, p_ref, c).wait()
        chunk(1, s_hbm, s_ref, c).wait()
        return levels_of(c, share, down, carry)

    def up_chunk(c, carry):
        chunk(2, wy_hbm, wy_ref, c).wait()
        return levels_of(c, share, up, carry)

    carry = lax.fori_loop(0, CHUNKS, down_chunk, (packer.start, ones, ones))
    pres = packer.done(carry[0])
    zeros = [jnp.zeros_like(one) for one in ones]
    carry = lax.fori_loop(0, CHUNKS, up_chunk, (packer.start, zeros))
    wind = packer.done(carry[0])
    put_tiles(stat_ref, 0, carry[1])
    stat_ref[1] = q_ref[levels - 1]
    stat_ref[2] = i_ref[levels - 1]
    stat_ref[3] = r_ref[0]
    stat_ref[4] = r_ref[levels - 1]

    for copy in ends_in:
        copy.wait()
    jac = planes_of(jac_ref, count)
    ends = both_ends(jac)
    edge = row_edge()

    def step(level, state):
        rows_ref[level] = edge.payload(
            both_ends(tiles_of(p_ref, level, count)),
            both_ends(tiles_of(wx_ref, level, count)),
            ends,
        )
        return state

    lax.fori_loop(0, levels, step, 0, unroll=UNROLL)
    rows_ref[levels] = ends
    down_out, up_out = lane_payload(pres, wind, jac)
    put_pair(inner_ref, outer_ref, 0, down_out, up_out)
    put_pair(
        inner_ref,
        outer_ref,
        1,
        [spread_slots(j, True) for j in jac],
        [spread_slots(j, False) for j in jac],
    )
    put_tiles(pp_ref, 0, pres[0])
    put_tiles(pp_ref, 1, pres[1])


def kernel_n(wy_ref, pw_ref):
    levels, rows, _ = wy_ref.shape
    count = rows // ROWS
    wind = pack_levels(wy_ref, count, levels)
    put_tiles(pw_ref, 0, wind[0])
    put_tiles(pw_ref, 1, wind[1])


def kernel_m(p_ref, wx_ref, wy_ref, jac_ref, nx_ref, ny_ref, ps_ref):
    levels, rows, _ = p_ref.shape
    count = rows // ROWS
    jac = planes_of(jac_ref, count)
    inv_jac = [CD / j for j in jac]
    closed = Closed()

    def step(level, state):
        pres = tiles_of(p_ref, level, count)
        wind_x = tiles_of(wx_ref, level, count)
        wind_y = tiles_of(wy_ref, level, count)
        new_x = [w - CG * d for w, d in zip(wind_x, closed.along_x(pres))]
        new_y = [w - CG * closed.along_y(p) for w, p in zip(wind_y, pres)]
        put_tiles(nx_ref, level, new_x)
        put_tiles(ny_ref, level, new_y)
        spread_x = closed.along_x([j * n for j, n in zip(jac, new_x)])
        spread_y = [closed.along_y(j * n) for j, n in zip(jac, new_y)]
        put_tiles(
            ps_ref,
            level,
            [p - i * (x + y) for p, i, x, y in zip(pres, inv_jac, spread_x, spread_y)],
        )
        return state

    lax.fori_loop(0, levels, step, 0, unroll=UNROLL)


def kernel_b(
    p_ref,
    nxc_ref,
    nyc_ref,
    psc_ref,
    wz_ref,
    jac_ref,
    sx_ref,
    sy_ref,
    r_ref,
    i_ref,
    v_ref,
    pp_ref,
    rows_ref,
    inner_ref,
    outer_ref,
    got_rows_ref,
    got_inner_ref,
    got_outer_ref,
    srows_ref,
    sinner_ref,
    souter_ref,
    got_srows_ref,
    got_sinner_ref,
    got_souter_ref,
    coef_ref,
    far_ref,
    nx_ref,
    ny_ref,
    ps_ref,
    y_ref,
    *outs,
):
    levels, rows, _ = p_ref.shape
    count = rows // ROWS
    last = count - 1
    lane, row = lane_index(), row_index()
    low_edge, high_edge, edge = lane_edge(LOW), lane_edge(HIGH), row_edge()
    wind_fix, low_fix, high_fix = [], [], []
    for t in range(count):
        part = slice(ROWS * t, ROWS * (t + 1))
        jac_low, jac_high = get_pair(sinner_ref, souter_ref, 1, part)
        jac_below, jac_above = get_pair(got_sinner_ref, got_souter_ref, 1, part)
        down, up = get_pair(inner_ref, outer_ref, 0, part)
        below, above = get_pair(got_inner_ref, got_outer_ref, 0, part)
        low_wind, low_star = low_edge.correct(
            below - up, pp_ref[0, part, :], jac_low, low_edge.shifted(jac_below - jac_high, 2)
        )
        high_wind, high_star = high_edge.correct(
            above - down, pp_ref[1, part, :], jac_high, high_edge.shifted(jac_above - jac_low, -2)
        )
        wind_fix.append(low_wind + pltpu.roll(high_wind, 128 - SLOT, 1))
        low_fix.append(low_star)
        high_fix.append(pltpu.roll(high_star, 128 - SLOT, 1))
    ends = srows_ref[levels]
    change = got_srows_ref[levels] - ends
    ends_change = jnp.where(row < 4, edge.shifted(change, -2), edge.shifted(change, 2))
    outer = (lane < 2) | (lane >= 126)
    low_lanes, high_lanes = lane < SLOT, lane >= 128 - SLOT
    first_rows = row < 4

    def star(level, which):
        new_x = {t: nxc_ref[level, ROWS * t : ROWS * (t + 1), :] for t in which}
        stars = {t: psc_ref[level, ROWS * t : ROWS * (t + 1), :] for t in which}
        if 0 in which:
            wind, press = edge.correct(
                got_rows_ref[level] - rows_ref[level],
                jnp.where(first_rows, p_ref[level, :ROWS, :], p_ref[level, ROWS * last :, :]),
                ends,
                ends_change,
                base=4,
            )
            new_x[0] = new_x[0] - jnp.where(first_rows, wind, 0.0)
            new_x[last] = new_x[last] - jnp.where(first_rows, 0.0, wind)
            stars[0] = stars[0] - jnp.where(first_rows, press, 0.0)
            stars[last] = stars[last] - jnp.where(first_rows, 0.0, press)
        back = lax.rem(128 - SLOT * level, 128)
        forces = []
        for t in which:
            part = slice(ROWS * t, ROWS * (t + 1))
            new_y = nyc_ref[level, part, :] - jnp.where(
                outer, pltpu.roll(wind_fix[t], back, 1), 0.0
            )
            fix = jnp.where(
                low_lanes,
                pltpu.roll(low_fix[t], back, 1),
                jnp.where(high_lanes, pltpu.roll(high_fix[t], back, 1), 0.0),
            )
            stars[t] = stars[t] - fix
            forces.append(
                wz_ref[level, part, :] + sx_ref[part, :] * new_x[t] + sy_ref[part, :] * new_y
            )
            nx_ref[level, part, :] = new_x[t]
            ny_ref[level, part, :] = new_y
            ps_ref[level, part, :] = stars[t]
        return [stars[t] for t in which], forces

    def sweep(level, which, below, above, force, value, first):
        values, firsts = [], []
        for k, t in enumerate(which):
            part = slice(ROWS * t, ROWS * (t + 1))
            rhs = r_ref[level, part, :] * (force[k] - vert_coef * (above[k] - below[k]))
            firsts.append(first[k] + v_ref[level, part, :] * rhs)
            values.append((rhs + value[k]) * i_ref[level, part, :])
            y_ref[level, part, :] = values[k]
        return values, firsts

    which = tuple(range(count))
    put_tiles(y_ref, 0, [jnp.zeros((ROWS, 128), jnp.float32)] * count)
    zeros = tiles_of(y_ref, 0, count)

    def step(level, carry):
        below, here, force, value, first = carry
        above, force_next = star(level, which)
        before = jnp.maximum(level - 1, 0)
        new_value, new_first = sweep(before, which, below, above, force, value, first)
        started = jnp.where(level > 0, 1.0, 0.0)
        value = [started * n for n in new_value]
        first = [started * n for n in new_first]
        return here, above, force_next, value, first

    below, here, force, value, first = lax.fori_loop(
        0, levels, step, (zeros, zeros, zeros, zeros, zeros), unroll=UNROLL // 2
    )
    value, first = sweep(levels - 1, which, below, zeros, force, value, first)
    bottom = tiles_of(ps_ref, 0, count)
    interface(first, value, bottom, here, coef_ref, far_ref, outs)


PAIR_COEFS = ("own", "other", "den", "den_end", "den_link", "outer", "total", "facing", "first", "last")


def place_in_column():
    mine = lax.axis_index("lev")
    return (mine == 0) | (mine == 3), mine < 2, lax.rem(mine, 2) == 0


def kernel_s(stat_ref, mate_ref, coef_ref, send_ref):
    outermost, lower, even = place_in_column()
    for t in range(coef_ref.shape[1] // ROWS):
        part = slice(ROWS * t, ROWS * (t + 1))
        mine = [stat_ref[k, part, :] for k in range(STATS)]
        mate = [mate_ref[k, part, :] for k in range(STATS)]
        outer = [jnp.where(outermost, a, b) for a, b in zip(mine, mate)]
        inner = [jnp.where(outermost, b, a) for a, b in zip(mine, mate)]
        outer_end = jnp.where(lower, outer[2], outer[0])
        end = jnp.where(lower, inner[0], inner[2])
        centre = jnp.where(lower, inner[2], inner[0])
        link = inner[1]
        den = 1.0 / (1.0 - end * outer_end)
        den_link = den * link
        weight = outer_end * den_link
        one, zero = jnp.ones_like(den), jnp.zeros_like(den)
        coefs = dict(
            own=jnp.where(outermost, den_link, one),
            other=jnp.where(outermost, zero, weight),
            den=den,
            den_end=den * end,
            den_link=den_link,
            outer=outer_end,
            total=centre + weight * link,
            facing=vert_coef * jnp.where(even, mate[3], mate[4]),
            first=vert_coef * mine[3],
            last=vert_coef * mine[4],
        )
        for k, name in enumerate(PAIR_COEFS):
            coef_ref[k, part, :] = coefs[name]
        send_ref[0, part, :] = coefs["total"]
        send_ref[1, part, :] = vert_coef * jnp.where(lower, inner[4], inner[3])


def interface(first, value, star_first, star_last, coef_ref, far_ref, outs):
    next_ref, cross_ref, own_ref, star_ref, share_ref = outs
    outermost, lower, even = place_in_column()
    for t in range(len(first)):
        part = slice(ROWS * t, ROWS * (t + 1))
        coef = {name: coef_ref[k, part, :] for k, name in enumerate(PAIR_COEFS)}
        sign = jnp.where(lower, 1.0, -1.0)
        star_centre = jnp.where(lower, star_last[t], star_first[t])
        star_outer = jnp.where(lower, star_first[t], star_last[t])
        facing = jnp.where(outermost, coef["facing"], far_ref[1, part, :])
        centre = jnp.where(lower, value[t], first[t]) + sign * facing * star_centre
        outer = jnp.where(lower, first[t], value[t]) - sign * coef["facing"] * star_outer
        total = coef["own"] * centre + coef["other"] * outer
        next_ref[0, part, :] = total
        next_ref[1, part, :] = star_centre
        cross_ref[part, :] = total
        own_ref[part, :] = jnp.where(outermost, centre, outer)
        star_ref[part, :] = jnp.where(even, star_last[t], star_first[t])
        share_ref[part, :] = total


def boundary(
    count,
    got_next_ref,
    got_cross_ref,
    got_own_ref,
    got_star_ref,
    got_share_ref,
    own_ref,
    share_ref,
    coef_ref,
    far_ref,
):
    outermost, lower, _ = place_in_column()
    parts = []
    for t in range(count):
        part = slice(ROWS * t, ROWS * (t + 1))
        coef = {name: coef_ref[k, part, :] for k, name in enumerate(PAIR_COEFS)}
        far_total = far_ref[0, part, :]
        own, got = own_ref[part, :], got_own_ref[part, :]
        this = share_ref[part, :] + got_share_ref[part, :]
        that = got_cross_ref[part, :] + got_next_ref[0, part, :]
        middle = (that + far_total * this) / (1.0 - coef["total"] * far_total)
        from_outer = jnp.where(outermost, own, got)
        from_inner = jnp.where(outermost, got, own)
        between = (
            coef["den"] * from_inner + coef["den_end"] * from_outer + coef["den_link"] * middle
        )
        zero = jnp.zeros_like(own)
        centre = jnp.where(outermost, between, middle)
        outer = jnp.where(outermost, zero, from_outer + coef["outer"] * between)
        mate_star = got_star_ref[part, :]
        star_centre = jnp.where(outermost, mate_star, got_next_ref[1, part, :])
        star_outer = jnp.where(outermost, zero, mate_star)
        below, above = jnp.where(lower, outer, centre), jnp.where(lower, centre, outer)
        star_below = jnp.where(lower, star_outer, star_centre)
        star_above = jnp.where(lower, star_centre, star_outer)
        under = below - coef["first"] * star_below
        over = above + coef["last"] * star_above
        parts.append((below, above, under, over))
    return [[part[k] for part in parts] for k in range(4)]


def finish(count, levels, y_ref, q_ref, i_ref, ps_ref, x_ref, p_ref, column_refs, ready=None):
    lower, upper, under, over = boundary(count, *column_refs)

    def solved(level, above):
        value = tiles_of(y_ref, level, count)
        prod = tiles_of(q_ref, level, count)
        inv = tiles_of(i_ref, level, count)
        out = [(y + q * u) + i * a for y, q, u, i, a in zip(value, prod, lower, inv, above)]
        put_tiles(x_ref, level, out)
        return out

    def pressed(level, above, below):
        star = tiles_of(ps_ref, level, count)
        put_tiles(p_ref, level, [s - vert_coef * (a - b) for s, a, b in zip(star, above, below)])

    def step(index, carry):
        above, here = carry
        level = levels - 1 - index
        below = solved(level, here)
        pressed(jnp.minimum(level + 1, levels - 1), above, below)
        return [jnp.where(index == 0, o, h) for o, h in zip(over, here)], below

    share = levels // CHUNKS

    def chunk(c, carry):
        carry = levels_of(c, share, step, carry)
        if ready is not None:
            ready(c)
        return carry

    above, here = lax.fori_loop(0, CHUNKS, chunk, (over, upper))
    pressed(0, above, under)


def kernel_c(*refs):
    column_refs = refs[:COLUMN]
    y_ref, q_ref, i_ref, ps_ref, wx_ref, pw_ref, jac_ref = refs[COLUMN : COLUMN + 7]
    x_ref, p_ref, rows_ref, inner_ref, outer_ref, pp_ref = refs[COLUMN + 7 :]
    levels, rows, _ = y_ref.shape
    count = rows // ROWS
    edge = row_edge()
    ends = both_ends(planes_of(jac_ref, count))
    finish(count, levels, y_ref, q_ref, i_ref, ps_ref, x_ref, p_ref, column_refs)

    def step(level, state):
        rows_ref[level] = edge.payload(
            both_ends(tiles_of(p_ref, level, count)),
            both_ends(tiles_of(wx_ref, level, count)),
            ends,
        )
        return state

    lax.fori_loop(0, levels, step, 0, unroll=UNROLL)
    pres = pack_levels(p_ref, count, levels)
    wind = tiles_of(pw_ref, 0, count), tiles_of(pw_ref, 1, count)
    down, up = lane_payload(pres, wind, planes_of(jac_ref, count))
    put_pair(inner_ref, outer_ref, 0, down, up)
    put_tiles(pp_ref, 0, pres[0])
    put_tiles(pp_ref, 1, pres[1])


def kernel_d(*refs):
    column_refs = refs[:COLUMN]
    y_ref, q_ref, i_ref, ps_ref = refs[COLUMN : COLUMN + 4]
    x_hbm, p_hbm, x_ref, p_ref, sems = refs[COLUMN + 4 :]
    levels, rows, _ = y_ref.shape
    share = levels // CHUNKS

    def copy(index, source, target, c):
        part = pl.ds(c * share, share)
        return pltpu.make_async_copy(source.at[part], target.at[part], sems.at[index, c])

    def ready(step):
        c = CHUNKS - 1 - step
        copy(0, x_ref, x_hbm, c).start()

        @pl.when(step > 0)
        def _():
            copy(1, p_ref, p_hbm, c + 1).start()

    finish(
        rows // ROWS,
        levels,
        y_ref,
        q_ref,
        i_ref,
        ps_ref,
        x_ref,
        p_ref,
        column_refs,
        ready,
    )
    copy(1, p_ref, p_hbm, 0).start()
    for c in range(CHUNKS):
        copy(0, x_ref, x_hbm, c).wait()
        copy(1, p_ref, p_hbm, c).wait()


def call(kernel, name, shapes, *args, far_in=(), far_out=False, scratch=(), keep=()):
    near, far = pl.BlockSpec(memory_space=pltpu.VMEM), pl.BlockSpec(memory_space=pl.ANY)
    size = sum(a.size for a in args) + sum(functools.reduce(lambda a, b: a * b, s) for s in shapes)
    if len(far_in) == len(args):
        args = [pltpu.with_memory_space_constraint(a, pltpu.HBM) for a in args]
    return pl.pallas_call(
        kernel,
        out_shape=[
            pltpu.VMEM(s, jnp.float32) if k in keep else jax.ShapeDtypeStruct(s, jnp.float32)
            for k, s in enumerate(shapes)
        ],
        in_specs=[far if k in far_in else near for k in range(len(args))],
        out_specs=[far if far_out else near] * len(shapes),
        scratch_shapes=list(scratch),
        compiler_params=pltpu.CompilerParams(vmem_limit_bytes=32 * 1024 * 1024),
        cost_estimate=pl.CostEstimate(
            flops=8 * size, bytes_accessed=4 * size, transcendentals=0
        ),
        name=name,
    )(*args)


def swap(value, axis, partner):
    count = lax.axis_size(axis)
    return lax.ppermute(value, axis, [(i, partner(i)) for i in range(count)])


def exchange_rows(rows):
    count = lax.axis_size("gx")
    if count == 2:
        return swap(rows, "gx", lambda i: 1 - i)
    down = swap(rows[:, : ROWS // 2], "gx", lambda i: (i - 1) % count)
    up = swap(rows[:, ROWS // 2 :], "gx", lambda i: (i + 1) % count)
    return jnp.concatenate([down, up], axis=1)


def exchange_lanes(inner, outer):
    count = lax.axis_size("gy")
    got_inner = swap(inner, "gy", lambda i: i ^ 1)
    got_outer = swap(outer, "gy", lambda i: (i + 1 if i % 2 else i - 1) % count)
    return got_inner, got_outer


def exchange_column(following, cross, own, star, share):
    got_cross = swap(cross, "lev", lambda i: i ^ 2)
    got_next = swap(following, "lev", lambda i: i ^ 3)
    mates = [swap(value, "lev", lambda i: i ^ 1) for value in (own, star, share)]
    return [got_next, got_cross, *mates, own, share]


def local(wind_x, wind_y, wind_z, pressure, jacobian, slope_x, slope_y, stiffness):
    field = wind_x.shape
    levels, rows, lanes = field
    plane = (rows, lanes)
    pair = (2,) + plane
    assert lanes == 128 and levels * SLOT == 128 and rows % ROWS == 0
    assert lax.axis_size("lev") == 4 and lax.axis_size("gy") % 2 == 0

    edge, inner, outer, ends, rate, inv, prod, gain, stat, *fields = call(
        kernel_a,
        "start",
        [(levels + 1, ROWS, lanes), pair, (3,) + plane, pair]
        + [field] * 4
        + [(STATS,) + plane]
        + [field] * 3,
        pressure,
        wind_x,
        wind_y,
        jacobian,
        stiffness,
        far_in=(0, 1, 2, 3, 4),
        keep=(9, 10, 11),
        scratch=[
            pltpu.VMEM(plane, jnp.float32),
            pltpu.VMEM(field, jnp.float32),
            pltpu.SemaphoreType.DMA((4, CHUNKS)),
        ],
    )
    pressure, wind_x, wind_y = fields
    mate = swap(stat, "lev", lambda i: i ^ 1)
    coef, send = call(kernel_s, "pairs", [(len(PAIR_COEFS),) + plane, pair], stat, mate)
    far = swap(send, "lev", lambda i: i ^ 2)
    sent = (edge, inner, outer)
    got = (exchange_rows(edge),) + exchange_lanes(inner, outer)
    static_edges = sent + got
    for substep in range(SUBSTEPS):
        closed = call(
            kernel_m, "interior", [field, field, field], pressure, wind_x, wind_y, jacobian
        )
        wind_x, wind_y, star, value, *faces = call(
            kernel_b,
            "sweep",
            [field] * 4 + [pair] + [plane] * 4,
            pressure,
            *closed,
            wind_z,
            jacobian,
            slope_x,
            slope_y,
            rate,
            inv,
            gain,
            ends,
            *sent,
            *got,
            *static_edges,
            coef,
            far,
            keep=tuple(range(9)),
        )
        column = exchange_column(*faces) + [coef, far]
        if substep < SUBSTEPS - 1:
            (packed,) = call(kernel_n, "pack", [pair], wind_y)
            wind_z, pressure, edge, inner, outer, ends = call(
                kernel_c,
                "finish",
                [field, field, (levels, ROWS, lanes), (1,) + plane, pair, pair],
                *column,
                value,
                prod,
                inv,
                star,
                wind_x,
                packed,
                jacobian,
            )
            sent = (edge, inner, outer)
            got = (exchange_rows(edge),) + exchange_lanes(inner, outer)
        else:
            wind_z, pressure = call(
                kernel_d,
                "last",
                [field, field],
                *column,
                value,
                prod,
                inv,
                star,
                far_out=True,
                scratch=[
                    pltpu.VMEM(field, jnp.float32),
                    pltpu.VMEM(field, jnp.float32),
                    pltpu.SemaphoreType.DMA((2, CHUNKS)),
                ],
            )
    return wind_x, wind_y, wind_z, pressure


def solution(mesh):
    field = P("lev", "gx", "gy")
    column = P("gx", "gy")
    return jax.shard_map(
        local,
        mesh=mesh,
        in_specs=(field,) * 4 + (column,) * 3 + (field,),
        out_specs=(field,) * 4,
        check_vma=False,
    )
```

```python
import functools

import jax
import jax.numpy as jnp
from jax import lax
from jax.experimental import pallas as pl
from jax.experimental.pallas import tpu as pltpu
from jax.sharding import PartitionSpec as P

SUBSTEPS = 2

grad_coef = 0.35
div_coef = 0.35
vert_coef = 0.25

CG = grad_coef / 12.0
CD = div_coef / 12.0
ROWS = 8
SLOT = 4
UNROLL = 8
CHUNKS = 4
COLUMN = 9
STATS = 5


def lane_index():
    return lax.broadcasted_iota(jnp.int32, (ROWS, 128), 1)


def row_index():
    return lax.broadcasted_iota(jnp.int32, (ROWS, 128), 0)


def only(mask, value):
    return jnp.where(mask, jnp.float32(value), jnp.float32(0.0))


def tiles_of(ref, level, count):
    return [ref[level, ROWS * t : ROWS * (t + 1), :] for t in range(count)]


def planes_of(ref, count):
    return [ref[ROWS * t : ROWS * (t + 1), :] for t in range(count)]


def put_tiles(ref, level, tiles):
    for t, tile in enumerate(tiles):
        ref[level, ROWS * t : ROWS * (t + 1), :] = tile


def put_planes(ref, tiles):
    for t, tile in enumerate(tiles):
        ref[ROWS * t : ROWS * (t + 1), :] = tile


class Edge:
    def __init__(self, place, axis, held):
        self.place, self.axis, self.held = place, axis, held
        self.size = place.shape[axis]

    def at(self, places):
        total = None
        for position, value in places.items():
            if position in self.held:
                term = only(self.place == position, value)
                total = term if total is None else total + term
        return total

    def shifted(self, field, by):
        return field if by % self.size == 0 else pltpu.roll(field, (-by) % self.size, self.axis)

    def mix(self, field, table):
        total = None
        for by, places in table.items():
            weight = self.at(places)
            if weight is not None:
                term = weight * self.shifted(field, by)
                total = term if total is None else total + term
        return total

    def payload(self, pres, wind, jac):
        partial = self.mix(
            pres,
            {
                1: {0: 8.0, 1: 8.0, 6: 8.0},
                2: {0: -1.0, 1: -1.0},
                -1: {1: -8.0, 6: -8.0, 7: -8.0},
                -2: {6: 1.0, 7: 1.0},
            },
        )
        flux = jac * (wind - CG * partial)
        outer = self.mix(pres, {0: {0: 1.0, 1: 1.0, 6: 1.0, 7: 1.0}})
        return outer + self.mix(flux, {-2: {2: 1.0, 3: 1.0}, 2: {4: 1.0, 5: 1.0}})

    def correct(self, delta, pres, jac, delta_jac, base=0):
        grad = self.mix(
            delta,
            {
                base + 2: {0: 1.0, 1: 1.0},
                base + 3: {0: -8.0},
                base - 2: {6: -1.0, 7: -1.0},
                base - 3: {7: 8.0},
            },
        )
        wind = CG * grad
        own = -(jac * wind)
        far = self.mix(delta, {base: {0: 1.0, 1: 1.0, 6: 1.0, 7: 1.0}}) + CG * delta_jac * self.mix(
            pres, {0: {0: 1.0, 1: 1.0, 6: -1.0, 7: -1.0}, -1: {1: -8.0}, 1: {6: 8.0}}
        )
        spread = (
            self.mix(far, {0: {0: 1.0, 1: 1.0, 6: -1.0, 7: -1.0}})
            + self.mix(far - own, {1: {0: -8.0}, -1: {7: 8.0}})
            + self.mix(
                own,
                {
                    -1: {1: -8.0, 2: -8.0},
                    -2: {2: 1.0, 3: 1.0},
                    1: {5: 8.0, 6: 8.0},
                    2: {4: -1.0, 5: -1.0},
                },
            )
        )
        return wind, CD * spread / jac


LOW, HIGH = (0, 1, 2, 3), (4, 5, 6, 7)


def row_edge():
    return Edge(row_index(), 0, LOW + HIGH)


def lane_edge(held):
    return Edge((lane_index() & 3) + held[0], 1, held)


def both_ends(tiles):
    return jnp.where(row_index() < 4, tiles[0], tiles[-1])


def spread_slots(tile, low):
    lane = lane_index()
    if low:
        out = jnp.where(lane < SLOT, tile, 0.0)
    else:
        out = pltpu.roll(jnp.where(lane >= 128 - SLOT, tile, 0.0), SLOT, 1)
    for by in (SLOT, 4 * SLOT):
        out = (out + pltpu.roll(out, by, 1)) + (
            pltpu.roll(out, 2 * by, 1) + pltpu.roll(out, 3 * by, 1)
        )
    return out + pltpu.roll(out, 64, 1)


class Packer:
    def __init__(self, count):
        self.slot = lax.shift_right_logical(lane_index(), 2)
        self.start = [jnp.zeros((ROWS, 128), jnp.float32)] * (2 * count)
        self.count = count

    def add(self, level, tiles, state):
        before = lax.rem(level + 31, 32)
        rolled = [pltpu.roll(tile, SLOT * level, 1) for tile in tiles]
        low = [jnp.where(self.slot == level, r, s) for r, s in zip(rolled, state)]
        high = [jnp.where(self.slot == before, r, s) for r, s in zip(rolled, state[self.count :])]
        return low + high

    def done(self, state):
        return state[: self.count], [pltpu.roll(s, SLOT, 1) for s in state[self.count :]]


class Closed:
    def __init__(self):
        self.row = row_index()

    def along_y(self, tile):
        pair = tile - pltpu.roll(tile, 126, 1)
        return (pltpu.roll(pair, 2, 1) + pair) - 8.0 * pltpu.roll(pair, 1, 1)

    def moved(self, tiles, by):
        count = len(tiles)
        rolled = [pltpu.roll(tile, by % ROWS, 0) for tile in tiles]
        if by > 0:
            return [jnp.where(self.row < by, rolled[t - 1], rolled[t]) for t in range(count)]
        return [
            jnp.where(self.row >= ROWS + by, rolled[(t + 1) % count], rolled[t])
            for t in range(count)
        ]

    def along_x(self, tiles):
        pair = [f - m for f, m in zip(tiles, self.moved(tiles, -2))]
        return [
            (two + here) - 8.0 * one
            for two, here, one in zip(self.moved(pair, 2), pair, self.moved(pair, 1))
        ]


def even_place():
    return lax.rem(lax.axis_index("gy"), 2) == 0


def put_pair(inner_ref, outer_ref, index, down, up):
    even = even_place()
    put_tiles(inner_ref, index, [jnp.where(even, u, d) for u, d in zip(up, down)])
    put_tiles(outer_ref, index, [jnp.where(even, d, u) for u, d in zip(up, down)])


def get_pair(inner_ref, outer_ref, index, part):
    even = even_place()
    inner, outer = inner_ref[index, part, :], outer_ref[index, part, :]
    return jnp.where(even, outer, inner), jnp.where(even, inner, outer)


def lane_payload(pres, wind, jac):
    low, high = lane_edge(LOW), lane_edge(HIGH)
    down = [low.payload(p, w, j) for p, w, j in zip(pres[0], wind[0], jac[0])]
    up = [high.payload(p, w, j) for p, w, j in zip(pres[1], wind[1], jac[1])]
    return down, up


def levels_of(chunk, share, body, carry):
    for k in range(share):
        carry = body(chunk * share + k, carry)
    return carry


def pack_levels(ref, count, levels):
    packer = Packer(count)

    def step(level, state):
        return packer.add(level, tiles_of(ref, level, count), state)

    return packer.done(lax.fori_loop(0, levels, step, packer.start, unroll=UNROLL))


def kernel_a(
    p_hbm,
    wx_hbm,
    wy_hbm,
    jac_hbm,
    s_hbm,
    rows_ref,
    inner_ref,
    outer_ref,
    pp_ref,
    r_ref,
    i_ref,
    q_ref,
    v_ref,
    stat_ref,
    p_ref,
    wx_ref,
    wy_ref,
    jac_ref,
    s_ref,
    sems,
):
    levels, rows, _ = p_hbm.shape
    count = rows // ROWS
    share = levels // CHUNKS

    def fetch(source, target, sem):
        copy = pltpu.make_async_copy(source, target, sem)
        copy.start()
        return copy

    def chunk(index, source, target, c):
        part = pl.ds(c * share, share)
        return pltpu.make_async_copy(source.at[part], target.at[part], sems.at[index, c])

    for c in range(CHUNKS):
        chunk(0, p_hbm, p_ref, c).start()
        chunk(1, s_hbm, s_ref, c).start()
    for c in range(CHUNKS):
        chunk(2, wy_hbm, wy_ref, c).start()
    ends_in = [
        fetch(jac_hbm, jac_ref, sems.at[3, 0]),
        fetch(wx_hbm, wx_ref, sems.at[3, 1]),
    ]
    packer = Packer(count)

    def down(level, carry):
        state, excess, prod = carry[0], list(carry[1]), list(carry[2])
        for t in range(count):
            part = slice(ROWS * t, ROWS * (t + 1))
            rate = 1.0 / s_ref[level, part, :]
            grown = rate + excess[t]
            inv = 1.0 / (1.0 + grown)
            excess[t] = grown * inv
            prod[t] = prod[t] * inv
            r_ref[level, part, :] = rate
            i_ref[level, part, :] = inv
            q_ref[level, part, :] = prod[t]
        return packer.add(level, tiles_of(p_ref, level, count), state), excess, prod

    def up(step, carry):
        state, value = carry[0], list(carry[1])
        level = levels - 1 - step
        for t in range(count):
            part = slice(ROWS * t, ROWS * (t + 1))
            value[t] = q_ref[level, part, :] + i_ref[level, part, :] * value[t]
            v_ref[level, part, :] = value[t]
        return packer.add(step, tiles_of(wy_ref, step, count), state), value

    ones = [jnp.ones((ROWS, 128), jnp.float32)] * count

    def down_chunk(c, carry):
        chunk(0, p_hbm, p_ref, c).wait()
        chunk(1, s_hbm, s_ref, c).wait()
        return levels_of(c, share, down, carry)

    def up_chunk(c, carry):
        chunk(2, wy_hbm, wy_ref, c).wait()
        return levels_of(c, share, up, carry)

    carry = lax.fori_loop(0, CHUNKS, down_chunk, (packer.start, ones, ones))
    pres = packer.done(carry[0])
    zeros = [jnp.zeros_like(one) for one in ones]
    carry = lax.fori_loop(0, CHUNKS, up_chunk, (packer.start, zeros))
    wind = packer.done(carry[0])
    put_tiles(stat_ref, 0, carry[1])
    stat_ref[1] = q_ref[levels - 1]
    stat_ref[2] = i_ref[levels - 1]
    stat_ref[3] = r_ref[0]
    stat_ref[4] = r_ref[levels - 1]

    for copy in ends_in:
        copy.wait()
    jac = planes_of(jac_ref, count)
    ends = both_ends(jac)
    edge = row_edge()

    def step(level, state):
        rows_ref[level] = edge.payload(
            both_ends(tiles_of(p_ref, level, count)),
            both_ends(tiles_of(wx_ref, level, count)),
            ends,
        )
        return state

    lax.fori_loop(0, levels, step, 0, unroll=UNROLL)
    rows_ref[levels] = ends
    slots = [[spread_slots(j, low) for j in jac] for low in (True, False)]
    put_pair(inner_ref, outer_ref, 1, *slots)
    down_out, up_out = lane_payload(pres, wind, slots)
    put_pair(inner_ref, outer_ref, 0, down_out, up_out)
    put_tiles(pp_ref, 0, pres[0])
    put_tiles(pp_ref, 1, pres[1])


def kernel_n(wy_ref, pw_ref):
    levels, rows, _ = wy_ref.shape
    count = rows // ROWS
    wind = pack_levels(wy_ref, count, levels)
    put_tiles(pw_ref, 0, wind[0])
    put_tiles(pw_ref, 1, wind[1])


def kernel_m(p_ref, wx_ref, wy_ref, jac_ref, nx_ref, ny_ref, ps_ref):
    levels, rows, _ = p_ref.shape
    count = rows // ROWS
    jac = planes_of(jac_ref, count)
    inv_jac = [CD / j for j in jac]
    closed = Closed()

    def step(level, state):
        pres = tiles_of(p_ref, level, count)
        wind_x = tiles_of(wx_ref, level, count)
        wind_y = tiles_of(wy_ref, level, count)
        new_x = [w - CG * d for w, d in zip(wind_x, closed.along_x(pres))]
        new_y = [w - CG * closed.along_y(p) for w, p in zip(wind_y, pres)]
        put_tiles(nx_ref, level, new_x)
        put_tiles(ny_ref, level, new_y)
        spread_x = closed.along_x([j * n for j, n in zip(jac, new_x)])
        spread_y = [closed.along_y(j * n) for j, n in zip(jac, new_y)]
        put_tiles(
            ps_ref,
            level,
            [p - i * (x + y) for p, i, x, y in zip(pres, inv_jac, spread_x, spread_y)],
        )
        return state

    lax.fori_loop(0, levels, step, 0, unroll=UNROLL)


def kernel_b(
    p_ref,
    nxc_ref,
    nyc_ref,
    psc_ref,
    wz_ref,
    jac_ref,
    sx_ref,
    sy_ref,
    r_ref,
    i_ref,
    v_ref,
    pp_ref,
    rows_ref,
    inner_ref,
    outer_ref,
    got_rows_ref,
    got_inner_ref,
    got_outer_ref,
    srows_ref,
    sinner_ref,
    souter_ref,
    got_srows_ref,
    got_sinner_ref,
    got_souter_ref,
    coef_ref,
    far_ref,
    nx_ref,
    ny_ref,
    ps_ref,
    y_ref,
    *outs,
):
    levels, rows, _ = p_ref.shape
    count = rows // ROWS
    last = count - 1
    lane, row = lane_index(), row_index()
    low_edge, high_edge, edge = lane_edge(LOW), lane_edge(HIGH), row_edge()
    wind_fix, low_fix, high_fix = [], [], []
    for t in range(count):
        part = slice(ROWS * t, ROWS * (t + 1))
        jac_low, jac_high = get_pair(sinner_ref, souter_ref, 1, part)
        jac_below, jac_above = get_pair(got_sinner_ref, got_souter_ref, 1, part)
        down, up = get_pair(inner_ref, outer_ref, 0, part)
        below, above = get_pair(got_inner_ref, got_outer_ref, 0, part)
        low_wind, low_star = low_edge.correct(
            below - up, pp_ref[0, part, :], jac_low, low_edge.shifted(jac_below - jac_high, 2)
        )
        high_wind, high_star = high_edge.correct(
            above - down, pp_ref[1, part, :], jac_high, high_edge.shifted(jac_above - jac_low, -2)
        )
        wind_fix.append(low_wind + pltpu.roll(high_wind, 128 - SLOT, 1))
        low_fix.append(low_star)
        high_fix.append(pltpu.roll(high_star, 128 - SLOT, 1))
    ends = srows_ref[levels]
    change = got_srows_ref[levels] - ends
    ends_change = jnp.where(row < 4, edge.shifted(change, -2), edge.shifted(change, 2))
    outer = (lane < 2) | (lane >= 126)
    low_lanes, high_lanes = lane < SLOT, lane >= 128 - SLOT
    first_rows = row < 4

    def star(level, which):
        new_x = {t: nxc_ref[level, ROWS * t : ROWS * (t + 1), :] for t in which}
        stars = {t: psc_ref[level, ROWS * t : ROWS * (t + 1), :] for t in which}
        if 0 in which:
            wind, press = edge.correct(
                got_rows_ref[level] - rows_ref[level],
                jnp.where(first_rows, p_ref[level, :ROWS, :], p_ref[level, ROWS * last :, :]),
                ends,
                ends_change,
                base=4,
            )
            new_x[0] = new_x[0] - jnp.where(first_rows, wind, 0.0)
            new_x[last] = new_x[last] - jnp.where(first_rows, 0.0, wind)
            stars[0] = stars[0] - jnp.where(first_rows, press, 0.0)
            stars[last] = stars[last] - jnp.where(first_rows, 0.0, press)
        back = lax.rem(128 - SLOT * level, 128)
        forces = []
        for t in which:
            part = slice(ROWS * t, ROWS * (t + 1))
            new_y = nyc_ref[level, part, :] - jnp.where(
                outer, pltpu.roll(wind_fix[t], back, 1), 0.0
            )
            fix = jnp.where(
                low_lanes,
                pltpu.roll(low_fix[t], back, 1),
                jnp.where(high_lanes, pltpu.roll(high_fix[t], back, 1), 0.0),
            )
            stars[t] = stars[t] - fix
            forces.append(
                wz_ref[level, part, :] + sx_ref[part, :] * new_x[t] + sy_ref[part, :] * new_y
            )
            nx_ref[level, part, :] = new_x[t]
            ny_ref[level, part, :] = new_y
            ps_ref[level, part, :] = stars[t]
        return [stars[t] for t in which], forces

    def sweep(level, which, below, above, force, value, first):
        values, firsts = [], []
        for k, t in enumerate(which):
            part = slice(ROWS * t, ROWS * (t + 1))
            rhs = r_ref[level, part, :] * (force[k] - vert_coef * (above[k] - below[k]))
            firsts.append(first[k] + v_ref[level, part, :] * rhs)
            values.append((rhs + value[k]) * i_ref[level, part, :])
            y_ref[level, part, :] = values[k]
        return values, firsts

    which = tuple(range(count))
    put_tiles(y_ref, 0, [jnp.zeros((ROWS, 128), jnp.float32)] * count)
    zeros = tiles_of(y_ref, 0, count)

    def step(level, carry):
        below, here, force, value, first = carry
        above, force_next = star(level, which)
        before = jnp.maximum(level - 1, 0)
        new_value, new_first = sweep(before, which, below, above, force, value, first)
        started = jnp.where(level > 0, 1.0, 0.0)
        value = [started * n for n in new_value]
        first = [started * n for n in new_first]
        return here, above, force_next, value, first

    below, here, force, value, first = lax.fori_loop(
        0, levels, step, (zeros, zeros, zeros, zeros, zeros), unroll=UNROLL // 2
    )
    value, first = sweep(levels - 1, which, below, zeros, force, value, first)
    bottom = tiles_of(ps_ref, 0, count)
    interface(first, value, bottom, here, coef_ref, far_ref, outs)


PAIR_COEFS = ("own", "other", "den", "den_end", "den_link", "outer", "total", "facing", "first", "last")


def place_in_column():
    mine = lax.axis_index("lev")
    return (mine == 0) | (mine == 3), mine < 2, lax.rem(mine, 2) == 0


def kernel_s(stat_ref, mate_ref, coef_ref, send_ref):
    outermost, lower, even = place_in_column()
    for t in range(coef_ref.shape[1] // ROWS):
        part = slice(ROWS * t, ROWS * (t + 1))
        mine = [stat_ref[k, part, :] for k in range(STATS)]
        mate = [mate_ref[k, part, :] for k in range(STATS)]
        outer = [jnp.where(outermost, a, b) for a, b in zip(mine, mate)]
        inner = [jnp.where(outermost, b, a) for a, b in zip(mine, mate)]
        outer_end = jnp.where(lower, outer[2], outer[0])
        end = jnp.where(lower, inner[0], inner[2])
        centre = jnp.where(lower, inner[2], inner[0])
        link = inner[1]
        den = 1.0 / (1.0 - end * outer_end)
        den_link = den * link
        weight = outer_end * den_link
        one, zero = jnp.ones_like(den), jnp.zeros_like(den)
        coefs = dict(
            own=jnp.where(outermost, den_link, one),
            other=jnp.where(outermost, zero, weight),
            den=den,
            den_end=den * end,
            den_link=den_link,
            outer=outer_end,
            total=centre + weight * link,
            facing=vert_coef * jnp.where(even, mate[3], mate[4]),
            first=vert_coef * mine[3],
            last=vert_coef * mine[4],
        )
        for k, name in enumerate(PAIR_COEFS):
            coef_ref[k, part, :] = coefs[name]
        send_ref[0, part, :] = coefs["total"]
        send_ref[1, part, :] = vert_coef * jnp.where(lower, inner[4], inner[3])


def interface(first, value, star_first, star_last, coef_ref, far_ref, outs):
    next_ref, cross_ref, own_ref, star_ref, share_ref = outs
    outermost, lower, even = place_in_column()
    for t in range(len(first)):
        part = slice(ROWS * t, ROWS * (t + 1))
        coef = {name: coef_ref[k, part, :] for k, name in enumerate(PAIR_COEFS)}
        sign = jnp.where(lower, 1.0, -1.0)
        star_centre = jnp.where(lower, star_last[t], star_first[t])
        star_outer = jnp.where(lower, star_first[t], star_last[t])
        facing = jnp.where(outermost, coef["facing"], far_ref[1, part, :])
        centre = jnp.where(lower, value[t], first[t]) + sign * facing * star_centre
        outer = jnp.where(lower, first[t], value[t]) - sign * coef["facing"] * star_outer
        total = coef["own"] * centre + coef["other"] * outer
        next_ref[0, part, :] = total
        next_ref[1, part, :] = star_centre
        cross_ref[part, :] = total
        own_ref[part, :] = jnp.where(outermost, centre, outer)
        star_ref[part, :] = jnp.where(even, star_last[t], star_first[t])
        share_ref[part, :] = total


def boundary(
    count,
    got_next_ref,
    got_cross_ref,
    got_own_ref,
    got_star_ref,
    got_share_ref,
    own_ref,
    share_ref,
    coef_ref,
    far_ref,
):
    outermost, lower, _ = place_in_column()
    parts = []
    for t in range(count):
        part = slice(ROWS * t, ROWS * (t + 1))
        coef = {name: coef_ref[k, part, :] for k, name in enumerate(PAIR_COEFS)}
        far_total = far_ref[0, part, :]
        own, got = own_ref[part, :], got_own_ref[part, :]
        this = share_ref[part, :] + got_share_ref[part, :]
        that = got_cross_ref[part, :] + got_next_ref[0, part, :]
        middle = (that + far_total * this) / (1.0 - coef["total"] * far_total)
        from_outer = jnp.where(outermost, own, got)
        from_inner = jnp.where(outermost, got, own)
        between = (
            coef["den"] * from_inner + coef["den_end"] * from_outer + coef["den_link"] * middle
        )
        zero = jnp.zeros_like(own)
        centre = jnp.where(outermost, between, middle)
        outer = jnp.where(outermost, zero, from_outer + coef["outer"] * between)
        mate_star = got_star_ref[part, :]
        star_centre = jnp.where(outermost, mate_star, got_next_ref[1, part, :])
        star_outer = jnp.where(outermost, zero, mate_star)
        below, above = jnp.where(lower, outer, centre), jnp.where(lower, centre, outer)
        star_below = jnp.where(lower, star_outer, star_centre)
        star_above = jnp.where(lower, star_centre, star_outer)
        under = below - coef["first"] * star_below
        over = above + coef["last"] * star_above
        parts.append((below, above, under, over))
    return [[part[k] for part in parts] for k in range(4)]


def finish(count, levels, y_ref, q_ref, i_ref, ps_ref, x_ref, p_ref, column_refs, ready=None):
    lower, upper, under, over = boundary(count, *column_refs)

    def solved(level, above):
        value = tiles_of(y_ref, level, count)
        prod = tiles_of(q_ref, level, count)
        inv = tiles_of(i_ref, level, count)
        out = [(y + q * u) + i * a for y, q, u, i, a in zip(value, prod, lower, inv, above)]
        put_tiles(x_ref, level, out)
        return out

    def pressed(level, above, below):
        star = tiles_of(ps_ref, level, count)
        put_tiles(p_ref, level, [s - vert_coef * (a - b) for s, a, b in zip(star, above, below)])

    def step(index, carry):
        above, here = carry
        level = levels - 1 - index
        below = solved(level, here)
        pressed(jnp.minimum(level + 1, levels - 1), above, below)
        return [jnp.where(index == 0, o, h) for o, h in zip(over, here)], below

    share = levels // CHUNKS

    def chunk(c, carry):
        carry = levels_of(c, share, step, carry)
        if ready is not None:
            ready(c)
        return carry

    above, here = lax.fori_loop(0, CHUNKS, chunk, (over, upper))
    pressed(0, above, under)


def kernel_c(*refs):
    column_refs = refs[:COLUMN]
    y_ref, q_ref, i_ref, ps_ref, wx_ref, pw_ref, srows_ref, sinner_ref, souter_ref = refs[
        COLUMN : COLUMN + 9
    ]
    x_ref, p_ref, rows_ref, inner_ref, outer_ref, pp_ref = refs[COLUMN + 9 :]
    levels, rows, _ = y_ref.shape
    count = rows // ROWS
    edge = row_edge()
    ends = srows_ref[levels]
    finish(count, levels, y_ref, q_ref, i_ref, ps_ref, x_ref, p_ref, column_refs)

    def step(level, state):
        rows_ref[level] = edge.payload(
            both_ends(tiles_of(p_ref, level, count)),
            both_ends(tiles_of(wx_ref, level, count)),
            ends,
        )
        return state

    lax.fori_loop(0, levels, step, 0, unroll=UNROLL)
    pres = pack_levels(p_ref, count, levels)
    wind = tiles_of(pw_ref, 0, count), tiles_of(pw_ref, 1, count)
    slots = zip(
        *(
            get_pair(sinner_ref, souter_ref, 1, slice(ROWS * t, ROWS * (t + 1)))
            for t in range(count)
        )
    )
    down, up = lane_payload(pres, wind, list(slots))
    put_pair(inner_ref, outer_ref, 0, down, up)
    put_tiles(pp_ref, 0, pres[0])
    put_tiles(pp_ref, 1, pres[1])


def kernel_d(*refs):
    column_refs = refs[:COLUMN]
    y_ref, q_ref, i_ref, ps_ref, nx_ref, ny_ref = refs[COLUMN : COLUMN + 6]
    nx_hbm, ny_hbm, x_hbm, p_hbm, x_ref, p_ref, sems = refs[COLUMN + 6 :]
    levels, rows, _ = y_ref.shape
    share = levels // CHUNKS

    winds = [
        pltpu.make_async_copy(source, target, sems.at[2, k])
        for k, (source, target) in enumerate(((nx_ref, nx_hbm), (ny_ref, ny_hbm)))
    ]
    for wind in winds:
        wind.start()

    def copy(index, source, target, c):
        part = pl.ds(c * share, share)
        return pltpu.make_async_copy(source.at[part], target.at[part], sems.at[index, c])

    def ready(step):
        c = CHUNKS - 1 - step
        copy(0, x_ref, x_hbm, c).start()

        @pl.when(step > 0)
        def _():
            copy(1, p_ref, p_hbm, c + 1).start()

    finish(
        rows // ROWS,
        levels,
        y_ref,
        q_ref,
        i_ref,
        ps_ref,
        x_ref,
        p_ref,
        column_refs,
        ready,
    )
    copy(1, p_ref, p_hbm, 0).start()
    for c in range(CHUNKS):
        copy(0, x_ref, x_hbm, c).wait()
        copy(1, p_ref, p_hbm, c).wait()
    for wind in winds:
        wind.wait()


def call(kernel, name, shapes, *args, far_in=(), far_out=False, scratch=(), keep=()):
    near, far = pl.BlockSpec(memory_space=pltpu.VMEM), pl.BlockSpec(memory_space=pl.ANY)
    size = sum(a.size for a in args) + sum(functools.reduce(lambda a, b: a * b, s) for s in shapes)
    if len(far_in) == len(args):
        args = [pltpu.with_memory_space_constraint(a, pltpu.HBM) for a in args]
    return pl.pallas_call(
        kernel,
        out_shape=[
            pltpu.VMEM(s, jnp.float32) if k in keep else jax.ShapeDtypeStruct(s, jnp.float32)
            for k, s in enumerate(shapes)
        ],
        in_specs=[far if k in far_in else near for k in range(len(args))],
        out_specs=[far if far_out else near] * len(shapes),
        scratch_shapes=list(scratch),
        compiler_params=pltpu.CompilerParams(vmem_limit_bytes=32 * 1024 * 1024),
        cost_estimate=pl.CostEstimate(
            flops=8 * size, bytes_accessed=4 * size, transcendentals=0
        ),
        name=name,
    )(*args)


def swap(value, axis, partner):
    count = lax.axis_size(axis)
    return lax.ppermute(value, axis, [(i, partner(i)) for i in range(count)])


def exchange_rows(rows):
    count = lax.axis_size("gx")
    if count == 2:
        return swap(rows, "gx", lambda i: 1 - i)
    down = swap(rows[:, : ROWS // 2], "gx", lambda i: (i - 1) % count)
    up = swap(rows[:, ROWS // 2 :], "gx", lambda i: (i + 1) % count)
    return jnp.concatenate([down, up], axis=1)


def exchange_lanes(inner, outer):
    count = lax.axis_size("gy")
    got_inner = swap(inner, "gy", lambda i: i ^ 1)
    got_outer = swap(outer, "gy", lambda i: (i + 1 if i % 2 else i - 1) % count)
    return got_inner, got_outer


def exchange_column(following, cross, own, star, share):
    got_cross = swap(cross, "lev", lambda i: i ^ 2)
    got_next = swap(following, "lev", lambda i: i ^ 3)
    mates = [swap(value, "lev", lambda i: i ^ 1) for value in (own, star, share)]
    return [got_next, got_cross, *mates, own, share]


def local(wind_x, wind_y, wind_z, pressure, jacobian, slope_x, slope_y, stiffness):
    field = wind_x.shape
    levels, rows, lanes = field
    plane = (rows, lanes)
    pair = (2,) + plane
    assert lanes == 128 and levels * SLOT == 128 and rows % ROWS == 0
    assert lax.axis_size("lev") == 4 and lax.axis_size("gy") % 2 == 0

    edge, inner, outer, ends, rate, inv, prod, gain, stat, *fields = call(
        kernel_a,
        "start",
        [(levels + 1, ROWS, lanes), pair, (3,) + plane, pair]
        + [field] * 4
        + [(STATS,) + plane]
        + [field] * 3,
        pressure,
        wind_x,
        wind_y,
        jacobian,
        stiffness,
        far_in=(0, 1, 2, 3, 4),
        keep=(9, 10, 11),
        scratch=[
            pltpu.VMEM(plane, jnp.float32),
            pltpu.VMEM(field, jnp.float32),
            pltpu.SemaphoreType.DMA((4, CHUNKS)),
        ],
    )
    pressure, wind_x, wind_y = fields
    mate = swap(stat, "lev", lambda i: i ^ 1)
    coef, send = call(kernel_s, "pairs", [(len(PAIR_COEFS),) + plane, pair], stat, mate)
    far = swap(send, "lev", lambda i: i ^ 2)
    sent = (edge, inner, outer)
    got = (exchange_rows(edge),) + exchange_lanes(inner, outer)
    static_edges = sent + got
    for substep in range(SUBSTEPS):
        closed = call(
            kernel_m, "interior", [field, field, field], pressure, wind_x, wind_y, jacobian
        )
        wind_x, wind_y, star, value, *faces = call(
            kernel_b,
            "sweep",
            [field] * 4 + [pair] + [plane] * 4,
            pressure,
            *closed,
            wind_z,
            jacobian,
            slope_x,
            slope_y,
            rate,
            inv,
            gain,
            ends,
            *sent,
            *got,
            *static_edges,
            coef,
            far,
            keep=tuple(range(9)),
        )
        column = exchange_column(*faces) + [coef, far]
        if substep < SUBSTEPS - 1:
            (packed,) = call(kernel_n, "pack", [pair], wind_y)
            wind_z, pressure, edge, inner, outer, ends = call(
                kernel_c,
                "finish",
                [field, field, (levels, ROWS, lanes), (1,) + plane, pair, pair],
                *column,
                value,
                prod,
                inv,
                star,
                wind_x,
                packed,
                *static_edges[:3],
            )
            sent = (edge, inner, outer)
            got = (exchange_rows(edge),) + exchange_lanes(inner, outer)
        else:
            wind_x, wind_y, wind_z, pressure = call(
                kernel_d,
                "last",
                [field] * 4,
                *column,
                value,
                prod,
                inv,
                star,
                wind_x,
                wind_y,
                far_out=True,
                scratch=[
                    pltpu.VMEM(field, jnp.float32),
                    pltpu.VMEM(field, jnp.float32),
                    pltpu.SemaphoreType.DMA((3, CHUNKS)),
                ],
            )
    return wind_x, wind_y, wind_z, pressure


def solution(mesh):
    field = P("lev", "gx", "gy")
    column = P("gx", "gy")
    return jax.shard_map(
        local,
        mesh=mesh,
        in_specs=(field,) * 4 + (column,) * 3 + (field,),
        out_specs=(field,) * 4,
        check_vma=False,
    )
```

```python
import functools

import jax
import jax.numpy as jnp
from jax import lax
from jax.experimental import pallas as pl
from jax.experimental.pallas import tpu as pltpu
from jax.sharding import PartitionSpec as P

SUBSTEPS = 2

grad_coef = 0.35
div_coef = 0.35
vert_coef = 0.25

CG = grad_coef / 12.0
CD = div_coef / 12.0
ROWS = 8
SLOT = 4
UNROLL = 8
CHUNKS = 4
COLUMN = 9
STATS = 5


def lane_index():
    return lax.broadcasted_iota(jnp.int32, (ROWS, 128), 1)


def row_index():
    return lax.broadcasted_iota(jnp.int32, (ROWS, 128), 0)


def only(mask, value):
    return jnp.where(mask, jnp.float32(value), jnp.float32(0.0))


def tiles_of(ref, level, count):
    return [ref[level, ROWS * t : ROWS * (t + 1), :] for t in range(count)]


def planes_of(ref, count):
    return [ref[ROWS * t : ROWS * (t + 1), :] for t in range(count)]


def put_tiles(ref, level, tiles):
    for t, tile in enumerate(tiles):
        ref[level, ROWS * t : ROWS * (t + 1), :] = tile


def put_planes(ref, tiles):
    for t, tile in enumerate(tiles):
        ref[ROWS * t : ROWS * (t + 1), :] = tile


class Edge:
    def __init__(self, place, axis, held):
        self.place, self.axis, self.held = place, axis, held
        self.size = place.shape[axis]

    def at(self, places):
        total = None
        for position, value in places.items():
            if position in self.held:
                term = only(self.place == position, value)
                total = term if total is None else total + term
        return total

    def shifted(self, field, by):
        return field if by % self.size == 0 else pltpu.roll(field, (-by) % self.size, self.axis)

    def mix(self, field, table):
        total = None
        for by, places in table.items():
            weight = self.at(places)
            if weight is not None:
                term = weight * self.shifted(field, by)
                total = term if total is None else total + term
        return total

    def payload(self, pres, wind, jac):
        partial = self.mix(
            pres,
            {
                1: {0: 8.0, 1: 8.0, 6: 8.0},
                2: {0: -1.0, 1: -1.0},
                -1: {1: -8.0, 6: -8.0, 7: -8.0},
                -2: {6: 1.0, 7: 1.0},
            },
        )
        flux = jac * (wind - CG * partial)
        outer = self.mix(pres, {0: {0: 1.0, 1: 1.0, 6: 1.0, 7: 1.0}})
        return outer + self.mix(flux, {-2: {2: 1.0, 3: 1.0}, 2: {4: 1.0, 5: 1.0}})

    def correct(self, delta, pres, jac, delta_jac, base=0):
        grad = self.mix(
            delta,
            {
                base + 2: {0: 1.0, 1: 1.0},
                base + 3: {0: -8.0},
                base - 2: {6: -1.0, 7: -1.0},
                base - 3: {7: 8.0},
            },
        )
        wind = CG * grad
        own = -(jac * wind)
        far = self.mix(delta, {base: {0: 1.0, 1: 1.0, 6: 1.0, 7: 1.0}}) + CG * delta_jac * self.mix(
            pres, {0: {0: 1.0, 1: 1.0, 6: -1.0, 7: -1.0}, -1: {1: -8.0}, 1: {6: 8.0}}
        )
        spread = (
            self.mix(far, {0: {0: 1.0, 1: 1.0, 6: -1.0, 7: -1.0}})
            + self.mix(far - own, {1: {0: -8.0}, -1: {7: 8.0}})
            + self.mix(
                own,
                {
                    -1: {1: -8.0, 2: -8.0},
                    -2: {2: 1.0, 3: 1.0},
                    1: {5: 8.0, 6: 8.0},
                    2: {4: -1.0, 5: -1.0},
                },
            )
        )
        return wind, CD * spread / jac


LOW, HIGH = (0, 1, 2, 3), (4, 5, 6, 7)


def row_edge():
    return Edge(row_index(), 0, LOW + HIGH)


def lane_edge(held):
    return Edge((lane_index() & 3) + held[0], 1, held)


def both_ends(tiles):
    return jnp.where(row_index() < 4, tiles[0], tiles[-1])


def spread_slots(tile, low):
    lane = lane_index()
    if low:
        out = jnp.where(lane < SLOT, tile, 0.0)
    else:
        out = pltpu.roll(jnp.where(lane >= 128 - SLOT, tile, 0.0), SLOT, 1)
    for by in (SLOT, 4 * SLOT):
        out = (out + pltpu.roll(out, by, 1)) + (
            pltpu.roll(out, 2 * by, 1) + pltpu.roll(out, 3 * by, 1)
        )
    return out + pltpu.roll(out, 64, 1)


class Packer:
    def __init__(self, count):
        self.slot = lax.shift_right_logical(lane_index(), 2)
        self.start = [jnp.zeros((ROWS, 128), jnp.float32)] * (2 * count)
        self.count = count

    def add(self, level, tiles, state):
        before = lax.rem(level + 31, 32)
        rolled = [pltpu.roll(tile, SLOT * level, 1) for tile in tiles]
        low = [jnp.where(self.slot == level, r, s) for r, s in zip(rolled, state)]
        high = [jnp.where(self.slot == before, r, s) for r, s in zip(rolled, state[self.count :])]
        return low + high

    def done(self, state):
        return state[: self.count], [pltpu.roll(s, SLOT, 1) for s in state[self.count :]]


class Closed:
    def __init__(self):
        self.row = row_index()

    def along_y(self, tile):
        pair = tile - pltpu.roll(tile, 126, 1)
        return (pltpu.roll(pair, 2, 1) + pair) - 8.0 * pltpu.roll(pair, 1, 1)

    def moved(self, tiles, by):
        count = len(tiles)
        rolled = [pltpu.roll(tile, by % ROWS, 0) for tile in tiles]
        if by > 0:
            return [jnp.where(self.row < by, rolled[t - 1], rolled[t]) for t in range(count)]
        return [
            jnp.where(self.row >= ROWS + by, rolled[(t + 1) % count], rolled[t])
            for t in range(count)
        ]

    def along_x(self, tiles):
        pair = [f - m for f, m in zip(tiles, self.moved(tiles, -2))]
        return [
            (two + here) - 8.0 * one
            for two, here, one in zip(self.moved(pair, 2), pair, self.moved(pair, 1))
        ]


def even_place():
    return lax.rem(lax.axis_index("gy"), 2) == 0


def put_pair(inner_ref, outer_ref, index, down, up):
    even = even_place()
    put_tiles(inner_ref, index, [jnp.where(even, u, d) for u, d in zip(up, down)])
    put_tiles(outer_ref, index, [jnp.where(even, d, u) for u, d in zip(up, down)])


def get_pair(inner_ref, outer_ref, index, part):
    even = even_place()
    inner, outer = inner_ref[index, part, :], outer_ref[index, part, :]
    return jnp.where(even, outer, inner), jnp.where(even, inner, outer)


def lane_payload(pres, wind, jac):
    low, high = lane_edge(LOW), lane_edge(HIGH)
    down = [low.payload(p, w, j) for p, w, j in zip(pres[0], wind[0], jac[0])]
    up = [high.payload(p, w, j) for p, w, j in zip(pres[1], wind[1], jac[1])]
    return down, up


def levels_of(chunk, share, body, carry):
    for k in range(share):
        carry = body(chunk * share + k, carry)
    return carry


def pack_levels(ref, count, levels):
    packer = Packer(count)

    def step(level, state):
        return packer.add(level, tiles_of(ref, level, count), state)

    return packer.done(lax.fori_loop(0, levels, step, packer.start, unroll=UNROLL))


def kernel_a(
    p_hbm,
    wx_hbm,
    wy_hbm,
    jac_hbm,
    s_hbm,
    rows_ref,
    inner_ref,
    outer_ref,
    pp_ref,
    r_ref,
    i_ref,
    q_ref,
    v_ref,
    stat_ref,
    p_ref,
    wx_ref,
    wy_ref,
    jac_ref,
    s_ref,
    sems,
):
    levels, rows, _ = p_hbm.shape
    count = rows // ROWS
    share = levels // CHUNKS

    def fetch(source, target, sem):
        copy = pltpu.make_async_copy(source, target, sem)
        copy.start()
        return copy

    def chunk(index, source, target, c):
        part = pl.ds(c * share, share)
        return pltpu.make_async_copy(source.at[part], target.at[part], sems.at[index, c])

    for c in range(CHUNKS):
        chunk(0, p_hbm, p_ref, c).start()
        chunk(1, s_hbm, s_ref, c).start()
    for c in range(CHUNKS):
        chunk(2, wy_hbm, wy_ref, c).start()
    ends_in = [
        fetch(jac_hbm, jac_ref, sems.at[3, 0]),
        fetch(wx_hbm, wx_ref, sems.at[3, 1]),
    ]
    packer = Packer(count)

    def down(level, carry):
        state, excess, prod = carry[0], list(carry[1]), list(carry[2])
        for t in range(count):
            part = slice(ROWS * t, ROWS * (t + 1))
            rate = 1.0 / s_ref[level, part, :]
            grown = rate + excess[t]
            inv = 1.0 / (1.0 + grown)
            excess[t] = grown * inv
            prod[t] = prod[t] * inv
            r_ref[level, part, :] = rate
            i_ref[level, part, :] = inv
            q_ref[level, part, :] = prod[t]
        return packer.add(level, tiles_of(p_ref, level, count), state), excess, prod

    def up(step, carry):
        state, value = carry[0], list(carry[1])
        level = levels - 1 - step
        for t in range(count):
            part = slice(ROWS * t, ROWS * (t + 1))
            value[t] = q_ref[level, part, :] + i_ref[level, part, :] * value[t]
            v_ref[level, part, :] = value[t]
        return packer.add(step, tiles_of(wy_ref, step, count), state), value

    ones = [jnp.ones((ROWS, 128), jnp.float32)] * count

    def down_chunk(c, carry):
        chunk(0, p_hbm, p_ref, c).wait()
        chunk(1, s_hbm, s_ref, c).wait()
        return levels_of(c, share, down, carry)

    def up_chunk(c, carry):
        chunk(2, wy_hbm, wy_ref, c).wait()
        return levels_of(c, share, up, carry)

    carry = lax.fori_loop(0, CHUNKS, down_chunk, (packer.start, ones, ones))
    pres = packer.done(carry[0])
    zeros = [jnp.zeros_like(one) for one in ones]
    carry = lax.fori_loop(0, CHUNKS, up_chunk, (packer.start, zeros))
    wind = packer.done(carry[0])
    put_tiles(stat_ref, 0, carry[1])
    stat_ref[1] = q_ref[levels - 1]
    stat_ref[2] = i_ref[levels - 1]
    stat_ref[3] = r_ref[0]
    stat_ref[4] = r_ref[levels - 1]

    for copy in ends_in:
        copy.wait()
    jac = planes_of(jac_ref, count)
    ends = both_ends(jac)
    edge = row_edge()

    def step(level, state):
        rows_ref[level] = edge.payload(
            both_ends(tiles_of(p_ref, level, count)),
            both_ends(tiles_of(wx_ref, level, count)),
            ends,
        )
        return state

    lax.fori_loop(0, levels, step, 0, unroll=UNROLL)
    rows_ref[levels] = ends
    slots = [[spread_slots(j, low) for j in jac] for low in (True, False)]
    put_pair(inner_ref, outer_ref, 1, *slots)
    down_out, up_out = lane_payload(pres, wind, slots)
    put_pair(inner_ref, outer_ref, 0, down_out, up_out)
    put_tiles(pp_ref, 0, pres[0])
    put_tiles(pp_ref, 1, pres[1])


def kernel_n(wy_ref, pw_ref):
    levels, rows, _ = wy_ref.shape
    count = rows // ROWS
    wind = pack_levels(wy_ref, count, levels)
    put_tiles(pw_ref, 0, wind[0])
    put_tiles(pw_ref, 1, wind[1])


def kernel_m(p_ref, wx_ref, wy_ref, jac_ref, nx_ref, ny_ref, ps_ref):
    levels, rows, _ = p_ref.shape
    count = rows // ROWS
    jac = planes_of(jac_ref, count)
    inv_jac = [CD / j for j in jac]
    closed = Closed()

    def step(level, state):
        pres = tiles_of(p_ref, level, count)
        wind_x = tiles_of(wx_ref, level, count)
        wind_y = tiles_of(wy_ref, level, count)
        new_x = [w - CG * d for w, d in zip(wind_x, closed.along_x(pres))]
        new_y = [w - CG * closed.along_y(p) for w, p in zip(wind_y, pres)]
        put_tiles(nx_ref, level, new_x)
        put_tiles(ny_ref, level, new_y)
        spread_x = closed.along_x([j * n for j, n in zip(jac, new_x)])
        spread_y = [closed.along_y(j * n) for j, n in zip(jac, new_y)]
        put_tiles(
            ps_ref,
            level,
            [p - i * (x + y) for p, i, x, y in zip(pres, inv_jac, spread_x, spread_y)],
        )
        return state

    lax.fori_loop(0, levels, step, 0, unroll=UNROLL)


def kernel_b(
    p_ref,
    nxc_ref,
    nyc_ref,
    psc_ref,
    wz_ref,
    jac_ref,
    sx_ref,
    sy_ref,
    r_ref,
    i_ref,
    v_ref,
    pp_ref,
    rows_ref,
    inner_ref,
    outer_ref,
    got_rows_ref,
    got_inner_ref,
    got_outer_ref,
    srows_ref,
    sinner_ref,
    souter_ref,
    got_srows_ref,
    got_sinner_ref,
    got_souter_ref,
    coef_ref,
    far_ref,
    nx_ref,
    ny_ref,
    ps_ref,
    y_ref,
    *outs,
):
    levels, rows, _ = p_ref.shape
    count = rows // ROWS
    last = count - 1
    lane, row = lane_index(), row_index()
    low_edge, high_edge, edge = lane_edge(LOW), lane_edge(HIGH), row_edge()
    wind_fix, low_fix, high_fix = [], [], []
    for t in range(count):
        part = slice(ROWS * t, ROWS * (t + 1))
        jac_low, jac_high = get_pair(sinner_ref, souter_ref, 1, part)
        jac_below, jac_above = get_pair(got_sinner_ref, got_souter_ref, 1, part)
        down, up = get_pair(inner_ref, outer_ref, 0, part)
        below, above = get_pair(got_inner_ref, got_outer_ref, 0, part)
        low_wind, low_star = low_edge.correct(
            below - up, pp_ref[0, part, :], jac_low, low_edge.shifted(jac_below - jac_high, 2)
        )
        high_wind, high_star = high_edge.correct(
            above - down, pp_ref[1, part, :], jac_high, high_edge.shifted(jac_above - jac_low, -2)
        )
        wind_fix.append(low_wind + pltpu.roll(high_wind, 128 - SLOT, 1))
        low_fix.append(low_star)
        high_fix.append(pltpu.roll(high_star, 128 - SLOT, 1))
    ends = srows_ref[levels]
    change = got_srows_ref[levels] - ends
    ends_change = jnp.where(row < 4, edge.shifted(change, -2), edge.shifted(change, 2))
    outer = (lane < 2) | (lane >= 126)
    low_lanes, high_lanes = lane < SLOT, lane >= 128 - SLOT
    first_rows = row < 4

    def star(level, which):
        new_x = {t: nxc_ref[level, ROWS * t : ROWS * (t + 1), :] for t in which}
        stars = {t: psc_ref[level, ROWS * t : ROWS * (t + 1), :] for t in which}
        if 0 in which:
            wind, press = edge.correct(
                got_rows_ref[level] - rows_ref[level],
                jnp.where(first_rows, p_ref[level, :ROWS, :], p_ref[level, ROWS * last :, :]),
                ends,
                ends_change,
                base=4,
            )
            new_x[0] = new_x[0] - jnp.where(first_rows, wind, 0.0)
            new_x[last] = new_x[last] - jnp.where(first_rows, 0.0, wind)
            stars[0] = stars[0] - jnp.where(first_rows, press, 0.0)
            stars[last] = stars[last] - jnp.where(first_rows, 0.0, press)
        back = lax.rem(128 - SLOT * level, 128)
        forces = []
        for t in which:
            part = slice(ROWS * t, ROWS * (t + 1))
            new_y = nyc_ref[level, part, :] - jnp.where(
                outer, pltpu.roll(wind_fix[t], back, 1), 0.0
            )
            fix = jnp.where(
                low_lanes,
                pltpu.roll(low_fix[t], back, 1),
                jnp.where(high_lanes, pltpu.roll(high_fix[t], back, 1), 0.0),
            )
            stars[t] = stars[t] - fix
            forces.append(
                wz_ref[level, part, :] + sx_ref[part, :] * new_x[t] + sy_ref[part, :] * new_y
            )
            nx_ref[level, part, :] = new_x[t]
            ny_ref[level, part, :] = new_y
            ps_ref[level, part, :] = stars[t]
        return [stars[t] for t in which], forces

    def sweep(level, which, below, above, force, value, first):
        values, firsts = [], []
        for k, t in enumerate(which):
            part = slice(ROWS * t, ROWS * (t + 1))
            rhs = r_ref[level, part, :] * (force[k] - vert_coef * (above[k] - below[k]))
            firsts.append(first[k] + v_ref[level, part, :] * rhs)
            values.append((rhs + value[k]) * i_ref[level, part, :])
            y_ref[level, part, :] = values[k]
        return values, firsts

    which = tuple(range(count))
    put_tiles(y_ref, 0, [jnp.zeros((ROWS, 128), jnp.float32)] * count)
    zeros = tiles_of(y_ref, 0, count)

    def step(level, carry):
        below, here, force, value, first = carry
        above, force_next = star(level, which)
        before = jnp.maximum(level - 1, 0)
        new_value, new_first = sweep(before, which, below, above, force, value, first)
        started = jnp.where(level > 0, 1.0, 0.0)
        value = [started * n for n in new_value]
        first = [started * n for n in new_first]
        return here, above, force_next, value, first

    below, here, force, value, first = lax.fori_loop(
        0, levels, step, (zeros, zeros, zeros, zeros, zeros), unroll=UNROLL // 2
    )
    value, first = sweep(levels - 1, which, below, zeros, force, value, first)
    bottom = tiles_of(ps_ref, 0, count)
    interface(first, value, bottom, here, coef_ref, far_ref, outs)


PAIR_COEFS = ("own", "other", "den", "den_end", "den_link", "outer", "total", "facing", "first", "last")


def place_in_column():
    mine = lax.axis_index("lev")
    return (mine == 0) | (mine == 3), mine < 2, lax.rem(mine, 2) == 0


def kernel_s(stat_ref, mate_ref, coef_ref, send_ref):
    outermost, lower, even = place_in_column()
    for t in range(coef_ref.shape[1] // ROWS):
        part = slice(ROWS * t, ROWS * (t + 1))
        mine = [stat_ref[k, part, :] for k in range(STATS)]
        mate = [mate_ref[k, part, :] for k in range(STATS)]
        outer = [jnp.where(outermost, a, b) for a, b in zip(mine, mate)]
        inner = [jnp.where(outermost, b, a) for a, b in zip(mine, mate)]
        outer_end = jnp.where(lower, outer[2], outer[0])
        end = jnp.where(lower, inner[0], inner[2])
        centre = jnp.where(lower, inner[2], inner[0])
        link = inner[1]
        den = 1.0 / (1.0 - end * outer_end)
        den_link = den * link
        weight = outer_end * den_link
        one, zero = jnp.ones_like(den), jnp.zeros_like(den)
        coefs = dict(
            own=jnp.where(outermost, den_link, one),
            other=jnp.where(outermost, zero, weight),
            den=den,
            den_end=den * end,
            den_link=den_link,
            outer=outer_end,
            total=centre + weight * link,
            facing=vert_coef * jnp.where(even, mate[3], mate[4]),
            first=vert_coef * mine[3],
            last=vert_coef * mine[4],
        )
        for k, name in enumerate(PAIR_COEFS):
            coef_ref[k, part, :] = coefs[name]
        send_ref[0, part, :] = coefs["total"]
        send_ref[1, part, :] = vert_coef * jnp.where(lower, inner[4], inner[3])


def interface(first, value, star_first, star_last, coef_ref, far_ref, outs):
    next_ref, cross_ref, own_ref, star_ref, share_ref = outs
    outermost, lower, even = place_in_column()
    for t in range(len(first)):
        part = slice(ROWS * t, ROWS * (t + 1))
        coef = {name: coef_ref[k, part, :] for k, name in enumerate(PAIR_COEFS)}
        sign = jnp.where(lower, 1.0, -1.0)
        star_centre = jnp.where(lower, star_last[t], star_first[t])
        star_outer = jnp.where(lower, star_first[t], star_last[t])
        facing = jnp.where(outermost, coef["facing"], far_ref[1, part, :])
        centre = jnp.where(lower, value[t], first[t]) + sign * facing * star_centre
        outer = jnp.where(lower, first[t], value[t]) - sign * coef["facing"] * star_outer
        total = coef["own"] * centre + coef["other"] * outer
        next_ref[0, part, :] = total
        next_ref[1, part, :] = star_centre
        cross_ref[part, :] = total
        own_ref[part, :] = jnp.where(outermost, centre, outer)
        star_ref[part, :] = jnp.where(even, star_last[t], star_first[t])
        share_ref[part, :] = total


def boundary(
    count,
    got_next_ref,
    got_cross_ref,
    got_own_ref,
    got_star_ref,
    got_share_ref,
    own_ref,
    share_ref,
    coef_ref,
    far_ref,
):
    outermost, lower, _ = place_in_column()
    parts = []
    for t in range(count):
        part = slice(ROWS * t, ROWS * (t + 1))
        coef = {name: coef_ref[k, part, :] for k, name in enumerate(PAIR_COEFS)}
        far_total = far_ref[0, part, :]
        own, got = own_ref[part, :], got_own_ref[part, :]
        this = share_ref[part, :] + got_share_ref[part, :]
        that = got_cross_ref[part, :] + got_next_ref[0, part, :]
        middle = (that + far_total * this) / (1.0 - coef["total"] * far_total)
        from_outer = jnp.where(outermost, own, got)
        from_inner = jnp.where(outermost, got, own)
        between = (
            coef["den"] * from_inner + coef["den_end"] * from_outer + coef["den_link"] * middle
        )
        zero = jnp.zeros_like(own)
        centre = jnp.where(outermost, between, middle)
        outer = jnp.where(outermost, zero, from_outer + coef["outer"] * between)
        mate_star = got_star_ref[part, :]
        star_centre = jnp.where(outermost, mate_star, got_next_ref[1, part, :])
        star_outer = jnp.where(outermost, zero, mate_star)
        below, above = jnp.where(lower, outer, centre), jnp.where(lower, centre, outer)
        star_below = jnp.where(lower, star_outer, star_centre)
        star_above = jnp.where(lower, star_centre, star_outer)
        under = below - coef["first"] * star_below
        over = above + coef["last"] * star_above
        parts.append((below, above, under, over))
    return [[part[k] for part in parts] for k in range(4)]


def finish(count, levels, y_ref, q_ref, i_ref, ps_ref, x_ref, p_ref, column_refs, ready=None):
    lower, upper, under, over = boundary(count, *column_refs)

    def solved(level, above):
        value = tiles_of(y_ref, level, count)
        prod = tiles_of(q_ref, level, count)
        inv = tiles_of(i_ref, level, count)
        out = [(y + q * u) + i * a for y, q, u, i, a in zip(value, prod, lower, inv, above)]
        put_tiles(x_ref, level, out)
        return out

    def pressed(level, above, below):
        star = tiles_of(ps_ref, level, count)
        put_tiles(p_ref, level, [s - vert_coef * (a - b) for s, a, b in zip(star, above, below)])

    def step(index, carry):
        above, here = carry
        level = levels - 1 - index
        below = solved(level, here)
        pressed(jnp.minimum(level + 1, levels - 1), above, below)
        return [jnp.where(index == 0, o, h) for o, h in zip(over, here)], below

    share = levels // CHUNKS

    def chunk(c, carry):
        carry = levels_of(c, share, step, carry)
        if ready is not None:
            ready(c)
        return carry

    above, here = lax.fori_loop(0, CHUNKS, chunk, (over, upper))
    pressed(0, above, under)


def kernel_c(*refs):
    column_refs = refs[:COLUMN]
    y_ref, q_ref, i_ref, ps_ref, wx_ref, pw_ref, srows_ref, sinner_ref, souter_ref = refs[
        COLUMN : COLUMN + 9
    ]
    x_ref, p_ref, rows_ref, inner_ref, outer_ref, pp_ref = refs[COLUMN + 9 :]
    levels, rows, _ = y_ref.shape
    count = rows // ROWS
    edge = row_edge()
    ends = srows_ref[levels]
    finish(count, levels, y_ref, q_ref, i_ref, ps_ref, x_ref, p_ref, column_refs)

    def step(level, state):
        rows_ref[level] = edge.payload(
            both_ends(tiles_of(p_ref, level, count)),
            both_ends(tiles_of(wx_ref, level, count)),
            ends,
        )
        return state

    lax.fori_loop(0, levels, step, 0, unroll=UNROLL)
    pres = pack_levels(p_ref, count, levels)
    wind = tiles_of(pw_ref, 0, count), tiles_of(pw_ref, 1, count)
    slots = zip(
        *(
            get_pair(sinner_ref, souter_ref, 1, slice(ROWS * t, ROWS * (t + 1)))
            for t in range(count)
        )
    )
    down, up = lane_payload(pres, wind, list(slots))
    put_pair(inner_ref, outer_ref, 0, down, up)
    put_tiles(pp_ref, 0, pres[0])
    put_tiles(pp_ref, 1, pres[1])


def kernel_d(*refs):
    column_refs = refs[:COLUMN]
    y_ref, q_ref, i_ref, ps_ref = refs[COLUMN : COLUMN + 4]
    x_hbm, p_hbm, x_ref, p_ref, sems = refs[COLUMN + 4 :]
    levels, rows, _ = y_ref.shape
    share = levels // CHUNKS

    def copy(index, source, target, c):
        part = pl.ds(c * share, share)
        return pltpu.make_async_copy(source.at[part], target.at[part], sems.at[index, c])

    def ready(step):
        c = CHUNKS - 1 - step
        copy(0, x_ref, x_hbm, c).start()

        @pl.when(step > 0)
        def _():
            copy(1, p_ref, p_hbm, c + 1).start()

    finish(
        rows // ROWS,
        levels,
        y_ref,
        q_ref,
        i_ref,
        ps_ref,
        x_ref,
        p_ref,
        column_refs,
        ready,
    )
    copy(1, p_ref, p_hbm, 0).start()
    for c in range(CHUNKS):
        copy(0, x_ref, x_hbm, c).wait()
        copy(1, p_ref, p_hbm, c).wait()


def call(kernel, name, shapes, *args, far_in=(), far_out=False, scratch=(), keep=()):
    near, far = pl.BlockSpec(memory_space=pltpu.VMEM), pl.BlockSpec(memory_space=pl.ANY)
    size = sum(a.size for a in args) + sum(functools.reduce(lambda a, b: a * b, s) for s in shapes)
    if len(far_in) == len(args):
        args = [pltpu.with_memory_space_constraint(a, pltpu.HBM) for a in args]
    return pl.pallas_call(
        kernel,
        out_shape=[
            pltpu.VMEM(s, jnp.float32) if k in keep else jax.ShapeDtypeStruct(s, jnp.float32)
            for k, s in enumerate(shapes)
        ],
        in_specs=[far if k in far_in else near for k in range(len(args))],
        out_specs=[far if far_out else near] * len(shapes),
        scratch_shapes=list(scratch),
        compiler_params=pltpu.CompilerParams(vmem_limit_bytes=32 * 1024 * 1024),
        cost_estimate=pl.CostEstimate(
            flops=8 * size, bytes_accessed=4 * size, transcendentals=0
        ),
        name=name,
    )(*args)


def swap(value, axis, partner):
    count = lax.axis_size(axis)
    return lax.ppermute(value, axis, [(i, partner(i)) for i in range(count)])


def exchange_rows(rows):
    count = lax.axis_size("gx")
    if count == 2:
        return swap(rows, "gx", lambda i: 1 - i)
    down = swap(rows[:, : ROWS // 2], "gx", lambda i: (i - 1) % count)
    up = swap(rows[:, ROWS // 2 :], "gx", lambda i: (i + 1) % count)
    return jnp.concatenate([down, up], axis=1)


def exchange_lanes(inner, outer):
    count = lax.axis_size("gy")
    got_inner = swap(inner, "gy", lambda i: i ^ 1)
    got_outer = swap(outer, "gy", lambda i: (i + 1 if i % 2 else i - 1) % count)
    return got_inner, got_outer


def exchange_column(following, cross, own, star, share):
    got_cross = swap(cross, "lev", lambda i: i ^ 2)
    got_next = swap(following, "lev", lambda i: i ^ 3)
    mates = [swap(value, "lev", lambda i: i ^ 1) for value in (own, star, share)]
    return [got_next, got_cross, *mates, own, share]


def local(wind_x, wind_y, wind_z, pressure, jacobian, slope_x, slope_y, stiffness):
    field = wind_x.shape
    levels, rows, lanes = field
    plane = (rows, lanes)
    pair = (2,) + plane
    assert lanes == 128 and levels * SLOT == 128 and rows % ROWS == 0
    assert lax.axis_size("lev") == 4 and lax.axis_size("gy") % 2 == 0

    edge, inner, outer, ends, rate, inv, prod, gain, stat, *fields = call(
        kernel_a,
        "start",
        [(levels + 1, ROWS, lanes), pair, (3,) + plane, pair]
        + [field] * 4
        + [(STATS,) + plane]
        + [field] * 3,
        pressure,
        wind_x,
        wind_y,
        jacobian,
        stiffness,
        far_in=(0, 1, 2, 3, 4),
        keep=(9, 10, 11),
        scratch=[
            pltpu.VMEM(plane, jnp.float32),
            pltpu.VMEM(field, jnp.float32),
            pltpu.SemaphoreType.DMA((4, CHUNKS)),
        ],
    )
    pressure, wind_x, wind_y = fields
    mate = swap(stat, "lev", lambda i: i ^ 1)
    coef, send = call(kernel_s, "pairs", [(len(PAIR_COEFS),) + plane, pair], stat, mate)
    far = swap(send, "lev", lambda i: i ^ 2)
    sent = (edge, inner, outer)
    got = (exchange_rows(edge),) + exchange_lanes(inner, outer)
    static_edges = sent + got
    for substep in range(SUBSTEPS):
        closed = call(
            kernel_m, "interior", [field, field, field], pressure, wind_x, wind_y, jacobian
        )
        wind_x, wind_y, star, value, *faces = call(
            kernel_b,
            "sweep",
            [field] * 4 + [pair] + [plane] * 4,
            pressure,
            *closed,
            wind_z,
            jacobian,
            slope_x,
            slope_y,
            rate,
            inv,
            gain,
            ends,
            *sent,
            *got,
            *static_edges,
            coef,
            far,
            keep=tuple(range(9)),
        )
        column = exchange_column(*faces) + [coef, far]
        if substep < SUBSTEPS - 1:
            (packed,) = call(kernel_n, "pack", [pair], wind_y)
            wind_z, pressure, edge, inner, outer, ends = call(
                kernel_c,
                "finish",
                [field, field, (levels, ROWS, lanes), (1,) + plane, pair, pair],
                *column,
                value,
                prod,
                inv,
                star,
                wind_x,
                packed,
                *static_edges[:3],
            )
            sent = (edge, inner, outer)
            got = (exchange_rows(edge),) + exchange_lanes(inner, outer)
        else:
            wind_z, pressure = call(
                kernel_d,
                "last",
                [field] * 2,
                *column,
                value,
                prod,
                inv,
                star,
                far_out=True,
                scratch=[
                    pltpu.VMEM(field, jnp.float32),
                    pltpu.VMEM(field, jnp.float32),
                    pltpu.SemaphoreType.DMA((2, CHUNKS)),
                ],
            )
    return wind_x, wind_y, wind_z, pressure


def solution(mesh):
    field = P("lev", "gx", "gy")
    column = P("gx", "gy")
    return jax.shard_map(
        local,
        mesh=mesh,
        in_specs=(field,) * 4 + (column,) * 3 + (field,),
        out_specs=(field,) * 4,
        check_vma=False,
    )
```

```python
import functools

import jax
import jax.numpy as jnp
from jax import lax
from jax.experimental import pallas as pl
from jax.experimental.pallas import tpu as pltpu
from jax.sharding import PartitionSpec as P

SUBSTEPS = 2

grad_coef = 0.35
div_coef = 0.35
vert_coef = 0.25

CG = grad_coef / 12.0
CD = div_coef / 12.0
ROWS = 8
SLOT = 4
UNROLL = 8
CHUNKS = 4
COLUMN = 9
STATS = 5


def lane_index():
    return lax.broadcasted_iota(jnp.int32, (ROWS, 128), 1)


def row_index():
    return lax.broadcasted_iota(jnp.int32, (ROWS, 128), 0)


def only(mask, value):
    return jnp.where(mask, jnp.float32(value), jnp.float32(0.0))


def tiles_of(ref, level, count):
    return [ref[level, ROWS * t : ROWS * (t + 1), :] for t in range(count)]


def planes_of(ref, count):
    return [ref[ROWS * t : ROWS * (t + 1), :] for t in range(count)]


def put_tiles(ref, level, tiles):
    for t, tile in enumerate(tiles):
        ref[level, ROWS * t : ROWS * (t + 1), :] = tile


def put_planes(ref, tiles):
    for t, tile in enumerate(tiles):
        ref[ROWS * t : ROWS * (t + 1), :] = tile


class Edge:
    def __init__(self, place, axis, held):
        self.place, self.axis, self.held = place, axis, held
        self.size = place.shape[axis]

    def at(self, places):
        total = None
        for position, value in places.items():
            if position in self.held:
                term = only(self.place == position, value)
                total = term if total is None else total + term
        return total

    def shifted(self, field, by):
        return field if by % self.size == 0 else pltpu.roll(field, (-by) % self.size, self.axis)

    def mix(self, field, table):
        total = None
        for by, places in table.items():
            weight = self.at(places)
            if weight is not None:
                term = weight * self.shifted(field, by)
                total = term if total is None else total + term
        return total

    def payload(self, pres, wind, jac):
        partial = self.mix(
            pres,
            {
                1: {0: 8.0, 1: 8.0, 6: 8.0},
                2: {0: -1.0, 1: -1.0},
                -1: {1: -8.0, 6: -8.0, 7: -8.0},
                -2: {6: 1.0, 7: 1.0},
            },
        )
        flux = jac * (wind - CG * partial)
        outer = self.mix(pres, {0: {0: 1.0, 1: 1.0, 6: 1.0, 7: 1.0}})
        return outer + self.mix(flux, {-2: {2: 1.0, 3: 1.0}, 2: {4: 1.0, 5: 1.0}})

    def correct(self, delta, pres, jac, delta_jac, base=0):
        grad = self.mix(
            delta,
            {
                base + 2: {0: 1.0, 1: 1.0},
                base + 3: {0: -8.0},
                base - 2: {6: -1.0, 7: -1.0},
                base - 3: {7: 8.0},
            },
        )
        wind = CG * grad
        own = -(jac * wind)
        far = self.mix(delta, {base: {0: 1.0, 1: 1.0, 6: 1.0, 7: 1.0}}) + CG * delta_jac * self.mix(
            pres, {0: {0: 1.0, 1: 1.0, 6: -1.0, 7: -1.0}, -1: {1: -8.0}, 1: {6: 8.0}}
        )
        spread = (
            self.mix(far, {0: {0: 1.0, 1: 1.0, 6: -1.0, 7: -1.0}})
            + self.mix(far - own, {1: {0: -8.0}, -1: {7: 8.0}})
            + self.mix(
                own,
                {
                    -1: {1: -8.0, 2: -8.0},
                    -2: {2: 1.0, 3: 1.0},
                    1: {5: 8.0, 6: 8.0},
                    2: {4: -1.0, 5: -1.0},
                },
            )
        )
        return wind, CD * spread / jac


LOW, HIGH = (0, 1, 2, 3), (4, 5, 6, 7)


def row_edge():
    return Edge(row_index(), 0, LOW + HIGH)


def lane_edge(held):
    return Edge((lane_index() & 3) + held[0], 1, held)


def both_ends(tiles):
    return jnp.where(row_index() < 4, tiles[0], tiles[-1])


def spread_slots(tile, low):
    lane = lane_index()
    if low:
        out = jnp.where(lane < SLOT, tile, 0.0)
    else:
        out = pltpu.roll(jnp.where(lane >= 128 - SLOT, tile, 0.0), SLOT, 1)
    for by in (SLOT, 4 * SLOT):
        out = (out + pltpu.roll(out, by, 1)) + (
            pltpu.roll(out, 2 * by, 1) + pltpu.roll(out, 3 * by, 1)
        )
    return out + pltpu.roll(out, 64, 1)


class Packer:
    def __init__(self, count):
        self.slot = lax.shift_right_logical(lane_index(), 2)
        self.start = [jnp.zeros((ROWS, 128), jnp.float32)] * (2 * count)
        self.count = count

    def add(self, level, tiles, state):
        before = lax.rem(level + 31, 32)
        rolled = [pltpu.roll(tile, SLOT * level, 1) for tile in tiles]
        low = [jnp.where(self.slot == level, r, s) for r, s in zip(rolled, state)]
        high = [jnp.where(self.slot == before, r, s) for r, s in zip(rolled, state[self.count :])]
        return low + high

    def done(self, state):
        return state[: self.count], [pltpu.roll(s, SLOT, 1) for s in state[self.count :]]


class Closed:
    def __init__(self):
        self.row = row_index()

    def along_y(self, tile):
        pair = tile - pltpu.roll(tile, 126, 1)
        return (pltpu.roll(pair, 2, 1) + pair) - 8.0 * pltpu.roll(pair, 1, 1)

    def moved(self, tiles, by):
        count = len(tiles)
        rolled = [pltpu.roll(tile, by % ROWS, 0) for tile in tiles]
        if by > 0:
            return [jnp.where(self.row < by, rolled[t - 1], rolled[t]) for t in range(count)]
        return [
            jnp.where(self.row >= ROWS + by, rolled[(t + 1) % count], rolled[t])
            for t in range(count)
        ]

    def along_x(self, tiles):
        pair = [f - m for f, m in zip(tiles, self.moved(tiles, -2))]
        return [
            (two + here) - 8.0 * one
            for two, here, one in zip(self.moved(pair, 2), pair, self.moved(pair, 1))
        ]


def even_place():
    return lax.rem(lax.axis_index("gy"), 2) == 0


def put_pair(inner_ref, outer_ref, index, down, up):
    even = even_place()
    put_tiles(inner_ref, index, [jnp.where(even, u, d) for u, d in zip(up, down)])
    put_tiles(outer_ref, index, [jnp.where(even, d, u) for u, d in zip(up, down)])


def get_pair(inner_ref, outer_ref, index, part):
    even = even_place()
    inner, outer = inner_ref[index, part, :], outer_ref[index, part, :]
    return jnp.where(even, outer, inner), jnp.where(even, inner, outer)


def lane_payload(pres, wind, jac):
    low, high = lane_edge(LOW), lane_edge(HIGH)
    down = [low.payload(p, w, j) for p, w, j in zip(pres[0], wind[0], jac[0])]
    up = [high.payload(p, w, j) for p, w, j in zip(pres[1], wind[1], jac[1])]
    return down, up


def levels_of(chunk, share, body, carry):
    for k in range(share):
        carry = body(chunk * share + k, carry)
    return carry


def pack_levels(ref, count, levels):
    packer = Packer(count)

    def step(level, state):
        return packer.add(level, tiles_of(ref, level, count), state)

    return packer.done(lax.fori_loop(0, levels, step, packer.start, unroll=UNROLL))


def kernel_a(
    p_hbm,
    wx_hbm,
    wy_hbm,
    jac_hbm,
    s_hbm,
    rows_ref,
    inner_ref,
    outer_ref,
    pp_ref,
    r_ref,
    i_ref,
    q_ref,
    v_ref,
    stat_ref,
    p_ref,
    wx_ref,
    wy_ref,
    jac_ref,
    s_ref,
    sems,
):
    levels, rows, _ = p_hbm.shape
    count = rows // ROWS
    share = levels // CHUNKS

    def fetch(source, target, sem):
        copy = pltpu.make_async_copy(source, target, sem)
        copy.start()
        return copy

    def chunk(index, source, target, c):
        part = pl.ds(c * share, share)
        return pltpu.make_async_copy(source.at[part], target.at[part], sems.at[index, c])

    for c in range(CHUNKS):
        chunk(0, p_hbm, p_ref, c).start()
        chunk(1, s_hbm, s_ref, c).start()
    for c in range(CHUNKS):
        chunk(2, wy_hbm, wy_ref, c).start()
    ends_in = [
        fetch(jac_hbm, jac_ref, sems.at[3, 0]),
        fetch(wx_hbm, wx_ref, sems.at[3, 1]),
    ]
    packer = Packer(count)

    def down(level, carry):
        state, excess, prod = carry[0], list(carry[1]), list(carry[2])
        for t in range(count):
            part = slice(ROWS * t, ROWS * (t + 1))
            rate = 1.0 / s_ref[level, part, :]
            grown = rate + excess[t]
            inv = 1.0 / (1.0 + grown)
            excess[t] = grown * inv
            prod[t] = prod[t] * inv
            r_ref[level, part, :] = rate
            i_ref[level, part, :] = inv
            q_ref[level, part, :] = prod[t]
        return packer.add(level, tiles_of(p_ref, level, count), state), excess, prod

    def up(step, carry):
        state, value = carry[0], list(carry[1])
        level = levels - 1 - step
        for t in range(count):
            part = slice(ROWS * t, ROWS * (t + 1))
            value[t] = q_ref[level, part, :] + i_ref[level, part, :] * value[t]
            v_ref[level, part, :] = value[t]
        return packer.add(step, tiles_of(wy_ref, step, count), state), value

    ones = [jnp.ones((ROWS, 128), jnp.float32)] * count

    def down_chunk(c, carry):
        chunk(0, p_hbm, p_ref, c).wait()
        chunk(1, s_hbm, s_ref, c).wait()
        return levels_of(c, share, down, carry)

    def up_chunk(c, carry):
        chunk(2, wy_hbm, wy_ref, c).wait()
        return levels_of(c, share, up, carry)

    carry = lax.fori_loop(0, CHUNKS, down_chunk, (packer.start, ones, ones))
    pres = packer.done(carry[0])
    zeros = [jnp.zeros_like(one) for one in ones]
    carry = lax.fori_loop(0, CHUNKS, up_chunk, (packer.start, zeros))
    wind = packer.done(carry[0])
    put_tiles(stat_ref, 0, carry[1])
    stat_ref[1] = q_ref[levels - 1]
    stat_ref[2] = i_ref[levels - 1]
    stat_ref[3] = r_ref[0]
    stat_ref[4] = r_ref[levels - 1]

    for copy in ends_in:
        copy.wait()
    jac = planes_of(jac_ref, count)
    ends = both_ends(jac)
    edge = row_edge()

    def step(level, state):
        rows_ref[level] = edge.payload(
            both_ends(tiles_of(p_ref, level, count)),
            both_ends(tiles_of(wx_ref, level, count)),
            ends,
        )
        return state

    lax.fori_loop(0, levels, step, 0, unroll=UNROLL)
    rows_ref[levels] = ends
    slots = [[spread_slots(j, low) for j in jac] for low in (True, False)]
    put_pair(inner_ref, outer_ref, 1, *slots)
    down_out, up_out = lane_payload(pres, wind, slots)
    put_pair(inner_ref, outer_ref, 0, down_out, up_out)
    put_tiles(pp_ref, 0, pres[0])
    put_tiles(pp_ref, 1, pres[1])


def kernel_n(wy_ref, pw_ref):
    levels, rows, _ = wy_ref.shape
    count = rows // ROWS
    wind = pack_levels(wy_ref, count, levels)
    put_tiles(pw_ref, 0, wind[0])
    put_tiles(pw_ref, 1, wind[1])


def kernel_m(p_ref, wx_ref, wy_ref, jac_ref, nx_ref, ny_ref, ps_ref):
    levels, rows, _ = p_ref.shape
    count = rows // ROWS
    jac = planes_of(jac_ref, count)
    inv_jac = [CD / j for j in jac]
    closed = Closed()

    def step(level, state):
        pres = tiles_of(p_ref, level, count)
        wind_x = tiles_of(wx_ref, level, count)
        wind_y = tiles_of(wy_ref, level, count)
        new_x = [w - CG * d for w, d in zip(wind_x, closed.along_x(pres))]
        new_y = [w - CG * closed.along_y(p) for w, p in zip(wind_y, pres)]
        put_tiles(nx_ref, level, new_x)
        put_tiles(ny_ref, level, new_y)
        spread_x = closed.along_x([j * n for j, n in zip(jac, new_x)])
        spread_y = [closed.along_y(j * n) for j, n in zip(jac, new_y)]
        put_tiles(
            ps_ref,
            level,
            [p - i * (x + y) for p, i, x, y in zip(pres, inv_jac, spread_x, spread_y)],
        )
        return state

    lax.fori_loop(0, levels, step, 0, unroll=UNROLL)


def kernel_b(
    p_ref,
    nxc_ref,
    nyc_ref,
    psc_ref,
    wz_ref,
    jac_ref,
    sx_ref,
    sy_ref,
    r_ref,
    i_ref,
    v_ref,
    pp_ref,
    rows_ref,
    inner_ref,
    outer_ref,
    got_rows_ref,
    got_inner_ref,
    got_outer_ref,
    srows_ref,
    sinner_ref,
    souter_ref,
    got_srows_ref,
    got_sinner_ref,
    got_souter_ref,
    coef_ref,
    far_ref,
    nx_ref,
    ny_ref,
    ps_ref,
    y_ref,
    *outs,
):
    levels, rows, _ = p_ref.shape
    count = rows // ROWS
    last = count - 1
    lane, row = lane_index(), row_index()
    low_edge, high_edge, edge = lane_edge(LOW), lane_edge(HIGH), row_edge()
    wind_fix, low_fix, high_fix = [], [], []
    for t in range(count):
        part = slice(ROWS * t, ROWS * (t + 1))
        jac_low, jac_high = get_pair(sinner_ref, souter_ref, 1, part)
        jac_below, jac_above = get_pair(got_sinner_ref, got_souter_ref, 1, part)
        down, up = get_pair(inner_ref, outer_ref, 0, part)
        below, above = get_pair(got_inner_ref, got_outer_ref, 0, part)
        low_wind, low_star = low_edge.correct(
            below - up, pp_ref[0, part, :], jac_low, low_edge.shifted(jac_below - jac_high, 2)
        )
        high_wind, high_star = high_edge.correct(
            above - down, pp_ref[1, part, :], jac_high, high_edge.shifted(jac_above - jac_low, -2)
        )
        wind_fix.append(low_wind + pltpu.roll(high_wind, 128 - SLOT, 1))
        low_fix.append(low_star)
        high_fix.append(pltpu.roll(high_star, 128 - SLOT, 1))
    ends = srows_ref[levels]
    change = got_srows_ref[levels] - ends
    ends_change = jnp.where(row < 4, edge.shifted(change, -2), edge.shifted(change, 2))
    outer = (lane < 2) | (lane >= 126)
    low_lanes, high_lanes = lane < SLOT, lane >= 128 - SLOT
    first_rows = row < 4

    def star(level, which):
        new_x = {t: nxc_ref[level, ROWS * t : ROWS * (t + 1), :] for t in which}
        stars = {t: psc_ref[level, ROWS * t : ROWS * (t + 1), :] for t in which}
        if 0 in which:
            wind, press = edge.correct(
                got_rows_ref[level] - rows_ref[level],
                jnp.where(first_rows, p_ref[level, :ROWS, :], p_ref[level, ROWS * last :, :]),
                ends,
                ends_change,
                base=4,
            )
            new_x[0] = new_x[0] - jnp.where(first_rows, wind, 0.0)
            new_x[last] = new_x[last] - jnp.where(first_rows, 0.0, wind)
            stars[0] = stars[0] - jnp.where(first_rows, press, 0.0)
            stars[last] = stars[last] - jnp.where(first_rows, 0.0, press)
        back = lax.rem(128 - SLOT * level, 128)
        forces = []
        for t in which:
            part = slice(ROWS * t, ROWS * (t + 1))
            new_y = nyc_ref[level, part, :] - jnp.where(
                outer, pltpu.roll(wind_fix[t], back, 1), 0.0
            )
            fix = jnp.where(
                low_lanes,
                pltpu.roll(low_fix[t], back, 1),
                jnp.where(high_lanes, pltpu.roll(high_fix[t], back, 1), 0.0),
            )
            stars[t] = stars[t] - fix
            forces.append(
                wz_ref[level, part, :] + sx_ref[part, :] * new_x[t] + sy_ref[part, :] * new_y
            )
            nx_ref[level, part, :] = new_x[t]
            ny_ref[level, part, :] = new_y
            ps_ref[level, part, :] = stars[t]
        return [stars[t] for t in which], forces

    def sweep(level, which, below, above, force, value, first):
        values, firsts = [], []
        for k, t in enumerate(which):
            part = slice(ROWS * t, ROWS * (t + 1))
            rhs = r_ref[level, part, :] * (force[k] - vert_coef * (above[k] - below[k]))
            firsts.append(first[k] + v_ref[level, part, :] * rhs)
            values.append((rhs + value[k]) * i_ref[level, part, :])
            y_ref[level, part, :] = values[k]
        return values, firsts

    which = tuple(range(count))
    put_tiles(y_ref, 0, [jnp.zeros((ROWS, 128), jnp.float32)] * count)
    zeros = tiles_of(y_ref, 0, count)

    def step(level, carry):
        below, here, force, value, first = carry
        above, force_next = star(level, which)
        before = jnp.maximum(level - 1, 0)
        new_value, new_first = sweep(before, which, below, above, force, value, first)
        started = jnp.where(level > 0, 1.0, 0.0)
        value = [started * n for n in new_value]
        first = [started * n for n in new_first]
        return here, above, force_next, value, first

    below, here, force, value, first = lax.fori_loop(
        0, levels, step, (zeros, zeros, zeros, zeros, zeros), unroll=UNROLL
    )
    value, first = sweep(levels - 1, which, below, zeros, force, value, first)
    bottom = tiles_of(ps_ref, 0, count)
    interface(first, value, bottom, here, coef_ref, far_ref, outs)


PAIR_COEFS = ("own", "other", "den", "den_end", "den_link", "outer", "total", "facing", "first", "last")


def place_in_column():
    mine = lax.axis_index("lev")
    return (mine == 0) | (mine == 3), mine < 2, lax.rem(mine, 2) == 0


def kernel_s(stat_ref, mate_ref, coef_ref, send_ref):
    outermost, lower, even = place_in_column()
    for t in range(coef_ref.shape[1] // ROWS):
        part = slice(ROWS * t, ROWS * (t + 1))
        mine = [stat_ref[k, part, :] for k in range(STATS)]
        mate = [mate_ref[k, part, :] for k in range(STATS)]
        outer = [jnp.where(outermost, a, b) for a, b in zip(mine, mate)]
        inner = [jnp.where(outermost, b, a) for a, b in zip(mine, mate)]
        outer_end = jnp.where(lower, outer[2], outer[0])
        end = jnp.where(lower, inner[0], inner[2])
        centre = jnp.where(lower, inner[2], inner[0])
        link = inner[1]
        den = 1.0 / (1.0 - end * outer_end)
        den_link = den * link
        weight = outer_end * den_link
        one, zero = jnp.ones_like(den), jnp.zeros_like(den)
        coefs = dict(
            own=jnp.where(outermost, den_link, one),
            other=jnp.where(outermost, zero, weight),
            den=den,
            den_end=den * end,
            den_link=den_link,
            outer=outer_end,
            total=centre + weight * link,
            facing=vert_coef * jnp.where(even, mate[3], mate[4]),
            first=vert_coef * mine[3],
            last=vert_coef * mine[4],
        )
        for k, name in enumerate(PAIR_COEFS):
            coef_ref[k, part, :] = coefs[name]
        send_ref[0, part, :] = coefs["total"]
        send_ref[1, part, :] = vert_coef * jnp.where(lower, inner[4], inner[3])


def interface(first, value, star_first, star_last, coef_ref, far_ref, outs):
    next_ref, cross_ref, own_ref, star_ref, share_ref = outs
    outermost, lower, even = place_in_column()
    for t in range(len(first)):
        part = slice(ROWS * t, ROWS * (t + 1))
        coef = {name: coef_ref[k, part, :] for k, name in enumerate(PAIR_COEFS)}
        sign = jnp.where(lower, 1.0, -1.0)
        star_centre = jnp.where(lower, star_last[t], star_first[t])
        star_outer = jnp.where(lower, star_first[t], star_last[t])
        facing = jnp.where(outermost, coef["facing"], far_ref[1, part, :])
        centre = jnp.where(lower, value[t], first[t]) + sign * facing * star_centre
        outer = jnp.where(lower, first[t], value[t]) - sign * coef["facing"] * star_outer
        total = coef["own"] * centre + coef["other"] * outer
        next_ref[0, part, :] = total
        next_ref[1, part, :] = star_centre
        cross_ref[part, :] = total
        own_ref[part, :] = jnp.where(outermost, centre, outer)
        star_ref[part, :] = jnp.where(even, star_last[t], star_first[t])
        share_ref[part, :] = total


def boundary(
    count,
    got_next_ref,
    got_cross_ref,
    got_own_ref,
    got_star_ref,
    got_share_ref,
    own_ref,
    share_ref,
    coef_ref,
    far_ref,
):
    outermost, lower, _ = place_in_column()
    parts = []
    for t in range(count):
        part = slice(ROWS * t, ROWS * (t + 1))
        coef = {name: coef_ref[k, part, :] for k, name in enumerate(PAIR_COEFS)}
        far_total = far_ref[0, part, :]
        own, got = own_ref[part, :], got_own_ref[part, :]
        this = share_ref[part, :] + got_share_ref[part, :]
        that = got_cross_ref[part, :] + got_next_ref[0, part, :]
        middle = (that + far_total * this) / (1.0 - coef["total"] * far_total)
        from_outer = jnp.where(outermost, own, got)
        from_inner = jnp.where(outermost, got, own)
        between = (
            coef["den"] * from_inner + coef["den_end"] * from_outer + coef["den_link"] * middle
        )
        zero = jnp.zeros_like(own)
        centre = jnp.where(outermost, between, middle)
        outer = jnp.where(outermost, zero, from_outer + coef["outer"] * between)
        mate_star = got_star_ref[part, :]
        star_centre = jnp.where(outermost, mate_star, got_next_ref[1, part, :])
        star_outer = jnp.where(outermost, zero, mate_star)
        below, above = jnp.where(lower, outer, centre), jnp.where(lower, centre, outer)
        star_below = jnp.where(lower, star_outer, star_centre)
        star_above = jnp.where(lower, star_centre, star_outer)
        under = below - coef["first"] * star_below
        over = above + coef["last"] * star_above
        parts.append((below, above, under, over))
    return [[part[k] for part in parts] for k in range(4)]


def finish(count, levels, y_ref, q_ref, i_ref, ps_ref, x_ref, p_ref, column_refs, ready=None):
    lower, upper, under, over = boundary(count, *column_refs)

    def solved(level, above):
        value = tiles_of(y_ref, level, count)
        prod = tiles_of(q_ref, level, count)
        inv = tiles_of(i_ref, level, count)
        out = [(y + q * u) + i * a for y, q, u, i, a in zip(value, prod, lower, inv, above)]
        put_tiles(x_ref, level, out)
        return out

    def pressed(level, above, below):
        star = tiles_of(ps_ref, level, count)
        put_tiles(p_ref, level, [s - vert_coef * (a - b) for s, a, b in zip(star, above, below)])

    def step(index, carry):
        above, here = carry
        level = levels - 1 - index
        below = solved(level, here)
        pressed(jnp.minimum(level + 1, levels - 1), above, below)
        return [jnp.where(index == 0, o, h) for o, h in zip(over, here)], below

    share = levels // CHUNKS

    def chunk(c, carry):
        carry = levels_of(c, share, step, carry)
        if ready is not None:
            ready(c)
        return carry

    above, here = lax.fori_loop(0, CHUNKS, chunk, (over, upper))
    pressed(0, above, under)


def kernel_c(*refs):
    column_refs = refs[:COLUMN]
    y_ref, q_ref, i_ref, ps_ref, wx_ref, pw_ref, srows_ref, sinner_ref, souter_ref = refs[
        COLUMN : COLUMN + 9
    ]
    x_ref, p_ref, rows_ref, inner_ref, outer_ref, pp_ref = refs[COLUMN + 9 :]
    levels, rows, _ = y_ref.shape
    count = rows // ROWS
    edge = row_edge()
    ends = srows_ref[levels]
    finish(count, levels, y_ref, q_ref, i_ref, ps_ref, x_ref, p_ref, column_refs)

    def step(level, state):
        rows_ref[level] = edge.payload(
            both_ends(tiles_of(p_ref, level, count)),
            both_ends(tiles_of(wx_ref, level, count)),
            ends,
        )
        return state

    lax.fori_loop(0, levels, step, 0, unroll=UNROLL)
    pres = pack_levels(p_ref, count, levels)
    wind = tiles_of(pw_ref, 0, count), tiles_of(pw_ref, 1, count)
    slots = zip(
        *(
            get_pair(sinner_ref, souter_ref, 1, slice(ROWS * t, ROWS * (t + 1)))
            for t in range(count)
        )
    )
    down, up = lane_payload(pres, wind, list(slots))
    put_pair(inner_ref, outer_ref, 0, down, up)
    put_tiles(pp_ref, 0, pres[0])
    put_tiles(pp_ref, 1, pres[1])


def kernel_d(*refs):
    column_refs = refs[:COLUMN]
    y_ref, q_ref, i_ref, ps_ref = refs[COLUMN : COLUMN + 4]
    x_hbm, p_hbm, x_ref, p_ref, sems = refs[COLUMN + 4 :]
    levels, rows, _ = y_ref.shape
    share = levels // CHUNKS

    def copy(index, source, target, c):
        part = pl.ds(c * share, share)
        return pltpu.make_async_copy(source.at[part], target.at[part], sems.at[index, c])

    def ready(step):
        c = CHUNKS - 1 - step
        copy(0, x_ref, x_hbm, c).start()

        @pl.when(step > 0)
        def _():
            copy(1, p_ref, p_hbm, c + 1).start()

    finish(
        rows // ROWS,
        levels,
        y_ref,
        q_ref,
        i_ref,
        ps_ref,
        x_ref,
        p_ref,
        column_refs,
        ready,
    )
    copy(1, p_ref, p_hbm, 0).start()
    for c in range(CHUNKS):
        copy(0, x_ref, x_hbm, c).wait()
        copy(1, p_ref, p_hbm, c).wait()


def call(kernel, name, shapes, *args, far_in=(), far_out=False, scratch=(), keep=()):
    near, far = pl.BlockSpec(memory_space=pltpu.VMEM), pl.BlockSpec(memory_space=pl.ANY)
    size = sum(a.size for a in args) + sum(functools.reduce(lambda a, b: a * b, s) for s in shapes)
    if len(far_in) == len(args):
        args = [pltpu.with_memory_space_constraint(a, pltpu.HBM) for a in args]
    return pl.pallas_call(
        kernel,
        out_shape=[
            pltpu.VMEM(s, jnp.float32) if k in keep else jax.ShapeDtypeStruct(s, jnp.float32)
            for k, s in enumerate(shapes)
        ],
        in_specs=[far if k in far_in else near for k in range(len(args))],
        out_specs=[far if far_out else near] * len(shapes),
        scratch_shapes=list(scratch),
        compiler_params=pltpu.CompilerParams(vmem_limit_bytes=32 * 1024 * 1024),
        cost_estimate=pl.CostEstimate(
            flops=8 * size, bytes_accessed=4 * size, transcendentals=0
        ),
        name=name,
    )(*args)


def swap(value, axis, partner):
    count = lax.axis_size(axis)
    return lax.ppermute(value, axis, [(i, partner(i)) for i in range(count)])


def exchange_rows(rows):
    count = lax.axis_size("gx")
    if count == 2:
        return swap(rows, "gx", lambda i: 1 - i)
    down = swap(rows[:, : ROWS // 2], "gx", lambda i: (i - 1) % count)
    up = swap(rows[:, ROWS // 2 :], "gx", lambda i: (i + 1) % count)
    return jnp.concatenate([down, up], axis=1)


def exchange_lanes(inner, outer):
    count = lax.axis_size("gy")
    got_inner = swap(inner, "gy", lambda i: i ^ 1)
    got_outer = swap(outer, "gy", lambda i: (i + 1 if i % 2 else i - 1) % count)
    return got_inner, got_outer


def exchange_column(following, cross, own, star, share):
    got_cross = swap(cross, "lev", lambda i: i ^ 2)
    got_next = swap(following, "lev", lambda i: i ^ 3)
    mates = [swap(value, "lev", lambda i: i ^ 1) for value in (own, star, share)]
    return [got_next, got_cross, *mates, own, share]


def local(wind_x, wind_y, wind_z, pressure, jacobian, slope_x, slope_y, stiffness):
    field = wind_x.shape
    levels, rows, lanes = field
    plane = (rows, lanes)
    pair = (2,) + plane
    assert lanes == 128 and levels * SLOT == 128 and rows % ROWS == 0
    assert lax.axis_size("lev") == 4 and lax.axis_size("gy") % 2 == 0

    edge, inner, outer, ends, rate, inv, prod, gain, stat, *fields = call(
        kernel_a,
        "start",
        [(levels + 1, ROWS, lanes), pair, (3,) + plane, pair]
        + [field] * 4
        + [(STATS,) + plane]
        + [field] * 3,
        pressure,
        wind_x,
        wind_y,
        jacobian,
        stiffness,
        far_in=(0, 1, 2, 3, 4),
        keep=(9, 10, 11),
        scratch=[
            pltpu.VMEM(plane, jnp.float32),
            pltpu.VMEM(field, jnp.float32),
            pltpu.SemaphoreType.DMA((4, CHUNKS)),
        ],
    )
    pressure, wind_x, wind_y = fields
    mate = swap(stat, "lev", lambda i: i ^ 1)
    coef, send = call(kernel_s, "pairs", [(len(PAIR_COEFS),) + plane, pair], stat, mate)
    far = swap(send, "lev", lambda i: i ^ 2)
    sent = (edge, inner, outer)
    got = (exchange_rows(edge),) + exchange_lanes(inner, outer)
    static_edges = sent + got
    for substep in range(SUBSTEPS):
        closed = call(
            kernel_m, "interior", [field, field, field], pressure, wind_x, wind_y, jacobian
        )
        wind_x, wind_y, star, value, *faces = call(
            kernel_b,
            "sweep",
            [field] * 4 + [pair] + [plane] * 4,
            pressure,
            *closed,
            wind_z,
            jacobian,
            slope_x,
            slope_y,
            rate,
            inv,
            gain,
            ends,
            *sent,
            *got,
            *static_edges,
            coef,
            far,
            keep=tuple(range(9)),
        )
        column = exchange_column(*faces) + [coef, far]
        if substep < SUBSTEPS - 1:
            (packed,) = call(kernel_n, "pack", [pair], wind_y)
            wind_z, pressure, edge, inner, outer, ends = call(
                kernel_c,
                "finish",
                [field, field, (levels, ROWS, lanes), (1,) + plane, pair, pair],
                *column,
                value,
                prod,
                inv,
                star,
                wind_x,
                packed,
                *static_edges[:3],
            )
            sent = (edge, inner, outer)
            got = (exchange_rows(edge),) + exchange_lanes(inner, outer)
        else:
            wind_z, pressure = call(
                kernel_d,
                "last",
                [field] * 2,
                *column,
                value,
                prod,
                inv,
                star,
                far_out=True,
                scratch=[
                    pltpu.VMEM(field, jnp.float32),
                    pltpu.VMEM(field, jnp.float32),
                    pltpu.SemaphoreType.DMA((2, CHUNKS)),
                ],
            )
    return wind_x, wind_y, wind_z, pressure


def solution(mesh):
    field = P("lev", "gx", "gy")
    column = P("gx", "gy")
    return jax.shard_map(
        local,
        mesh=mesh,
        in_specs=(field,) * 4 + (column,) * 3 + (field,),
        out_specs=(field,) * 4,
        check_vma=False,
    )
```

```python
import functools

import jax
import jax.numpy as jnp
from jax import lax
from jax.experimental import pallas as pl
from jax.experimental.pallas import tpu as pltpu
from jax.sharding import PartitionSpec as P

SUBSTEPS = 2

grad_coef = 0.35
div_coef = 0.35
vert_coef = 0.25

CG = grad_coef / 12.0
CD = div_coef / 12.0
ROWS = 8
SLOT = 4
UNROLL = 8
CHUNKS = 4
COLUMN = 9
STATS = 5


def lane_index():
    return lax.broadcasted_iota(jnp.int32, (ROWS, 128), 1)


def row_index():
    return lax.broadcasted_iota(jnp.int32, (ROWS, 128), 0)


def only(mask, value):
    return jnp.where(mask, jnp.float32(value), jnp.float32(0.0))


def tiles_of(ref, level, count):
    return [ref[level, ROWS * t : ROWS * (t + 1), :] for t in range(count)]


def planes_of(ref, count):
    return [ref[ROWS * t : ROWS * (t + 1), :] for t in range(count)]


def put_tiles(ref, level, tiles):
    for t, tile in enumerate(tiles):
        ref[level, ROWS * t : ROWS * (t + 1), :] = tile


def put_planes(ref, tiles):
    for t, tile in enumerate(tiles):
        ref[ROWS * t : ROWS * (t + 1), :] = tile


class Edge:
    def __init__(self, place, axis, held):
        self.place, self.axis, self.held = place, axis, held
        self.size = place.shape[axis]

    def at(self, places):
        total = None
        for position, value in places.items():
            if position in self.held:
                term = only(self.place == position, value)
                total = term if total is None else total + term
        return total

    def shifted(self, field, by):
        return field if by % self.size == 0 else pltpu.roll(field, (-by) % self.size, self.axis)

    def mix(self, field, table):
        total = None
        for by, places in table.items():
            weight = self.at(places)
            if weight is not None:
                term = weight * self.shifted(field, by)
                total = term if total is None else total + term
        return total

    def payload(self, pres, wind, jac):
        partial = self.mix(
            pres,
            {
                1: {0: 8.0, 1: 8.0, 6: 8.0},
                2: {0: -1.0, 1: -1.0},
                -1: {1: -8.0, 6: -8.0, 7: -8.0},
                -2: {6: 1.0, 7: 1.0},
            },
        )
        flux = jac * (wind - CG * partial)
        outer = self.mix(pres, {0: {0: 1.0, 1: 1.0, 6: 1.0, 7: 1.0}})
        return outer + self.mix(flux, {-2: {2: 1.0, 3: 1.0}, 2: {4: 1.0, 5: 1.0}})

    def correct(self, delta, pres, jac, delta_jac, base=0):
        grad = self.mix(
            delta,
            {
                base + 2: {0: 1.0, 1: 1.0},
                base + 3: {0: -8.0},
                base - 2: {6: -1.0, 7: -1.0},
                base - 3: {7: 8.0},
            },
        )
        wind = CG * grad
        own = -(jac * wind)
        far = self.mix(delta, {base: {0: 1.0, 1: 1.0, 6: 1.0, 7: 1.0}}) + CG * delta_jac * self.mix(
            pres, {0: {0: 1.0, 1: 1.0, 6: -1.0, 7: -1.0}, -1: {1: -8.0}, 1: {6: 8.0}}
        )
        spread = (
            self.mix(far, {0: {0: 1.0, 1: 1.0, 6: -1.0, 7: -1.0}})
            + self.mix(far - own, {1: {0: -8.0}, -1: {7: 8.0}})
            + self.mix(
                own,
                {
                    -1: {1: -8.0, 2: -8.0},
                    -2: {2: 1.0, 3: 1.0},
                    1: {5: 8.0, 6: 8.0},
                    2: {4: -1.0, 5: -1.0},
                },
            )
        )
        return wind, CD * spread / jac


LOW, HIGH = (0, 1, 2, 3), (4, 5, 6, 7)


def row_edge():
    return Edge(row_index(), 0, LOW + HIGH)


def lane_edge(held):
    return Edge((lane_index() & 3) + held[0], 1, held)


def both_ends(tiles):
    return jnp.where(row_index() < 4, tiles[0], tiles[-1])


def spread_slots(tile, low):
    lane = lane_index()
    if low:
        out = jnp.where(lane < SLOT, tile, 0.0)
    else:
        out = pltpu.roll(jnp.where(lane >= 128 - SLOT, tile, 0.0), SLOT, 1)
    for by in (SLOT, 4 * SLOT):
        out = (out + pltpu.roll(out, by, 1)) + (
            pltpu.roll(out, 2 * by, 1) + pltpu.roll(out, 3 * by, 1)
        )
    return out + pltpu.roll(out, 64, 1)


class Packer:
    def __init__(self, count):
        self.slot = lax.shift_right_logical(lane_index(), 2)
        self.start = [jnp.zeros((ROWS, 128), jnp.float32)] * (2 * count)
        self.count = count

    def add(self, level, tiles, state):
        before = lax.rem(level + 31, 32)
        rolled = [pltpu.roll(tile, SLOT * level, 1) for tile in tiles]
        low = [jnp.where(self.slot == level, r, s) for r, s in zip(rolled, state)]
        high = [jnp.where(self.slot == before, r, s) for r, s in zip(rolled, state[self.count :])]
        return low + high

    def done(self, state):
        return state[: self.count], [pltpu.roll(s, SLOT, 1) for s in state[self.count :]]


class Closed:
    def __init__(self):
        self.row = row_index()

    def along_y(self, tile):
        pair = tile - pltpu.roll(tile, 126, 1)
        return (pltpu.roll(pair, 2, 1) + pair) - 8.0 * pltpu.roll(pair, 1, 1)

    def moved(self, tiles, by):
        count = len(tiles)
        rolled = [pltpu.roll(tile, by % ROWS, 0) for tile in tiles]
        if by > 0:
            return [jnp.where(self.row < by, rolled[t - 1], rolled[t]) for t in range(count)]
        return [
            jnp.where(self.row >= ROWS + by, rolled[(t + 1) % count], rolled[t])
            for t in range(count)
        ]

    def along_x(self, tiles):
        pair = [f - m for f, m in zip(tiles, self.moved(tiles, -2))]
        return [
            (two + here) - 8.0 * one
            for two, here, one in zip(self.moved(pair, 2), pair, self.moved(pair, 1))
        ]


def even_place():
    return lax.rem(lax.axis_index("gy"), 2) == 0


def put_pair(inner_ref, outer_ref, index, down, up):
    even = even_place()
    put_tiles(inner_ref, index, [jnp.where(even, u, d) for u, d in zip(up, down)])
    put_tiles(outer_ref, index, [jnp.where(even, d, u) for u, d in zip(up, down)])


def get_pair(inner_ref, outer_ref, index, part):
    even = even_place()
    inner, outer = inner_ref[index, part, :], outer_ref[index, part, :]
    return jnp.where(even, outer, inner), jnp.where(even, inner, outer)


def lane_payload(pres, wind, jac):
    low, high = lane_edge(LOW), lane_edge(HIGH)
    down = [low.payload(p, w, j) for p, w, j in zip(pres[0], wind[0], jac[0])]
    up = [high.payload(p, w, j) for p, w, j in zip(pres[1], wind[1], jac[1])]
    return down, up


def levels_of(chunk, share, body, carry):
    for k in range(share):
        carry = body(chunk * share + k, carry)
    return carry


def pack_levels(ref, count, levels):
    packer = Packer(count)

    def step(level, state):
        return packer.add(level, tiles_of(ref, level, count), state)

    return packer.done(lax.fori_loop(0, levels, step, packer.start, unroll=UNROLL))


def kernel_a(
    p_hbm,
    wx_hbm,
    wy_hbm,
    jac_hbm,
    s_hbm,
    rows_ref,
    inner_ref,
    outer_ref,
    pp_ref,
    r_ref,
    i_ref,
    q_ref,
    v_ref,
    stat_ref,
    p_ref,
    wx_ref,
    wy_ref,
    jac_ref,
    s_ref,
    sems,
):
    levels, rows, _ = p_hbm.shape
    count = rows // ROWS
    share = levels // CHUNKS

    def fetch(source, target, sem):
        copy = pltpu.make_async_copy(source, target, sem)
        copy.start()
        return copy

    def chunk(index, source, target, c):
        part = pl.ds(c * share, share)
        return pltpu.make_async_copy(source.at[part], target.at[part], sems.at[index, c])

    for c in range(CHUNKS):
        chunk(0, p_hbm, p_ref, c).start()
        chunk(1, s_hbm, s_ref, c).start()
    for c in range(CHUNKS):
        chunk(2, wy_hbm, wy_ref, c).start()
    ends_in = [
        fetch(jac_hbm, jac_ref, sems.at[3, 0]),
        fetch(wx_hbm, wx_ref, sems.at[3, 1]),
    ]
    packer = Packer(count)

    def down(level, carry):
        state, excess, prod = carry[0], list(carry[1]), list(carry[2])
        for t in range(count):
            part = slice(ROWS * t, ROWS * (t + 1))
            rate = 1.0 / s_ref[level, part, :]
            grown = rate + excess[t]
            inv = 1.0 / (1.0 + grown)
            excess[t] = grown * inv
            prod[t] = prod[t] * inv
            r_ref[level, part, :] = rate
            i_ref[level, part, :] = inv
            q_ref[level, part, :] = prod[t]
        return packer.add(level, tiles_of(p_ref, level, count), state), excess, prod

    def up(step, carry):
        state, value = carry[0], list(carry[1])
        level = levels - 1 - step
        for t in range(count):
            part = slice(ROWS * t, ROWS * (t + 1))
            value[t] = q_ref[level, part, :] + i_ref[level, part, :] * value[t]
            v_ref[level, part, :] = value[t]
        return packer.add(step, tiles_of(wy_ref, step, count), state), value

    ones = [jnp.ones((ROWS, 128), jnp.float32)] * count

    def down_chunk(c, carry):
        chunk(0, p_hbm, p_ref, c).wait()
        chunk(1, s_hbm, s_ref, c).wait()
        return levels_of(c, share, down, carry)

    def up_chunk(c, carry):
        chunk(2, wy_hbm, wy_ref, c).wait()
        return levels_of(c, share, up, carry)

    carry = lax.fori_loop(0, CHUNKS, down_chunk, (packer.start, ones, ones))
    pres = packer.done(carry[0])
    zeros = [jnp.zeros_like(one) for one in ones]
    carry = lax.fori_loop(0, CHUNKS, up_chunk, (packer.start, zeros))
    wind = packer.done(carry[0])
    put_tiles(stat_ref, 0, carry[1])
    stat_ref[1] = q_ref[levels - 1]
    stat_ref[2] = i_ref[levels - 1]
    stat_ref[3] = r_ref[0]
    stat_ref[4] = r_ref[levels - 1]

    for copy in ends_in:
        copy.wait()
    jac = planes_of(jac_ref, count)
    ends = both_ends(jac)
    edge = row_edge()

    def step(level, state):
        rows_ref[level] = edge.payload(
            both_ends(tiles_of(p_ref, level, count)),
            both_ends(tiles_of(wx_ref, level, count)),
            ends,
        )
        return state

    lax.fori_loop(0, levels, step, 0, unroll=UNROLL)
    rows_ref[levels] = ends
    slots = [[spread_slots(j, low) for j in jac] for low in (True, False)]
    put_pair(inner_ref, outer_ref, 1, *slots)
    down_out, up_out = lane_payload(pres, wind, slots)
    put_pair(inner_ref, outer_ref, 0, down_out, up_out)
    put_tiles(pp_ref, 0, pres[0])
    put_tiles(pp_ref, 1, pres[1])


def kernel_n(wy_ref, pw_ref):
    levels, rows, _ = wy_ref.shape
    count = rows // ROWS
    wind = pack_levels(wy_ref, count, levels)
    put_tiles(pw_ref, 0, wind[0])
    put_tiles(pw_ref, 1, wind[1])


def kernel_m(p_ref, wx_ref, wy_ref, jac_ref, nx_ref, ny_ref, ps_ref):
    levels, rows, _ = p_ref.shape
    count = rows // ROWS
    jac = planes_of(jac_ref, count)
    inv_jac = [CD / j for j in jac]
    closed = Closed()

    def step(level, state):
        pres = tiles_of(p_ref, level, count)
        wind_x = tiles_of(wx_ref, level, count)
        wind_y = tiles_of(wy_ref, level, count)
        new_x = [w - CG * d for w, d in zip(wind_x, closed.along_x(pres))]
        new_y = [w - CG * closed.along_y(p) for w, p in zip(wind_y, pres)]
        put_tiles(nx_ref, level, new_x)
        put_tiles(ny_ref, level, new_y)
        spread_x = closed.along_x([j * n for j, n in zip(jac, new_x)])
        spread_y = [closed.along_y(j * n) for j, n in zip(jac, new_y)]
        put_tiles(
            ps_ref,
            level,
            [p - i * (x + y) for p, i, x, y in zip(pres, inv_jac, spread_x, spread_y)],
        )
        return state

    lax.fori_loop(0, levels, step, 0, unroll=UNROLL)


def kernel_b(
    p_ref,
    nxc_ref,
    nyc_ref,
    psc_ref,
    wz_ref,
    jac_ref,
    sx_ref,
    sy_ref,
    r_ref,
    i_ref,
    v_ref,
    pp_ref,
    rows_ref,
    inner_ref,
    outer_ref,
    got_rows_ref,
    got_inner_ref,
    got_outer_ref,
    srows_ref,
    sinner_ref,
    souter_ref,
    got_srows_ref,
    got_sinner_ref,
    got_souter_ref,
    coef_ref,
    far_ref,
    nx_ref,
    ny_ref,
    ps_ref,
    y_ref,
    *outs,
):
    levels, rows, _ = p_ref.shape
    count = rows // ROWS
    last = count - 1
    lane, row = lane_index(), row_index()
    low_edge, high_edge, edge = lane_edge(LOW), lane_edge(HIGH), row_edge()
    wind_fix, low_fix, high_fix = [], [], []
    for t in range(count):
        part = slice(ROWS * t, ROWS * (t + 1))
        jac_low, jac_high = get_pair(sinner_ref, souter_ref, 1, part)
        jac_below, jac_above = get_pair(got_sinner_ref, got_souter_ref, 1, part)
        down, up = get_pair(inner_ref, outer_ref, 0, part)
        below, above = get_pair(got_inner_ref, got_outer_ref, 0, part)
        low_wind, low_star = low_edge.correct(
            below - up, pp_ref[0, part, :], jac_low, low_edge.shifted(jac_below - jac_high, 2)
        )
        high_wind, high_star = high_edge.correct(
            above - down, pp_ref[1, part, :], jac_high, high_edge.shifted(jac_above - jac_low, -2)
        )
        wind_fix.append(low_wind + pltpu.roll(high_wind, 128 - SLOT, 1))
        low_fix.append(low_star)
        high_fix.append(pltpu.roll(high_star, 128 - SLOT, 1))
    ends = srows_ref[levels]
    change = got_srows_ref[levels] - ends
    ends_change = jnp.where(row < 4, edge.shifted(change, -2), edge.shifted(change, 2))
    outer = (lane < 2) | (lane >= 126)
    low_lanes, high_lanes = lane < SLOT, lane >= 128 - SLOT
    first_rows = row < 4

    def star(level, which):
        new_x = {t: nxc_ref[level, ROWS * t : ROWS * (t + 1), :] for t in which}
        stars = {t: psc_ref[level, ROWS * t : ROWS * (t + 1), :] for t in which}
        if 0 in which:
            wind, press = edge.correct(
                got_rows_ref[level] - rows_ref[level],
                jnp.where(first_rows, p_ref[level, :ROWS, :], p_ref[level, ROWS * last :, :]),
                ends,
                ends_change,
                base=4,
            )
            new_x[0] = new_x[0] - jnp.where(first_rows, wind, 0.0)
            new_x[last] = new_x[last] - jnp.where(first_rows, 0.0, wind)
            stars[0] = stars[0] - jnp.where(first_rows, press, 0.0)
            stars[last] = stars[last] - jnp.where(first_rows, 0.0, press)
        back = lax.rem(128 - SLOT * level, 128)
        forces = []
        for t in which:
            part = slice(ROWS * t, ROWS * (t + 1))
            new_y = nyc_ref[level, part, :] - jnp.where(
                outer, pltpu.roll(wind_fix[t], back, 1), 0.0
            )
            fix = jnp.where(
                low_lanes,
                pltpu.roll(low_fix[t], back, 1),
                jnp.where(high_lanes, pltpu.roll(high_fix[t], back, 1), 0.0),
            )
            stars[t] = stars[t] - fix
            forces.append(
                wz_ref[level, part, :] + sx_ref[part, :] * new_x[t] + sy_ref[part, :] * new_y
            )
            nx_ref[level, part, :] = new_x[t]
            ny_ref[level, part, :] = new_y
            ps_ref[level, part, :] = stars[t]
        return [stars[t] for t in which], forces

    def sweep(level, which, below, above, force, value, first):
        values, firsts = [], []
        for k, t in enumerate(which):
            part = slice(ROWS * t, ROWS * (t + 1))
            rhs = r_ref[level, part, :] * (force[k] - vert_coef * (above[k] - below[k]))
            firsts.append(first[k] + v_ref[level, part, :] * rhs)
            values.append((rhs + value[k]) * i_ref[level, part, :])
            y_ref[level, part, :] = values[k]
        return values, firsts

    which = tuple(range(count))
    put_tiles(y_ref, 0, [jnp.zeros((ROWS, 128), jnp.float32)] * count)
    zeros = tiles_of(y_ref, 0, count)

    def step(level, carry):
        below, here, force, value, first = carry
        above, force_next = star(level, which)
        before = jnp.maximum(level - 1, 0)
        new_value, new_first = sweep(before, which, below, above, force, value, first)
        started = jnp.where(level > 0, 1.0, 0.0)
        value = [started * n for n in new_value]
        first = [started * n for n in new_first]
        return here, above, force_next, value, first

    below, here, force, value, first = lax.fori_loop(
        0, levels, step, (zeros, zeros, zeros, zeros, zeros), unroll=2 * UNROLL
    )
    value, first = sweep(levels - 1, which, below, zeros, force, value, first)
    bottom = tiles_of(ps_ref, 0, count)
    interface(first, value, bottom, here, coef_ref, far_ref, outs)


PAIR_COEFS = ("own", "other", "den", "den_end", "den_link", "outer", "total", "facing", "first", "last")


def place_in_column():
    mine = lax.axis_index("lev")
    return (mine == 0) | (mine == 3), mine < 2, lax.rem(mine, 2) == 0


def kernel_s(stat_ref, mate_ref, coef_ref, send_ref):
    outermost, lower, even = place_in_column()
    for t in range(coef_ref.shape[1] // ROWS):
        part = slice(ROWS * t, ROWS * (t + 1))
        mine = [stat_ref[k, part, :] for k in range(STATS)]
        mate = [mate_ref[k, part, :] for k in range(STATS)]
        outer = [jnp.where(outermost, a, b) for a, b in zip(mine, mate)]
        inner = [jnp.where(outermost, b, a) for a, b in zip(mine, mate)]
        outer_end = jnp.where(lower, outer[2], outer[0])
        end = jnp.where(lower, inner[0], inner[2])
        centre = jnp.where(lower, inner[2], inner[0])
        link = inner[1]
        den = 1.0 / (1.0 - end * outer_end)
        den_link = den * link
        weight = outer_end * den_link
        one, zero = jnp.ones_like(den), jnp.zeros_like(den)
        coefs = dict(
            own=jnp.where(outermost, den_link, one),
            other=jnp.where(outermost, zero, weight),
            den=den,
            den_end=den * end,
            den_link=den_link,
            outer=outer_end,
            total=centre + weight * link,
            facing=vert_coef * jnp.where(even, mate[3], mate[4]),
            first=vert_coef * mine[3],
            last=vert_coef * mine[4],
        )
        for k, name in enumerate(PAIR_COEFS):
            coef_ref[k, part, :] = coefs[name]
        send_ref[0, part, :] = coefs["total"]
        send_ref[1, part, :] = vert_coef * jnp.where(lower, inner[4], inner[3])


def interface(first, value, star_first, star_last, coef_ref, far_ref, outs):
    next_ref, cross_ref, own_ref, star_ref, share_ref = outs
    outermost, lower, even = place_in_column()
    for t in range(len(first)):
        part = slice(ROWS * t, ROWS * (t + 1))
        coef = {name: coef_ref[k, part, :] for k, name in enumerate(PAIR_COEFS)}
        sign = jnp.where(lower, 1.0, -1.0)
        star_centre = jnp.where(lower, star_last[t], star_first[t])
        star_outer = jnp.where(lower, star_first[t], star_last[t])
        facing = jnp.where(outermost, coef["facing"], far_ref[1, part, :])
        centre = jnp.where(lower, value[t], first[t]) + sign * facing * star_centre
        outer = jnp.where(lower, first[t], value[t]) - sign * coef["facing"] * star_outer
        total = coef["own"] * centre + coef["other"] * outer
        next_ref[0, part, :] = total
        next_ref[1, part, :] = star_centre
        cross_ref[part, :] = total
        own_ref[part, :] = jnp.where(outermost, centre, outer)
        star_ref[part, :] = jnp.where(even, star_last[t], star_first[t])
        share_ref[part, :] = total


def boundary(
    count,
    got_next_ref,
    got_cross_ref,
    got_own_ref,
    got_star_ref,
    got_share_ref,
    own_ref,
    share_ref,
    coef_ref,
    far_ref,
):
    outermost, lower, _ = place_in_column()
    parts = []
    for t in range(count):
        part = slice(ROWS * t, ROWS * (t + 1))
        coef = {name: coef_ref[k, part, :] for k, name in enumerate(PAIR_COEFS)}
        far_total = far_ref[0, part, :]
        own, got = own_ref[part, :], got_own_ref[part, :]
        this = share_ref[part, :] + got_share_ref[part, :]
        that = got_cross_ref[part, :] + got_next_ref[0, part, :]
        middle = (that + far_total * this) / (1.0 - coef["total"] * far_total)
        from_outer = jnp.where(outermost, own, got)
        from_inner = jnp.where(outermost, got, own)
        between = (
            coef["den"] * from_inner + coef["den_end"] * from_outer + coef["den_link"] * middle
        )
        zero = jnp.zeros_like(own)
        centre = jnp.where(outermost, between, middle)
        outer = jnp.where(outermost, zero, from_outer + coef["outer"] * between)
        mate_star = got_star_ref[part, :]
        star_centre = jnp.where(outermost, mate_star, got_next_ref[1, part, :])
        star_outer = jnp.where(outermost, zero, mate_star)
        below, above = jnp.where(lower, outer, centre), jnp.where(lower, centre, outer)
        star_below = jnp.where(lower, star_outer, star_centre)
        star_above = jnp.where(lower, star_centre, star_outer)
        under = below - coef["first"] * star_below
        over = above + coef["last"] * star_above
        parts.append((below, above, under, over))
    return [[part[k] for part in parts] for k in range(4)]


def finish(count, levels, y_ref, q_ref, i_ref, ps_ref, x_ref, p_ref, column_refs, ready=None):
    lower, upper, under, over = boundary(count, *column_refs)

    def solved(level, above):
        value = tiles_of(y_ref, level, count)
        prod = tiles_of(q_ref, level, count)
        inv = tiles_of(i_ref, level, count)
        out = [(y + q * u) + i * a for y, q, u, i, a in zip(value, prod, lower, inv, above)]
        put_tiles(x_ref, level, out)
        return out

    def pressed(level, above, below):
        star = tiles_of(ps_ref, level, count)
        put_tiles(p_ref, level, [s - vert_coef * (a - b) for s, a, b in zip(star, above, below)])

    def step(index, carry):
        above, here = carry
        level = levels - 1 - index
        below = solved(level, here)
        pressed(jnp.minimum(level + 1, levels - 1), above, below)
        return [jnp.where(index == 0, o, h) for o, h in zip(over, here)], below

    share = levels // CHUNKS

    def chunk(c, carry):
        carry = levels_of(c, share, step, carry)
        if ready is not None:
            ready(c)
        return carry

    above, here = lax.fori_loop(0, CHUNKS, chunk, (over, upper))
    pressed(0, above, under)


def kernel_c(*refs):
    column_refs = refs[:COLUMN]
    y_ref, q_ref, i_ref, ps_ref, wx_ref, pw_ref, srows_ref, sinner_ref, souter_ref = refs[
        COLUMN : COLUMN + 9
    ]
    x_ref, p_ref, rows_ref, inner_ref, outer_ref, pp_ref = refs[COLUMN + 9 :]
    levels, rows, _ = y_ref.shape
    count = rows // ROWS
    edge = row_edge()
    ends = srows_ref[levels]
    finish(count, levels, y_ref, q_ref, i_ref, ps_ref, x_ref, p_ref, column_refs)

    def step(level, state):
        rows_ref[level] = edge.payload(
            both_ends(tiles_of(p_ref, level, count)),
            both_ends(tiles_of(wx_ref, level, count)),
            ends,
        )
        return state

    lax.fori_loop(0, levels, step, 0, unroll=UNROLL)
    pres = pack_levels(p_ref, count, levels)
    wind = tiles_of(pw_ref, 0, count), tiles_of(pw_ref, 1, count)
    slots = zip(
        *(
            get_pair(sinner_ref, souter_ref, 1, slice(ROWS * t, ROWS * (t + 1)))
            for t in range(count)
        )
    )
    down, up = lane_payload(pres, wind, list(slots))
    put_pair(inner_ref, outer_ref, 0, down, up)
    put_tiles(pp_ref, 0, pres[0])
    put_tiles(pp_ref, 1, pres[1])


def kernel_d(*refs):
    column_refs = refs[:COLUMN]
    y_ref, q_ref, i_ref, ps_ref = refs[COLUMN : COLUMN + 4]
    x_hbm, p_hbm, x_ref, p_ref, sems = refs[COLUMN + 4 :]
    levels, rows, _ = y_ref.shape
    share = levels // CHUNKS

    def copy(index, source, target, c):
        part = pl.ds(c * share, share)
        return pltpu.make_async_copy(source.at[part], target.at[part], sems.at[index, c])

    def ready(step):
        c = CHUNKS - 1 - step
        copy(0, x_ref, x_hbm, c).start()

        @pl.when(step > 0)
        def _():
            copy(1, p_ref, p_hbm, c + 1).start()

    finish(
        rows // ROWS,
        levels,
        y_ref,
        q_ref,
        i_ref,
        ps_ref,
        x_ref,
        p_ref,
        column_refs,
        ready,
    )
    copy(1, p_ref, p_hbm, 0).start()
    for c in range(CHUNKS):
        copy(0, x_ref, x_hbm, c).wait()
        copy(1, p_ref, p_hbm, c).wait()


def call(kernel, name, shapes, *args, far_in=(), far_out=False, scratch=(), keep=()):
    near, far = pl.BlockSpec(memory_space=pltpu.VMEM), pl.BlockSpec(memory_space=pl.ANY)
    size = sum(a.size for a in args) + sum(functools.reduce(lambda a, b: a * b, s) for s in shapes)
    if len(far_in) == len(args):
        args = [pltpu.with_memory_space_constraint(a, pltpu.HBM) for a in args]
    return pl.pallas_call(
        kernel,
        out_shape=[
            pltpu.VMEM(s, jnp.float32) if k in keep else jax.ShapeDtypeStruct(s, jnp.float32)
            for k, s in enumerate(shapes)
        ],
        in_specs=[far if k in far_in else near for k in range(len(args))],
        out_specs=[far if far_out else near] * len(shapes),
        scratch_shapes=list(scratch),
        compiler_params=pltpu.CompilerParams(vmem_limit_bytes=32 * 1024 * 1024),
        cost_estimate=pl.CostEstimate(
            flops=8 * size, bytes_accessed=4 * size, transcendentals=0
        ),
        name=name,
    )(*args)


def swap(value, axis, partner):
    count = lax.axis_size(axis)
    return lax.ppermute(value, axis, [(i, partner(i)) for i in range(count)])


def exchange_rows(rows):
    count = lax.axis_size("gx")
    if count == 2:
        return swap(rows, "gx", lambda i: 1 - i)
    down = swap(rows[:, : ROWS // 2], "gx", lambda i: (i - 1) % count)
    up = swap(rows[:, ROWS // 2 :], "gx", lambda i: (i + 1) % count)
    return jnp.concatenate([down, up], axis=1)


def exchange_lanes(inner, outer):
    count = lax.axis_size("gy")
    got_inner = swap(inner, "gy", lambda i: i ^ 1)
    got_outer = swap(outer, "gy", lambda i: (i + 1 if i % 2 else i - 1) % count)
    return got_inner, got_outer


def exchange_column(following, cross, own, star, share):
    got_cross = swap(cross, "lev", lambda i: i ^ 2)
    got_next = swap(following, "lev", lambda i: i ^ 3)
    mates = [swap(value, "lev", lambda i: i ^ 1) for value in (own, star, share)]
    return [got_next, got_cross, *mates, own, share]


def local(wind_x, wind_y, wind_z, pressure, jacobian, slope_x, slope_y, stiffness):
    field = wind_x.shape
    levels, rows, lanes = field
    plane = (rows, lanes)
    pair = (2,) + plane
    assert lanes == 128 and levels * SLOT == 128 and rows % ROWS == 0
    assert lax.axis_size("lev") == 4 and lax.axis_size("gy") % 2 == 0

    edge, inner, outer, ends, rate, inv, prod, gain, stat, *fields = call(
        kernel_a,
        "start",
        [(levels + 1, ROWS, lanes), pair, (3,) + plane, pair]
        + [field] * 4
        + [(STATS,) + plane]
        + [field] * 3,
        pressure,
        wind_x,
        wind_y,
        jacobian,
        stiffness,
        far_in=(0, 1, 2, 3, 4),
        keep=(9, 10, 11),
        scratch=[
            pltpu.VMEM(plane, jnp.float32),
            pltpu.VMEM(field, jnp.float32),
            pltpu.SemaphoreType.DMA((4, CHUNKS)),
        ],
    )
    pressure, wind_x, wind_y = fields
    mate = swap(stat, "lev", lambda i: i ^ 1)
    coef, send = call(kernel_s, "pairs", [(len(PAIR_COEFS),) + plane, pair], stat, mate)
    far = swap(send, "lev", lambda i: i ^ 2)
    sent = (edge, inner, outer)
    got = (exchange_rows(edge),) + exchange_lanes(inner, outer)
    static_edges = sent + got
    for substep in range(SUBSTEPS):
        closed = call(
            kernel_m, "interior", [field, field, field], pressure, wind_x, wind_y, jacobian
        )
        wind_x, wind_y, star, value, *faces = call(
            kernel_b,
            "sweep",
            [field] * 4 + [pair] + [plane] * 4,
            pressure,
            *closed,
            wind_z,
            jacobian,
            slope_x,
            slope_y,
            rate,
            inv,
            gain,
            ends,
            *sent,
            *got,
            *static_edges,
            coef,
            far,
            keep=tuple(range(9)),
        )
        column = exchange_column(*faces) + [coef, far]
        if substep < SUBSTEPS - 1:
            (packed,) = call(kernel_n, "pack", [pair], wind_y)
            wind_z, pressure, edge, inner, outer, ends = call(
                kernel_c,
                "finish",
                [field, field, (levels, ROWS, lanes), (1,) + plane, pair, pair],
                *column,
                value,
                prod,
                inv,
                star,
                wind_x,
                packed,
                *static_edges[:3],
            )
            sent = (edge, inner, outer)
            got = (exchange_rows(edge),) + exchange_lanes(inner, outer)
        else:
            wind_z, pressure = call(
                kernel_d,
                "last",
                [field] * 2,
                *column,
                value,
                prod,
                inv,
                star,
                far_out=True,
                scratch=[
                    pltpu.VMEM(field, jnp.float32),
                    pltpu.VMEM(field, jnp.float32),
                    pltpu.SemaphoreType.DMA((2, CHUNKS)),
                ],
            )
    return wind_x, wind_y, wind_z, pressure


def solution(mesh):
    field = P("lev", "gx", "gy")
    column = P("gx", "gy")
    return jax.shard_map(
        local,
        mesh=mesh,
        in_specs=(field,) * 4 + (column,) * 3 + (field,),
        out_specs=(field,) * 4,
        check_vma=False,
    )
```
